32 devices in a mesh: group: 4 (over y, core), tensor: 8 (over z, x).
Axes of the slice: x: 2, y: 2, z: 4, core: 2. Of those that a mesh axis runs over, the one named last changes fastest.
Arguments:
- resp_query: bfloat16 [256, 4096], P('group', 'tensor'), may hold values from -80 to 80
- resp_key: bfloat16 [256, 4096], P('group', 'tensor'), may hold values from -4 to 4
- resp_value: bfloat16 [256, 4096], P('group', 'tensor'), may hold values from -8 to 8
- prompt_keys: bfloat16 [2048, 4096], P('group', 'tensor'), may hold values from -5 to 5
- prompt_values: bfloat16 [2048, 4096], P('group', 'tensor'), may hold values from -8 to 8
- prompt_of: int32 [8], P('group'), may hold values from 0 to 3
- lengths: int32 [8], P('group'), may hold values from 1 to 32
- residual: bfloat16 [256, 5120], P('group'), may hold values from -4 to 4
- out_weight: bfloat16 [4096, 5120], P('tensor'), may hold values from -0.09375 to 0.09375
- norm_gain: bfloat16 [5120], replicated, may hold values from 0.25 to 1.75
- lm_weight: bfloat16 [5120, 98304], P(None, ('group', 'tensor')), may hold values from -10 to 10
- targets: int32 [256], replicated, may hold values from 0 to 98303
Outputs:
- logprobs: float32 [256], P(('group', 'tensor'))
The draws below stay inside these ranges and needn't reach their ends.
Inputs may be any that keep to these rules, and one draw needn't show every extreme that they name: prompt_of[r] names the prompt whose keys and values precede response r.
All inputs are finite; a program needn't handle non-finite values.
Results may differ from the reference program's by a relative error of at most 0.0013.
Values may be sent and summed in bfloat16 or wider, within the bound.
No kernel may reach another device: no remote copies, remote signals or barrier semaphores. Data moves between devices by JAX's collectives and lax.ppermute only.
A program may use at most 128 MiB of HBM per device.

```python
import math
import jax
import jax.numpy as jnp
import numpy as np
from jax import lax

D = 5120
HEADS = 32
HEAD_DIM = 128
VOCAB = 98304
PLEN = 512
LEN = 32
PROMPTS = 4
RESPONSES = 8
TOKENS = 256


def shared_keys(key):
    return jnp.clip(jax.random.normal(key, (TOKENS, HEADS * HEAD_DIM), jnp.float32), -4.0, 4.0)


def draw_resp_key(key, part):
    base = shared_keys(key)
    return base.astype(jnp.bfloat16)


def draw_resp_query(key, part):
    key = jax.random.fold_in(key, 12)
    fresh = jnp.clip(1.5 * jax.random.normal(key, (TOKENS, HEADS * HEAD_DIM), jnp.float32), -8.0, 8.0)
    return fresh.astype(jnp.bfloat16)


def draw_lm_weight(key, part):
    key = jax.random.fold_in(key, 13)
    values = jnp.clip(jax.random.normal(key, (D, VOCAB), jnp.float32), -6.0, 6.0) * (3.0 / math.sqrt(D))
    values = jnp.clip(values, -10.0, 10.0)
    return values.astype(jnp.bfloat16)


def place_ends(values, rng, smallest, largest):
    extent = values.shape
    place = [jax.random.randint(jax.random.fold_in(rng, axis), (), 0, extent[axis]) for axis in range(len(extent))]
    values = values.at[tuple(place)].set(smallest)
    longest = extent.index(max(extent))
    place[longest] = (place[longest] + 1) % extent[longest]
    return values.at[tuple(place)].set(largest)


def block_scale(rng, dims, cuts, low, high):
    loudness = 1.0
    for dim, shards_of in cuts:
        heights = jax.random.uniform(jax.random.fold_in(jax.random.fold_in(rng, 6), dim), (shards_of,), jnp.float32, low / len(cuts), high / len(cuts))
        loudness = loudness * jnp.repeat(jnp.exp(heights), dims[dim] // shards_of).reshape((-1,) + (1,) * (len(dims) - 1 - dim))
    return loudness


def rank_table(amount, skew):
    loads = [(1 << 20) // math.isqrt(rank ** skew) + 1 for rank in range(1, amount + 1)]
    scale = 1 + sum(loads) // (1 << 30)
    return np.cumsum(np.array([max(1, weight // scale) for weight in loads]))


def ranked_ids(key, dims, count, skew):
    listing = rank_table(count, skew)
    lot = jax.random.randint(jax.random.fold_in(key, 1), dims, 0, int(listing[count - 1]))
    standing = jnp.searchsorted(jnp.asarray(listing, jnp.int32), lot, side="right")
    return jax.random.permutation(jax.random.fold_in(key, 2), count)[standing].astype(jnp.int32)


def ranked_wide(own_key, dims, amount, slope):
    loads = [min(1 << octave, amount + 1 - (1 << octave)) * (1 << 20) // math.isqrt((1 << octave) ** slope) + 1 for octave in range((amount + 1).bit_length()) if 1 << octave <= amount]
    deviation = 1 + sum(loads) // (1 << 30)
    grid = np.cumsum(np.array([max(1, weight // deviation) for weight in loads]))
    ticket = jax.random.randint(jax.random.fold_in(own_key, 1), dims, 0, int(grid[len(loads) - 1]))
    start = jnp.left_shift(1, jnp.searchsorted(jnp.asarray(grid, jnp.int32), ticket, side="right").astype(jnp.int32))
    grade = start - 1 + jax.random.randint(jax.random.fold_in(own_key, 4), dims, 0, 1 << 30) % jnp.minimum(start, amount + 1 - start)
    return jax.random.permutation(jax.random.fold_in(own_key, 2), amount)[grade].astype(jnp.int32)


def scatter_about(rng, extent, deviation, most, cuts=(), kind=jnp.bfloat16):
    values = jax.random.normal(rng, extent, jnp.float32) * deviation
    if len(cuts) > 0:
        values = block_scale(rng, extent, cuts, -0.22, 0.18) * values
    return jnp.clip(values, min=-most, max=most).astype(kind)


def setup_inputs(seed: int = 0) -> dict:
    key_of = jax.random.split(jax.random.key(seed), 13)
    return {
        "resp_query": draw_resp_query(jax.random.fold_in(key_of[12], 71), 0),
        "resp_key": draw_resp_key(jax.random.fold_in(key_of[12], 71), 0),
        "resp_value": scatter_about(key_of[2], (TOKENS, HEADS * HEAD_DIM), 2.0, 8.0, ((0, 4), (1, 8))),
        "prompt_keys": scatter_about(key_of[3], (PROMPTS * PLEN, HEADS * HEAD_DIM), 1.0, 5.0, ((0, 4), (1, 8))),
        "prompt_values": scatter_about(key_of[4], (PROMPTS * PLEN, HEADS * HEAD_DIM), 2.0, 8.0, ((0, 4), (1, 8))),
        "prompt_of": place_ends(ranked_ids(key_of[5], (RESPONSES,), PROMPTS, 2), jax.random.fold_in(key_of[5], 3), 0, PROMPTS - 1).astype(jnp.int32),
        "lengths": place_ends(jax.random.randint(key_of[6], (RESPONSES,), 1, LEN + 1), jax.random.fold_in(key_of[6], 1), 1, LEN).astype(jnp.int32),
        "residual": scatter_about(key_of[7], (TOKENS, D), 0.25, 4.0, ((0, 4),)),
        "out_weight": scatter_about(key_of[8], (HEADS * HEAD_DIM, D), (HEADS * HEAD_DIM) ** -0.5, 0.09375, ((0, 8),)),
        "norm_gain": jnp.clip(1.0 + 0.15 * jax.random.normal(key_of[9], (D,), jnp.float32), 0.25, 1.75).astype(jnp.bfloat16),
        "lm_weight": draw_lm_weight(jax.random.fold_in(key_of[12], 71), 0),
        "targets": place_ends(ranked_wide(key_of[11], (TOKENS,), VOCAB, 2), jax.random.fold_in(key_of[11], 3), 0, VOCAB - 1).astype(jnp.int32),
    }


NEG = -1e+30

def normalize(hidden, norm_gain):
    squares = lax.optimization_barrier(jnp.mean(hidden * hidden, axis=-1, keepdims=True))
    return (hidden * lax.rsqrt(squares + 1e-06) * norm_gain.astype(jnp.float32)).astype(jnp.bfloat16)

def reference(resp_query, resp_key, resp_value, prompt_keys, prompt_values, prompt_of, lengths, residual, out_weight, norm_gain, lm_weight, targets):
    factor = HEAD_DIM ** (-0.5)
    queries = resp_query.reshape(RESPONSES, LEN, HEADS, HEAD_DIM)
    own_keys = resp_key.reshape(RESPONSES, LEN, HEADS, HEAD_DIM)
    own_values = resp_value.reshape(RESPONSES, LEN, HEADS, HEAD_DIM)
    cache_keys = prompt_keys.reshape(PROMPTS, PLEN, HEADS, HEAD_DIM)
    cache_values = prompt_values.reshape(PROMPTS, PLEN, HEADS, HEAD_DIM)
    positions = jnp.arange(LEN, dtype=jnp.int32)

    def respond(number):
        owner = prompt_of[number]
        key_block = jnp.concatenate([cache_keys[owner], own_keys[number]], axis=0).astype(jnp.float32)
        value_block = jnp.concatenate([cache_values[owner], own_values[number]], axis=0).astype(jnp.float32)
        causal = (positions[None, :] <= positions[:, None]) & (positions[None, :] < lengths[number])
        allowed = jnp.concatenate([jnp.ones((LEN, PLEN), dtype=bool), causal], axis=1)
        scores = jnp.einsum('qhd,khd->hqk', queries[number].astype(jnp.float32), key_block, precision=lax.Precision.HIGHEST) * factor
        scores = jnp.where(allowed[None], scores, NEG)
        peak = lax.optimization_barrier(jnp.max(scores, axis=2, keepdims=True))
        weights = jnp.where(allowed[None], jnp.exp(scores - peak), 0.0)
        mixed = jnp.einsum('hqk,khd->qhd', weights, value_block, precision=lax.Precision.HIGHEST)
        return (mixed / lax.optimization_barrier(jnp.sum(weights, axis=2)).T[:, :, None]).astype(jnp.bfloat16)
    attended = lax.map(respond, jnp.arange(RESPONSES, dtype=jnp.int32)).reshape(TOKENS, HEADS * HEAD_DIM)
    projected = jnp.dot(attended, out_weight, preferred_element_type=jnp.float32)
    normed = normalize(residual.astype(jnp.float32) + projected, norm_gain)
    block = math.gcd(VOCAB, 8192)

    def vocab_step(state, number):
        peak, totals, picked = state
        offset = number * block
        columns = lax.dynamic_slice_in_dim(lm_weight, offset, block, 1)
        logits = jnp.dot(normed, columns, preferred_element_type=jnp.float32)
        newpeak = jnp.maximum(peak, lax.optimization_barrier(jnp.max(logits, axis=1)))
        totals = totals * jnp.exp(peak - newpeak) + lax.optimization_barrier(jnp.sum(jnp.exp(logits - newpeak[:, None]), axis=1))
        labels = offset + jnp.arange(block, dtype=jnp.int32)
        picked = picked + lax.optimization_barrier(jnp.sum(jnp.where(targets[:, None] == labels[None, :], logits, 0.0), axis=1))
        return ((newpeak, totals, picked), None)
    start_state = (jnp.full((TOKENS,), NEG, jnp.float32), jnp.zeros((TOKENS,), jnp.float32), jnp.zeros((TOKENS,), jnp.float32))
    final_state, unused = lax.scan(vocab_step, start_state, jnp.arange(VOCAB // block, dtype=jnp.int32))
    peak, totals, picked = final_state
    logprob_all = picked - peak - jnp.log(totals)
    token_index = jnp.arange(TOKENS, dtype=jnp.int32)
    token_len = lengths[token_index // LEN]
    return jnp.where(token_index % LEN < token_len, logprob_all, 0.0)
```

```python
import functools

import jax
import jax.numpy as jnp
from jax import lax
from jax.experimental import pallas as pl
from jax.experimental.pallas import tpu as pltpu
from jax.sharding import PartitionSpec as P

HEAD_DIM = 128
PLEN = 512
NEG = -1e30
BF16 = jnp.bfloat16
F32 = jnp.float32
VMEM_LIMIT = 56 * 1024 * 1024


def params():
    return pltpu.CompilerParams(vmem_limit_bytes=VMEM_LIMIT)


def vmem():
    return pl.BlockSpec(memory_space=pltpu.VMEM)


def smem():
    return pl.BlockSpec(memory_space=pltpu.SMEM)


def swap(x, axis, distance, size):
    return lax.ppermute(x, axis, [(i, i ^ distance) for i in range(size)])


def head_attend(q, k, v, allowed):
    scores = lax.dot_general(q, k, (((1,), (1,)), ((), ())), preferred_element_type=F32)
    scores = scores * (HEAD_DIM**-0.5)
    if allowed is not None:
        scores = jnp.where(allowed, scores, NEG)
    peak = jnp.max(scores, axis=1, keepdims=True)
    weights = jnp.exp(scores - peak)
    if allowed is not None:
        weights = jnp.where(allowed, weights, 0.0)
    total = jnp.sum(weights, axis=1, keepdims=True)
    high = weights.astype(BF16)
    low = (weights - high.astype(F32)).astype(BF16)
    mixed = jnp.dot(high, v, preferred_element_type=F32) + jnp.dot(
        low, v, preferred_element_type=F32
    )
    return mixed / total, peak + jnp.log(total)


def pack_logs(logs, rows):
    lane = lax.broadcasted_iota(jnp.int32, (rows, 128), 1)
    packed = jnp.zeros((rows, 128), F32)
    for head, log in enumerate(logs):
        first = log.astype(BF16).astype(F32)
        second = (log - first).astype(BF16).astype(F32)
        third = log - first - second
        for part, value in enumerate((first, second, third)):
            packed = jnp.where(lane == 3 * head + part, value, packed)
    return packed.astype(BF16)


def own_kernel(heads, seq, lengths_ref, q_ref, rk_ref, rv_ref, k_ref, v_ref, own_ref, pre_ref):
    rows = q_ref.shape[0]
    row = lax.broadcasted_iota(jnp.int32, (rows, rows), 0)
    col = lax.broadcasted_iota(jnp.int32, (rows, rows), 1)
    live = jnp.zeros((rows, rows), jnp.int32)
    for r in range(rows // seq):
        live = jnp.where(col // seq == r, lengths_ref[r], live)
    allowed = (row // seq == col // seq) & (col <= row) & (col % seq < live)
    logs, pre_logs = [], []
    for h in range(heads):
        part = slice(h * HEAD_DIM, (h + 1) * HEAD_DIM)
        mixed, log = head_attend(q_ref[:, part], rk_ref[:, part], rv_ref[:, part], allowed)
        own_ref[:, part] = mixed
        logs.append(log)
        mixed, log = head_attend(q_ref[:, part], k_ref[:, part], v_ref[:, part], None)
        pre_ref[:, part] = mixed
        pre_logs.append(log)
    lane = lax.broadcasted_iota(jnp.int32, (rows, 128), 1)
    for ref, values in ((own_ref, logs), (pre_ref, pre_logs)):
        packed = jnp.zeros((rows, 128), F32)
        for h in range(heads):
            packed = jnp.where(lane == h, values[h], packed)
        ref[:, heads * HEAD_DIM :] = packed


def prefix_kernel(heads, count, *refs):
    q_refs, (k_ref, v_ref), out_refs = refs[:count], refs[count : count + 2], refs[count + 2 :]
    rows = q_refs[0].shape[0]
    logs = [[] for _ in range(count)]
    for h in range(heads):
        part = slice(h * HEAD_DIM, (h + 1) * HEAD_DIM)
        q = jnp.concatenate([ref[:, part] for ref in q_refs], axis=0)
        mixed, log = head_attend(q, k_ref[:, part], v_ref[:, part], None)
        for i in range(count):
            out_refs[i][:, part] = mixed[i * rows : (i + 1) * rows].astype(BF16)
            logs[i].append(log[i * rows : (i + 1) * rows])
    for i in range(count):
        out_refs[i][:, heads * HEAD_DIM :] = pack_logs(logs[i], rows)


def project_kernel(heads, seq, count, share, plan_ref, *refs):
    own_ref, pre_ref = refs[:2]
    got_refs = refs[2 : 2 + count]
    weight_ref, send_ref, keep_ref, attended_ref, partial_ref = refs[2 + count :]
    rows = own_ref.shape[0]
    blocks = rows // share

    @pl.when(pl.program_id(0) == 0)
    def _():
        row = lax.broadcasted_iota(jnp.int32, (rows, 1), 0)
        wanted = jnp.zeros((rows, 1), jnp.int32)
        for r in range(rows // seq):
            wanted = jnp.where(row // seq == r, plan_ref[1 + count + 1 + r], wanted)
        for h in range(heads):
            part = slice(h * HEAD_DIM, (h + 1) * HEAD_DIM)
            at = heads * HEAD_DIM
            logs = [own_ref[:, at + h : at + h + 1]]
            values = [own_ref[:, part]]
            pre_log = pre_ref[:, at + h : at + h + 1]
            logs.append(jnp.where(wanted == plan_ref[1], pre_log, NEG))
            values.append(pre_ref[:, part])
            for i, ref in enumerate(got_refs):
                three = ref[:, at : at + 128].astype(F32)
                log = (
                    three[:, 3 * h : 3 * h + 1]
                    + three[:, 3 * h + 1 : 3 * h + 2]
                    + three[:, 3 * h + 2 : 3 * h + 3]
                )
                logs.append(jnp.where(wanted == plan_ref[2 + i], log, NEG))
                values.append(ref[:, part].astype(F32))
            peak = functools.reduce(jnp.maximum, logs)
            loads = [jnp.exp(log - peak) for log in logs]
            total = functools.reduce(jnp.add, loads)
            mixed = functools.reduce(jnp.add, [w * v for w, v in zip(loads, values)])
            attended_ref[:, part] = (mixed / total).astype(BF16)

    partial = jnp.dot(attended_ref[...], weight_ref[...], preferred_element_type=F32)
    for b in range(blocks):
        partial_ref[b] = partial[b * share : (b + 1) * share]
    me = plan_ref[0]
    for d in range(blocks):
        block = partial_ref[me ^ d]
        if d % 2:
            send_ref[d // 2] = block.astype(BF16)
        else:
            keep_ref[d // 2] = block


def fold_kernel(keep_ref, got_ref, *out_refs):
    for i, ref in enumerate(out_refs):
        ref[...] = (keep_ref[i] + got_ref[i].astype(F32)).astype(ref.dtype)


def norm_kernel(plan_ref, residual_ref, gain_ref, own_ref, *refs):
    got_refs, out_ref = refs[:-1], refs[-1]
    hidden = own_ref[...]
    for ref in got_refs:
        hidden = hidden + ref[...].astype(F32)
    hidden = hidden + residual_ref[0].astype(F32)
    squares = jnp.mean(hidden * hidden, axis=-1, keepdims=True)
    out_ref[...] = (hidden * lax.rsqrt(squares + 1e-06) * gain_ref[...].astype(F32)).astype(BF16)


def logits_kernel(left_ref, right_ref, target_ref, weight_ref, out_ref, x_ref, peak_ref, sum_ref, pick_ref):
    step = pl.program_id(0)
    half = left_ref.shape[0]
    rows = 2 * half
    width = weight_ref.shape[1]

    @pl.when(step == 0)
    def _():
        x_ref[:half] = left_ref[...]
        x_ref[half:] = right_ref[...]
        peak_ref[...] = jnp.full_like(peak_ref, NEG)
        sum_ref[...] = jnp.zeros_like(sum_ref)
        pick_ref[...] = jnp.zeros_like(pick_ref)

    logits = jnp.dot(x_ref[...], weight_ref[...], preferred_element_type=F32)
    parts = [logits[:, c : c + 128] for c in range(0, width, 128)]
    if width % 128:
        spare = jnp.full((rows, 128 - width % 128), NEG, F32)
        parts[-1] = jnp.concatenate([parts[-1], spare], axis=1)
    lane = lax.broadcasted_iota(jnp.int32, (rows, 128), 1) + step * width
    peak = peak_ref[...]
    higher = functools.reduce(jnp.maximum, parts, peak)
    total = sum_ref[...] * jnp.exp(peak - higher)
    picked = pick_ref[...]
    target = target_ref[...]
    for c, part in enumerate(parts):
        total = total + jnp.exp(part - higher)
        picked = picked + jnp.where(lane + c * 128 == target, part, 0.0)
    peak_ref[...] = higher
    sum_ref[...] = total
    pick_ref[...] = picked

    @pl.when(step == pl.num_programs(0) - 1)
    def _():
        peak = jnp.max(higher, axis=1, keepdims=True)
        sums = jnp.sum(total * jnp.exp(higher - peak), axis=1, keepdims=True)
        pick = jnp.sum(picked, axis=1, keepdims=True)
        place = lax.broadcasted_iota(jnp.int32, (rows, 128), 1)
        three = jnp.where(place == 0, peak, jnp.where(place == 1, sums, pick))
        out_ref[...] = jnp.transpose(three)[:8]


def local(
    group_size,
    tensor_size,
    resp_query,
    resp_key,
    resp_value,
    prompt_keys,
    prompt_values,
    prompt_of,
    lengths,
    residual,
    out_weight,
    norm_gain,
    lm_weight,
    targets,
):
    rows, span = resp_query.shape
    heads = span // HEAD_DIM
    seq = rows // prompt_of.shape[0]
    key_rows = prompt_keys.shape[0]
    assert PLEN % key_rows == 0
    share = rows // tensor_size
    depth = out_weight.shape[1]
    vocab = lm_weight.shape[1]
    group_index = lax.axis_index("group")
    tensor_index = lax.axis_index("tensor")
    i32 = jnp.int32

    distances = list(range(1, group_size))
    queries = [swap(resp_query, "group", d, group_size) for d in distances]
    own, prefix = pl.pallas_call(
        functools.partial(own_kernel, heads, seq),
        out_shape=[jax.ShapeDtypeStruct((rows, span + 128), F32)] * 2,
        in_specs=[smem()] + [vmem()] * 5,
        out_specs=[vmem()] * 2,
        compiler_params=params(),
        name="own_attention",
    )(lengths, resp_query, resp_key, resp_value, prompt_keys, prompt_values)
    answers = pl.pallas_call(
        functools.partial(prefix_kernel, heads, len(distances)),
        out_shape=[jax.ShapeDtypeStruct((rows, span + 128), BF16)] * len(distances),
        in_specs=[vmem()] * (len(distances) + 2),
        out_specs=[vmem()] * len(distances),
        compiler_params=params(),
        name="prefix_attention",
    )(*queries, prompt_keys, prompt_values)
    got = [swap(x, "group", d, group_size) for x, d in zip(answers, distances)]

    holders = (group_index ^ jnp.arange(group_size, dtype=i32)) * key_rows // PLEN
    plan = jnp.concatenate([tensor_index.astype(i32)[None], holders, prompt_of])
    wide = 640 if depth % 640 == 0 else depth
    half_blocks = tensor_size // 2
    send, keep = pl.pallas_call(
        functools.partial(project_kernel, heads, seq, len(distances), share),
        out_shape=[
            jax.ShapeDtypeStruct((half_blocks, share, depth), BF16),
            jax.ShapeDtypeStruct((half_blocks, share, depth), F32),
        ],
        grid=(depth // wide,),
        in_specs=[smem()]
        + [pl.BlockSpec((rows, span + 128), lambda n: (0, 0))] * (2 + len(distances))
        + [pl.BlockSpec((span, wide), lambda n: (0, n))],
        out_specs=[pl.BlockSpec((half_blocks, share, wide), lambda n: (0, 0, n))] * 2,
        scratch_shapes=[pltpu.VMEM((rows, span), BF16), pltpu.VMEM((tensor_size, share, wide), F32)],
        compiler_params=params(),
        name="project",
    )(plan, own, prefix, *got, out_weight)

    got = swap(send, "tensor", 1, tensor_size)
    far = list(range(2, tensor_size, 2))
    folded = pl.pallas_call(
        fold_kernel,
        out_shape=[jax.ShapeDtypeStruct((share, depth), F32)]
        + [jax.ShapeDtypeStruct((share, depth), BF16)] * len(far),
        in_specs=[vmem()] * 2,
        out_specs=[vmem()] * (1 + len(far)),
        compiler_params=params(),
        name="fold",
    )(keep, got)
    got = [swap(x, "tensor", d, tensor_size) for x, d in zip(folded[1:], far)]
    whole = lambda shape: pl.BlockSpec(shape, lambda n, plan: (0,) * len(shape))
    normed = pl.pallas_call(
        norm_kernel,
        out_shape=jax.ShapeDtypeStruct((share, depth), BF16),
        grid_spec=pltpu.PrefetchScalarGridSpec(
            num_scalar_prefetch=1,
            grid=(1,),
            in_specs=[pl.BlockSpec((1, share, depth), lambda n, plan: (plan[0], 0, 0)), whole((1, depth))]
            + [whole((share, depth))] * (1 + len(far)),
            out_specs=whole((share, depth)),
        ),
        compiler_params=params(),
        name="norm",
    )(plan, residual.reshape(tensor_size, share, depth), norm_gain[None], folded[0], *got)

    order = [0] + far
    tokens = jnp.stack([normed] + [swap(normed, "tensor", d, tensor_size) for d in far])
    tokens = jnp.concatenate([tokens, swap(tokens, "tensor", 1, tensor_size)])
    order = order + [d + 1 for d in order]
    above = list(range(2, group_size, 2))
    tokens = jnp.concatenate([tokens] + [swap(tokens, "group", d, group_size) for d in above])
    tokens = tokens.reshape(-1, depth)
    other = swap(tokens, "group", 1, group_size)
    group_order = [0] + above
    group_order = group_order + [d + 1 for d in group_order]
    group_ids = group_index ^ jnp.asarray(group_order, i32)
    tensor_ids = tensor_index ^ jnp.asarray(order, i32)
    block_ids = (group_ids[:, None] * tensor_size + tensor_ids[None, :]).reshape(-1)
    device = group_index * tensor_size + tensor_index
    table = targets.reshape(-1, share)
    wanted = jnp.take(table, block_ids, axis=0).reshape(-1, 1) - device * vocab
    wanted = jnp.where((wanted >= 0) & (wanted < vocab), wanted, -1)

    total_rows = 2 * tokens.shape[0]
    narrow = 256
    stats = pl.pallas_call(
        logits_kernel,
        out_shape=jax.ShapeDtypeStruct((8, total_rows), F32),
        grid=(vocab // narrow,) if vocab % narrow == 0 else (1,),
        in_specs=[
            pl.BlockSpec(tokens.shape, lambda n: (0, 0)),
            pl.BlockSpec(tokens.shape, lambda n: (0, 0)),
            pl.BlockSpec((total_rows, 1), lambda n: (0, 0)),
            pl.BlockSpec((depth, narrow if vocab % narrow == 0 else vocab), lambda n: (0, n)),
        ],
        out_specs=pl.BlockSpec((8, total_rows), lambda n: (0, 0)),
        scratch_shapes=[pltpu.VMEM((total_rows, depth), BF16)]
        + [pltpu.VMEM((total_rows, 128), F32)] * 3,
        compiler_params=params(),
        name="logits",
    )(tokens, other, wanted, lm_weight)

    blocks = stats[:3].reshape(3, -1, share).transpose(1, 0, 2).reshape(-1, 3 * share)
    ids = jnp.arange(group_size * tensor_size, dtype=i32)
    group_step = group_index ^ (ids // tensor_size)
    tensor_step = tensor_index ^ (ids % tensor_size)
    group_place = group_step % 2 * (group_size // 2) + group_step // 2
    tensor_place = tensor_step % 2 * (tensor_size // 2) + tensor_step // 2
    places = group_place * tensor_size + tensor_place
    blocks = jnp.take(blocks, places, axis=0)
    blocks = lax.all_to_all(blocks, ("group", "tensor"), 0, 0, tiled=True)
    peaks, sums, picks = blocks[:, :share], blocks[:, share : 2 * share], blocks[:, 2 * share :]
    peak = jnp.max(peaks, axis=0)
    total = jnp.sum(sums * jnp.exp(peaks - peak[None]), axis=0)
    values = jnp.sum(picks, axis=0) - peak - jnp.log(total)
    local_rows = tensor_index * share + jnp.arange(share, dtype=i32)
    slots = jnp.arange(prompt_of.shape[0], dtype=i32)
    local_len = jnp.sum(
        jnp.where((local_rows // seq)[:, None] == slots[None, :], lengths[None, :], 0), axis=1
    )
    return jnp.where(local_rows % seq < local_len, values, 0.0)


def solution(mesh):
    return jax.shard_map(
        functools.partial(local, mesh.shape["group"], mesh.shape["tensor"]),
        mesh=mesh,
        in_specs=(
            P("group", "tensor"),
            P("group", "tensor"),
            P("group", "tensor"),
            P("group", "tensor"),
            P("group", "tensor"),
            P("group"),
            P("group"),
            P("group", None),
            P("tensor", None),
            P(),
            P(None, ("group", "tensor")),
            P(),
        ),
        out_specs=P(("group", "tensor")),
        check_vma=False,
    )
```

```python
import functools

import jax
import jax.numpy as jnp
from jax import lax
from jax.experimental import pallas as pl
from jax.experimental.pallas import tpu as pltpu
from jax.sharding import PartitionSpec as P

HEAD_DIM = 128
PLEN = 512
NEG = -1e30
BF16 = jnp.bfloat16
F32 = jnp.float32
MIB = 1024 * 1024


def params(mib):
    return pltpu.CompilerParams(vmem_limit_bytes=mib * MIB)


def held(x):
    return pltpu.with_memory_space_constraint(x, pltpu.VMEM)


def stored(x):
    return pltpu.with_memory_space_constraint(x, pltpu.HBM)


def anywhere():
    return pl.BlockSpec(memory_space=pl.ANY)


def cost(flops=0, moved=0):
    return pl.CostEstimate(flops=flops, bytes_accessed=moved, transcendentals=0)


def vmem():
    return pl.BlockSpec(memory_space=pltpu.VMEM)


def smem():
    return pl.BlockSpec(memory_space=pltpu.SMEM)


def swap(x, axis, distance, size):
    return lax.ppermute(x, axis, [(i, i ^ distance) for i in range(size)])


def attend(jobs):
    factor = HEAD_DIM**-0.5
    scores = [
        lax.dot_general(q, k, (((1,), (1,)), ((), ())), preferred_element_type=F32)
        for q, k, _, _ in jobs
    ]
    scores = [
        s if job[3] is None else jnp.where(job[3], s, NEG) for s, job in zip(scores, jobs)
    ]
    peaks = [jnp.max(s, axis=1, keepdims=True) for s in scores]
    weights = [jnp.exp((s - peak) * factor) for s, peak in zip(scores, peaks)]
    weights = [
        w if job[3] is None else jnp.where(job[3], w, 0.0) for w, job in zip(weights, jobs)
    ]
    weights = [w.astype(BF16) for w in weights]
    totals = [jnp.sum(w.astype(F32), axis=1, keepdims=True) for w in weights]
    mixed = [
        jnp.dot(w, job[2], preferred_element_type=F32) for w, job in zip(weights, jobs)
    ]
    return [
        (m / total, peak * factor + jnp.log(total))
        for m, total, peak in zip(mixed, totals, peaks)
    ]


def pack_logs(logs, rows):
    lane = lax.broadcasted_iota(jnp.int32, (rows, 128), 1)
    packed = jnp.zeros((rows, 128), F32)
    for head, log in enumerate(logs):
        first = log.astype(BF16).astype(F32)
        second = (log - first).astype(BF16).astype(F32)
        third = log - first - second
        for part, value in enumerate((first, second, third)):
            packed = jnp.where(lane == 3 * head + part, value, packed)
    return packed.astype(BF16)


def own_kernel(heads, seq, lengths_ref, *refs):
    sources, (own_ref, pre_ref), kept, scratch, sems = refs[:6], refs[6:8], refs[8:11], refs[11:14], refs[14]
    places = scratch + kept
    copies = [
        pltpu.make_async_copy(src, dst, sems.at[i]) for i, (src, dst) in enumerate(zip(sources, places))
    ]
    for copy in copies:
        copy.start()
    q_ref, rk_ref, rv_ref, k_ref, v_ref, _ = places
    rows = q_ref.shape[0]
    row = lax.broadcasted_iota(jnp.int32, (rows, rows), 0)
    col = lax.broadcasted_iota(jnp.int32, (rows, rows), 1)
    live = jnp.zeros((rows, rows), jnp.int32)
    for r in range(rows // seq):
        live = jnp.where(col // seq == r, lengths_ref[r], live)
    allowed = (row // seq == col // seq) & (col <= row) & (col % seq < live)
    parts = [slice(h * HEAD_DIM, (h + 1) * HEAD_DIM) for h in range(heads)]
    for copy in copies[:5]:
        copy.wait()
    found = attend(
        [(q_ref[:, p], rk_ref[:, p], rv_ref[:, p], allowed) for p in parts]
        + [(q_ref[:, p], k_ref[:, p], v_ref[:, p], None) for p in parts]
    )
    for h, p in enumerate(parts):
        own_ref[:, p] = found[h][0]
        pre_ref[:, p] = found[heads + h][0]
    logs = [log for _, log in found[:heads]]
    pre_logs = [log for _, log in found[heads:]]
    lane = lax.broadcasted_iota(jnp.int32, (rows, 128), 1)
    for ref, values in ((own_ref, logs), (pre_ref, pre_logs)):
        packed = jnp.zeros((rows, 128), F32)
        for h in range(heads):
            packed = jnp.where(lane == h, values[h], packed)
        ref[:, heads * HEAD_DIM :] = packed
    copies[5].wait()


def prefix_kernel(heads, count, *refs):
    q_refs, (k_ref, v_ref), out_refs = refs[:count], refs[count : count + 2], refs[count + 2 :]
    rows = q_refs[0].shape[0]
    parts = [slice(h * HEAD_DIM, (h + 1) * HEAD_DIM) for h in range(heads)]
    found = attend(
        [
            (jnp.concatenate([ref[:, p] for ref in q_refs], axis=0), k_ref[:, p], v_ref[:, p], None)
            for p in parts
        ]
    )
    for i in range(count):
        rung = slice(i * rows, (i + 1) * rows)
        for h, p in enumerate(parts):
            out_refs[i][:, p] = found[h][0][rung].astype(BF16)
        out_refs[i][:, heads * HEAD_DIM :] = pack_logs([log[rung] for _, log in found], rows)


def project_kernel(heads, seq, share, wide, group_size, key_rows, prompt_ref, *refs):
    count = group_size - 1
    own_ref, pre_ref = refs[:2]
    got_refs = refs[2 : 2 + count]
    weight_ref = refs[2 + count]
    out_refs, (attended_ref, partial_ref) = refs[3 + count : -2], refs[-2:]
    rows = own_ref.shape[0]
    row = lax.broadcasted_iota(jnp.int32, (rows, 1), 0)
    wanted = jnp.zeros((rows, 1), jnp.int32)
    for r in range(rows // seq):
        wanted = jnp.where(row // seq == r, prompt_ref[r], wanted)
    group = lax.axis_index("group")
    holders = [(group ^ d) * key_rows // PLEN for d in range(group_size)]
    for h in range(heads):
        part = slice(h * HEAD_DIM, (h + 1) * HEAD_DIM)
        at = heads * HEAD_DIM
        logs = [own_ref[:, at + h : at + h + 1]]
        values = [own_ref[:, part]]
        pre_log = pre_ref[:, at + h : at + h + 1]
        logs.append(jnp.where(wanted == holders[0], pre_log, NEG))
        values.append(pre_ref[:, part])
        for i, ref in enumerate(got_refs):
            three = ref[:, at : at + 128].astype(F32)
            log = (
                three[:, 3 * h : 3 * h + 1]
                + three[:, 3 * h + 1 : 3 * h + 2]
                + three[:, 3 * h + 2 : 3 * h + 3]
            )
            logs.append(jnp.where(wanted == holders[1 + i], log, NEG))
            values.append(ref[:, part].astype(F32))
        peak = functools.reduce(jnp.maximum, logs)
        loads = [jnp.exp(log - peak) for log in logs]
        total = functools.reduce(jnp.add, loads)
        mixed = functools.reduce(jnp.add, [w * v for w, v in zip(loads, values)])
        attended_ref[:, part] = (mixed / total).astype(BF16)

    me = lax.axis_index("tensor")

    @pl.loop(0, weight_ref.shape[1] // wide)
    def _(n):
        columns = pl.ds(pl.multiple_of(n * wide, 128), wide)
        partial = jnp.dot(attended_ref[...], weight_ref[:, columns], preferred_element_type=F32)
        for b in range(rows // share):
            partial_ref[b] = partial[b * share : (b + 1) * share]
        for d, ref in enumerate(out_refs):
            ref[:, columns] = partial_ref[me ^ d].astype(ref.dtype)


def fetch_kernel(start, count, source_ref, gate_ref, out_ref, sems):
    rows = out_ref.shape[0] // count
    copies = [
        pltpu.make_async_copy(
            source_ref.at[pl.ds(start + i * rows, rows)], out_ref.at[pl.ds(i * rows, rows)], sems.at[i]
        )
        for i in range(count)
    ]
    for copy in copies:
        copy.start()
    for copy in copies:
        copy.wait()


def norm_kernel(residual_ref, gain_ref, *refs):
    terms, out_refs = refs[2:-2], refs[-2:]
    hidden = residual_ref[lax.axis_index("tensor")].astype(F32)
    for ref in terms:
        hidden = hidden + ref[...].astype(F32)
    squares = jnp.mean(hidden * hidden, axis=-1, keepdims=True)
    normed = (hidden * lax.rsqrt(squares + 1e-06) * gain_ref[...].astype(F32)).astype(BF16)
    width = normed.shape[1] // 2
    for i, ref in enumerate(out_refs):
        ref[...] = normed[:, i * width : (i + 1) * width]


def first_kernel(narrow, left_ref, right_ref, weight_ref, out_ref, x_ref):
    half = left_ref.shape[0]
    x_ref[:half] = left_ref[...]
    x_ref[half:] = right_ref[...]

    @pl.loop(0, weight_ref.shape[1] // narrow)
    def _(n):
        columns = pl.ds(n * narrow if narrow % 128 else pl.multiple_of(n * narrow, 128), narrow)
        out_ref[:, columns] = jnp.dot(
            x_ref[...], weight_ref[:, columns], preferred_element_type=F32
        )


def logits_kernel(
    narrow,
    spots,
    tensor_size,
    sum_in_ref,
    left_ref,
    right_ref,
    target_ref,
    weight_ref,
    out_ref,
    x_ref,
    peak_ref,
    sum_ref,
    pick_ref,
    wanted_ref,
    stats_ref,
):
    half = left_ref.shape[0]
    rows = 2 * half
    share = target_ref.shape[1]
    group, tensor = lax.axis_index("group"), lax.axis_index("tensor")
    vocab = weight_ref.shape[1]
    places = [(group ^ g) * tensor_size + (tensor ^ t) for g, t in spots]
    for i, place in enumerate(places):
        wanted_ref[i * share : (i + 1) * share] = target_ref[place]
    wanted = wanted_ref[...] - (group * tensor_size + tensor) * vocab
    wanted_ref[...] = jnp.where((wanted >= 0) & (wanted < vocab), wanted, -1)
    x_ref[:half] = left_ref[...]
    x_ref[half:] = right_ref[...]
    peak_ref[...] = jnp.full_like(peak_ref, NEG)
    sum_ref[...] = jnp.zeros_like(sum_ref)
    pick_ref[...] = jnp.zeros_like(pick_ref)

    @pl.loop(0, weight_ref.shape[1] // narrow)
    def _(n):
        columns = pl.ds(n * narrow if narrow % 128 else pl.multiple_of(n * narrow, 128), narrow)
        logits = sum_in_ref[:, columns] + jnp.dot(
            x_ref[...], weight_ref[:, columns], preferred_element_type=F32
        )
        parts = [logits[:, c : c + 128] for c in range(0, narrow, 128)]
        if narrow % 128:
            spare = jnp.full((rows, 128 - narrow % 128), NEG, F32)
            parts[-1] = jnp.concatenate([parts[-1], spare], axis=1)
        lane = lax.broadcasted_iota(jnp.int32, (rows, 128), 1) + n * narrow
        peak = peak_ref[...]
        higher = functools.reduce(jnp.maximum, parts, peak)
        total = sum_ref[...] * jnp.exp(peak - higher)
        picked = pick_ref[...]
        target = wanted_ref[...]
        for c, part in enumerate(parts):
            total = total + jnp.exp(part - higher)
            picked = picked + jnp.where(lane + c * 128 == target, part, 0.0)
        peak_ref[...] = higher
        sum_ref[...] = total
        pick_ref[...] = picked

    higher = peak_ref[...]
    peak = jnp.max(higher, axis=1, keepdims=True)
    sums = jnp.sum(sum_ref[...] * jnp.exp(higher - peak), axis=1, keepdims=True)
    pick = jnp.sum(pick_ref[...], axis=1, keepdims=True)
    place = lax.broadcasted_iota(jnp.int32, (rows, 128), 1)
    three = jnp.where(place == 0, peak, jnp.where(place == 1, sums, pick))
    for i, place in enumerate(places):
        stats_ref[place] = three[i * share : (i + 1) * share]
    out_ref[...] = jnp.transpose(stats_ref[...].reshape(rows, 128))[:8]


def local(
    group_size,
    tensor_size,
    resp_query,
    resp_key,
    resp_value,
    prompt_keys,
    prompt_values,
    prompt_of,
    lengths,
    residual,
    out_weight,
    norm_gain,
    lm_weight,
    targets,
):
    rows, span = resp_query.shape
    heads = span // HEAD_DIM
    seq = rows // prompt_of.shape[0]
    key_rows = prompt_keys.shape[0]
    assert PLEN % key_rows == 0
    share = rows // tensor_size
    depth = out_weight.shape[1]
    vocab = lm_weight.shape[1]
    tensor_index = lax.axis_index("tensor")
    i32 = jnp.int32

    distances = list(range(1, group_size))
    queries = [swap(resp_query, "group", d, group_size) for d in distances]
    inputs = (resp_query, resp_key, resp_value, prompt_keys, prompt_values, out_weight)
    own, prefix, keys, values, weight = pl.pallas_call(
        functools.partial(own_kernel, heads, seq),
        out_shape=[jax.ShapeDtypeStruct((rows, span + 128), F32)] * 2
        + [pltpu.VMEM(x.shape, x.dtype) for x in inputs[3:]],
        in_specs=[smem()] + [anywhere()] * 6,
        out_specs=[vmem()] * 5,
        scratch_shapes=[pltpu.VMEM(x.shape, x.dtype) for x in inputs[:3]]
        + [pltpu.SemaphoreType.DMA((6,))],
        compiler_params=params(6),
        cost_estimate=cost(moved=14 * MIB),
        name="own_attention",
    )(lengths, *map(stored, inputs))
    keys, values, weight = held(keys), held(values), held(weight)
    answers = pl.pallas_call(
        functools.partial(prefix_kernel, heads, len(distances)),
        out_shape=[jax.ShapeDtypeStruct((rows, span + 128), BF16)] * len(distances),
        in_specs=[vmem()] * (len(distances) + 2),
        out_specs=[vmem()] * len(distances),
        compiler_params=params(8),
        name="prefix_attention",
    )(*map(held, queries), keys, values)
    got = [swap(x, "group", d, group_size) for x, d in zip(answers, distances)]

    wide = 640 if depth % 640 == 0 else depth
    shares = pl.pallas_call(
        functools.partial(project_kernel, heads, seq, share, wide, group_size, key_rows),
        out_shape=[
            jax.ShapeDtypeStruct((share, depth), BF16 if d else F32) for d in range(tensor_size)
        ],
        in_specs=[smem()] + [vmem()] * (3 + len(distances)),
        out_specs=[vmem()] * tensor_size,
        scratch_shapes=[
            pltpu.VMEM((rows, span), BF16),
            pltpu.VMEM((tensor_size, share, wide), F32),
        ],
        compiler_params=params(6),
        name="project",
    )(prompt_of, *map(held, (own, prefix, *got)), weight)

    weights = []
    for i in range(2):
        weights.append(
            pl.pallas_call(
                functools.partial(fetch_kernel, i * (depth // 2), 4),
                out_shape=pltpu.VMEM((depth // 2, vocab), BF16),
                in_specs=[anywhere()] * 2,
                out_specs=vmem(),
                scratch_shapes=[pltpu.SemaphoreType.DMA((4,))],
                compiler_params=params(1),
                cost_estimate=cost(moved=depth // 2 * vocab * 2),
                name="fetch",
            )(stored(lm_weight), shares[1])
        )

    got = [swap(x, "tensor", d, tensor_size) for d, x in enumerate(shares) if d]
    normed = pl.pallas_call(
        norm_kernel,
        out_shape=[jax.ShapeDtypeStruct((share, depth // 2), BF16)] * 2,
        in_specs=[vmem()] * 2 + [anywhere()] * 2 + [vmem()] * tensor_size,
        out_specs=[vmem()] * 2,
        compiler_params=params(4),
        name="norm",
    )(
        *map(held, (residual.reshape(tensor_size, share, depth), norm_gain[None], *weights)),
        *map(held, (shares[0], *got)),
    )

    far = list(range(2, tensor_size, 2))
    above = list(range(2, group_size, 2))
    order = [0] + far
    here = [(g, x) for g in [0] + above for x in (0, 1)]
    mesh_ids = [(g, t) for g in range(group_size) for t in range(tensor_size)]
    routes = {
        (g, x): [(a * tensor_size + b, (a ^ g) * tensor_size + (b ^ x)) for a, b in mesh_ids]
        for g, x in here
    }
    halves = []
    for part in normed:
        tokens = jnp.stack([part] + [swap(part, "tensor", d, tensor_size) for d in far])
        pieces = [
            lax.ppermute(tokens, ("group", "tensor"), routes[place]) if any(place) else tokens
            for place in here
        ]
        tokens = jnp.concatenate(pieces).reshape(-1, depth // 2)
        halves.append((tokens, swap(tokens, "group", 1, group_size)))
    spots = [(g + c, t + x) for c in (0, 1) for g, x in here for t in order]
    total_rows = 2 * tokens.shape[0]
    narrow = 512 if vocab % 512 == 0 else vocab
    limit = 10 if total_rows <= 256 else 24
    work = 2 * total_rows * (depth // 2) * vocab
    first = pl.pallas_call(
        functools.partial(first_kernel, narrow),
        out_shape=pltpu.VMEM((total_rows, vocab), F32),
        in_specs=[vmem()] * 3,
        out_specs=vmem(),
        scratch_shapes=[pltpu.VMEM((total_rows, depth // 2), BF16)],
        compiler_params=params(limit),
        cost_estimate=cost(flops=work),
        name="logits_first",
    )(*map(held, (*halves[0], weights[0])))
    stats = pl.pallas_call(
        functools.partial(logits_kernel, narrow, spots, tensor_size),
        out_shape=jax.ShapeDtypeStruct((8, total_rows), F32),
        in_specs=[vmem()] * 5,
        out_specs=vmem(),
        scratch_shapes=[pltpu.VMEM((total_rows, depth // 2), BF16)]
        + [pltpu.VMEM((total_rows, 128), F32)] * 3
        + [pltpu.VMEM((total_rows, 1), i32), pltpu.VMEM((len(spots), share, 128), F32)],
        compiler_params=params(limit),
        cost_estimate=cost(flops=work),
        name="logits",
    )(*map(held, (first, *halves[1])), targets.reshape(-1, share, 1), held(weights[1]))

    blocks = stats[:3].reshape(3, -1, share).transpose(1, 0, 2).reshape(-1, 3 * share)
    blocks = lax.all_to_all(blocks, ("group", "tensor"), 0, 0, tiled=True)
    peaks, sums, picks = blocks[:, :share], blocks[:, share : 2 * share], blocks[:, 2 * share :]
    peak = jnp.max(peaks, axis=0)
    total = jnp.sum(sums * jnp.exp(peaks - peak[None]), axis=0)
    values = jnp.sum(picks, axis=0) - peak - jnp.log(total)
    local_rows = tensor_index * share + jnp.arange(share, dtype=i32)
    slots = jnp.arange(prompt_of.shape[0], dtype=i32)
    local_len = jnp.sum(
        jnp.where((local_rows // seq)[:, None] == slots[None, :], lengths[None, :], 0), axis=1
    )
    return jnp.where(local_rows % seq < local_len, values, 0.0)


def solution(mesh):
    return jax.shard_map(
        functools.partial(local, mesh.shape["group"], mesh.shape["tensor"]),
        mesh=mesh,
        in_specs=(
            P("group", "tensor"),
            P("group", "tensor"),
            P("group", "tensor"),
            P("group", "tensor"),
            P("group", "tensor"),
            P("group"),
            P("group"),
            P("group", None),
            P("tensor", None),
            P(),
            P(None, ("group", "tensor")),
            P(),
        ),
        out_specs=P(("group", "tensor")),
        check_vma=False,
    )
```

```python
import functools

import jax
import jax.numpy as jnp
from jax import lax
from jax.experimental import pallas as pl
from jax.experimental.pallas import tpu as pltpu
from jax.sharding import PartitionSpec as P

HEAD_DIM = 128
PLEN = 512
NEG = -1e30
BF16 = jnp.bfloat16
F32 = jnp.float32
MIB = 1024 * 1024


def params(mib):
    return pltpu.CompilerParams(vmem_limit_bytes=mib * MIB)


def held(x):
    return pltpu.with_memory_space_constraint(x, pltpu.VMEM)


def stored(x):
    return pltpu.with_memory_space_constraint(x, pltpu.HBM)


def anywhere():
    return pl.BlockSpec(memory_space=pl.ANY)


def cost(flops=0, moved=0):
    return pl.CostEstimate(flops=flops, bytes_accessed=moved, transcendentals=0)


def vmem():
    return pl.BlockSpec(memory_space=pltpu.VMEM)


def smem():
    return pl.BlockSpec(memory_space=pltpu.SMEM)


def swap(x, axis, distance, size):
    return lax.ppermute(x, axis, [(i, i ^ distance) for i in range(size)])


def attend(jobs):
    factor = HEAD_DIM**-0.5
    scores = [
        lax.dot_general(q, k, (((1,), (1,)), ((), ())), preferred_element_type=F32)
        for q, k, _, _ in jobs
    ]
    scores = [
        s if job[3] is None else jnp.where(job[3], s, NEG) for s, job in zip(scores, jobs)
    ]
    peaks = [jnp.max(s, axis=1, keepdims=True) for s in scores]
    weights = [jnp.exp((s - peak) * factor) for s, peak in zip(scores, peaks)]
    weights = [
        w if job[3] is None else jnp.where(job[3], w, 0.0) for w, job in zip(weights, jobs)
    ]
    weights = [w.astype(BF16) for w in weights]
    totals = [jnp.sum(w.astype(F32), axis=1, keepdims=True) for w in weights]
    mixed = [
        jnp.dot(w, job[2], preferred_element_type=F32) for w, job in zip(weights, jobs)
    ]
    return [
        (m / total, peak * factor + jnp.log(total))
        for m, total, peak in zip(mixed, totals, peaks)
    ]


def pack_logs(logs, rows):
    lane = lax.broadcasted_iota(jnp.int32, (rows, 128), 1)
    packed = jnp.zeros((rows, 128), F32)
    for head, log in enumerate(logs):
        first = log.astype(BF16).astype(F32)
        second = (log - first).astype(BF16).astype(F32)
        third = log - first - second
        for part, value in enumerate((first, second, third)):
            packed = jnp.where(lane == 3 * head + part, value, packed)
    return packed.astype(BF16)


def load_kernel(count, *refs):
    sems = refs[2 * count]
    copies = [
        pltpu.make_async_copy(refs[i], refs[count + i], sems.at[i]) for i in range(count)
    ]
    for copy in copies:
        copy.start()
    for copy in copies:
        copy.wait()


def own_kernel(
    heads, seq, lengths_ref, q_ref, rk_ref, rv_ref, k_ref, v_ref, gate_ref, early_ref, own_ref, pre_ref
):
    rows = q_ref.shape[0]
    row = lax.broadcasted_iota(jnp.int32, (rows, rows), 0)
    col = lax.broadcasted_iota(jnp.int32, (rows, rows), 1)
    live = jnp.zeros((rows, rows), jnp.int32)
    for r in range(rows // seq):
        live = jnp.where(col // seq == r, lengths_ref[r], live)
    allowed = (row // seq == col // seq) & (col <= row) & (col % seq < live)
    parts = [slice(h * HEAD_DIM, (h + 1) * HEAD_DIM) for h in range(heads)]
    found = attend(
        [(q_ref[:, p], rk_ref[:, p], rv_ref[:, p], allowed) for p in parts]
        + [(q_ref[:, p], k_ref[:, p], v_ref[:, p], None) for p in parts]
    )
    for h, p in enumerate(parts):
        own_ref[:, p] = found[h][0]
        pre_ref[:, p] = found[heads + h][0]
    lane = lax.broadcasted_iota(jnp.int32, (rows, 128), 1)
    for ref, values in ((own_ref, found[:heads]), (pre_ref, found[heads:])):
        packed = jnp.zeros((rows, 128), F32)
        for h in range(heads):
            packed = jnp.where(lane == h, values[h][1], packed)
        ref[:, heads * HEAD_DIM :] = packed


def prefix_kernel(heads, count, *refs):
    q_refs, (k_ref, v_ref), out_refs = refs[:count], refs[count : count + 2], refs[count + 2 :]
    rows = q_refs[0].shape[0]
    parts = [slice(h * HEAD_DIM, (h + 1) * HEAD_DIM) for h in range(heads)]
    found = attend(
        [
            (jnp.concatenate([ref[:, p] for ref in q_refs], axis=0), k_ref[:, p], v_ref[:, p], None)
            for p in parts
        ]
    )
    for i in range(count):
        rung = slice(i * rows, (i + 1) * rows)
        for h, p in enumerate(parts):
            out_refs[i][:, p] = found[h][0][rung].astype(BF16)
        out_refs[i][:, heads * HEAD_DIM :] = pack_logs([log[rung] for _, log in found], rows)


def project_kernel(heads, seq, share, wide, group_size, key_rows, gate_ref, prompt_ref, *refs):
    count = group_size - 1
    own_ref, pre_ref = refs[:2]
    got_refs = refs[2 : 2 + count]
    weight_ref = refs[2 + count]
    out_refs, (attended_ref, partial_ref) = refs[3 + count : -2], refs[-2:]
    rows = own_ref.shape[0]
    row = lax.broadcasted_iota(jnp.int32, (rows, 1), 0)
    wanted = jnp.zeros((rows, 1), jnp.int32)
    for r in range(rows // seq):
        wanted = jnp.where(row // seq == r, prompt_ref[r], wanted)
    group = lax.axis_index("group")
    holders = [(group ^ d) * key_rows // PLEN for d in range(group_size)]
    for h in range(heads):
        part = slice(h * HEAD_DIM, (h + 1) * HEAD_DIM)
        at = heads * HEAD_DIM
        logs = [own_ref[:, at + h : at + h + 1]]
        values = [own_ref[:, part]]
        pre_log = pre_ref[:, at + h : at + h + 1]
        logs.append(jnp.where(wanted == holders[0], pre_log, NEG))
        values.append(pre_ref[:, part])
        for i, ref in enumerate(got_refs):
            three = ref[:, at : at + 128].astype(F32)
            log = (
                three[:, 3 * h : 3 * h + 1]
                + three[:, 3 * h + 1 : 3 * h + 2]
                + three[:, 3 * h + 2 : 3 * h + 3]
            )
            logs.append(jnp.where(wanted == holders[1 + i], log, NEG))
            values.append(ref[:, part].astype(F32))
        peak = functools.reduce(jnp.maximum, logs)
        loads = [jnp.exp(log - peak) for log in logs]
        total = functools.reduce(jnp.add, loads)
        mixed = functools.reduce(jnp.add, [w * v for w, v in zip(loads, values)])
        attended_ref[:, part] = (mixed / total).astype(BF16)

    me = lax.axis_index("tensor")

    @pl.loop(0, weight_ref.shape[1] // wide)
    def _(n):
        columns = pl.ds(pl.multiple_of(n * wide, 128), wide)
        partial = jnp.dot(attended_ref[...], weight_ref[:, columns], preferred_element_type=F32)
        for b in range(rows // share):
            partial_ref[b] = partial[b * share : (b + 1) * share]
        for d, ref in enumerate(out_refs):
            ref[:, columns] = partial_ref[me ^ d].astype(ref.dtype)


def fetch_kernel(start, count, source_ref, gate_ref, out_ref, sems):
    rows = out_ref.shape[0] // count
    copies = [
        pltpu.make_async_copy(
            source_ref.at[pl.ds(start + i * rows, rows)], out_ref.at[pl.ds(i * rows, rows)], sems.at[i]
        )
        for i in range(count)
    ]
    for copy in copies:
        copy.start()
    for copy in copies:
        copy.wait()


def column_kernel(count, *refs):
    terms, out_refs = refs[:count], refs[-2:]
    width = out_refs[0].shape[2]
    for i, ref in enumerate(terms):
        for half, out_ref in enumerate(out_refs):
            out_ref[i] = ref[:, half * width : (half + 1) * width]


def norm_kernel(first_gate_ref, second_gate_ref, residual_ref, gain_ref, *refs):
    terms, out_ref = refs[:-1], refs[-1]
    hidden = residual_ref[lax.axis_index("tensor")].astype(F32)
    for ref in terms:
        hidden = hidden + ref[...].astype(F32)
    squares = jnp.mean(hidden * hidden, axis=-1, keepdims=True)
    normed = (hidden * lax.rsqrt(squares + 1e-06) * gain_ref[...].astype(F32)).astype(BF16)
    out_ref[...] = normed


def quarter_dots(x_ref, weight_refs, columns):
    depth = weight_refs[0].shape[0]
    return functools.reduce(
        jnp.add,
        [
            jnp.dot(x_ref[:, i * depth : (i + 1) * depth], ref[:, columns], preferred_element_type=F32)
            for i, ref in enumerate(weight_refs)
        ],
    )


def first_kernel(narrow, left_ref, right_ref, weight_ref, next_ref, out_ref, x_ref):
    half = left_ref.shape[0]
    x_ref[:half] = left_ref[...]
    x_ref[half:] = right_ref[...]

    @pl.loop(0, weight_ref.shape[1] // narrow)
    def _(n):
        columns = pl.ds(n * narrow if narrow % 128 else pl.multiple_of(n * narrow, 128), narrow)
        out_ref[:, columns] = quarter_dots(x_ref, (weight_ref, next_ref), columns)


def logits_kernel(
    narrow,
    spots,
    tensor_size,
    sum_in_ref,
    left_ref,
    right_ref,
    target_ref,
    weight_ref,
    next_ref,
    out_ref,
    x_ref,
    peak_ref,
    sum_ref,
    pick_ref,
    wanted_ref,
):
    half = left_ref.shape[0]
    rows = 2 * half
    share = target_ref.shape[1]
    group, tensor = lax.axis_index("group"), lax.axis_index("tensor")
    vocab = weight_ref.shape[1]
    places = [(group ^ g) * tensor_size + (tensor ^ t) for g, t in spots]
    for i, place in enumerate(places):
        wanted_ref[i * share : (i + 1) * share] = target_ref[place]
    wanted = wanted_ref[...] - (group * tensor_size + tensor) * vocab
    wanted_ref[...] = jnp.where((wanted >= 0) & (wanted < vocab), wanted, -1)
    x_ref[:half] = left_ref[...]
    x_ref[half:] = right_ref[...]
    peak_ref[...] = jnp.full_like(peak_ref, NEG)
    sum_ref[...] = jnp.zeros_like(sum_ref)
    pick_ref[...] = jnp.zeros_like(pick_ref)

    @pl.loop(0, weight_ref.shape[1] // narrow)
    def _(n):
        columns = pl.ds(n * narrow if narrow % 128 else pl.multiple_of(n * narrow, 128), narrow)
        logits = sum_in_ref[:, columns] + quarter_dots(x_ref, (weight_ref, next_ref), columns)
        parts = [logits[:, c : c + 128] for c in range(0, narrow, 128)]
        if narrow % 128:
            spare = jnp.full((rows, 128 - narrow % 128), NEG, F32)
            parts[-1] = jnp.concatenate([parts[-1], spare], axis=1)
        lane = lax.broadcasted_iota(jnp.int32, (rows, 128), 1) + n * narrow
        peak = peak_ref[...]
        higher = functools.reduce(jnp.maximum, parts, peak)
        total = sum_ref[...] * jnp.exp(peak - higher)
        picked = pick_ref[...]
        target = wanted_ref[...]
        for c, part in enumerate(parts):
            total = total + jnp.exp(part - higher)
            picked = picked + jnp.where(lane + c * 128 == target, part, 0.0)
        peak_ref[...] = higher
        sum_ref[...] = total
        pick_ref[...] = picked

    higher = peak_ref[...]
    peak = jnp.max(higher, axis=1, keepdims=True)
    sums = jnp.sum(sum_ref[...] * jnp.exp(higher - peak), axis=1, keepdims=True)
    pick = jnp.sum(pick_ref[...], axis=1, keepdims=True)
    row = lax.broadcasted_iota(jnp.int32, (rows, 128), 0)
    lane = lax.broadcasted_iota(jnp.int32, (rows, 128), 1)
    three = jnp.where(lane // share == 0, peak, jnp.where(lane // share == 1, sums, pick))
    three = jnp.where((row - lane) % share == 0, three, 0.0)
    for i, place in enumerate(places):
        out_ref[place] = jnp.sum(three[i * share : (i + 1) * share], axis=0, keepdims=True)


def final_kernel(seq, share, lengths_ref, stats_ref, out_ref):
    stats = stats_ref[...].reshape(stats_ref.shape[0], 128)
    count = lengths_ref.shape[0]
    peak = jnp.max(stats, axis=0, keepdims=True)
    sums = pltpu.roll(stats, 128 - share, 1)
    picks = pltpu.roll(stats, 128 - 2 * share, 1)
    total = jnp.sum(sums * jnp.exp(stats - peak), axis=0, keepdims=True)
    values = jnp.sum(picks, axis=0, keepdims=True) - peak - jnp.log(total)
    token = lax.broadcasted_iota(jnp.int32, (1, 128), 1) + lax.axis_index("tensor") * share
    live = jnp.zeros((1, 128), jnp.int32)
    for r in range(count):
        live = jnp.where(token // seq == r, lengths_ref[r], live)
    out_ref[...] = jnp.where(token % seq < live, values, 0.0)


def local(
    group_size,
    tensor_size,
    resp_query,
    resp_key,
    resp_value,
    prompt_keys,
    prompt_values,
    prompt_of,
    lengths,
    residual,
    out_weight,
    norm_gain,
    lm_weight,
    targets,
):
    rows, span = resp_query.shape
    heads = span // HEAD_DIM
    seq = rows // prompt_of.shape[0]
    key_rows = prompt_keys.shape[0]
    assert PLEN % key_rows == 0
    share = rows // tensor_size
    depth = out_weight.shape[1]
    vocab = lm_weight.shape[1]
    i32 = jnp.int32

    distances = list(range(1, group_size))
    queries = [swap(resp_query, "group", d, group_size) for d in distances]
    wanted = targets.reshape(-1, share, 1)
    inputs = (resp_query, resp_key, resp_value, prompt_keys, prompt_values, out_weight)
    loaded = pl.pallas_call(
        functools.partial(load_kernel, len(inputs)),
        out_shape=[pltpu.VMEM(x.shape, x.dtype) for x in inputs],
        in_specs=[anywhere()] * len(inputs),
        out_specs=[vmem()] * len(inputs),
        scratch_shapes=[pltpu.SemaphoreType.DMA((len(inputs),))],
        compiler_params=params(1),
        cost_estimate=cost(moved=7 * MIB),
        name="load",
    )(*map(stored, inputs))
    query, own_keys, own_values, keys, values, weight = map(held, loaded)
    answers = pl.pallas_call(
        functools.partial(prefix_kernel, heads, len(distances)),
        out_shape=[jax.ShapeDtypeStruct((rows, span + 128), BF16)] * len(distances),
        in_specs=[vmem()] * (len(distances) + 2),
        out_specs=[vmem()] * len(distances),
        compiler_params=params(8),
        name="prefix_attention",
    )(*map(held, queries), keys, values)
    got = [swap(x, "group", d, group_size) for x, d in zip(answers, distances)]
    own, prefix = pl.pallas_call(
        functools.partial(own_kernel, heads, seq),
        out_shape=[jax.ShapeDtypeStruct((rows, span + 128), F32)] * 2,
        in_specs=[smem()] + [vmem()] * 5 + [anywhere()] * 2,
        out_specs=[vmem()] * 2,
        compiler_params=params(6),
        cost_estimate=cost(moved=8 * MIB),
        name="own_attention",
    )(stored(lengths), query, own_keys, own_values, keys, values, answers[0], wanted)

    def fetch(quarter, gate):
        return held(
            pl.pallas_call(
                functools.partial(fetch_kernel, quarter * (depth // 4), 4),
                out_shape=pltpu.VMEM((depth // 4, vocab), BF16),
                in_specs=[anywhere()] * 2,
                out_specs=vmem(),
                scratch_shapes=[pltpu.SemaphoreType.DMA((4,))],
                compiler_params=params(1),
                cost_estimate=cost(moved=depth // 4 * vocab * 2),
                name="fetch",
            )(stored(lm_weight), gate)
        )

    quarters = [fetch(0, answers[0])]

    wide = 640 if depth % 640 == 0 else depth
    shares = pl.pallas_call(
        functools.partial(project_kernel, heads, seq, share, wide, group_size, key_rows),
        out_shape=[
            jax.ShapeDtypeStruct((share, depth), BF16 if d else F32) for d in range(tensor_size)
        ],
        in_specs=[anywhere(), smem()] + [vmem()] * (3 + len(distances)),
        out_specs=[vmem()] * tensor_size,
        scratch_shapes=[
            pltpu.VMEM((rows, span), BF16),
            pltpu.VMEM((tensor_size, share, wide), F32),
        ],
        compiler_params=params(6),
        name="project",
    )(quarters[0], stored(prompt_of), *map(held, (own, prefix, *got)), weight)
    quarters += [fetch(1, shares[1]), fetch(2, shares[1])]

    got = [swap(x, "tensor", d, tensor_size) for d, x in enumerate(shares) if d]
    normed = pl.pallas_call(
        norm_kernel,
        out_shape=jax.ShapeDtypeStruct((share, depth), BF16),
        in_specs=[anywhere()] * 2 + [vmem()] * (2 + tensor_size),
        out_specs=vmem(),
        compiler_params=params(4),
        name="norm",
    )(
        *quarters[1:],
        *map(held, (residual.reshape(tensor_size, share, depth), norm_gain[None])),
        *map(held, (shares[0], *got)),
    )

    far = list(range(2, tensor_size, 2))
    above = list(range(2, group_size, 2))
    order = [0] + far
    here = [(g, x) for g in [0] + above for x in (0, 1)]
    mesh_ids = [(g, t) for g in range(group_size) for t in range(tensor_size)]
    routes = {
        (g, x): [(a * tensor_size + b, (a ^ g) * tensor_size + (b ^ x)) for a, b in mesh_ids]
        for g, x in here
    }
    column = [normed] + [swap(normed, "tensor", d, tensor_size) for d in far]
    quarters.append(fetch(3, normed))
    columns = pl.pallas_call(
        functools.partial(column_kernel, len(column)),
        out_shape=[jax.ShapeDtypeStruct((len(column), share, depth // 2), BF16)] * 2,
        in_specs=[vmem()] * len(column) + [anywhere()],
        out_specs=[vmem()] * 2,
        compiler_params=params(2),
        name="column",
    )(*map(held, column), quarters[3])
    halves = []
    for tokens in columns:
        pieces = [
            lax.ppermute(tokens, ("group", "tensor"), routes[place]) if any(place) else tokens
            for place in here
        ]
        tokens = jnp.concatenate(pieces).reshape(-1, depth // 2)
        halves.append((tokens, swap(tokens, "group", 1, group_size)))
    spots = [(g + c, t + x) for c in (0, 1) for g, x in here for t in order]
    total_rows = 2 * tokens.shape[0]
    narrow = 1024 if vocab % 1024 == 0 else vocab
    limit = 10 if total_rows <= 256 else 24
    work = 2 * total_rows * (depth // 2) * vocab
    first = pl.pallas_call(
        functools.partial(first_kernel, narrow),
        out_shape=pltpu.VMEM((total_rows, vocab), F32),
        in_specs=[vmem()] * 4,
        out_specs=vmem(),
        scratch_shapes=[pltpu.VMEM((total_rows, depth // 2), BF16)],
        compiler_params=params(limit),
        cost_estimate=cost(flops=work),
        name="logits_first",
    )(*map(held, (*halves[0], *quarters[:2])))
    stats = pl.pallas_call(
        functools.partial(logits_kernel, narrow, spots, tensor_size),
        out_shape=jax.ShapeDtypeStruct((len(spots), 1, 128), F32),
        in_specs=[vmem()] * 6,
        out_specs=vmem(),
        scratch_shapes=[pltpu.VMEM((total_rows, depth // 2), BF16)]
        + [pltpu.VMEM((total_rows, 128), F32)] * 3
        + [pltpu.VMEM((total_rows, 1), i32)],
        compiler_params=params(limit),
        cost_estimate=cost(flops=work),
        name="logits",
    )(*map(held, (first, *halves[1])), wanted, *map(held, quarters[2:]))

    stats = lax.all_to_all(stats, ("group", "tensor"), 0, 0, tiled=True)
    values = pl.pallas_call(
        functools.partial(final_kernel, seq, share),
        out_shape=jax.ShapeDtypeStruct((1, 128), F32),
        in_specs=[smem(), vmem()],
        out_specs=vmem(),
        compiler_params=params(4),
        name="final",
    )(stored(lengths), stats)
    return values[0, :share]


def solution(mesh):
    return jax.shard_map(
        functools.partial(local, mesh.shape["group"], mesh.shape["tensor"]),
        mesh=mesh,
        in_specs=(
            P("group", "tensor"),
            P("group", "tensor"),
            P("group", "tensor"),
            P("group", "tensor"),
            P("group", "tensor"),
            P("group"),
            P("group"),
            P("group", None),
            P("tensor", None),
            P(),
            P(None, ("group", "tensor")),
            P(),
        ),
        out_specs=P(("group", "tensor")),
        check_vma=False,
    )
```

```python
import functools

import jax
import jax.numpy as jnp
from jax import lax
from jax.experimental import pallas as pl
from jax.experimental.pallas import tpu as pltpu
from jax.sharding import PartitionSpec as P

HEAD_DIM = 128
PLEN = 512
NEG = -1e30
BF16 = jnp.bfloat16
F32 = jnp.float32
MIB = 1024 * 1024


def params(mib):
    return pltpu.CompilerParams(vmem_limit_bytes=mib * MIB)


def held(x):
    return pltpu.with_memory_space_constraint(x, pltpu.VMEM)


def stored(x):
    return pltpu.with_memory_space_constraint(x, pltpu.HBM)


def anywhere():
    return pl.BlockSpec(memory_space=pl.ANY)


def cost(flops=0, moved=0):
    return pl.CostEstimate(flops=flops, bytes_accessed=moved, transcendentals=0)


def vmem():
    return pl.BlockSpec(memory_space=pltpu.VMEM)


def smem():
    return pl.BlockSpec(memory_space=pltpu.SMEM)


def swap(x, axis, distance, size):
    return lax.ppermute(x, axis, [(i, i ^ distance) for i in range(size)])


def attend(jobs):
    factor = HEAD_DIM**-0.5
    scores = [
        lax.dot_general(q, k, (((1,), (1,)), ((), ())), preferred_element_type=F32)
        for q, k, _, _ in jobs
    ]
    scores = [
        s if job[3] is None else jnp.where(job[3], s, NEG) for s, job in zip(scores, jobs)
    ]
    peaks = [jnp.max(s, axis=1, keepdims=True) for s in scores]
    weights = [jnp.exp((s - peak) * factor) for s, peak in zip(scores, peaks)]
    weights = [
        w if job[3] is None else jnp.where(job[3], w, 0.0) for w, job in zip(weights, jobs)
    ]
    weights = [w.astype(BF16) for w in weights]
    totals = [jnp.sum(w.astype(F32), axis=1, keepdims=True) for w in weights]
    mixed = [
        jnp.dot(w, job[2], preferred_element_type=F32) for w, job in zip(weights, jobs)
    ]
    return [
        (m / total, peak * factor + jnp.log(total))
        for m, total, peak in zip(mixed, totals, peaks)
    ]


def pack_logs(logs, rows):
    lane = lax.broadcasted_iota(jnp.int32, (rows, 128), 1)
    packed = jnp.zeros((rows, 128), F32)
    for head, log in enumerate(logs):
        first = log.astype(BF16).astype(F32)
        second = (log - first).astype(BF16).astype(F32)
        third = log - first - second
        for part, value in enumerate((first, second, third)):
            packed = jnp.where(lane == 3 * head + part, value, packed)
    return packed.astype(BF16)


def load_kernel(count, gate_ref, *refs):
    sems = refs[2 * count]
    copies = [
        pltpu.make_async_copy(refs[i], refs[count + i], sems.at[i]) for i in range(count)
    ]
    for copy in copies:
        copy.start()
    for copy in copies:
        copy.wait()


def own_kernel(
    heads, seq, lengths_ref, prompt_ref, q_ref, rk_ref, rv_ref, k_ref, v_ref, gate_ref, own_ref
):
    rows = q_ref.shape[0]
    row = lax.broadcasted_iota(jnp.int32, (rows, rows), 0)
    col = lax.broadcasted_iota(jnp.int32, (rows, rows), 1)
    live = jnp.zeros((rows, rows), jnp.int32)
    for r in range(rows // seq):
        live = jnp.where(col // seq == r, lengths_ref[r], live)
    allowed = (row // seq == col // seq) & (col <= row) & (col % seq < live)
    parts = [slice(h * HEAD_DIM, (h + 1) * HEAD_DIM) for h in range(heads)]
    found = attend(
        [(q_ref[:, p], rk_ref[:, p], rv_ref[:, p], allowed) for p in parts]
        + [(q_ref[:, p], k_ref[:, p], v_ref[:, p], None) for p in parts]
    )
    here = wanted_prompts(seq, rows, prompt_ref) == lax.axis_index("group") * k_ref.shape[0] // PLEN
    lane = lax.broadcasted_iota(jnp.int32, (rows, 128), 1)
    packed = jnp.zeros((rows, 128), F32)
    for h, p in enumerate(parts):
        (first, log), (second, other) = found[h], found[heads + h]
        other = jnp.where(here, other, NEG)
        peak = jnp.maximum(log, other)
        left, right = jnp.exp(log - peak), jnp.exp(other - peak)
        own_ref[:, p] = (first * left + second * right) / (left + right)
        packed = jnp.where(lane == h, peak + jnp.log(left + right), packed)
    own_ref[:, heads * HEAD_DIM :] = packed


def wanted_prompts(seq, rows, prompt_ref):
    row = lax.broadcasted_iota(jnp.int32, (rows, 1), 0)
    wanted = jnp.zeros((rows, 1), jnp.int32)
    for r in range(rows // seq):
        wanted = jnp.where(row // seq == r, prompt_ref[r], wanted)
    return wanted


def prefix_kernel(heads, count, *refs):
    q_refs, (k_ref, v_ref), out_refs = refs[:count], refs[count : count + 2], refs[count + 2 :]
    rows = q_refs[0].shape[0]
    parts = [slice(h * HEAD_DIM, (h + 1) * HEAD_DIM) for h in range(heads)]
    found = attend(
        [
            (jnp.concatenate([ref[:, p] for ref in q_refs], axis=0), k_ref[:, p], v_ref[:, p], None)
            for p in parts
        ]
    )
    for i in range(count):
        rung = slice(i * rows, (i + 1) * rows)
        for h, p in enumerate(parts):
            out_refs[i][:, p] = found[h][0][rung].astype(BF16)
        out_refs[i][:, heads * HEAD_DIM :] = pack_logs([log[rung] for _, log in found], rows)


def project_kernel(heads, seq, share, wide, group_size, key_rows, prompt_ref, own_ref, *refs):
    got_refs, weight_ref = refs[: group_size - 1], refs[group_size - 1]
    out_refs, (attended_ref, partial_ref) = refs[group_size:-2], refs[-2:]
    rows = own_ref.shape[0]
    wanted = wanted_prompts(seq, rows, prompt_ref)
    group = lax.axis_index("group")
    holders = [(group ^ d) * key_rows // PLEN for d in range(1, group_size)]
    for h in range(heads):
        part = slice(h * HEAD_DIM, (h + 1) * HEAD_DIM)
        at = heads * HEAD_DIM
        logs = [own_ref[:, at + h : at + h + 1]]
        values = [own_ref[:, part]]
        for holder, ref in zip(holders, got_refs):
            three = ref[:, at : at + 128].astype(F32)
            log = (
                three[:, 3 * h : 3 * h + 1]
                + three[:, 3 * h + 1 : 3 * h + 2]
                + three[:, 3 * h + 2 : 3 * h + 3]
            )
            logs.append(jnp.where(wanted == holder, log, NEG))
            values.append(ref[:, part].astype(F32))
        peak = functools.reduce(jnp.maximum, logs)
        loads = [jnp.exp(log - peak) for log in logs]
        total = functools.reduce(jnp.add, loads)
        mixed = functools.reduce(jnp.add, [w * v for w, v in zip(loads, values)])
        attended_ref[:, part] = (mixed / total).astype(BF16)

    me = lax.axis_index("tensor")

    @pl.loop(0, weight_ref.shape[1] // wide)
    def _(n):
        columns = pl.ds(pl.multiple_of(n * wide, 128), wide)
        partial = jnp.dot(attended_ref[...], weight_ref[:, columns], preferred_element_type=F32)
        for b in range(rows // share):
            partial_ref[b] = partial[b * share : (b + 1) * share]
        for d, ref in enumerate(out_refs):
            ref[:, columns] = partial_ref[me ^ d].astype(ref.dtype)


def fetch_kernel(start, count, source_ref, gate_ref, out_ref, sems):
    rows = out_ref.shape[0] // count
    copies = [
        pltpu.make_async_copy(
            source_ref.at[pl.ds(start + i * rows, rows)], out_ref.at[pl.ds(i * rows, rows)], sems.at[i]
        )
        for i in range(count)
    ]
    for copy in copies:
        copy.start()
    for copy in copies:
        copy.wait()


def column_kernel(count, *refs):
    terms, out_refs = refs[:count], refs[-2:]
    width = out_refs[0].shape[2]
    for i, ref in enumerate(terms):
        for half, out_ref in enumerate(out_refs):
            out_ref[i] = ref[:, half * width : (half + 1) * width]


def norm_kernel(residual_ref, gain_ref, *refs):
    terms, out_ref = refs[3:-1], refs[-1]
    hidden = residual_ref[lax.axis_index("tensor")].astype(F32)
    for ref in terms:
        hidden = hidden + ref[...].astype(F32)
    squares = jnp.mean(hidden * hidden, axis=-1, keepdims=True)
    normed = (hidden * lax.rsqrt(squares + 1e-06) * gain_ref[...].astype(F32)).astype(BF16)
    out_ref[...] = normed


def quarter_dots(x_ref, weight_refs, columns):
    depth = weight_refs[0].shape[0]
    return functools.reduce(
        jnp.add,
        [
            jnp.dot(x_ref[:, i * depth : (i + 1) * depth], ref[:, columns], preferred_element_type=F32)
            for i, ref in enumerate(weight_refs)
        ],
    )


def first_kernel(narrow, left_ref, right_ref, weight_ref, next_ref, out_ref, x_ref):
    half = left_ref.shape[0]
    x_ref[:half] = left_ref[...]
    x_ref[half:] = right_ref[...]

    @pl.loop(0, weight_ref.shape[1] // narrow)
    def _(n):
        columns = pl.ds(n * narrow if narrow % 128 else pl.multiple_of(n * narrow, 128), narrow)
        out_ref[:, columns] = quarter_dots(x_ref, (weight_ref, next_ref), columns)


def logits_kernel(
    narrow,
    spots,
    tensor_size,
    sum_in_ref,
    left_ref,
    right_ref,
    target_ref,
    weight_ref,
    next_ref,
    out_ref,
    x_ref,
    peak_ref,
    sum_ref,
    pick_ref,
    wanted_ref,
):
    half = left_ref.shape[0]
    rows = 2 * half
    share = target_ref.shape[1]
    group, tensor = lax.axis_index("group"), lax.axis_index("tensor")
    vocab = weight_ref.shape[1]
    places = [(group ^ g) * tensor_size + (tensor ^ t) for g, t in spots]
    for i, place in enumerate(places):
        wanted_ref[i * share : (i + 1) * share] = target_ref[place]
    wanted = wanted_ref[...] - (group * tensor_size + tensor) * vocab
    wanted_ref[...] = jnp.where((wanted >= 0) & (wanted < vocab), wanted, -1)
    x_ref[:half] = left_ref[...]
    x_ref[half:] = right_ref[...]
    peak_ref[...] = jnp.full_like(peak_ref, NEG)
    sum_ref[...] = jnp.zeros_like(sum_ref)
    pick_ref[...] = jnp.zeros_like(pick_ref)

    @pl.loop(0, weight_ref.shape[1] // narrow)
    def _(n):
        columns = pl.ds(n * narrow if narrow % 128 else pl.multiple_of(n * narrow, 128), narrow)
        logits = sum_in_ref[:, columns] + quarter_dots(x_ref, (weight_ref, next_ref), columns)
        parts = [logits[:, c : c + 128] for c in range(0, narrow, 128)]
        if narrow % 128:
            spare = jnp.full((rows, 128 - narrow % 128), NEG, F32)
            parts[-1] = jnp.concatenate([parts[-1], spare], axis=1)
        lane = lax.broadcasted_iota(jnp.int32, (rows, 128), 1) + n * narrow
        peak = peak_ref[...]
        higher = functools.reduce(jnp.maximum, parts, peak)
        total = sum_ref[...] * jnp.exp(peak - higher)
        picked = pick_ref[...]
        target = wanted_ref[...]
        for c, part in enumerate(parts):
            total = total + jnp.exp(part - higher)
            picked = picked + jnp.where(lane + c * 128 == target, part, 0.0)
        peak_ref[...] = higher
        sum_ref[...] = total
        pick_ref[...] = picked

    higher = peak_ref[...]
    peak = jnp.max(higher, axis=1, keepdims=True)
    sums = jnp.sum(sum_ref[...] * jnp.exp(higher - peak), axis=1, keepdims=True)
    pick = jnp.sum(pick_ref[...], axis=1, keepdims=True)
    row = lax.broadcasted_iota(jnp.int32, (rows, 128), 0)
    lane = lax.broadcasted_iota(jnp.int32, (rows, 128), 1)
    three = jnp.where(lane // share == 0, peak, jnp.where(lane // share == 1, sums, pick))
    three = jnp.where((row - lane) % share == 0, three, 0.0)
    for i, place in enumerate(places):
        out_ref[place] = jnp.sum(three[i * share : (i + 1) * share], axis=0, keepdims=True)


def final_kernel(seq, share, lengths_ref, stats_ref, out_ref):
    stats = stats_ref[...].reshape(stats_ref.shape[0], 128)
    count = lengths_ref.shape[0]
    peak = jnp.max(stats, axis=0, keepdims=True)
    sums = pltpu.roll(stats, 128 - share, 1)
    picks = pltpu.roll(stats, 128 - 2 * share, 1)
    total = jnp.sum(sums * jnp.exp(stats - peak), axis=0, keepdims=True)
    values = jnp.sum(picks, axis=0, keepdims=True) - peak - jnp.log(total)
    token = lax.broadcasted_iota(jnp.int32, (1, 128), 1) + lax.axis_index("tensor") * share
    live = jnp.zeros((1, 128), jnp.int32)
    for r in range(count):
        live = jnp.where(token // seq == r, lengths_ref[r], live)
    out_ref[...] = jnp.where(token % seq < live, values, 0.0)[0, :share]


def local(
    group_size,
    tensor_size,
    resp_query,
    resp_key,
    resp_value,
    prompt_keys,
    prompt_values,
    prompt_of,
    lengths,
    residual,
    out_weight,
    norm_gain,
    lm_weight,
    targets,
):
    rows, span = resp_query.shape
    heads = span // HEAD_DIM
    seq = rows // prompt_of.shape[0]
    key_rows = prompt_keys.shape[0]
    assert PLEN % key_rows == 0
    share = rows // tensor_size
    depth = out_weight.shape[1]
    vocab = lm_weight.shape[1]
    i32 = jnp.int32

    distances = list(range(1, group_size))
    queries = [swap(resp_query, "group", d, group_size) for d in distances]
    wanted = targets.reshape(-1, share, 1)
    inputs = (resp_query, resp_key, resp_value, prompt_keys, prompt_values)
    loaded = pl.pallas_call(
        functools.partial(load_kernel, len(inputs)),
        out_shape=[pltpu.VMEM(x.shape, x.dtype) for x in inputs],
        in_specs=[anywhere()] * (1 + len(inputs)),
        out_specs=[vmem()] * len(inputs),
        scratch_shapes=[pltpu.SemaphoreType.DMA((len(inputs),))],
        compiler_params=params(1),
        cost_estimate=cost(moved=2 * MIB),
        name="load",
    )(wanted, *map(stored, inputs))
    query, own_keys, own_values, keys, values = map(held, loaded)
    answers = pl.pallas_call(
        functools.partial(prefix_kernel, heads, len(distances)),
        out_shape=[jax.ShapeDtypeStruct((rows, span + 128), BF16)] * len(distances),
        in_specs=[vmem()] * (len(distances) + 2),
        out_specs=[vmem()] * len(distances),
        compiler_params=params(8),
        name="prefix_attention",
    )(*map(held, queries), keys, values)
    got = [swap(x, "group", d, group_size) for x, d in zip(answers, distances)]
    own = pl.pallas_call(
        functools.partial(own_kernel, heads, seq),
        out_shape=jax.ShapeDtypeStruct((rows, span + 128), F32),
        in_specs=[smem()] * 2 + [vmem()] * 5 + [anywhere()],
        out_specs=vmem(),
        compiler_params=params(6),
        cost_estimate=cost(moved=8 * MIB),
        name="own_attention",
    )(stored(lengths), stored(prompt_of), query, own_keys, own_values, keys, values, answers[0])

    def fetch(source, start, count, gate):
        return held(
            pl.pallas_call(
                functools.partial(fetch_kernel, start, 4),
                out_shape=pltpu.VMEM((count, source.shape[1]), BF16),
                in_specs=[anywhere()] * 2,
                out_specs=vmem(),
                scratch_shapes=[pltpu.SemaphoreType.DMA((4,))],
                compiler_params=params(1),
                cost_estimate=cost(moved=count * source.shape[1] * 2),
                name="fetch",
            )(stored(source), gate)
        )

    weight = fetch(out_weight, 0, span, answers[0])

    wide = 1024 if depth % 1024 == 0 else depth
    shares = pl.pallas_call(
        functools.partial(project_kernel, heads, seq, share, wide, group_size, key_rows),
        out_shape=[
            jax.ShapeDtypeStruct((share, depth), BF16 if d else F32) for d in range(tensor_size)
        ],
        in_specs=[smem()] + [vmem()] * (2 + len(distances)),
        out_specs=[vmem()] * tensor_size,
        scratch_shapes=[
            pltpu.VMEM((rows, span), BF16),
            pltpu.VMEM((tensor_size, share, wide), F32),
        ],
        compiler_params=params(6),
        name="project",
    )(stored(prompt_of), *map(held, (own, *got)), weight)
    quarter = depth // 4
    quarters = [fetch(lm_weight, i * quarter, quarter, shares[1]) for i in range(3)]

    got = [swap(shares[d], "tensor", d, tensor_size) for d in range(tensor_size - 1, 0, -1)]
    normed = pl.pallas_call(
        norm_kernel,
        out_shape=jax.ShapeDtypeStruct((share, depth), BF16),
        in_specs=[vmem()] * 2 + [anywhere()] * 3 + [vmem()] * tensor_size,
        out_specs=vmem(),
        compiler_params=params(4),
        name="norm",
    )(
        *map(held, (residual.reshape(tensor_size, share, depth), norm_gain[None])),
        *quarters,
        *map(held, (shares[0], *got)),
    )

    far = list(range(2, tensor_size, 2))
    above = list(range(2, group_size, 2))
    order = [0] + far
    here = [(g, x) for g in [0] + above for x in (0, 1)]
    column = [swap(normed, "tensor", d, tensor_size) for d in far[::-1]]
    column = [normed] + column[::-1]
    quarters.append(fetch(lm_weight, 3 * quarter, quarter, normed))
    columns = pl.pallas_call(
        functools.partial(column_kernel, len(column)),
        out_shape=[jax.ShapeDtypeStruct((len(column), share, depth // 2), BF16)] * 2,
        in_specs=[vmem()] * len(column) + [anywhere()],
        out_specs=[vmem()] * 2,
        compiler_params=params(2),
        name="column",
    )(*map(held, column), quarters[3])
    left, right = columns
    left = jnp.concatenate([left, swap(left, "tensor", 1, tensor_size)])
    right = [right] + [swap(right, "group", d, group_size) for d in above]
    left = [left] + [swap(left, "group", d, group_size) for d in above]
    across = swap(jnp.concatenate(right), "tensor", 1, tensor_size)
    across = jnp.split(across, len(right))
    right = [x for pair in zip(right, across) for x in pair]
    halves = []
    for pieces in (left, right):
        tokens = jnp.concatenate(pieces).reshape(-1, depth // 2)
        halves.append((tokens, swap(tokens, "group", 1, group_size)))
    spots = [(g + c, t + x) for c in (0, 1) for g, x in here for t in order]
    total_rows = 2 * tokens.shape[0]
    narrow = 1536 if vocab % 1536 == 0 else vocab
    limit = 10 if total_rows <= 256 else 24
    work = 2 * total_rows * (depth // 2) * vocab
    first = pl.pallas_call(
        functools.partial(first_kernel, narrow),
        out_shape=pltpu.VMEM((total_rows, vocab), F32),
        in_specs=[vmem()] * 4,
        out_specs=vmem(),
        scratch_shapes=[pltpu.VMEM((total_rows, depth // 2), BF16)],
        compiler_params=params(limit),
        cost_estimate=cost(flops=work),
        name="logits_first",
    )(*map(held, (*halves[0], *quarters[:2])))
    stats = pl.pallas_call(
        functools.partial(logits_kernel, narrow, spots, tensor_size),
        out_shape=jax.ShapeDtypeStruct((len(spots), 1, 128), F32),
        in_specs=[vmem()] * 6,
        out_specs=vmem(),
        scratch_shapes=[pltpu.VMEM((total_rows, depth // 2), BF16)]
        + [pltpu.VMEM((total_rows, 128), F32)] * 3
        + [pltpu.VMEM((total_rows, 1), i32)],
        compiler_params=params(limit),
        cost_estimate=cost(flops=work),
        name="logits",
    )(*map(held, (first, *halves[1])), wanted, *map(held, quarters[2:]))

    stats = lax.all_to_all(stats, ("group", "tensor"), 0, 0, tiled=True)
    return pl.pallas_call(
        functools.partial(final_kernel, seq, share),
        out_shape=jax.ShapeDtypeStruct((share,), F32),
        in_specs=[smem(), vmem()],
        out_specs=vmem(),
        compiler_params=params(4),
        name="final",
    )(stored(lengths), stats)


def solution(mesh):
    return jax.shard_map(
        functools.partial(local, mesh.shape["group"], mesh.shape["tensor"]),
        mesh=mesh,
        in_specs=(
            P("group", "tensor"),
            P("group", "tensor"),
            P("group", "tensor"),
            P("group", "tensor"),
            P("group", "tensor"),
            P("group"),
            P("group"),
            P("group", None),
            P("tensor", None),
            P(),
            P(None, ("group", "tensor")),
            P(),
        ),
        out_specs=P(("group", "tensor")),
        check_vma=False,
    )
```

```python
import functools

import jax
import jax.numpy as jnp
from jax import lax
from jax.experimental import pallas as pl
from jax.experimental.pallas import tpu as pltpu
from jax.sharding import PartitionSpec as P

HEAD_DIM = 128
PLEN = 512
NEG = -1e30
BF16 = jnp.bfloat16
F32 = jnp.float32
MIB = 1024 * 1024


def params(mib):
    return pltpu.CompilerParams(vmem_limit_bytes=mib * MIB)


def held(x):
    return pltpu.with_memory_space_constraint(x, pltpu.VMEM)


def stored(x):
    return pltpu.with_memory_space_constraint(x, pltpu.HBM)


def anywhere():
    return pl.BlockSpec(memory_space=pl.ANY)


def cost(flops=0, moved=0):
    return pl.CostEstimate(flops=flops, bytes_accessed=moved, transcendentals=0)


def vmem():
    return pl.BlockSpec(memory_space=pltpu.VMEM)


def smem():
    return pl.BlockSpec(memory_space=pltpu.SMEM)


def swap(x, axis, distance, size):
    return lax.ppermute(x, axis, [(i, i ^ distance) for i in range(size)])


def attend(jobs):
    factor = HEAD_DIM**-0.5
    scores = [
        lax.dot_general(q, k, (((1,), (1,)), ((), ())), preferred_element_type=F32)
        for q, k, _, _ in jobs
    ]
    scores = [
        s if job[3] is None else jnp.where(job[3], s, NEG) for s, job in zip(scores, jobs)
    ]
    peaks = [jnp.max(s, axis=1, keepdims=True) for s in scores]
    weights = [jnp.exp((s - peak) * factor) for s, peak in zip(scores, peaks)]
    weights = [
        w if job[3] is None else jnp.where(job[3], w, 0.0) for w, job in zip(weights, jobs)
    ]
    weights = [w.astype(BF16) for w in weights]
    totals = [jnp.sum(w.astype(F32), axis=1, keepdims=True) for w in weights]
    mixed = [
        jnp.dot(w, job[2], preferred_element_type=F32) for w, job in zip(weights, jobs)
    ]
    return [
        (m / total, peak * factor + jnp.log(total))
        for m, total, peak in zip(mixed, totals, peaks)
    ]


def pack_logs(logs, rows):
    lane = lax.broadcasted_iota(jnp.int32, (rows, 128), 1)
    packed = jnp.zeros((rows, 128), F32)
    for head, log in enumerate(logs):
        first = log.astype(BF16).astype(F32)
        second = (log - first).astype(BF16).astype(F32)
        third = log - first - second
        for part, value in enumerate((first, second, third)):
            packed = jnp.where(lane == 3 * head + part, value, packed)
    return packed.astype(BF16)


def load_kernel(count, gate_ref, *refs):
    sems = refs[2 * count]
    copies = [
        pltpu.make_async_copy(refs[i], refs[count + i], sems.at[i]) for i in range(count)
    ]
    for copy in copies:
        copy.start()
    for copy in copies:
        copy.wait()


def carried(source_ref, start, out_ref, sems):
    count = sems.shape[0]
    rows = out_ref.shape[0] // count
    return [
        pltpu.make_async_copy(
            source_ref.at[pl.ds(start + i * rows, rows)], out_ref.at[pl.ds(i * rows, rows)], sems.at[i]
        )
        for i in range(count)
    ]


def own_kernel(
    heads,
    seq,
    lengths_ref,
    prompt_ref,
    q_ref,
    rk_ref,
    rv_ref,
    k_ref,
    v_ref,
    source_ref,
    gate_ref,
    own_ref,
    weight_ref,
    sems,
):
    copies = carried(source_ref, 0, weight_ref, sems)
    for copy in copies:
        copy.start()
    rows = q_ref.shape[0]
    row = lax.broadcasted_iota(jnp.int32, (rows, rows), 0)
    col = lax.broadcasted_iota(jnp.int32, (rows, rows), 1)
    live = jnp.zeros((rows, rows), jnp.int32)
    for r in range(rows // seq):
        live = jnp.where(col // seq == r, lengths_ref[r], live)
    allowed = (row // seq == col // seq) & (col <= row) & (col % seq < live)
    parts = [slice(h * HEAD_DIM, (h + 1) * HEAD_DIM) for h in range(heads)]
    found = attend(
        [(q_ref[:, p], rk_ref[:, p], rv_ref[:, p], allowed) for p in parts]
        + [(q_ref[:, p], k_ref[:, p], v_ref[:, p], None) for p in parts]
    )
    here = wanted_prompts(seq, rows, prompt_ref) == lax.axis_index("group") * k_ref.shape[0] // PLEN
    lane = lax.broadcasted_iota(jnp.int32, (rows, 128), 1)
    packed = jnp.zeros((rows, 128), F32)
    for h, p in enumerate(parts):
        (first, log), (second, other) = found[h], found[heads + h]
        other = jnp.where(here, other, NEG)
        peak = jnp.maximum(log, other)
        left, right = jnp.exp(log - peak), jnp.exp(other - peak)
        own_ref[:, p] = (first * left + second * right) / (left + right)
        packed = jnp.where(lane == h, peak + jnp.log(left + right), packed)
    own_ref[:, heads * HEAD_DIM :] = packed
    for copy in copies:
        copy.wait()


def wanted_prompts(seq, rows, prompt_ref):
    row = lax.broadcasted_iota(jnp.int32, (rows, 1), 0)
    wanted = jnp.zeros((rows, 1), jnp.int32)
    for r in range(rows // seq):
        wanted = jnp.where(row // seq == r, prompt_ref[r], wanted)
    return wanted


def prefix_kernel(heads, count, *refs):
    q_refs, (k_ref, v_ref), out_refs = refs[:count], refs[count : count + 2], refs[count + 2 :]
    rows = q_refs[0].shape[0]
    parts = [slice(h * HEAD_DIM, (h + 1) * HEAD_DIM) for h in range(heads)]
    found = attend(
        [
            (jnp.concatenate([ref[:, p] for ref in q_refs], axis=0), k_ref[:, p], v_ref[:, p], None)
            for p in parts
        ]
    )
    for i in range(count):
        rung = slice(i * rows, (i + 1) * rows)
        for h, p in enumerate(parts):
            out_refs[i][:, p] = found[h][0][rung].astype(BF16)
        out_refs[i][:, heads * HEAD_DIM :] = pack_logs([log[rung] for _, log in found], rows)


def project_kernel(heads, seq, share, wide, group_size, key_rows, prompt_ref, own_ref, *refs):
    got_refs, refs = refs[: group_size - 1], refs[group_size - 1 :]
    weight_ref, source_ref, send_left_ref, keep_left_ref, keep_right_ref = refs[:5]
    send_right_refs, (quarter_ref, attended_ref, partial_ref, sems) = refs[5:-4], refs[-4:]
    copies = carried(source_ref, 0, quarter_ref, sems)
    for copy in copies:
        copy.start()
    rows = own_ref.shape[0]
    wanted = wanted_prompts(seq, rows, prompt_ref)
    group = lax.axis_index("group")
    holders = [(group ^ d) * key_rows // PLEN for d in range(1, group_size)]
    for h in range(heads):
        part = slice(h * HEAD_DIM, (h + 1) * HEAD_DIM)
        at = heads * HEAD_DIM
        logs = [own_ref[:, at + h : at + h + 1]]
        values = [own_ref[:, part]]
        for holder, ref in zip(holders, got_refs):
            three = ref[:, at : at + 128].astype(F32)
            log = (
                three[:, 3 * h : 3 * h + 1]
                + three[:, 3 * h + 1 : 3 * h + 2]
                + three[:, 3 * h + 2 : 3 * h + 3]
            )
            logs.append(jnp.where(wanted == holder, log, NEG))
            values.append(ref[:, part].astype(F32))
        peak = functools.reduce(jnp.maximum, logs)
        loads = [jnp.exp(log - peak) for log in logs]
        total = functools.reduce(jnp.add, loads)
        mixed = functools.reduce(jnp.add, [w * v for w, v in zip(loads, values)])
        attended_ref[:, part] = (mixed / total).astype(BF16)

    me = lax.axis_index("tensor")
    blocks = rows // share
    half = send_left_ref.shape[2]

    def multiply(columns):
        partial = jnp.dot(attended_ref[...], weight_ref[:, columns], preferred_element_type=F32)
        for b in range(blocks):
            partial_ref[b] = partial[b * share : (b + 1) * share]

    @pl.loop(0, half // wide)
    def _(n):
        columns = pl.ds(pl.multiple_of(n * wide, 128), wide)
        multiply(columns)
        for d in range(0, blocks, 2):
            keep_left_ref[d // 2, :, columns] = partial_ref[me ^ d]
            send_left_ref[d // 2, :, columns] = partial_ref[me ^ (d + 1)].astype(BF16)

    @pl.loop(0, half // wide)
    def _(n):
        columns = pl.ds(pl.multiple_of(n * wide, 128), wide)
        multiply(pl.ds(pl.multiple_of(half + n * wide, 128), wide))
        for d in range(blocks):
            block = partial_ref[me ^ d]
            if d < 2:
                keep_right_ref[d, :, columns] = block
            else:
                send_right_refs[d // 2 - 1][d % 2, :, columns] = block.astype(BF16)

    for copy in copies:
        copy.wait()


def fold_left_kernel(gate_ref, keep_ref, got_ref, *out_refs):
    for i, ref in enumerate(out_refs):
        ref[...] = (keep_ref[i] + got_ref[i].astype(F32)).astype(ref.dtype)


def fold_right_kernel(gate_ref, keep_ref, *refs):
    got_refs, out_refs = refs[:-2], refs[-2:]
    for i, ref in enumerate(out_refs):
        total = keep_ref[i]
        for got_ref in got_refs:
            total = total + got_ref[i].astype(F32)
        ref[...] = total.astype(ref.dtype)


def fetch_kernel(start, source_ref, gate_ref, out_ref, sems):
    copies = carried(source_ref, start, out_ref, sems)
    for copy in copies:
        copy.start()
    for copy in copies:
        copy.wait()


def column_kernel(count, *refs):
    terms, out_refs = refs[:count], refs[-2:]
    width = out_refs[0].shape[2]
    for i, ref in enumerate(terms):
        for half, out_ref in enumerate(out_refs):
            out_ref[i] = ref[:, half * width : (half + 1) * width]


def norm_kernel(far_count, residual_ref, gain_ref, *refs):
    left_refs, right_refs, out_ref = refs[: 1 + far_count], refs[1 + far_count : -1], refs[-1]
    residual = residual_ref[lax.axis_index("tensor")].astype(F32)
    width = residual.shape[1] // 2
    halves = []
    for i, terms in enumerate((left_refs, right_refs)):
        hidden = residual[:, i * width : (i + 1) * width]
        for ref in terms:
            hidden = hidden + ref[...].astype(F32)
        halves.append(hidden)
    squares = sum(jnp.sum(hidden * hidden, axis=-1, keepdims=True) for hidden in halves)
    scale = lax.rsqrt(squares / residual.shape[1] + 1e-06)
    for i, hidden in enumerate(halves):
        columns = slice(i * width, (i + 1) * width)
        out_ref[:, columns] = (hidden * scale * gain_ref[:, columns].astype(F32)).astype(BF16)


def quarter_dots(x_ref, weight_refs, columns):
    depth = weight_refs[0].shape[0]
    return functools.reduce(
        jnp.add,
        [
            jnp.dot(x_ref[:, i * depth : (i + 1) * depth], ref[:, columns], preferred_element_type=F32)
            for i, ref in enumerate(weight_refs)
        ],
    )


def first_kernel(
    narrow, left_ref, right_ref, weight_ref, next_ref, source_ref, out_ref, last_ref, x_ref, sems
):
    copies = carried(source_ref, source_ref.shape[0] - last_ref.shape[0], last_ref, sems)
    for copy in copies:
        copy.start()
    half = left_ref.shape[0]
    x_ref[:half] = left_ref[...]
    x_ref[half:] = right_ref[...]

    @pl.loop(0, weight_ref.shape[1] // narrow)
    def _(n):
        columns = pl.ds(n * narrow if narrow % 128 else pl.multiple_of(n * narrow, 128), narrow)
        out_ref[:, columns] = quarter_dots(x_ref, (weight_ref, next_ref), columns)

    for copy in copies:
        copy.wait()


def logits_kernel(
    narrow,
    spots,
    tensor_size,
    sum_in_ref,
    left_ref,
    right_ref,
    target_ref,
    weight_ref,
    next_ref,
    out_ref,
    x_ref,
    peak_ref,
    sum_ref,
    pick_ref,
    wanted_ref,
):
    half = left_ref.shape[0]
    rows = 2 * half
    share = target_ref.shape[1]
    group, tensor = lax.axis_index("group"), lax.axis_index("tensor")
    vocab = weight_ref.shape[1]
    places = [(group ^ g) * tensor_size + (tensor ^ t) for g, t in spots]
    for i, place in enumerate(places):
        wanted_ref[i * share : (i + 1) * share] = target_ref[place]
    wanted = wanted_ref[...] - (group * tensor_size + tensor) * vocab
    wanted_ref[...] = jnp.where((wanted >= 0) & (wanted < vocab), wanted, -1)
    x_ref[:half] = left_ref[...]
    x_ref[half:] = right_ref[...]
    peak_ref[...] = jnp.full_like(peak_ref, NEG)
    sum_ref[...] = jnp.zeros_like(sum_ref)
    pick_ref[...] = jnp.zeros_like(pick_ref)

    @pl.loop(0, weight_ref.shape[1] // narrow)
    def _(n):
        columns = pl.ds(n * narrow if narrow % 128 else pl.multiple_of(n * narrow, 128), narrow)
        logits = sum_in_ref[:, columns] + quarter_dots(x_ref, (weight_ref, next_ref), columns)
        parts = [logits[:, c : c + 128] for c in range(0, narrow, 128)]
        if narrow % 128:
            spare = jnp.full((rows, 128 - narrow % 128), NEG, F32)
            parts[-1] = jnp.concatenate([parts[-1], spare], axis=1)
        lane = lax.broadcasted_iota(jnp.int32, (rows, 128), 1) + n * narrow
        peak = peak_ref[...]
        higher = functools.reduce(jnp.maximum, parts, peak)
        total = sum_ref[...] * jnp.exp(peak - higher)
        picked = pick_ref[...]
        target = wanted_ref[...]
        for c, part in enumerate(parts):
            total = total + jnp.exp(part - higher)
            picked = picked + jnp.where(lane + c * 128 == target, part, 0.0)
        peak_ref[...] = higher
        sum_ref[...] = total
        pick_ref[...] = picked

    higher = peak_ref[...]
    peak = jnp.max(higher, axis=1, keepdims=True)
    sums = jnp.sum(sum_ref[...] * jnp.exp(higher - peak), axis=1, keepdims=True)
    pick = jnp.sum(pick_ref[...], axis=1, keepdims=True)
    row = lax.broadcasted_iota(jnp.int32, (rows, 128), 0)
    lane = lax.broadcasted_iota(jnp.int32, (rows, 128), 1)
    three = jnp.where(lane // share == 0, peak, jnp.where(lane // share == 1, sums, pick))
    three = jnp.where((row - lane) % share == 0, three, 0.0)
    for i, place in enumerate(places):
        out_ref[place] = jnp.sum(three[i * share : (i + 1) * share], axis=0, keepdims=True)


def final_kernel(seq, share, lengths_ref, stats_ref, out_ref):
    stats = stats_ref[...].reshape(stats_ref.shape[0], 128)
    count = lengths_ref.shape[0]
    peak = jnp.max(stats, axis=0, keepdims=True)
    sums = pltpu.roll(stats, 128 - share, 1)
    picks = pltpu.roll(stats, 128 - 2 * share, 1)
    total = jnp.sum(sums * jnp.exp(stats - peak), axis=0, keepdims=True)
    values = jnp.sum(picks, axis=0, keepdims=True) - peak - jnp.log(total)
    token = lax.broadcasted_iota(jnp.int32, (1, 128), 1) + lax.axis_index("tensor") * share
    live = jnp.zeros((1, 128), jnp.int32)
    for r in range(count):
        live = jnp.where(token // seq == r, lengths_ref[r], live)
    out_ref[...] = jnp.where(token % seq < live, values, 0.0)[0, :share]


def local(
    group_size,
    tensor_size,
    resp_query,
    resp_key,
    resp_value,
    prompt_keys,
    prompt_values,
    prompt_of,
    lengths,
    residual,
    out_weight,
    norm_gain,
    lm_weight,
    targets,
):
    rows, span = resp_query.shape
    heads = span // HEAD_DIM
    seq = rows // prompt_of.shape[0]
    key_rows = prompt_keys.shape[0]
    assert PLEN % key_rows == 0
    share = rows // tensor_size
    depth = out_weight.shape[1]
    vocab = lm_weight.shape[1]
    i32 = jnp.int32

    distances = list(range(1, group_size))
    queries = [swap(resp_query, "group", d, group_size) for d in distances]
    wanted = targets.reshape(-1, share, 1)
    inputs = (resp_query, resp_key, resp_value, prompt_keys, prompt_values)
    loaded = pl.pallas_call(
        functools.partial(load_kernel, len(inputs)),
        out_shape=[pltpu.VMEM(x.shape, x.dtype) for x in inputs],
        in_specs=[anywhere()] * (1 + len(inputs)),
        out_specs=[vmem()] * len(inputs),
        scratch_shapes=[pltpu.SemaphoreType.DMA((len(inputs),))],
        compiler_params=params(1),
        cost_estimate=cost(moved=2 * MIB),
        name="load",
    )(wanted, *map(stored, inputs))
    query, own_keys, own_values, keys, values = map(held, loaded)
    answers = pl.pallas_call(
        functools.partial(prefix_kernel, heads, len(distances)),
        out_shape=[jax.ShapeDtypeStruct((rows, span + 128), BF16)] * len(distances),
        in_specs=[vmem()] * (len(distances) + 2),
        out_specs=[vmem()] * len(distances),
        compiler_params=params(8),
        name="prefix_attention",
    )(*map(held, queries), keys, values)
    got = [swap(x, "group", d, group_size) for x, d in zip(answers, distances)]
    own, weight = pl.pallas_call(
        functools.partial(own_kernel, heads, seq),
        out_shape=[
            jax.ShapeDtypeStruct((rows, span + 128), F32),
            pltpu.VMEM(out_weight.shape, BF16),
        ],
        in_specs=[smem()] * 2 + [vmem()] * 5 + [anywhere()] * 2,
        out_specs=[vmem()] * 2,
        scratch_shapes=[pltpu.SemaphoreType.DMA((4,))],
        compiler_params=params(6),
        cost_estimate=cost(moved=8 * MIB),
        name="own_attention",
    )(
        stored(lengths),
        stored(prompt_of),
        query,
        own_keys,
        own_values,
        keys,
        values,
        stored(out_weight),
        answers[0],
    )

    def fetch(source, start, count, gate):
        return held(
            pl.pallas_call(
                functools.partial(fetch_kernel, start),
                out_shape=pltpu.VMEM((count, source.shape[1]), BF16),
                in_specs=[anywhere()] * 2,
                out_specs=vmem(),
                scratch_shapes=[pltpu.SemaphoreType.DMA((4,))],
                compiler_params=params(1),
                cost_estimate=cost(moved=count * source.shape[1] * 2),
                name="fetch",
            )(stored(source), gate)
        )

    half = depth // 2
    quarter = depth // 4
    wide = 1280 if half % 1280 == 0 else half
    pairs = tensor_size // 2
    send_left, keep_left, keep_right, *rest = pl.pallas_call(
        functools.partial(project_kernel, heads, seq, share, wide, group_size, key_rows),
        out_shape=[
            jax.ShapeDtypeStruct((pairs, share, half), BF16),
            jax.ShapeDtypeStruct((pairs, share, half), F32),
            jax.ShapeDtypeStruct((2, share, half), F32),
        ]
        + [jax.ShapeDtypeStruct((2, share, half), BF16)] * (pairs - 1)
        + [pltpu.VMEM((quarter, vocab), BF16)],
        in_specs=[smem()] + [vmem()] * (2 + len(distances)) + [anywhere()],
        out_specs=[vmem()] * (3 + pairs),
        scratch_shapes=[
            pltpu.VMEM((rows, span), BF16),
            pltpu.VMEM((tensor_size, share, wide), F32),
            pltpu.SemaphoreType.DMA((4,)),
        ],
        compiler_params=params(6),
        cost_estimate=cost(moved=quarter * vocab * 2),
        name="project",
    )(stored(prompt_of), *map(held, (own, *got)), held(weight), stored(lm_weight))
    quarters = [held(rest.pop()), fetch(lm_weight, quarter, quarter, send_left)]

    far = list(range(2, tensor_size, 2))
    got_left = swap(send_left, "tensor", 1, tensor_size)
    got_right = [swap(x, "tensor", d, tensor_size) for x, d in zip(rest[::-1], far[::-1])]
    left = pl.pallas_call(
        fold_left_kernel,
        out_shape=[jax.ShapeDtypeStruct((share, half), F32)]
        + [jax.ShapeDtypeStruct((share, half), BF16)] * len(far),
        in_specs=[anywhere()] + [vmem()] * 2,
        out_specs=[vmem()] * (1 + len(far)),
        compiler_params=params(2),
        name="fold_left",
    )(quarters[1], held(keep_left), held(got_left))
    got_left = [swap(x, "tensor", d, tensor_size) for x, d in zip(left[:0:-1], far[::-1])]
    right = pl.pallas_call(
        fold_right_kernel,
        out_shape=[
            jax.ShapeDtypeStruct((share, half), F32),
            jax.ShapeDtypeStruct((share, half), BF16),
        ],
        in_specs=[anywhere()] + [vmem()] * (1 + len(far)),
        out_specs=[vmem()] * 2,
        compiler_params=params(2),
        name="fold_right",
    )(left[1], *map(held, (keep_right, *got_right)))
    got_right = swap(right[1], "tensor", 1, tensor_size)
    normed = pl.pallas_call(
        functools.partial(norm_kernel, len(far)),
        out_shape=jax.ShapeDtypeStruct((share, depth), BF16),
        in_specs=[vmem()] * (5 + len(far)),
        out_specs=vmem(),
        compiler_params=params(4),
        name="norm",
    )(
        *map(held, (residual.reshape(tensor_size, share, depth), norm_gain[None])),
        *map(held, (left[0], *got_left, right[0], got_right)),
    )

    above = list(range(2, group_size, 2))
    order = [0] + far
    here = [(g, x) for g in [0] + above for x in (0, 1)]
    column = [swap(normed, "tensor", d, tensor_size) for d in far[::-1]]
    column = [normed] + column[::-1]
    quarters.append(fetch(lm_weight, 2 * quarter, quarter, normed))
    columns = pl.pallas_call(
        functools.partial(column_kernel, len(column)),
        out_shape=[jax.ShapeDtypeStruct((len(column), share, half), BF16)] * 2,
        in_specs=[vmem()] * len(column) + [anywhere()],
        out_specs=[vmem()] * 2,
        compiler_params=params(2),
        name="column",
    )(*map(held, column), quarters[2])
    left, right = columns
    left = jnp.concatenate([left, swap(left, "tensor", 1, tensor_size)])
    right = [right] + [swap(right, "group", d, group_size) for d in above]
    left = [left] + [swap(left, "group", d, group_size) for d in above]
    across = swap(jnp.concatenate(right), "tensor", 1, tensor_size)
    across = jnp.split(across, len(right))
    right = [x for pair in zip(right, across) for x in pair]
    halves = []
    for pieces in (left, right):
        tokens = jnp.concatenate(pieces).reshape(-1, half)
        halves.append((tokens, swap(tokens, "group", 1, group_size)))
    spots = [(g + c, t + x) for c in (0, 1) for g, x in here for t in order]
    total_rows = 2 * tokens.shape[0]
    narrow = 1536 if vocab % 1536 == 0 else vocab
    limit = 10 if total_rows <= 256 else 24
    work = 2 * total_rows * (half) * vocab
    first, last = pl.pallas_call(
        functools.partial(first_kernel, narrow),
        out_shape=[pltpu.VMEM((total_rows, vocab), F32), pltpu.VMEM((quarter, vocab), BF16)],
        in_specs=[vmem()] * 4 + [anywhere()],
        out_specs=[vmem()] * 2,
        scratch_shapes=[
            pltpu.VMEM((total_rows, half), BF16),
            pltpu.SemaphoreType.DMA((4,)),
        ],
        compiler_params=params(limit),
        cost_estimate=cost(flops=work),
        name="logits_first",
    )(*map(held, (*halves[0], *quarters[:2])), stored(lm_weight))
    stats = pl.pallas_call(
        functools.partial(logits_kernel, narrow, spots, tensor_size),
        out_shape=jax.ShapeDtypeStruct((len(spots), 1, 128), F32),
        in_specs=[vmem()] * 6,
        out_specs=vmem(),
        scratch_shapes=[pltpu.VMEM((total_rows, half), BF16)]
        + [pltpu.VMEM((total_rows, 128), F32)] * 3
        + [pltpu.VMEM((total_rows, 1), i32)],
        compiler_params=params(limit),
        cost_estimate=cost(flops=work),
        name="logits",
    )(*map(held, (first, *halves[1])), wanted, held(quarters[2]), held(last))

    stats = lax.all_to_all(stats, ("group", "tensor"), 0, 0, tiled=True)
    return pl.pallas_call(
        functools.partial(final_kernel, seq, share),
        out_shape=jax.ShapeDtypeStruct((share,), F32),
        in_specs=[smem(), vmem()],
        out_specs=vmem(),
        compiler_params=params(4),
        name="final",
    )(stored(lengths), stats)


def solution(mesh):
    return jax.shard_map(
        functools.partial(local, mesh.shape["group"], mesh.shape["tensor"]),
        mesh=mesh,
        in_specs=(
            P("group", "tensor"),
            P("group", "tensor"),
            P("group", "tensor"),
            P("group", "tensor"),
            P("group", "tensor"),
            P("group"),
            P("group"),
            P("group", None),
            P("tensor", None),
            P(),
            P(None, ("group", "tensor")),
            P(),
        ),
        out_specs=P(("group", "tensor")),
        check_vma=False,
    )
```

```python
import functools

import jax
import jax.numpy as jnp
from jax import lax
from jax.experimental import pallas as pl
from jax.experimental.pallas import tpu as pltpu
from jax.sharding import PartitionSpec as P

HEAD_DIM = 128
PLEN = 512
NEG = -1e30
BF16 = jnp.bfloat16
F32 = jnp.float32
MIB = 1024 * 1024


def params(mib):
    return pltpu.CompilerParams(vmem_limit_bytes=mib * MIB)


def held(x):
    return pltpu.with_memory_space_constraint(x, pltpu.VMEM)


def stored(x):
    return pltpu.with_memory_space_constraint(x, pltpu.HBM)


def anywhere():
    return pl.BlockSpec(memory_space=pl.ANY)


def cost(flops=0, moved=0):
    return pl.CostEstimate(flops=flops, bytes_accessed=moved, transcendentals=0)


def vmem():
    return pl.BlockSpec(memory_space=pltpu.VMEM)


def smem():
    return pl.BlockSpec(memory_space=pltpu.SMEM)


def swap(x, axis, distance, size):
    return lax.ppermute(x, axis, [(i, i ^ distance) for i in range(size)])


def attend(jobs):
    factor = HEAD_DIM**-0.5
    scores = [
        lax.dot_general(q, k, (((1,), (1,)), ((), ())), preferred_element_type=F32)
        for q, k, _, _ in jobs
    ]
    scores = [
        s if job[3] is None else jnp.where(job[3], s, NEG) for s, job in zip(scores, jobs)
    ]
    peaks = [jnp.max(s, axis=1, keepdims=True) for s in scores]
    weights = [jnp.exp((s - peak) * factor) for s, peak in zip(scores, peaks)]
    weights = [
        w if job[3] is None else jnp.where(job[3], w, 0.0) for w, job in zip(weights, jobs)
    ]
    weights = [w.astype(BF16) for w in weights]
    totals = [jnp.sum(w.astype(F32), axis=1, keepdims=True) for w in weights]
    mixed = [
        jnp.dot(w, job[2], preferred_element_type=F32) for w, job in zip(weights, jobs)
    ]
    return [
        (m / total, peak * factor + jnp.log(total))
        for m, total, peak in zip(mixed, totals, peaks)
    ]


def pack_logs(logs, rows):
    lane = lax.broadcasted_iota(jnp.int32, (rows, 128), 1)
    packed = jnp.zeros((rows, 128), F32)
    for head, log in enumerate(logs):
        first = log.astype(BF16).astype(F32)
        second = (log - first).astype(BF16).astype(F32)
        third = log - first - second
        for part, value in enumerate((first, second, third)):
            packed = jnp.where(lane == 3 * head + part, value, packed)
    return packed.astype(BF16)


def load_kernel(count, gate_ref, *refs):
    sems = refs[2 * count]
    copies = [
        pltpu.make_async_copy(refs[i], refs[count + i], sems.at[i]) for i in range(count)
    ]
    for copy in copies:
        copy.start()
    for copy in copies:
        copy.wait()


def carried(source_ref, start, out_ref, sems):
    count = sems.shape[0]
    rows = out_ref.shape[0] // count
    return [
        pltpu.make_async_copy(
            source_ref.at[pl.ds(start + i * rows, rows)], out_ref.at[pl.ds(i * rows, rows)], sems.at[i]
        )
        for i in range(count)
    ]


def own_kernel(
    heads,
    seq,
    share,
    lengths_ref,
    prompt_ref,
    q_ref,
    rk_ref,
    rv_ref,
    k_ref,
    v_ref,
    source_ref,
    gate_ref,
    own_ref,
    live_ref,
    weight_ref,
    sems,
):
    copies = carried(source_ref, 0, weight_ref, sems)
    for copy in copies:
        copy.start()
    rows = q_ref.shape[0]
    row = lax.broadcasted_iota(jnp.int32, (rows, rows), 0)
    col = lax.broadcasted_iota(jnp.int32, (rows, rows), 1)
    live = jnp.zeros((rows, rows), jnp.int32)
    for r in range(rows // seq):
        live = jnp.where(col // seq == r, lengths_ref[r], live)
    allowed = (row // seq == col // seq) & (col <= row) & (col % seq < live)
    parts = [slice(h * HEAD_DIM, (h + 1) * HEAD_DIM) for h in range(heads)]
    found = attend(
        [(q_ref[:, p], rk_ref[:, p], rv_ref[:, p], allowed) for p in parts]
        + [(q_ref[:, p], k_ref[:, p], v_ref[:, p], None) for p in parts]
    )
    here = wanted_prompts(seq, rows, prompt_ref) == lax.axis_index("group") * k_ref.shape[0] // PLEN
    lane = lax.broadcasted_iota(jnp.int32, (rows, 128), 1)
    packed = jnp.zeros((rows, 128), F32)
    for h, p in enumerate(parts):
        (first, log), (second, other) = found[h], found[heads + h]
        other = jnp.where(here, other, NEG)
        peak = jnp.maximum(log, other)
        left, right = jnp.exp(log - peak), jnp.exp(other - peak)
        own_ref[:, p] = (first * left + second * right) / (left + right)
        packed = jnp.where(lane == h, peak + jnp.log(left + right), packed)
    own_ref[:, heads * HEAD_DIM :] = packed
    token = lax.broadcasted_iota(jnp.int32, live_ref.shape, 1) + lax.axis_index("tensor") * share
    length = jnp.zeros(live_ref.shape, jnp.int32)
    for r in range(rows // seq):
        length = jnp.where(token // seq == r, lengths_ref[r], length)
    live_ref[...] = jnp.where(token % seq < length, 1.0, 0.0)
    for copy in copies:
        copy.wait()


def wanted_prompts(seq, rows, prompt_ref):
    row = lax.broadcasted_iota(jnp.int32, (rows, 1), 0)
    wanted = jnp.zeros((rows, 1), jnp.int32)
    for r in range(rows // seq):
        wanted = jnp.where(row // seq == r, prompt_ref[r], wanted)
    return wanted


def prefix_kernel(heads, count, *refs):
    q_refs, (k_ref, v_ref), out_refs = refs[:count], refs[count : count + 2], refs[count + 2 :]
    rows = q_refs[0].shape[0]
    parts = [slice(h * HEAD_DIM, (h + 1) * HEAD_DIM) for h in range(heads)]
    found = attend(
        [
            (jnp.concatenate([ref[:, p] for ref in q_refs], axis=0), k_ref[:, p], v_ref[:, p], None)
            for p in parts
        ]
    )
    for i in range(count):
        rung = slice(i * rows, (i + 1) * rows)
        for h, p in enumerate(parts):
            out_refs[i][:, p] = found[h][0][rung].astype(BF16)
        out_refs[i][:, heads * HEAD_DIM :] = pack_logs([log[rung] for _, log in found], rows)


def project_kernel(heads, seq, share, wide, group_size, key_rows, prompt_ref, own_ref, *refs):
    got_refs, refs = refs[: group_size - 1], refs[group_size - 1 :]
    weight_ref, send_left_ref, keep_left_ref, keep_right_ref = refs[:4]
    send_right_refs, (attended_ref, partial_ref) = refs[4:-2], refs[-2:]
    rows = own_ref.shape[0]
    wanted = wanted_prompts(seq, rows, prompt_ref)
    group = lax.axis_index("group")
    holders = [(group ^ d) * key_rows // PLEN for d in range(group_size - 1, 0, -1)]
    for h in range(heads):
        part = slice(h * HEAD_DIM, (h + 1) * HEAD_DIM)
        at = heads * HEAD_DIM
        logs = [own_ref[:, at + h : at + h + 1]]
        values = [own_ref[:, part]]
        for holder, ref in zip(holders, got_refs):
            three = ref[:, at : at + 128].astype(F32)
            log = (
                three[:, 3 * h : 3 * h + 1]
                + three[:, 3 * h + 1 : 3 * h + 2]
                + three[:, 3 * h + 2 : 3 * h + 3]
            )
            logs.append(jnp.where(wanted == holder, log, NEG))
            values.append(ref[:, part].astype(F32))
        peak = functools.reduce(jnp.maximum, logs)
        loads = [jnp.exp(log - peak) for log in logs]
        total = functools.reduce(jnp.add, loads)
        mixed = functools.reduce(jnp.add, [w * v for w, v in zip(loads, values)])
        attended_ref[:, part] = (mixed / total).astype(BF16)

    me = lax.axis_index("tensor")
    blocks = rows // share
    half = send_left_ref.shape[2]

    def multiply(columns):
        partial = jnp.dot(attended_ref[...], weight_ref[:, columns], preferred_element_type=F32)
        for b in range(blocks):
            partial_ref[b] = partial[b * share : (b + 1) * share]

    @pl.loop(0, half // wide)
    def _(n):
        columns = pl.ds(pl.multiple_of(n * wide, 128), wide)
        multiply(columns)
        for d in range(0, blocks, 2):
            keep_left_ref[d // 2, :, columns] = partial_ref[me ^ d]
            send_left_ref[d // 2, :, columns] = partial_ref[me ^ (d + 1)].astype(BF16)

    @pl.loop(0, half // wide)
    def _(n):
        columns = pl.ds(pl.multiple_of(n * wide, 128), wide)
        multiply(pl.ds(pl.multiple_of(half + n * wide, 128), wide))
        for d in range(blocks):
            block = partial_ref[me ^ d]
            if d < 2:
                keep_right_ref[d, :, columns] = block
            else:
                send_right_refs[d // 2 - 1][d % 2, :, columns] = block.astype(BF16)


def fold_left_kernel(keep_ref, got_ref, *out_refs):
    for i, ref in enumerate(out_refs):
        ref[...] = (keep_ref[i] + got_ref[i].astype(F32)).astype(ref.dtype)


def fold_right_kernel(gate_ref, keep_ref, *refs):
    got_refs, out_refs = refs[:-2], refs[-2:]
    for i, ref in enumerate(out_refs):
        total = keep_ref[i]
        for got_ref in got_refs:
            total = total + got_ref[i].astype(F32)
        ref[...] = total.astype(ref.dtype)


def fetch_kernel(start, source_ref, gate_ref, out_ref, sems):
    copies = carried(source_ref, start, out_ref, sems)
    for copy in copies:
        copy.start()
    for copy in copies:
        copy.wait()


def column_kernel(count, *refs):
    terms, out_refs = refs[:count], refs[-2:]
    width = out_refs[0].shape[2]
    for i, ref in enumerate(terms):
        for half, out_ref in enumerate(out_refs):
            out_ref[i] = ref[:, half * width : (half + 1) * width]


def norm_kernel(far_count, residual_ref, gain_ref, *refs):
    left_refs, right_refs, out_ref = refs[: 1 + far_count], refs[1 + far_count : -1], refs[-1]
    residual = residual_ref[lax.axis_index("tensor")].astype(F32)
    width = residual.shape[1] // 2
    halves = []
    for i, terms in enumerate((left_refs, right_refs)):
        hidden = residual[:, i * width : (i + 1) * width]
        for ref in terms:
            hidden = hidden + ref[...].astype(F32)
        halves.append(hidden)
    squares = sum(jnp.sum(hidden * hidden, axis=-1, keepdims=True) for hidden in halves)
    scale = lax.rsqrt(squares / residual.shape[1] + 1e-06)
    for i, hidden in enumerate(halves):
        columns = slice(i * width, (i + 1) * width)
        out_ref[:, columns] = (hidden * scale * gain_ref[:, columns].astype(F32)).astype(BF16)


def join_kernel(count, *refs):
    out_ref = refs[-1]
    start = 0
    for ref in refs[:count]:
        out_ref[start : start + ref.shape[0]] = ref[...]
        start += ref.shape[0]


def quarter_dots(x_ref, weight_refs, columns):
    depth = weight_refs[0].shape[0]
    return functools.reduce(
        jnp.add,
        [
            jnp.dot(x_ref[:, i * depth : (i + 1) * depth], ref[:, columns], preferred_element_type=F32)
            for i, ref in enumerate(weight_refs)
        ],
    )


def first_kernel(
    narrow, left_ref, right_ref, weight_ref, next_ref, source_ref, out_ref, last_ref, x_ref, sems
):
    copies = carried(source_ref, source_ref.shape[0] - last_ref.shape[0], last_ref, sems)
    for copy in copies:
        copy.start()
    half = left_ref.shape[0]
    x_ref[:half] = left_ref[...]
    x_ref[half:] = right_ref[...]

    @pl.loop(0, weight_ref.shape[1] // narrow)
    def _(n):
        columns = pl.ds(n * narrow if narrow % 128 else pl.multiple_of(n * narrow, 128), narrow)
        out_ref[:, columns] = quarter_dots(x_ref, (weight_ref, next_ref), columns)

    for copy in copies:
        copy.wait()


def logits_kernel(
    narrow,
    spots,
    tensor_size,
    sum_in_ref,
    left_ref,
    right_ref,
    target_ref,
    weight_ref,
    next_ref,
    out_ref,
    x_ref,
    peak_ref,
    sum_ref,
    pick_ref,
    wanted_ref,
):
    half = left_ref.shape[0]
    rows = 2 * half
    share = target_ref.shape[1]
    group, tensor = lax.axis_index("group"), lax.axis_index("tensor")
    vocab = weight_ref.shape[1]
    places = [(group ^ g) * tensor_size + (tensor ^ t) for g, t in spots]
    for i, place in enumerate(places):
        wanted_ref[i * share : (i + 1) * share] = target_ref[place]
    wanted = wanted_ref[...] - (group * tensor_size + tensor) * vocab
    wanted_ref[...] = jnp.where((wanted >= 0) & (wanted < vocab), wanted, -1)
    x_ref[:half] = left_ref[...]
    x_ref[half:] = right_ref[...]
    peak_ref[...] = jnp.full_like(peak_ref, NEG)
    sum_ref[...] = jnp.zeros_like(sum_ref)
    pick_ref[...] = jnp.zeros_like(pick_ref)

    @pl.loop(0, weight_ref.shape[1] // narrow)
    def _(n):
        columns = pl.ds(n * narrow if narrow % 128 else pl.multiple_of(n * narrow, 128), narrow)
        logits = sum_in_ref[:, columns] + quarter_dots(x_ref, (weight_ref, next_ref), columns)
        parts = [logits[:, c : c + 128] for c in range(0, narrow, 128)]
        if narrow % 128:
            spare = jnp.full((rows, 128 - narrow % 128), NEG, F32)
            parts[-1] = jnp.concatenate([parts[-1], spare], axis=1)
        lane = lax.broadcasted_iota(jnp.int32, (rows, 128), 1) + n * narrow
        peak = peak_ref[...]
        higher = functools.reduce(jnp.maximum, parts, peak)
        total = sum_ref[...] * jnp.exp(peak - higher)
        picked = pick_ref[...]
        target = wanted_ref[...]
        for c, part in enumerate(parts):
            total = total + jnp.exp(part - higher)
            picked = picked + jnp.where(lane + c * 128 == target, part, 0.0)
        peak_ref[...] = higher
        sum_ref[...] = total
        pick_ref[...] = picked

    higher = peak_ref[...]
    peak = jnp.max(higher, axis=1, keepdims=True)
    sums = jnp.sum(sum_ref[...] * jnp.exp(higher - peak), axis=1, keepdims=True)
    pick = jnp.sum(pick_ref[...], axis=1, keepdims=True)
    row = lax.broadcasted_iota(jnp.int32, (rows, 128), 0)
    lane = lax.broadcasted_iota(jnp.int32, (rows, 128), 1)
    three = jnp.where(lane // share == 0, peak, jnp.where(lane // share == 1, sums, pick))
    three = jnp.where((row - lane) % share == 0, three, 0.0)
    for i, place in enumerate(places):
        out_ref[place] = jnp.sum(three[i * share : (i + 1) * share], axis=0, keepdims=True)


def final_kernel(share, live_ref, stats_ref, out_ref):
    stats = stats_ref[...].reshape(stats_ref.shape[0], 128)
    peak = jnp.max(stats, axis=0, keepdims=True)
    sums = pltpu.roll(stats, 128 - share, 1)
    picks = pltpu.roll(stats, 128 - 2 * share, 1)
    total = jnp.sum(sums * jnp.exp(stats - peak), axis=0, keepdims=True)
    values = jnp.sum(picks, axis=0, keepdims=True) - peak - jnp.log(total)
    out_ref[...] = jnp.where(live_ref[:1] > 0.0, values, 0.0)[0, :share]


def local(
    group_size,
    tensor_size,
    resp_query,
    resp_key,
    resp_value,
    prompt_keys,
    prompt_values,
    prompt_of,
    lengths,
    residual,
    out_weight,
    norm_gain,
    lm_weight,
    targets,
):
    rows, span = resp_query.shape
    heads = span // HEAD_DIM
    seq = rows // prompt_of.shape[0]
    key_rows = prompt_keys.shape[0]
    assert PLEN % key_rows == 0
    share = rows // tensor_size
    depth = out_weight.shape[1]
    vocab = lm_weight.shape[1]
    i32 = jnp.int32

    distances = list(range(group_size - 1, 0, -1))
    queries = [swap(resp_query, "group", d, group_size) for d in distances]
    wanted = targets.reshape(-1, share, 1)
    inputs = (resp_query, resp_key, resp_value, prompt_keys, prompt_values)
    loaded = pl.pallas_call(
        functools.partial(load_kernel, len(inputs)),
        out_shape=[pltpu.VMEM(x.shape, x.dtype) for x in inputs],
        in_specs=[anywhere()] * (1 + len(inputs)),
        out_specs=[vmem()] * len(inputs),
        scratch_shapes=[pltpu.SemaphoreType.DMA((len(inputs),))],
        compiler_params=params(1),
        cost_estimate=cost(moved=2 * MIB),
        name="load",
    )(wanted, *map(stored, inputs))
    query, own_keys, own_values, keys, values = map(held, loaded)
    answers = pl.pallas_call(
        functools.partial(prefix_kernel, heads, len(distances)),
        out_shape=[jax.ShapeDtypeStruct((rows, span + 128), BF16)] * len(distances),
        in_specs=[vmem()] * (len(distances) + 2),
        out_specs=[vmem()] * len(distances),
        compiler_params=params(8),
        name="prefix_attention",
    )(*map(held, queries), keys, values)
    got = [swap(x, "group", d, group_size) for x, d in zip(answers, distances)]
    own, live, weight = pl.pallas_call(
        functools.partial(own_kernel, heads, seq, share),
        out_shape=[
            jax.ShapeDtypeStruct((rows, span + 128), F32),
            jax.ShapeDtypeStruct((8, 128), F32),
            pltpu.VMEM(out_weight.shape, BF16),
        ],
        in_specs=[smem()] * 2 + [vmem()] * 5 + [anywhere()] * 2,
        out_specs=[vmem()] * 3,
        scratch_shapes=[pltpu.SemaphoreType.DMA((4,))],
        compiler_params=params(6),
        cost_estimate=cost(moved=8 * MIB),
        name="own_attention",
    )(
        stored(lengths),
        stored(prompt_of),
        query,
        own_keys,
        own_values,
        keys,
        values,
        stored(out_weight),
        answers[0],
    )

    def fetch(source, start, count, gate):
        return held(
            pl.pallas_call(
                functools.partial(fetch_kernel, start),
                out_shape=pltpu.VMEM((count, source.shape[1]), BF16),
                in_specs=[anywhere()] * 2,
                out_specs=vmem(),
                scratch_shapes=[pltpu.SemaphoreType.DMA((4,))],
                compiler_params=params(1),
                cost_estimate=cost(moved=count * source.shape[1] * 2),
                name="fetch",
            )(stored(source), gate)
        )

    half = depth // 2
    quarter = depth // 4
    wide = 1280 if half % 1280 == 0 else half
    pairs = tensor_size // 2
    send_left, keep_left, keep_right, *rest = pl.pallas_call(
        functools.partial(project_kernel, heads, seq, share, wide, group_size, key_rows),
        out_shape=[
            jax.ShapeDtypeStruct((pairs, share, half), BF16),
            jax.ShapeDtypeStruct((pairs, share, half), F32),
            jax.ShapeDtypeStruct((2, share, half), F32),
        ]
        + [jax.ShapeDtypeStruct((2, share, half), BF16)] * (pairs - 1),
        in_specs=[smem()] + [vmem()] * (2 + len(distances)),
        out_specs=[vmem()] * (2 + pairs),
        scratch_shapes=[
            pltpu.VMEM((rows, span), BF16),
            pltpu.VMEM((tensor_size, share, wide), F32),
        ],
        compiler_params=params(6),
        name="project",
    )(stored(prompt_of), *map(held, (own, *got)), held(weight))

    far = list(range(2, tensor_size, 2))
    got_left = swap(send_left, "tensor", 1, tensor_size)
    got_right = [swap(x, "tensor", d, tensor_size) for x, d in zip(rest[::-1], far[::-1])]
    left = pl.pallas_call(
        fold_left_kernel,
        out_shape=[jax.ShapeDtypeStruct((share, half), F32)]
        + [jax.ShapeDtypeStruct((share, half), BF16)] * len(far),
        in_specs=[vmem()] * 2,
        out_specs=[vmem()] * (1 + len(far)),
        compiler_params=params(2),
        name="fold_left",
    )(held(keep_left), held(got_left))
    got_left = [swap(x, "tensor", d, tensor_size) for x, d in zip(left[:0:-1], far[::-1])]
    right = pl.pallas_call(
        fold_right_kernel,
        out_shape=[
            jax.ShapeDtypeStruct((share, half), F32),
            jax.ShapeDtypeStruct((share, half), BF16),
        ],
        in_specs=[anywhere()] + [vmem()] * (1 + len(far)),
        out_specs=[vmem()] * 2,
        compiler_params=params(2),
        name="fold_right",
    )(left[1], *map(held, (keep_right, *got_right)))
    got_right = swap(right[1], "tensor", 1, tensor_size)
    normed = pl.pallas_call(
        functools.partial(norm_kernel, len(far)),
        out_shape=jax.ShapeDtypeStruct((share, depth), BF16),
        in_specs=[vmem()] * (5 + len(far)),
        out_specs=vmem(),
        compiler_params=params(4),
        name="norm",
    )(
        *map(held, (residual.reshape(tensor_size, share, depth), norm_gain[None])),
        *map(held, (left[0], *got_left, right[0], got_right)),
    )

    above = list(range(2, group_size, 2))
    order = [0] + far
    here = [(g, x) for g in [0] + above for x in (0, 1)]
    column = [swap(normed, "tensor", d, tensor_size) for d in far[::-1]]
    column = [normed] + column[::-1]
    third = fetch(lm_weight, 2 * quarter, quarter, normed)
    columns = pl.pallas_call(
        functools.partial(column_kernel, len(column)),
        out_shape=[jax.ShapeDtypeStruct((len(column), share, half), BF16)] * 2,
        in_specs=[vmem()] * len(column) + [anywhere()],
        out_specs=[vmem()] * 2,
        compiler_params=params(2),
        name="column",
    )(*map(held, column), third)

    def join(pieces, gate):
        blocks = sum(x.shape[0] for x in pieces)
        return pl.pallas_call(
            functools.partial(join_kernel, len(pieces)),
            out_shape=jax.ShapeDtypeStruct((blocks, share, half), BF16),
            in_specs=[vmem()] * len(pieces) + [anywhere()],
            out_specs=vmem(),
            compiler_params=params(2),
            name="join",
        )(*map(held, pieces), gate)

    left, right = columns
    got_left = swap(left, "tensor", 1, tensor_size)
    first_quarter = fetch(lm_weight, 0, quarter, left)
    right = [right] + [swap(right, "group", d, group_size) for d in above]
    left = join([left, got_left], first_quarter)
    got_left = [swap(left, "group", d, group_size) for d in above]
    second_quarter = fetch(lm_weight, quarter, quarter, left)
    across = swap(jnp.concatenate(right), "tensor", 1, tensor_size)
    across = jnp.split(across, len(right))
    right = [x for pair in zip(right, across) for x in pair]
    halves = []
    for tokens in (join([left] + got_left, second_quarter), jnp.concatenate(right)):
        tokens = tokens.reshape(-1, half)
        halves.append((tokens, swap(tokens, "group", 1, group_size)))
    spots = [(g + c, t + x) for c in (0, 1) for g, x in here for t in order]
    total_rows = 2 * tokens.shape[0]
    narrow = 3072 if vocab % 3072 == 0 else vocab
    limit = 10 if total_rows <= 256 else 24
    work = 2 * total_rows * (half) * vocab
    first, last = pl.pallas_call(
        functools.partial(first_kernel, narrow),
        out_shape=[pltpu.VMEM((total_rows, vocab), F32), pltpu.VMEM((quarter, vocab), BF16)],
        in_specs=[vmem()] * 4 + [anywhere()],
        out_specs=[vmem()] * 2,
        scratch_shapes=[
            pltpu.VMEM((total_rows, half), BF16),
            pltpu.SemaphoreType.DMA((4,)),
        ],
        compiler_params=params(limit),
        cost_estimate=cost(flops=work),
        name="logits_first",
    )(*map(held, (*halves[0], first_quarter, second_quarter)), stored(lm_weight))
    stats = pl.pallas_call(
        functools.partial(logits_kernel, narrow, spots, tensor_size),
        out_shape=jax.ShapeDtypeStruct((len(spots), 1, 128), F32),
        in_specs=[vmem()] * 6,
        out_specs=vmem(),
        scratch_shapes=[pltpu.VMEM((total_rows, half), BF16)]
        + [pltpu.VMEM((total_rows, 128), F32)] * 3
        + [pltpu.VMEM((total_rows, 1), i32)],
        compiler_params=params(limit),
        cost_estimate=cost(flops=work),
        name="logits",
    )(*map(held, (first, *halves[1])), wanted, held(third), held(last))

    stats = lax.all_to_all(stats, ("group", "tensor"), 0, 0, tiled=True)
    return pl.pallas_call(
        functools.partial(final_kernel, share),
        out_shape=jax.ShapeDtypeStruct((share,), F32),
        in_specs=[vmem()] * 2,
        out_specs=vmem(),
        compiler_params=params(4),
        name="final",
    )(held(live), held(stats))


def solution(mesh):
    return jax.shard_map(
        functools.partial(local, mesh.shape["group"], mesh.shape["tensor"]),
        mesh=mesh,
        in_specs=(
            P("group", "tensor"),
            P("group", "tensor"),
            P("group", "tensor"),
            P("group", "tensor"),
            P("group", "tensor"),
            P("group"),
            P("group"),
            P("group", None),
            P("tensor", None),
            P(),
            P(None, ("group", "tensor")),
            P(),
        ),
        out_specs=P(("group", "tensor")),
        check_vma=False,
    )
```

```python
import functools

import jax
import jax.numpy as jnp
from jax import lax
from jax.experimental import pallas as pl
from jax.experimental.pallas import tpu as pltpu
from jax.sharding import PartitionSpec as P

HEAD_DIM = 128
PLEN = 512
NEG = -1e30
BF16 = jnp.bfloat16
F32 = jnp.float32
MIB = 1024 * 1024


def params(mib):
    return pltpu.CompilerParams(vmem_limit_bytes=mib * MIB)


def held(x):
    return pltpu.with_memory_space_constraint(x, pltpu.VMEM)


def stored(x):
    return pltpu.with_memory_space_constraint(x, pltpu.HBM)


def anywhere():
    return pl.BlockSpec(memory_space=pl.ANY)


def cost(flops=0, moved=0):
    return pl.CostEstimate(flops=flops, bytes_accessed=moved, transcendentals=0)


def vmem():
    return pl.BlockSpec(memory_space=pltpu.VMEM)


def smem():
    return pl.BlockSpec(memory_space=pltpu.SMEM)


def swap(x, axis, distance, size):
    return lax.ppermute(x, axis, [(i, i ^ distance) for i in range(size)])


def attend(jobs):
    factor = HEAD_DIM**-0.5
    scores = [
        lax.dot_general(q, k, (((1,), (1,)), ((), ())), preferred_element_type=F32)
        for q, k, _, _ in jobs
    ]
    scores = [
        s if job[3] is None else jnp.where(job[3], s, NEG) for s, job in zip(scores, jobs)
    ]
    peaks = [jnp.max(s, axis=1, keepdims=True) for s in scores]
    weights = [jnp.exp((s - peak) * factor) for s, peak in zip(scores, peaks)]
    weights = [
        w if job[3] is None else jnp.where(job[3], w, 0.0) for w, job in zip(weights, jobs)
    ]
    weights = [w.astype(BF16) for w in weights]
    totals = [jnp.sum(w.astype(F32), axis=1, keepdims=True) for w in weights]
    mixed = [
        jnp.dot(w, job[2], preferred_element_type=F32) for w, job in zip(weights, jobs)
    ]
    return [
        (m / total, peak * factor + jnp.log(total))
        for m, total, peak in zip(mixed, totals, peaks)
    ]


def pack_logs(logs, rows):
    lane = lax.broadcasted_iota(jnp.int32, (rows, 128), 1)
    packed = jnp.zeros((rows, 128), F32)
    for head, log in enumerate(logs):
        first = log.astype(BF16).astype(F32)
        second = (log - first).astype(BF16).astype(F32)
        third = log - first - second
        for part, value in enumerate((first, second, third)):
            packed = jnp.where(lane == 3 * head + part, value, packed)
    return packed.astype(BF16)


def pass_kernel(count, *refs):
    for ref, out_ref in zip(refs, refs[-count:]):
        out_ref[...] = ref[...]


def load_kernel(count, gate_ref, *refs):
    sems = refs[2 * count]
    copies = [
        pltpu.make_async_copy(refs[i], refs[count + i], sems.at[i]) for i in range(count)
    ]
    for copy in copies:
        copy.start()
    for copy in copies:
        copy.wait()


def carried(source_ref, start, out_ref, sems):
    count = sems.shape[0]
    rows = out_ref.shape[0] // count
    return [
        pltpu.make_async_copy(
            source_ref.at[pl.ds(start + i * rows, rows)], out_ref.at[pl.ds(i * rows, rows)], sems.at[i]
        )
        for i in range(count)
    ]


def own_kernel(
    heads,
    seq,
    share,
    lengths_ref,
    prompt_ref,
    q_ref,
    rk_ref,
    rv_ref,
    k_ref,
    v_ref,
    gate_ref,
    own_ref,
    live_ref,
):
    rows = q_ref.shape[0]
    row = lax.broadcasted_iota(jnp.int32, (rows, rows), 0)
    col = lax.broadcasted_iota(jnp.int32, (rows, rows), 1)
    live = jnp.zeros((rows, rows), jnp.int32)
    for r in range(rows // seq):
        live = jnp.where(col // seq == r, lengths_ref[r], live)
    allowed = (row // seq == col // seq) & (col <= row) & (col % seq < live)
    parts = [slice(h * HEAD_DIM, (h + 1) * HEAD_DIM) for h in range(heads)]
    found = attend(
        [(q_ref[:, p], rk_ref[:, p], rv_ref[:, p], allowed) for p in parts]
        + [(q_ref[:, p], k_ref[:, p], v_ref[:, p], None) for p in parts]
    )
    here = wanted_prompts(seq, rows, prompt_ref) == lax.axis_index("group") * k_ref.shape[0] // PLEN
    lane = lax.broadcasted_iota(jnp.int32, (rows, 128), 1)
    packed = jnp.zeros((rows, 128), F32)
    for h, p in enumerate(parts):
        (first, log), (second, other) = found[h], found[heads + h]
        other = jnp.where(here, other, NEG)
        peak = jnp.maximum(log, other)
        left, right = jnp.exp(log - peak), jnp.exp(other - peak)
        own_ref[:, p] = (first * left + second * right) / (left + right)
        packed = jnp.where(lane == h, peak + jnp.log(left + right), packed)
    own_ref[:, heads * HEAD_DIM :] = packed
    token = lax.broadcasted_iota(jnp.int32, live_ref.shape, 1) + lax.axis_index("tensor") * share
    length = jnp.zeros(live_ref.shape, jnp.int32)
    for r in range(rows // seq):
        length = jnp.where(token // seq == r, lengths_ref[r], length)
    live_ref[...] = jnp.where(token % seq < length, 1.0, 0.0)


def wanted_prompts(seq, rows, prompt_ref):
    row = lax.broadcasted_iota(jnp.int32, (rows, 1), 0)
    wanted = jnp.zeros((rows, 1), jnp.int32)
    for r in range(rows // seq):
        wanted = jnp.where(row // seq == r, prompt_ref[r], wanted)
    return wanted


def prefix_kernel(heads, count, *refs):
    q_refs, (k_ref, v_ref), out_refs = refs[:count], refs[count : count + 2], refs[count + 2 :]
    rows = q_refs[0].shape[0]
    places = [(ref, i) for ref in out_refs for i in range(ref.shape[0])]
    parts = [slice(h * HEAD_DIM, (h + 1) * HEAD_DIM) for h in range(heads)]
    found = attend(
        [
            (jnp.concatenate([ref[:, p] for ref in q_refs], axis=0), k_ref[:, p], v_ref[:, p], None)
            for p in parts
        ]
    )
    for i, (out_ref, place) in enumerate(places):
        rung = slice(i * rows, (i + 1) * rows)
        for h, p in enumerate(parts):
            out_ref[place, :, p] = found[h][0][rung].astype(BF16)
        out_ref[place, :, heads * HEAD_DIM :] = pack_logs([log[rung] for _, log in found], rows)


def unpack_log(three, h):
    three = three.astype(F32)
    return three[:, 3 * h : 3 * h + 1] + three[:, 3 * h + 1 : 3 * h + 2] + three[:, 3 * h + 2 : 3 * h + 3]


def blend(logs, values):
    peak = functools.reduce(jnp.maximum, logs)
    loads = [jnp.exp(log - peak) for log in logs]
    total = functools.reduce(jnp.add, loads)
    mixed = functools.reduce(jnp.add, [w * v for w, v in zip(loads, values)])
    return mixed / total, peak + jnp.log(total)


def merge_kernel(heads, seq, key_rows, count, *refs):
    prompt_refs, (stay_ref, cross_ref), out_refs = refs[:count], refs[count : count + 2], refs[count + 2 :]
    rows = stay_ref.shape[1]
    group = lax.axis_index("group")
    at = heads * HEAD_DIM
    for i, (prompt_ref, out_ref) in enumerate(zip(prompt_refs, out_refs)):
        wanted = wanted_prompts(seq, rows, prompt_ref)
        sources = [
            (stay_ref[i], wanted == group * key_rows // PLEN),
            (cross_ref[i + 1], wanted == (group ^ 1) * key_rows // PLEN),
        ]
        logs = []
        for h in range(heads):
            part = slice(h * HEAD_DIM, (h + 1) * HEAD_DIM)
            value, log = blend(
                [jnp.where(here, unpack_log(x[:, at:], h), NEG) for x, here in sources],
                [x[:, part].astype(F32) for x, _ in sources],
            )
            out_ref[:, part] = value.astype(BF16)
            logs.append(log)
        out_ref[:, at:] = pack_logs(logs, rows)


def project_kernel(heads, seq, key_rows, count, wide, prompt_ref, own_ref, cross_ref, *refs):
    got_refs, weight_ref, refs = refs[:count], refs[count], refs[count + 1 :]
    send_left_ref, keep_left_ref, keep_right_ref = refs[:3]
    send_right_refs, (attended_ref, partial_ref, near_ref, sems) = refs[3:-4], refs[-4:]
    rows = own_ref.shape[0]
    blocks, share = partial_ref.shape[:2]
    half = send_left_ref.shape[2]
    copies = [
        pltpu.make_async_copy(
            weight_ref.at[:, pl.ds(n * wide, wide)], near_ref.at[:, pl.ds(n * wide, wide)], sems.at[n]
        )
        for n in range(2 * half // wide)
    ]
    for copy in copies:
        copy.start()
    here = wanted_prompts(seq, rows, prompt_ref) == (lax.axis_index("group") ^ 1) * key_rows // PLEN
    at = heads * HEAD_DIM
    for h in range(heads):
        part = slice(h * HEAD_DIM, (h + 1) * HEAD_DIM)
        logs = [own_ref[:, at + h : at + h + 1]]
        logs.append(jnp.where(here, unpack_log(cross_ref[0, :, at:], h), NEG))
        logs += [unpack_log(ref[:, at:], h) for ref in got_refs]
        values = [own_ref[:, part], cross_ref[0, :, part].astype(F32)]
        values += [ref[:, part].astype(F32) for ref in got_refs]
        attended_ref[:, part] = blend(logs, values)[0].astype(BF16)

    me = lax.axis_index("tensor")
    for n, copy in enumerate(copies):
        copy.wait()
        start = n * wide % half
        columns = slice(start, start + wide)
        partial = jnp.dot(
            attended_ref[...], near_ref[:, n * wide : (n + 1) * wide], preferred_element_type=F32
        )
        for b in range(blocks):
            partial_ref[b] = partial[b * share : (b + 1) * share]
        for d in range(blocks):
            block = partial_ref[me ^ d]
            if n * wide < half:
                if d % 2:
                    send_left_ref[d // 2, :, columns] = block.astype(BF16)
                else:
                    keep_left_ref[d // 2, :, columns] = block
            elif d < 2:
                keep_right_ref[d, :, columns] = block
            else:
                send_right_refs[d // 2 - 1][d % 2, :, columns] = block.astype(BF16)


def fold_left_kernel(keep_ref, got_ref, *out_refs):
    for i, ref in enumerate(out_refs):
        ref[...] = (keep_ref[i] + got_ref[i].astype(F32)).astype(ref.dtype)


def fold_right_kernel(gate_ref, keep_ref, *refs):
    got_refs, out_refs = refs[:-2], refs[-2:]
    for i, ref in enumerate(out_refs):
        total = keep_ref[i]
        for got_ref in got_refs:
            total = total + got_ref[i].astype(F32)
        ref[...] = total.astype(ref.dtype)


def fetch_kernel(start, source_ref, gate_ref, out_ref, sems):
    copies = carried(source_ref, start, out_ref, sems)
    for copy in copies:
        copy.start()
    for copy in copies:
        copy.wait()


def column_kernel(count, *refs):
    terms, out_refs = refs[:count], refs[-2:]
    width = out_refs[0].shape[2]
    for i, ref in enumerate(terms):
        for half, out_ref in enumerate(out_refs):
            out_ref[i] = ref[:, half * width : (half + 1) * width]


def norm_kernel(far_count, residual_ref, gain_ref, *refs):
    left_refs, right_refs, out_ref = refs[: 1 + far_count], refs[1 + far_count : -1], refs[-1]
    residual = residual_ref[lax.axis_index("tensor")].astype(F32)
    width = residual.shape[1] // 2
    halves = []
    for i, terms in enumerate((left_refs, right_refs)):
        hidden = residual[:, i * width : (i + 1) * width]
        for ref in terms:
            hidden = hidden + ref[...].astype(F32)
        halves.append(hidden)
    squares = sum(jnp.sum(hidden * hidden, axis=-1, keepdims=True) for hidden in halves)
    scale = lax.rsqrt(squares / residual.shape[1] + 1e-06)
    for i, hidden in enumerate(halves):
        columns = slice(i * width, (i + 1) * width)
        out_ref[:, columns] = (hidden * scale * gain_ref[:, columns].astype(F32)).astype(BF16)


def join_kernel(count, *refs):
    out_ref = refs[-1]
    start = 0
    for ref in refs[:count]:
        out_ref[start : start + ref.shape[0]] = ref[...]
        start += ref.shape[0]


def quarter_dots(x_ref, weight_refs, columns):
    depth = weight_refs[0].shape[0]
    return functools.reduce(
        jnp.add,
        [
            jnp.dot(x_ref[:, i * depth : (i + 1) * depth], ref[:, columns], preferred_element_type=F32)
            for i, ref in enumerate(weight_refs)
        ],
    )


def first_kernel(
    narrow, left_ref, right_ref, weight_ref, next_ref, source_ref, out_ref, last_ref, x_ref, sems
):
    copies = carried(source_ref, source_ref.shape[0] - last_ref.shape[0], last_ref, sems)
    for copy in copies:
        copy.start()
    half = left_ref.shape[0]
    x_ref[:half] = left_ref[...]
    x_ref[half:] = right_ref[...]

    @pl.loop(0, weight_ref.shape[1] // narrow)
    def _(n):
        columns = pl.ds(n * narrow if narrow % 128 else pl.multiple_of(n * narrow, 128), narrow)
        out_ref[:, columns] = quarter_dots(x_ref, (weight_ref, next_ref), columns)

    for copy in copies:
        copy.wait()


def logits_kernel(
    narrow,
    spots,
    tensor_size,
    sum_in_ref,
    left_ref,
    right_ref,
    target_ref,
    weight_ref,
    next_ref,
    out_ref,
    x_ref,
    peak_ref,
    sum_ref,
    pick_ref,
    wanted_ref,
):
    half = left_ref.shape[0]
    rows = 2 * half
    share = target_ref.shape[1]
    group, tensor = lax.axis_index("group"), lax.axis_index("tensor")
    vocab = weight_ref.shape[1]
    places = [(group ^ g) * tensor_size + (tensor ^ t) for g, t in spots]
    for i, place in enumerate(places):
        wanted_ref[i * share : (i + 1) * share] = target_ref[place]
    wanted = wanted_ref[...] - (group * tensor_size + tensor) * vocab
    wanted_ref[...] = jnp.where((wanted >= 0) & (wanted < vocab), wanted, -1)
    x_ref[:half] = left_ref[...]
    x_ref[half:] = right_ref[...]
    peak_ref[...] = jnp.full_like(peak_ref, NEG)
    sum_ref[...] = jnp.zeros_like(sum_ref)
    pick_ref[...] = jnp.zeros_like(pick_ref)

    @pl.loop(0, weight_ref.shape[1] // narrow)
    def _(n):
        columns = pl.ds(n * narrow if narrow % 128 else pl.multiple_of(n * narrow, 128), narrow)
        logits = sum_in_ref[:, columns] + quarter_dots(x_ref, (weight_ref, next_ref), columns)
        parts = [logits[:, c : c + 128] for c in range(0, narrow, 128)]
        if narrow % 128:
            spare = jnp.full((rows, 128 - narrow % 128), NEG, F32)
            parts[-1] = jnp.concatenate([parts[-1], spare], axis=1)
        lane = lax.broadcasted_iota(jnp.int32, (rows, 128), 1) + n * narrow
        peak = peak_ref[...]
        higher = functools.reduce(jnp.maximum, parts, peak)
        total = sum_ref[...] * jnp.exp(peak - higher)
        picked = pick_ref[...]
        target = wanted_ref[...]
        for c, part in enumerate(parts):
            total = total + jnp.exp(part - higher)
            picked = picked + jnp.where(lane + c * 128 == target, part, 0.0)
        peak_ref[...] = higher
        sum_ref[...] = total
        pick_ref[...] = picked

    higher = peak_ref[...]
    peak = jnp.max(higher, axis=1, keepdims=True)
    sums = jnp.sum(sum_ref[...] * jnp.exp(higher - peak), axis=1, keepdims=True)
    pick = jnp.sum(pick_ref[...], axis=1, keepdims=True)
    row = lax.broadcasted_iota(jnp.int32, (rows, 128), 0)
    lane = lax.broadcasted_iota(jnp.int32, (rows, 128), 1)
    three = jnp.where(lane // share == 0, peak, jnp.where(lane // share == 1, sums, pick))
    three = jnp.where((row - lane) % share == 0, three, 0.0)
    for i, place in enumerate(places):
        out_ref[place] = jnp.sum(three[i * share : (i + 1) * share], axis=0, keepdims=True)


def final_kernel(share, live_ref, stats_ref, out_ref):
    stats = stats_ref[...].reshape(stats_ref.shape[0], 128)
    peak = jnp.max(stats, axis=0, keepdims=True)
    sums = pltpu.roll(stats, 128 - share, 1)
    picks = pltpu.roll(stats, 128 - 2 * share, 1)
    total = jnp.sum(sums * jnp.exp(stats - peak), axis=0, keepdims=True)
    values = jnp.sum(picks, axis=0, keepdims=True) - peak - jnp.log(total)
    out_ref[...] = jnp.where(live_ref[:1] > 0.0, values, 0.0)[0, :share]


def local(
    group_size,
    tensor_size,
    resp_query,
    resp_key,
    resp_value,
    prompt_keys,
    prompt_values,
    prompt_of,
    lengths,
    residual,
    out_weight,
    norm_gain,
    lm_weight,
    targets,
):
    rows, span = resp_query.shape
    heads = span // HEAD_DIM
    seq = rows // prompt_of.shape[0]
    key_rows = prompt_keys.shape[0]
    assert PLEN % key_rows == 0
    share = rows // tensor_size
    depth = out_weight.shape[1]
    vocab = lm_weight.shape[1]
    i32 = jnp.int32

    wanted = targets.reshape(-1, share, 1)
    above = list(range(2, group_size, 2))
    far_queries = [swap(resp_query, "group", a, group_size) for a in above[::-1]][::-1]
    far_prompts = [swap(prompt_of, "group", a, group_size) for a in above]
    near_queries = [swap(resp_query, "group", 1, group_size)]
    far_queries = pl.pallas_call(
        functools.partial(pass_kernel, len(above)),
        out_shape=[jax.ShapeDtypeStruct(x.shape, x.dtype) for x in far_queries],
        in_specs=[vmem()] * len(above) + [anywhere()] * (1 + len(above)),
        out_specs=[vmem()] * len(above),
        compiler_params=params(1),
        name="pass",
    )(*map(held, far_queries), wanted, *far_prompts)
    near_queries += [swap(x, "group", 1, group_size) for x in far_queries]
    inputs = (resp_query, resp_key, resp_value, prompt_keys, prompt_values)
    loaded = pl.pallas_call(
        functools.partial(load_kernel, len(inputs)),
        out_shape=[pltpu.VMEM(x.shape, x.dtype) for x in inputs],
        in_specs=[anywhere()] * (1 + len(inputs)),
        out_specs=[vmem()] * len(inputs),
        scratch_shapes=[pltpu.SemaphoreType.DMA((len(inputs),))],
        compiler_params=params(1),
        cost_estimate=cost(moved=2 * MIB),
        name="load",
    )(far_queries[0], *map(stored, inputs))
    query, own_keys, own_values, keys, values = map(held, loaded)
    packed = (rows, span + 128)
    queries = near_queries + list(far_queries)
    cross, stay = pl.pallas_call(
        functools.partial(prefix_kernel, heads, len(queries)),
        out_shape=[
            jax.ShapeDtypeStruct((len(near_queries), *packed), BF16),
            jax.ShapeDtypeStruct((len(above), *packed), BF16),
        ],
        in_specs=[vmem()] * (len(queries) + 2),
        out_specs=[vmem()] * 2,
        compiler_params=params(8),
        name="prefix_attention",
    )(*map(held, queries), keys, values)
    cross = swap(cross, "group", 1, group_size)
    merged = pl.pallas_call(
        functools.partial(merge_kernel, heads, seq, key_rows, len(above)),
        out_shape=[jax.ShapeDtypeStruct(packed, BF16)] * len(above),
        in_specs=[smem()] * len(above) + [vmem()] * 2,
        out_specs=[vmem()] * len(above),
        compiler_params=params(4),
        name="merge",
    )(*far_prompts, held(stay), held(cross))
    got = [swap(x, "group", a, group_size) for x, a in zip(merged, above)]
    own, live = pl.pallas_call(
        functools.partial(own_kernel, heads, seq, share),
        out_shape=[jax.ShapeDtypeStruct(packed, F32), jax.ShapeDtypeStruct((8, 128), F32)],
        in_specs=[smem()] * 2 + [vmem()] * 5 + [anywhere()],
        out_specs=[vmem()] * 2,
        compiler_params=params(6),
        cost_estimate=cost(moved=4 * MIB),
        name="own_attention",
    )(stored(lengths), stored(prompt_of), query, own_keys, own_values, keys, values, merged[0])

    def fetch(source, start, count, gate):
        return held(
            pl.pallas_call(
                functools.partial(fetch_kernel, start),
                out_shape=pltpu.VMEM((count, source.shape[1]), BF16),
                in_specs=[anywhere()] * 2,
                out_specs=vmem(),
                scratch_shapes=[pltpu.SemaphoreType.DMA((4,))],
                compiler_params=params(1),
                cost_estimate=cost(moved=count * source.shape[1] * 2),
                name="fetch",
            )(stored(source), gate)
        )

    half = depth // 2
    quarter = depth // 4
    wide = 1280 if half % 1280 == 0 else half
    pairs = tensor_size // 2
    send_left, keep_left, keep_right, *rest = pl.pallas_call(
        functools.partial(project_kernel, heads, seq, key_rows, len(got), wide),
        out_shape=[
            jax.ShapeDtypeStruct((pairs, share, half), BF16),
            jax.ShapeDtypeStruct((pairs, share, half), F32),
            jax.ShapeDtypeStruct((2, share, half), F32),
        ]
        + [jax.ShapeDtypeStruct((2, share, half), BF16)] * (pairs - 1),
        in_specs=[smem()] + [vmem()] * (2 + len(got)) + [anywhere()],
        out_specs=[vmem()] * (2 + pairs),
        scratch_shapes=[
            pltpu.VMEM((rows, span), BF16),
            pltpu.VMEM((tensor_size, share, wide), F32),
            pltpu.VMEM(out_weight.shape, BF16),
            pltpu.SemaphoreType.DMA((depth // wide,)),
        ],
        compiler_params=params(10),
        name="project",
    )(stored(prompt_of), *map(held, (own, cross, *got)), stored(out_weight))

    far = list(range(2, tensor_size, 2))
    got_left = swap(send_left, "tensor", 1, tensor_size)
    got_right = [swap(x, "tensor", d, tensor_size) for x, d in zip(rest[::-1], far[::-1])]
    left = pl.pallas_call(
        fold_left_kernel,
        out_shape=[jax.ShapeDtypeStruct((share, half), F32)]
        + [jax.ShapeDtypeStruct((share, half), BF16)] * len(far),
        in_specs=[vmem()] * 2,
        out_specs=[vmem()] * (1 + len(far)),
        compiler_params=params(2),
        name="fold_left",
    )(held(keep_left), held(got_left))
    got_left = [swap(x, "tensor", d, tensor_size) for x, d in zip(left[:0:-1], far[::-1])]
    right = pl.pallas_call(
        fold_right_kernel,
        out_shape=[
            jax.ShapeDtypeStruct((share, half), F32),
            jax.ShapeDtypeStruct((share, half), BF16),
        ],
        in_specs=[anywhere()] + [vmem()] * (1 + len(far)),
        out_specs=[vmem()] * 2,
        compiler_params=params(2),
        name="fold_right",
    )(left[1], *map(held, (keep_right, *got_right)))
    got_right = swap(right[1], "tensor", 1, tensor_size)
    normed = pl.pallas_call(
        functools.partial(norm_kernel, len(far)),
        out_shape=jax.ShapeDtypeStruct((share, depth), BF16),
        in_specs=[vmem()] * (5 + len(far)),
        out_specs=vmem(),
        compiler_params=params(4),
        name="norm",
    )(
        *map(held, (residual.reshape(tensor_size, share, depth), norm_gain[None])),
        *map(held, (left[0], *got_left, right[0], got_right)),
    )

    order = [0] + far
    here = [(g, x) for g in [0] + above for x in (0, 1)]
    column = [swap(normed, "tensor", d, tensor_size) for d in far[::-1]]
    column = [normed] + column[::-1]
    third = fetch(lm_weight, 2 * quarter, quarter, normed)
    columns = pl.pallas_call(
        functools.partial(column_kernel, len(column)),
        out_shape=[jax.ShapeDtypeStruct((len(column), share, half), BF16)] * 2,
        in_specs=[vmem()] * len(column) + [anywhere()],
        out_specs=[vmem()] * 2,
        compiler_params=params(2),
        name="column",
    )(*map(held, column), third)

    def join(pieces, gate):
        blocks = sum(x.shape[0] for x in pieces)
        return pl.pallas_call(
            functools.partial(join_kernel, len(pieces)),
            out_shape=jax.ShapeDtypeStruct((blocks, share, half), BF16),
            in_specs=[vmem()] * len(pieces) + [anywhere()],
            out_specs=vmem(),
            compiler_params=params(2),
            name="join",
        )(*map(held, pieces), gate)

    left, right = columns
    got_left = swap(left, "tensor", 1, tensor_size)
    first_quarter = fetch(lm_weight, 0, quarter, left)
    right = [right] + [swap(right, "group", d, group_size) for d in above]
    left = join([left, got_left], first_quarter)
    got_left = [swap(left, "group", d, group_size) for d in above]
    second_quarter = fetch(lm_weight, quarter, quarter, left)
    across = swap(jnp.concatenate(right), "tensor", 1, tensor_size)
    across = jnp.split(across, len(right))
    right = [x for pair in zip(right, across) for x in pair]
    halves = []
    for tokens in (join([left] + got_left, second_quarter), jnp.concatenate(right)):
        tokens = tokens.reshape(-1, half)
        halves.append((tokens, swap(tokens, "group", 1, group_size)))
    spots = [(g + c, t + x) for c in (0, 1) for g, x in here for t in order]
    total_rows = 2 * tokens.shape[0]
    narrow = 1536 if vocab % 1536 == 0 else vocab
    limit = 10 if total_rows <= 256 else 24
    work = 2 * total_rows * (half) * vocab
    first, last = pl.pallas_call(
        functools.partial(first_kernel, narrow),
        out_shape=[pltpu.VMEM((total_rows, vocab), F32), pltpu.VMEM((quarter, vocab), BF16)],
        in_specs=[vmem()] * 4 + [anywhere()],
        out_specs=[vmem()] * 2,
        scratch_shapes=[
            pltpu.VMEM((total_rows, half), BF16),
            pltpu.SemaphoreType.DMA((4,)),
        ],
        compiler_params=params(limit),
        cost_estimate=cost(flops=work),
        name="logits_first",
    )(*map(held, (*halves[0], first_quarter, second_quarter)), stored(lm_weight))
    stats = pl.pallas_call(
        functools.partial(logits_kernel, vocab, spots, tensor_size),
        out_shape=jax.ShapeDtypeStruct((len(spots), 1, 128), F32),
        in_specs=[vmem()] * 6,
        out_specs=vmem(),
        scratch_shapes=[pltpu.VMEM((total_rows, half), BF16)]
        + [pltpu.VMEM((total_rows, 128), F32)] * 3
        + [pltpu.VMEM((total_rows, 1), i32)],
        compiler_params=params(limit),
        cost_estimate=cost(flops=work),
        name="logits",
    )(*map(held, (first, *halves[1])), wanted, held(third), held(last))

    stats = lax.all_to_all(stats, ("group", "tensor"), 0, 0, tiled=True)
    return pl.pallas_call(
        functools.partial(final_kernel, share),
        out_shape=jax.ShapeDtypeStruct((share,), F32),
        in_specs=[vmem()] * 2,
        out_specs=vmem(),
        compiler_params=params(4),
        name="final",
    )(held(live), held(stats))


def solution(mesh):
    return jax.shard_map(
        functools.partial(local, mesh.shape["group"], mesh.shape["tensor"]),
        mesh=mesh,
        in_specs=(
            P("group", "tensor"),
            P("group", "tensor"),
            P("group", "tensor"),
            P("group", "tensor"),
            P("group", "tensor"),
            P("group"),
            P("group"),
            P("group", None),
            P("tensor", None),
            P(),
            P(None, ("group", "tensor")),
            P(),
        ),
        out_specs=P(("group", "tensor")),
        check_vma=False,
    )
```

```python
import functools

import jax
import jax.numpy as jnp
from jax import lax
from jax.experimental import pallas as pl
from jax.experimental.pallas import tpu as pltpu
from jax.sharding import PartitionSpec as P

HEAD_DIM = 128
PLEN = 512
NEG = -1e30
BF16 = jnp.bfloat16
F32 = jnp.float32
MIB = 1024 * 1024


def params(mib):
    return pltpu.CompilerParams(vmem_limit_bytes=mib * MIB)


def held(x):
    return pltpu.with_memory_space_constraint(x, pltpu.VMEM)


def stored(x):
    return pltpu.with_memory_space_constraint(x, pltpu.HBM)


def anywhere():
    return pl.BlockSpec(memory_space=pl.ANY)


def cost(flops=0, moved=0):
    return pl.CostEstimate(flops=flops, bytes_accessed=moved, transcendentals=0)


def vmem():
    return pl.BlockSpec(memory_space=pltpu.VMEM)


def smem():
    return pl.BlockSpec(memory_space=pltpu.SMEM)


def swap(x, axis, distance, size):
    return lax.ppermute(x, axis, [(i, i ^ distance) for i in range(size)])


def attend(jobs):
    factor = HEAD_DIM**-0.5
    scores = [
        lax.dot_general(q, k, (((1,), (1,)), ((), ())), preferred_element_type=F32)
        for q, k, _, _ in jobs
    ]
    scores = [
        s if job[3] is None else jnp.where(job[3], s, NEG) for s, job in zip(scores, jobs)
    ]
    peaks = [jnp.max(s, axis=1, keepdims=True) for s in scores]
    weights = [jnp.exp((s - peak) * factor) for s, peak in zip(scores, peaks)]
    weights = [
        w if job[3] is None else jnp.where(job[3], w, 0.0) for w, job in zip(weights, jobs)
    ]
    weights = [w.astype(BF16) for w in weights]
    totals = [jnp.sum(w.astype(F32), axis=1, keepdims=True) for w in weights]
    mixed = [
        jnp.dot(w, job[2], preferred_element_type=F32) for w, job in zip(weights, jobs)
    ]
    return [
        (m / total, peak * factor + jnp.log(total))
        for m, total, peak in zip(mixed, totals, peaks)
    ]


def pack_logs(logs, rows):
    lane = lax.broadcasted_iota(jnp.int32, (rows, 128), 1)
    packed = jnp.zeros((rows, 128), F32)
    for head, log in enumerate(logs):
        first = log.astype(BF16).astype(F32)
        second = (log - first).astype(BF16).astype(F32)
        third = log - first - second
        for part, value in enumerate((first, second, third)):
            packed = jnp.where(lane == 3 * head + part, value, packed)
    return packed.astype(BF16)


def pass_kernel(count, *refs):
    for ref, out_ref in zip(refs, refs[-count:]):
        out_ref[...] = ref[...]


def load_kernel(count, gate_ref, *refs):
    sems = refs[2 * count]
    copies = [
        pltpu.make_async_copy(refs[i], refs[count + i], sems.at[i]) for i in range(count)
    ]
    for copy in copies:
        copy.start()
    for copy in copies:
        copy.wait()


def carried(source_ref, start, out_ref, sems):
    count = sems.shape[0]
    rows = out_ref.shape[0] // count
    return [
        pltpu.make_async_copy(
            source_ref.at[pl.ds(start + i * rows, rows)], out_ref.at[pl.ds(i * rows, rows)], sems.at[i]
        )
        for i in range(count)
    ]


def own_kernel(
    heads,
    seq,
    share,
    lengths_ref,
    prompt_ref,
    q_ref,
    rk_ref,
    rv_ref,
    k_ref,
    v_ref,
    source_ref,
    gate_ref,
    own_ref,
    live_ref,
    weight_ref,
    sems,
):
    copies = carried(source_ref, 0, weight_ref, sems)
    for copy in copies:
        copy.start()
    rows = q_ref.shape[0]
    row = lax.broadcasted_iota(jnp.int32, (rows, rows), 0)
    col = lax.broadcasted_iota(jnp.int32, (rows, rows), 1)
    live = jnp.zeros((rows, rows), jnp.int32)
    for r in range(rows // seq):
        live = jnp.where(col // seq == r, lengths_ref[r], live)
    allowed = (row // seq == col // seq) & (col <= row) & (col % seq < live)
    parts = [slice(h * HEAD_DIM, (h + 1) * HEAD_DIM) for h in range(heads)]
    found = attend(
        [(q_ref[:, p], rk_ref[:, p], rv_ref[:, p], allowed) for p in parts]
        + [(q_ref[:, p], k_ref[:, p], v_ref[:, p], None) for p in parts]
    )
    here = wanted_prompts(seq, rows, prompt_ref) == lax.axis_index("group") * k_ref.shape[0] // PLEN
    lane = lax.broadcasted_iota(jnp.int32, (rows, 128), 1)
    packed = jnp.zeros((rows, 128), F32)
    for h, p in enumerate(parts):
        (first, log), (second, other) = found[h], found[heads + h]
        other = jnp.where(here, other, NEG)
        peak = jnp.maximum(log, other)
        left, right = jnp.exp(log - peak), jnp.exp(other - peak)
        own_ref[:, p] = (first * left + second * right) / (left + right)
        packed = jnp.where(lane == h, peak + jnp.log(left + right), packed)
    own_ref[:, heads * HEAD_DIM :] = packed
    token = lax.broadcasted_iota(jnp.int32, live_ref.shape, 1) + lax.axis_index("tensor") * share
    length = jnp.zeros(live_ref.shape, jnp.int32)
    for r in range(rows // seq):
        length = jnp.where(token // seq == r, lengths_ref[r], length)
    live_ref[...] = jnp.where(token % seq < length, 1.0, 0.0)
    for copy in copies:
        copy.wait()


def wanted_prompts(seq, rows, prompt_ref):
    row = lax.broadcasted_iota(jnp.int32, (rows, 1), 0)
    wanted = jnp.zeros((rows, 1), jnp.int32)
    for r in range(rows // seq):
        wanted = jnp.where(row // seq == r, prompt_ref[r], wanted)
    return wanted


def prefix_kernel(heads, count, *refs):
    q_refs, (k_ref, v_ref), out_refs = refs[:count], refs[count : count + 2], refs[count + 2 :]
    rows = q_refs[0].shape[0]
    parts = [slice(h * HEAD_DIM, (h + 1) * HEAD_DIM) for h in range(heads)]
    found = attend(
        [
            (jnp.concatenate([ref[:, p] for ref in q_refs], axis=0), k_ref[:, p], v_ref[:, p], None)
            for p in parts
        ]
    )
    for i in range(count):
        rung = slice(i * rows, (i + 1) * rows)
        for h, p in enumerate(parts):
            out_refs[i][:, p] = found[h][0][rung].astype(BF16)
        out_refs[i][:, heads * HEAD_DIM :] = pack_logs([log[rung] for _, log in found], rows)


def project_kernel(heads, seq, share, wide, group_size, key_rows, prompt_ref, own_ref, *refs):
    got_refs, refs = refs[: group_size - 1], refs[group_size - 1 :]
    weight_ref, send_left_ref, keep_left_ref, keep_right_ref = refs[:4]
    send_right_refs, (attended_ref, partial_ref) = refs[4:-2], refs[-2:]
    rows = own_ref.shape[0]
    wanted = wanted_prompts(seq, rows, prompt_ref)
    group = lax.axis_index("group")
    holders = [(group ^ d) * key_rows // PLEN for d in range(group_size - 1, 0, -1)]
    for h in range(heads):
        part = slice(h * HEAD_DIM, (h + 1) * HEAD_DIM)
        at = heads * HEAD_DIM
        logs = [own_ref[:, at + h : at + h + 1]]
        values = [own_ref[:, part]]
        for holder, ref in zip(holders, got_refs):
            three = ref[:, at : at + 128].astype(F32)
            log = (
                three[:, 3 * h : 3 * h + 1]
                + three[:, 3 * h + 1 : 3 * h + 2]
                + three[:, 3 * h + 2 : 3 * h + 3]
            )
            logs.append(jnp.where(wanted == holder, log, NEG))
            values.append(ref[:, part].astype(F32))
        peak = functools.reduce(jnp.maximum, logs)
        loads = [jnp.exp(log - peak) for log in logs]
        total = functools.reduce(jnp.add, loads)
        mixed = functools.reduce(jnp.add, [w * v for w, v in zip(loads, values)])
        attended_ref[:, part] = (mixed / total).astype(BF16)

    me = lax.axis_index("tensor")
    blocks = rows // share
    half = send_left_ref.shape[2]

    def multiply(columns):
        partial = jnp.dot(attended_ref[...], weight_ref[:, columns], preferred_element_type=F32)
        for b in range(blocks):
            partial_ref[b] = partial[b * share : (b + 1) * share]

    @pl.loop(0, half // wide)
    def _(n):
        columns = pl.ds(pl.multiple_of(n * wide, 128), wide)
        multiply(columns)
        for d in range(0, blocks, 2):
            keep_left_ref[d // 2, :, columns] = partial_ref[me ^ d]
            send_left_ref[d // 2, :, columns] = partial_ref[me ^ (d + 1)].astype(BF16)

    @pl.loop(0, half // wide)
    def _(n):
        columns = pl.ds(pl.multiple_of(n * wide, 128), wide)
        multiply(pl.ds(pl.multiple_of(half + n * wide, 128), wide))
        for d in range(blocks):
            block = partial_ref[me ^ d]
            if d < 2:
                keep_right_ref[d, :, columns] = block
            else:
                send_right_refs[d // 2 - 1][d % 2, :, columns] = block.astype(BF16)


def fold_left_kernel(keep_ref, got_ref, *out_refs):
    for i, ref in enumerate(out_refs):
        ref[...] = (keep_ref[i] + got_ref[i].astype(F32)).astype(ref.dtype)


def fold_right_kernel(gate_ref, keep_ref, *refs):
    got_refs, out_refs = refs[:-2], refs[-2:]
    for i, ref in enumerate(out_refs):
        total = keep_ref[i]
        for got_ref in got_refs:
            total = total + got_ref[i].astype(F32)
        ref[...] = total.astype(ref.dtype)


def fetch_kernel(start, source_ref, gate_ref, out_ref, sems):
    copies = carried(source_ref, start, out_ref, sems)
    for copy in copies:
        copy.start()
    for copy in copies:
        copy.wait()


def column_kernel(count, *refs):
    terms, out_refs = refs[:count], refs[-2:]
    width = out_refs[0].shape[2]
    for i, ref in enumerate(terms):
        for half, out_ref in enumerate(out_refs):
            out_ref[i] = ref[:, half * width : (half + 1) * width]


def norm_kernel(far_count, residual_ref, gain_ref, *refs):
    left_refs, right_refs, out_ref = refs[: 1 + far_count], refs[1 + far_count : -1], refs[-1]
    residual = residual_ref[lax.axis_index("tensor")].astype(F32)
    width = residual.shape[1] // 2
    halves = []
    for i, terms in enumerate((left_refs, right_refs)):
        hidden = residual[:, i * width : (i + 1) * width]
        for ref in terms:
            hidden = hidden + ref[...].astype(F32)
        halves.append(hidden)
    squares = sum(jnp.sum(hidden * hidden, axis=-1, keepdims=True) for hidden in halves)
    scale = lax.rsqrt(squares / residual.shape[1] + 1e-06)
    for i, hidden in enumerate(halves):
        columns = slice(i * width, (i + 1) * width)
        out_ref[:, columns] = (hidden * scale * gain_ref[:, columns].astype(F32)).astype(BF16)


def join_kernel(count, *refs):
    out_ref = refs[-1]
    start = 0
    for ref in refs[:count]:
        out_ref[start : start + ref.shape[0]] = ref[...]
        start += ref.shape[0]


def quarter_dots(x_ref, weight_refs, columns):
    depth = weight_refs[0].shape[0]
    return functools.reduce(
        jnp.add,
        [
            jnp.dot(x_ref[:, i * depth : (i + 1) * depth], ref[:, columns], preferred_element_type=F32)
            for i, ref in enumerate(weight_refs)
        ],
    )


def first_kernel(
    narrow, left_ref, right_ref, weight_ref, next_ref, source_ref, out_ref, last_ref, x_ref, sems
):
    copies = carried(source_ref, source_ref.shape[0] - last_ref.shape[0], last_ref, sems)
    for copy in copies:
        copy.start()
    half = left_ref.shape[0]
    x_ref[:half] = left_ref[...]
    x_ref[half:] = right_ref[...]

    @pl.loop(0, weight_ref.shape[1] // narrow)
    def _(n):
        columns = pl.ds(n * narrow if narrow % 128 else pl.multiple_of(n * narrow, 128), narrow)
        out_ref[:, columns] = quarter_dots(x_ref, (weight_ref, next_ref), columns)

    for copy in copies:
        copy.wait()


def logits_kernel(
    narrow,
    spots,
    tensor_size,
    sum_in_ref,
    left_ref,
    right_ref,
    target_ref,
    weight_ref,
    next_ref,
    out_ref,
    x_ref,
    peak_ref,
    sum_ref,
    pick_ref,
    wanted_ref,
):
    half = left_ref.shape[0]
    rows = 2 * half
    share = target_ref.shape[1]
    group, tensor = lax.axis_index("group"), lax.axis_index("tensor")
    vocab = weight_ref.shape[1]
    places = [(group ^ g) * tensor_size + (tensor ^ t) for g, t in spots]
    for i, place in enumerate(places):
        wanted_ref[i * share : (i + 1) * share] = target_ref[place]
    wanted = wanted_ref[...] - (group * tensor_size + tensor) * vocab
    wanted_ref[...] = jnp.where((wanted >= 0) & (wanted < vocab), wanted, -1)
    x_ref[:half] = left_ref[...]
    x_ref[half:] = right_ref[...]
    peak_ref[...] = jnp.full_like(peak_ref, NEG)
    sum_ref[...] = jnp.zeros_like(sum_ref)
    pick_ref[...] = jnp.zeros_like(pick_ref)

    @pl.loop(0, weight_ref.shape[1] // narrow)
    def _(n):
        columns = pl.ds(n * narrow if narrow % 128 else pl.multiple_of(n * narrow, 128), narrow)
        logits = sum_in_ref[:, columns] + quarter_dots(x_ref, (weight_ref, next_ref), columns)
        parts = [logits[:, c : c + 128] for c in range(0, narrow, 128)]
        if narrow % 128:
            spare = jnp.full((rows, 128 - narrow % 128), NEG, F32)
            parts[-1] = jnp.concatenate([parts[-1], spare], axis=1)
        lane = lax.broadcasted_iota(jnp.int32, (rows, 128), 1) + n * narrow
        peak = peak_ref[...]
        higher = functools.reduce(jnp.maximum, parts, peak)
        total = sum_ref[...] * jnp.exp(peak - higher)
        picked = pick_ref[...]
        target = wanted_ref[...]
        for c, part in enumerate(parts):
            total = total + jnp.exp(part - higher)
            picked = picked + jnp.where(lane + c * 128 == target, part, 0.0)
        peak_ref[...] = higher
        sum_ref[...] = total
        pick_ref[...] = picked

    higher = peak_ref[...]
    peak = jnp.max(higher, axis=1, keepdims=True)
    sums = jnp.sum(sum_ref[...] * jnp.exp(higher - peak), axis=1, keepdims=True)
    pick = jnp.sum(pick_ref[...], axis=1, keepdims=True)
    row = lax.broadcasted_iota(jnp.int32, (rows, 128), 0)
    lane = lax.broadcasted_iota(jnp.int32, (rows, 128), 1)
    three = jnp.where(lane // share == 0, peak, jnp.where(lane // share == 1, sums, pick))
    three = jnp.where((row - lane) % share == 0, three, 0.0)
    for i, place in enumerate(places):
        out_ref[place] = jnp.sum(three[i * share : (i + 1) * share], axis=0, keepdims=True)


def final_kernel(share, live_ref, stats_ref, out_ref):
    stats = stats_ref[...].reshape(stats_ref.shape[0], 128)
    peak = jnp.max(stats, axis=0, keepdims=True)
    sums = pltpu.roll(stats, 128 - share, 1)
    picks = pltpu.roll(stats, 128 - 2 * share, 1)
    total = jnp.sum(sums * jnp.exp(stats - peak), axis=0, keepdims=True)
    values = jnp.sum(picks, axis=0, keepdims=True) - peak - jnp.log(total)
    out_ref[...] = jnp.where(live_ref[:1] > 0.0, values, 0.0)[0, :share]


def local(
    group_size,
    tensor_size,
    resp_query,
    resp_key,
    resp_value,
    prompt_keys,
    prompt_values,
    prompt_of,
    lengths,
    residual,
    out_weight,
    norm_gain,
    lm_weight,
    targets,
):
    rows, span = resp_query.shape
    heads = span // HEAD_DIM
    seq = rows // prompt_of.shape[0]
    key_rows = prompt_keys.shape[0]
    assert PLEN % key_rows == 0
    share = rows // tensor_size
    depth = out_weight.shape[1]
    vocab = lm_weight.shape[1]
    i32 = jnp.int32

    wanted = targets.reshape(-1, share, 1)
    above = list(range(2, group_size, 2))
    distances = list(range(group_size - 1, 0, -1))
    far_queries = [swap(resp_query, "group", a, group_size) for a in above]
    queries = {1: swap(resp_query, "group", 1, group_size)}
    far_queries = pl.pallas_call(
        functools.partial(pass_kernel, len(above)),
        out_shape=[jax.ShapeDtypeStruct(x.shape, x.dtype) for x in far_queries],
        in_specs=[vmem()] * len(above) + [anywhere()],
        out_specs=[vmem()] * len(above),
        compiler_params=params(1),
        name="pass",
    )(*map(held, far_queries), wanted)
    for a, x in zip(above, far_queries):
        queries[a] = x
        queries[a + 1] = swap(x, "group", 1, group_size)
    queries = [queries[d] for d in distances]
    inputs = (resp_query, resp_key, resp_value, prompt_keys, prompt_values)
    loaded = pl.pallas_call(
        functools.partial(load_kernel, len(inputs)),
        out_shape=[pltpu.VMEM(x.shape, x.dtype) for x in inputs],
        in_specs=[anywhere()] * (1 + len(inputs)),
        out_specs=[vmem()] * len(inputs),
        scratch_shapes=[pltpu.SemaphoreType.DMA((len(inputs),))],
        compiler_params=params(1),
        cost_estimate=cost(moved=2 * MIB),
        name="load",
    )(far_queries[0], *map(stored, inputs))
    query, own_keys, own_values, keys, values = map(held, loaded)
    answers = pl.pallas_call(
        functools.partial(prefix_kernel, heads, len(distances)),
        out_shape=[jax.ShapeDtypeStruct((rows, span + 128), BF16)] * len(distances),
        in_specs=[vmem()] * (len(distances) + 2),
        out_specs=[vmem()] * len(distances),
        compiler_params=params(8),
        name="prefix_attention",
    )(*map(held, queries), keys, values)
    got = [swap(x, "group", d, group_size) for x, d in zip(answers, distances)]
    own, live, weight = pl.pallas_call(
        functools.partial(own_kernel, heads, seq, share),
        out_shape=[
            jax.ShapeDtypeStruct((rows, span + 128), F32),
            jax.ShapeDtypeStruct((8, 128), F32),
            pltpu.VMEM(out_weight.shape, BF16),
        ],
        in_specs=[smem()] * 2 + [vmem()] * 5 + [anywhere()] * 2,
        out_specs=[vmem()] * 3,
        scratch_shapes=[pltpu.SemaphoreType.DMA((4,))],
        compiler_params=params(6),
        cost_estimate=cost(moved=8 * MIB),
        name="own_attention",
    )(
        stored(lengths),
        stored(prompt_of),
        query,
        own_keys,
        own_values,
        keys,
        values,
        stored(out_weight),
        answers[0],
    )

    def fetch(source, start, count, gate):
        return held(
            pl.pallas_call(
                functools.partial(fetch_kernel, start),
                out_shape=pltpu.VMEM((count, source.shape[1]), BF16),
                in_specs=[anywhere()] * 2,
                out_specs=vmem(),
                scratch_shapes=[pltpu.SemaphoreType.DMA((4,))],
                compiler_params=params(1),
                cost_estimate=cost(moved=count * source.shape[1] * 2),
                name="fetch",
            )(stored(source), gate)
        )

    half = depth // 2
    quarter = depth // 4
    wide = 1280 if half % 1280 == 0 else half
    pairs = tensor_size // 2
    send_left, keep_left, keep_right, *rest = pl.pallas_call(
        functools.partial(project_kernel, heads, seq, share, wide, group_size, key_rows),
        out_shape=[
            jax.ShapeDtypeStruct((pairs, share, half), BF16),
            jax.ShapeDtypeStruct((pairs, share, half), F32),
            jax.ShapeDtypeStruct((2, share, half), F32),
        ]
        + [jax.ShapeDtypeStruct((2, share, half), BF16)] * (pairs - 1),
        in_specs=[smem()] + [vmem()] * (2 + len(distances)),
        out_specs=[vmem()] * (2 + pairs),
        scratch_shapes=[
            pltpu.VMEM((rows, span), BF16),
            pltpu.VMEM((tensor_size, share, wide), F32),
        ],
        compiler_params=params(6),
        name="project",
    )(stored(prompt_of), *map(held, (own, *got)), held(weight))

    far = list(range(2, tensor_size, 2))
    got_left = swap(send_left, "tensor", 1, tensor_size)
    got_right = [swap(x, "tensor", d, tensor_size) for x, d in zip(rest[::-1], far[::-1])]
    left = pl.pallas_call(
        fold_left_kernel,
        out_shape=[jax.ShapeDtypeStruct((share, half), F32)]
        + [jax.ShapeDtypeStruct((share, half), BF16)] * len(far),
        in_specs=[vmem()] * 2,
        out_specs=[vmem()] * (1 + len(far)),
        compiler_params=params(2),
        name="fold_left",
    )(held(keep_left), held(got_left))
    got_left = [swap(x, "tensor", d, tensor_size) for x, d in zip(left[:0:-1], far[::-1])]
    right = pl.pallas_call(
        fold_right_kernel,
        out_shape=[
            jax.ShapeDtypeStruct((share, half), F32),
            jax.ShapeDtypeStruct((share, half), BF16),
        ],
        in_specs=[anywhere()] + [vmem()] * (1 + len(far)),
        out_specs=[vmem()] * 2,
        compiler_params=params(2),
        name="fold_right",
    )(left[1], *map(held, (keep_right, *got_right)))
    got_right = swap(right[1], "tensor", 1, tensor_size)
    normed = pl.pallas_call(
        functools.partial(norm_kernel, len(far)),
        out_shape=jax.ShapeDtypeStruct((share, depth), BF16),
        in_specs=[vmem()] * (5 + len(far)),
        out_specs=vmem(),
        compiler_params=params(4),
        name="norm",
    )(
        *map(held, (residual.reshape(tensor_size, share, depth), norm_gain[None])),
        *map(held, (left[0], *got_left, right[0], got_right)),
    )

    order = [0] + far
    here = [(g, x) for g in [0] + above for x in (0, 1)]
    column = [swap(normed, "tensor", d, tensor_size) for d in far[::-1]]
    column = [normed] + column[::-1]
    third = fetch(lm_weight, 2 * quarter, quarter, normed)
    columns = pl.pallas_call(
        functools.partial(column_kernel, len(column)),
        out_shape=[jax.ShapeDtypeStruct((len(column), share, half), BF16)] * 2,
        in_specs=[vmem()] * len(column) + [anywhere()],
        out_specs=[vmem()] * 2,
        compiler_params=params(2),
        name="column",
    )(*map(held, column), third)

    def join(pieces, gate):
        blocks = sum(x.shape[0] for x in pieces)
        return pl.pallas_call(
            functools.partial(join_kernel, len(pieces)),
            out_shape=jax.ShapeDtypeStruct((blocks, share, half), BF16),
            in_specs=[vmem()] * len(pieces) + [anywhere()],
            out_specs=vmem(),
            compiler_params=params(2),
            name="join",
        )(*map(held, pieces), gate)

    left, right = columns
    got_left = swap(left, "tensor", 1, tensor_size)
    first_quarter = fetch(lm_weight, 0, quarter, left)
    right = [right] + [swap(right, "group", d, group_size) for d in above]
    left = join([left, got_left], first_quarter)
    got_left = [swap(left, "group", d, group_size) for d in above]
    second_quarter = fetch(lm_weight, quarter, quarter, left)
    across = swap(jnp.concatenate(right), "tensor", 1, tensor_size)
    across = jnp.split(across, len(right))
    right = [x for pair in zip(right, across) for x in pair]
    halves = []
    for tokens in (join([left] + got_left, second_quarter), jnp.concatenate(right)):
        tokens = tokens.reshape(-1, half)
        halves.append((tokens, swap(tokens, "group", 1, group_size)))
    spots = [(g + c, t + x) for c in (0, 1) for g, x in here for t in order]
    total_rows = 2 * tokens.shape[0]
    narrow = 1536 if vocab % 1536 == 0 else vocab
    limit = 10 if total_rows <= 256 else 24
    work = 2 * total_rows * (half) * vocab
    first, last = pl.pallas_call(
        functools.partial(first_kernel, narrow),
        out_shape=[pltpu.VMEM((total_rows, vocab), F32), pltpu.VMEM((quarter, vocab), BF16)],
        in_specs=[vmem()] * 4 + [anywhere()],
        out_specs=[vmem()] * 2,
        scratch_shapes=[
            pltpu.VMEM((total_rows, half), BF16),
            pltpu.SemaphoreType.DMA((4,)),
        ],
        compiler_params=params(limit),
        cost_estimate=cost(flops=work),
        name="logits_first",
    )(*map(held, (*halves[0], first_quarter, second_quarter)), stored(lm_weight))
    stats = pl.pallas_call(
        functools.partial(logits_kernel, vocab, spots, tensor_size),
        out_shape=jax.ShapeDtypeStruct((len(spots), 1, 128), F32),
        in_specs=[vmem()] * 6,
        out_specs=vmem(),
        scratch_shapes=[pltpu.VMEM((total_rows, half), BF16)]
        + [pltpu.VMEM((total_rows, 128), F32)] * 3
        + [pltpu.VMEM((total_rows, 1), i32)],
        compiler_params=params(limit),
        cost_estimate=cost(flops=work),
        name="logits",
    )(*map(held, (first, *halves[1])), wanted, held(third), held(last))

    stats = lax.all_to_all(stats, ("group", "tensor"), 0, 0, tiled=True)
    return pl.pallas_call(
        functools.partial(final_kernel, share),
        out_shape=jax.ShapeDtypeStruct((share,), F32),
        in_specs=[vmem()] * 2,
        out_specs=vmem(),
        compiler_params=params(4),
        name="final",
    )(held(live), held(stats))


def solution(mesh):
    return jax.shard_map(
        functools.partial(local, mesh.shape["group"], mesh.shape["tensor"]),
        mesh=mesh,
        in_specs=(
            P("group", "tensor"),
            P("group", "tensor"),
            P("group", "tensor"),
            P("group", "tensor"),
            P("group", "tensor"),
            P("group"),
            P("group"),
            P("group", None),
            P("tensor", None),
            P(),
            P(None, ("group", "tensor")),
            P(),
        ),
        out_specs=P(("group", "tensor")),
        check_vma=False,
    )
```

```python
import functools

import jax
import jax.numpy as jnp
from jax import lax
from jax.experimental import pallas as pl
from jax.experimental.pallas import tpu as pltpu
from jax.sharding import PartitionSpec as P

HEAD_DIM = 128
PLEN = 512
NEG = -1e30
BF16 = jnp.bfloat16
F32 = jnp.float32
MIB = 1024 * 1024


def params(mib):
    return pltpu.CompilerParams(vmem_limit_bytes=mib * MIB)


def held(x):
    return pltpu.with_memory_space_constraint(x, pltpu.VMEM)


def stored(x):
    return pltpu.with_memory_space_constraint(x, pltpu.HBM)


def anywhere():
    return pl.BlockSpec(memory_space=pl.ANY)


def cost(flops=0, moved=0):
    return pl.CostEstimate(flops=flops, bytes_accessed=moved, transcendentals=0)


def vmem():
    return pl.BlockSpec(memory_space=pltpu.VMEM)


def smem():
    return pl.BlockSpec(memory_space=pltpu.SMEM)


def swap(x, axis, distance, size):
    return lax.ppermute(x, axis, [(i, i ^ distance) for i in range(size)])


def attend(jobs):
    factor = HEAD_DIM**-0.5
    scores = [
        lax.dot_general(q, k, (((1,), (1,)), ((), ())), preferred_element_type=F32)
        for q, k, _, _ in jobs
    ]
    scores = [
        s if job[3] is None else jnp.where(job[3], s, NEG) for s, job in zip(scores, jobs)
    ]
    peaks = [jnp.max(s, axis=1, keepdims=True) for s in scores]
    weights = [jnp.exp((s - peak) * factor) for s, peak in zip(scores, peaks)]
    weights = [
        w if job[3] is None else jnp.where(job[3], w, 0.0) for w, job in zip(weights, jobs)
    ]
    weights = [w.astype(BF16) for w in weights]
    totals = [jnp.sum(w.astype(F32), axis=1, keepdims=True) for w in weights]
    mixed = [
        jnp.dot(w, job[2], preferred_element_type=F32) for w, job in zip(weights, jobs)
    ]
    return [
        (m / total, peak * factor + jnp.log(total))
        for m, total, peak in zip(mixed, totals, peaks)
    ]


def pack_logs(logs, rows):
    lane = lax.broadcasted_iota(jnp.int32, (rows, 128), 1)
    packed = jnp.zeros((rows, 128), F32)
    for head, log in enumerate(logs):
        first = log.astype(BF16).astype(F32)
        second = (log - first).astype(BF16).astype(F32)
        third = log - first - second
        for part, value in enumerate((first, second, third)):
            packed = jnp.where(lane == 3 * head + part, value, packed)
    return packed.astype(BF16)


def pass_kernel(count, *refs):
    for ref, out_ref in zip(refs, refs[-count:]):
        out_ref[...] = ref[...]


def load_kernel(count, gate_ref, *refs):
    sems = refs[2 * count]
    copies = [
        pltpu.make_async_copy(refs[i], refs[count + i], sems.at[i]) for i in range(count)
    ]
    for copy in copies:
        copy.start()
    for copy in copies:
        copy.wait()


def carried(source_ref, start, out_ref, sems):
    count = sems.shape[0]
    rows = out_ref.shape[0] // count
    return [
        pltpu.make_async_copy(
            source_ref.at[pl.ds(start + i * rows, rows)], out_ref.at[pl.ds(i * rows, rows)], sems.at[i]
        )
        for i in range(count)
    ]


def own_kernel(
    heads,
    seq,
    share,
    lengths_ref,
    prompt_ref,
    q_ref,
    rk_ref,
    rv_ref,
    k_ref,
    v_ref,
    source_ref,
    gate_ref,
    own_ref,
    live_ref,
    weight_ref,
    sems,
):
    copies = carried(source_ref, 0, weight_ref, sems)
    for copy in copies:
        copy.start()
    rows = q_ref.shape[0]
    row = lax.broadcasted_iota(jnp.int32, (rows, rows), 0)
    col = lax.broadcasted_iota(jnp.int32, (rows, rows), 1)
    live = jnp.zeros((rows, rows), jnp.int32)
    for r in range(rows // seq):
        live = jnp.where(col // seq == r, lengths_ref[r], live)
    allowed = (row // seq == col // seq) & (col <= row) & (col % seq < live)
    parts = [slice(h * HEAD_DIM, (h + 1) * HEAD_DIM) for h in range(heads)]
    found = attend(
        [(q_ref[:, p], rk_ref[:, p], rv_ref[:, p], allowed) for p in parts]
        + [(q_ref[:, p], k_ref[:, p], v_ref[:, p], None) for p in parts]
    )
    here = wanted_prompts(seq, rows, prompt_ref) == lax.axis_index("group") * k_ref.shape[0] // PLEN
    lane = lax.broadcasted_iota(jnp.int32, (rows, 128), 1)
    packed = jnp.zeros((rows, 128), F32)
    for h, p in enumerate(parts):
        (first, log), (second, other) = found[h], found[heads + h]
        other = jnp.where(here, other, NEG)
        peak = jnp.maximum(log, other)
        left, right = jnp.exp(log - peak), jnp.exp(other - peak)
        own_ref[:, p] = (first * left + second * right) / (left + right)
        packed = jnp.where(lane == h, peak + jnp.log(left + right), packed)
    own_ref[:, heads * HEAD_DIM :] = packed
    token = lax.broadcasted_iota(jnp.int32, live_ref.shape, 1) + lax.axis_index("tensor") * share
    length = jnp.zeros(live_ref.shape, jnp.int32)
    for r in range(rows // seq):
        length = jnp.where(token // seq == r, lengths_ref[r], length)
    live_ref[...] = jnp.where(token % seq < length, 1.0, 0.0)
    for copy in copies:
        copy.wait()


def wanted_prompts(seq, rows, prompt_ref):
    row = lax.broadcasted_iota(jnp.int32, (rows, 1), 0)
    wanted = jnp.zeros((rows, 1), jnp.int32)
    for r in range(rows // seq):
        wanted = jnp.where(row // seq == r, prompt_ref[r], wanted)
    return wanted


def prefix_kernel(heads, count, *refs):
    q_refs, (k_ref, v_ref), out_refs = refs[:count], refs[count : count + 2], refs[count + 2 :]
    rows = q_refs[0].shape[0]
    parts = [slice(h * HEAD_DIM, (h + 1) * HEAD_DIM) for h in range(heads)]
    found = attend(
        [
            (jnp.concatenate([ref[:, p] for ref in q_refs], axis=0), k_ref[:, p], v_ref[:, p], None)
            for p in parts
        ]
    )
    for i in range(count):
        rung = slice(i * rows, (i + 1) * rows)
        for h, p in enumerate(parts):
            out_refs[i][:, p] = found[h][0][rung].astype(BF16)
        out_refs[i][:, heads * HEAD_DIM :] = pack_logs([log[rung] for _, log in found], rows)


def project_kernel(heads, seq, wide, group_size, key_rows, prompt_ref, own_ref, *refs):
    got_refs, refs = refs[: group_size - 1], refs[group_size - 1 :]
    weight_ref, send_left_ref, keep_left_ref, send_right_ref, keep_right_ref = refs[:5]
    attended_ref, partial_ref = refs[5:]
    rows = own_ref.shape[0]
    wanted = wanted_prompts(seq, rows, prompt_ref)
    group = lax.axis_index("group")
    holders = [(group ^ d) * key_rows // PLEN for d in range(group_size - 1, 0, -1)]
    for h in range(heads):
        part = slice(h * HEAD_DIM, (h + 1) * HEAD_DIM)
        at = heads * HEAD_DIM
        logs = [own_ref[:, at + h : at + h + 1]]
        values = [own_ref[:, part]]
        for holder, ref in zip(holders, got_refs):
            three = ref[:, at : at + 128].astype(F32)
            log = (
                three[:, 3 * h : 3 * h + 1]
                + three[:, 3 * h + 1 : 3 * h + 2]
                + three[:, 3 * h + 2 : 3 * h + 3]
            )
            logs.append(jnp.where(wanted == holder, log, NEG))
            values.append(ref[:, part].astype(F32))
        peak = functools.reduce(jnp.maximum, logs)
        loads = [jnp.exp(log - peak) for log in logs]
        total = functools.reduce(jnp.add, loads)
        mixed = functools.reduce(jnp.add, [w * v for w, v in zip(loads, values)])
        attended_ref[:, part] = (mixed / total).astype(BF16)

    me = lax.axis_index("tensor") % 4
    block = rows // 4
    half = send_left_ref.shape[2]

    def multiply(columns):
        partial = jnp.dot(attended_ref[...], weight_ref[:, columns], preferred_element_type=F32)
        for b in range(4):
            partial_ref[b] = partial[b * block : (b + 1) * block]

    @pl.loop(0, half // wide)
    def _(n):
        columns = pl.ds(pl.multiple_of(n * wide, 128), wide)
        multiply(columns)
        for i in range(2):
            keep_left_ref[i, :, columns] = partial_ref[me ^ (2 * i)]
            send_left_ref[i, :, columns] = partial_ref[me ^ (2 * i + 1)].astype(BF16)

    @pl.loop(0, half // wide)
    def _(n):
        columns = pl.ds(pl.multiple_of(n * wide, 128), wide)
        multiply(pl.ds(pl.multiple_of(half + n * wide, 128), wide))
        for i in range(2):
            keep_right_ref[i, :, columns] = partial_ref[me ^ i]
            send_right_ref[i, :, columns] = partial_ref[me ^ (i + 2)].astype(BF16)


def fold_kernel(keep_ref, got_ref, own_ref, send_ref):
    own_ref[...] = keep_ref[0] + got_ref[0].astype(F32)
    send_ref[...] = (keep_ref[1] + got_ref[1].astype(F32)).astype(BF16)


def side_kernel(left_ref, got_left_ref, right_ref, got_right_ref, own_ref, send_ref):
    half = left_ref.shape[1]
    for i, (ref, got_ref) in enumerate(((left_ref, got_left_ref), (right_ref, got_right_ref))):
        total = ref[...] + got_ref[...].astype(F32)
        own_ref[:, i * half : (i + 1) * half] = total
        send_ref[:, i * half : (i + 1) * half] = total.astype(BF16)


def add_kernel(own_ref, got_ref, out_ref, send_ref):
    total = own_ref[...] + got_ref[...].astype(F32)
    out_ref[...] = total
    send_ref[...] = total.astype(BF16)


def fetch_kernel(start, source_ref, gate_ref, out_ref, sems):
    copies = carried(source_ref, start, out_ref, sems)
    for copy in copies:
        copy.start()
    for copy in copies:
        copy.wait()


def column_kernel(count, *refs):
    terms, out_refs = refs[:count], refs[-2:]
    width = out_refs[0].shape[2]
    for i, ref in enumerate(terms):
        for half, out_ref in enumerate(out_refs):
            out_ref[i] = ref[:, half * width : (half + 1) * width]


def norm_kernel(residual_ref, gain_ref, first_gate_ref, second_gate_ref, own_ref, got_ref, out_ref):
    hidden = residual_ref[lax.axis_index("tensor") % 4].astype(F32)
    hidden = hidden + (own_ref[...] + got_ref[...].astype(F32))
    squares = jnp.mean(hidden * hidden, axis=-1, keepdims=True)
    out_ref[...] = (hidden * lax.rsqrt(squares + 1e-06) * gain_ref[...].astype(F32)).astype(BF16)


def join_kernel(count, *refs):
    out_ref = refs[-1]
    start = 0
    for ref in refs[:count]:
        out_ref[start : start + ref.shape[0]] = ref[...]
        start += ref.shape[0]


def quarter_dots(x_ref, weight_refs, columns):
    depth = weight_refs[0].shape[0]
    return functools.reduce(
        jnp.add,
        [
            jnp.dot(x_ref[:, i * depth : (i + 1) * depth], ref[:, columns], preferred_element_type=F32)
            for i, ref in enumerate(weight_refs)
        ],
    )


def first_kernel(
    narrow, left_ref, right_ref, weight_ref, next_ref, source_ref, out_ref, last_ref, x_ref, sems
):
    copies = carried(source_ref, source_ref.shape[0] - last_ref.shape[0], last_ref, sems)
    for copy in copies:
        copy.start()
    half = left_ref.shape[0]
    x_ref[:half] = left_ref[...]
    x_ref[half:] = right_ref[...]

    @pl.loop(0, weight_ref.shape[1] // narrow)
    def _(n):
        columns = pl.ds(n * narrow if narrow % 128 else pl.multiple_of(n * narrow, 128), narrow)
        out_ref[:, columns] = quarter_dots(x_ref, (weight_ref, next_ref), columns)

    for copy in copies:
        copy.wait()


def logits_kernel(
    narrow,
    spots,
    tensor_size,
    sum_in_ref,
    left_ref,
    right_ref,
    target_ref,
    weight_ref,
    next_ref,
    out_ref,
    x_ref,
    peak_ref,
    sum_ref,
    pick_ref,
    wanted_ref,
):
    half = left_ref.shape[0]
    rows = 2 * half
    share = target_ref.shape[1]
    group, tensor = lax.axis_index("group"), lax.axis_index("tensor")
    vocab = weight_ref.shape[1]
    shares = tensor_size // 4
    places = [
        (group ^ g) * tensor_size + shares * ((tensor % 4) ^ d) + i for g, d in spots for i in range(shares)
    ]
    for i, place in enumerate(places):
        wanted_ref[i * share : (i + 1) * share] = target_ref[place]
    wanted = wanted_ref[...] - (group * tensor_size + tensor) * vocab
    wanted_ref[...] = jnp.where((wanted >= 0) & (wanted < vocab), wanted, -1)
    x_ref[:half] = left_ref[...]
    x_ref[half:] = right_ref[...]
    peak_ref[...] = jnp.full_like(peak_ref, NEG)
    sum_ref[...] = jnp.zeros_like(sum_ref)
    pick_ref[...] = jnp.zeros_like(pick_ref)

    @pl.loop(0, weight_ref.shape[1] // narrow)
    def _(n):
        columns = pl.ds(n * narrow if narrow % 128 else pl.multiple_of(n * narrow, 128), narrow)
        logits = sum_in_ref[:, columns] + quarter_dots(x_ref, (weight_ref, next_ref), columns)
        parts = [logits[:, c : c + 128] for c in range(0, narrow, 128)]
        if narrow % 128:
            spare = jnp.full((rows, 128 - narrow % 128), NEG, F32)
            parts[-1] = jnp.concatenate([parts[-1], spare], axis=1)
        lane = lax.broadcasted_iota(jnp.int32, (rows, 128), 1) + n * narrow
        peak = peak_ref[...]
        higher = functools.reduce(jnp.maximum, parts, peak)
        total = sum_ref[...] * jnp.exp(peak - higher)
        picked = pick_ref[...]
        target = wanted_ref[...]
        for c, part in enumerate(parts):
            total = total + jnp.exp(part - higher)
            picked = picked + jnp.where(lane + c * 128 == target, part, 0.0)
        peak_ref[...] = higher
        sum_ref[...] = total
        pick_ref[...] = picked

    higher = peak_ref[...]
    peak = jnp.max(higher, axis=1, keepdims=True)
    sums = jnp.sum(sum_ref[...] * jnp.exp(higher - peak), axis=1, keepdims=True)
    pick = jnp.sum(pick_ref[...], axis=1, keepdims=True)
    row = lax.broadcasted_iota(jnp.int32, (rows, 128), 0)
    lane = lax.broadcasted_iota(jnp.int32, (rows, 128), 1)
    three = jnp.where(lane // share == 0, peak, jnp.where(lane // share == 1, sums, pick))
    three = jnp.where((row - lane) % share == 0, three, 0.0)
    for i, place in enumerate(places):
        out_ref[place] = jnp.sum(three[i * share : (i + 1) * share], axis=0, keepdims=True)


def final_kernel(share, live_ref, stats_ref, out_ref):
    stats = stats_ref[...].reshape(stats_ref.shape[0], 128)
    peak = jnp.max(stats, axis=0, keepdims=True)
    sums = pltpu.roll(stats, 128 - share, 1)
    picks = pltpu.roll(stats, 128 - 2 * share, 1)
    total = jnp.sum(sums * jnp.exp(stats - peak), axis=0, keepdims=True)
    values = jnp.sum(picks, axis=0, keepdims=True) - peak - jnp.log(total)
    out_ref[...] = jnp.where(live_ref[:1] > 0.0, values, 0.0)[0, :share]


def local(
    group_size,
    tensor_size,
    resp_query,
    resp_key,
    resp_value,
    prompt_keys,
    prompt_values,
    prompt_of,
    lengths,
    residual,
    out_weight,
    norm_gain,
    lm_weight,
    targets,
):
    rows, span = resp_query.shape
    heads = span // HEAD_DIM
    seq = rows // prompt_of.shape[0]
    key_rows = prompt_keys.shape[0]
    assert PLEN % key_rows == 0
    share = rows // tensor_size
    depth = out_weight.shape[1]
    vocab = lm_weight.shape[1]
    i32 = jnp.int32

    wanted = targets.reshape(-1, share, 1)
    above = list(range(2, group_size, 2))
    distances = list(range(group_size - 1, 0, -1))
    far_queries = [swap(resp_query, "group", a, group_size) for a in above]
    queries = {1: swap(resp_query, "group", 1, group_size)}
    far_queries = pl.pallas_call(
        functools.partial(pass_kernel, len(above)),
        out_shape=[jax.ShapeDtypeStruct(x.shape, x.dtype) for x in far_queries],
        in_specs=[vmem()] * len(above) + [anywhere()],
        out_specs=[vmem()] * len(above),
        compiler_params=params(1),
        name="pass",
    )(*map(held, far_queries), wanted)
    for a, x in zip(above, far_queries):
        queries[a] = x
        queries[a + 1] = swap(x, "group", 1, group_size)
    queries = [queries[d] for d in distances]
    inputs = (resp_query, resp_key, resp_value, prompt_keys, prompt_values)
    loaded = pl.pallas_call(
        functools.partial(load_kernel, len(inputs)),
        out_shape=[pltpu.VMEM(x.shape, x.dtype) for x in inputs],
        in_specs=[anywhere()] * (1 + len(inputs)),
        out_specs=[vmem()] * len(inputs),
        scratch_shapes=[pltpu.SemaphoreType.DMA((len(inputs),))],
        compiler_params=params(1),
        cost_estimate=cost(moved=2 * MIB),
        name="load",
    )(far_queries[0], *map(stored, inputs))
    query, own_keys, own_values, keys, values = map(held, loaded)
    answers = pl.pallas_call(
        functools.partial(prefix_kernel, heads, len(distances)),
        out_shape=[jax.ShapeDtypeStruct((rows, span + 128), BF16)] * len(distances),
        in_specs=[vmem()] * (len(distances) + 2),
        out_specs=[vmem()] * len(distances),
        compiler_params=params(8),
        name="prefix_attention",
    )(*map(held, queries), keys, values)
    got = [swap(x, "group", d, group_size) for x, d in zip(answers, distances)]
    own, live, weight = pl.pallas_call(
        functools.partial(own_kernel, heads, seq, share),
        out_shape=[
            jax.ShapeDtypeStruct((rows, span + 128), F32),
            jax.ShapeDtypeStruct((8, 128), F32),
            pltpu.VMEM(out_weight.shape, BF16),
        ],
        in_specs=[smem()] * 2 + [vmem()] * 5 + [anywhere()] * 2,
        out_specs=[vmem()] * 3,
        scratch_shapes=[pltpu.SemaphoreType.DMA((4,))],
        compiler_params=params(6),
        cost_estimate=cost(moved=8 * MIB),
        name="own_attention",
    )(
        stored(lengths),
        stored(prompt_of),
        query,
        own_keys,
        own_values,
        keys,
        values,
        stored(out_weight),
        answers[0],
    )

    def fetch(source, start, count, gate):
        return held(
            pl.pallas_call(
                functools.partial(fetch_kernel, start),
                out_shape=pltpu.VMEM((count, source.shape[1]), BF16),
                in_specs=[anywhere()] * 2,
                out_specs=vmem(),
                scratch_shapes=[pltpu.SemaphoreType.DMA((4,))],
                compiler_params=params(1),
                cost_estimate=cost(moved=count * source.shape[1] * 2),
                name="fetch",
            )(stored(source), gate)
        )

    half = depth // 2
    quarter = depth // 4
    wide = 1280 if half % 1280 == 0 else half
    block = rows // 4
    send_left, keep_left, send_right, keep_right = pl.pallas_call(
        functools.partial(project_kernel, heads, seq, wide, group_size, key_rows),
        out_shape=[
            jax.ShapeDtypeStruct((2, block, half), BF16),
            jax.ShapeDtypeStruct((2, block, half), F32),
        ]
        * 2,
        in_specs=[smem()] + [vmem()] * (2 + len(distances)),
        out_specs=[vmem()] * 4,
        scratch_shapes=[
            pltpu.VMEM((rows, span), BF16),
            pltpu.VMEM((4, block, wide), F32),
        ],
        compiler_params=params(6),
        name="project",
    )(stored(prompt_of), *map(held, (own, *got)), held(weight))

    def add(kernel, name, size, *operands):
        return pl.pallas_call(
            kernel,
            out_shape=[jax.ShapeDtypeStruct(size, F32), jax.ShapeDtypeStruct(size, BF16)],
            in_specs=[vmem()] * len(operands),
            out_specs=[vmem()] * 2,
            compiler_params=params(2),
            name=name,
        )(*map(held, operands))

    got_left = swap(send_left, "tensor", 1, tensor_size)
    got_right = swap(send_right, "tensor", 2, tensor_size)
    left, send_left = add(fold_kernel, "fold_left", (block, half), keep_left, got_left)
    right, send_right = add(fold_kernel, "fold_right", (block, half), keep_right, got_right)
    got_left = swap(send_left, "tensor", 2, tensor_size)
    got_right = swap(send_right, "tensor", 1, tensor_size)
    total, send = add(side_kernel, "side", (block, depth), left, got_left, right, got_right)
    first_quarter = fetch(lm_weight, 0, quarter, send)
    second_quarter = fetch(lm_weight, quarter, quarter, send)
    far = 4
    while 2 * far < tensor_size:
        total, send = add(
            add_kernel, "add", (block, depth), total, swap(send, "tensor", far, tensor_size)
        )
        far = 2 * far
    normed = pl.pallas_call(
        norm_kernel,
        out_shape=jax.ShapeDtypeStruct((block, depth), BF16),
        in_specs=[vmem()] * 2 + [anywhere()] * 2 + [vmem()] * 2,
        out_specs=vmem(),
        compiler_params=params(4),
        name="norm",
    )(
        *map(held, (residual.reshape(4, block, depth), norm_gain[None])),
        first_quarter,
        second_quarter,
        *map(held, (total, swap(send, "tensor", far, tensor_size))),
    )

    order = [0, 2]
    here = [(g, x) for g in [0] + above for x in (0, 1)]
    column = [normed, swap(normed, "tensor", 2, tensor_size)]
    columns = pl.pallas_call(
        functools.partial(column_kernel, len(column)),
        out_shape=[jax.ShapeDtypeStruct((len(column), block, half), BF16)] * 2,
        in_specs=[vmem()] * len(column),
        out_specs=[vmem()] * 2,
        compiler_params=params(2),
        name="column",
    )(*map(held, column))

    def join(pieces, gate):
        blocks = sum(x.shape[0] for x in pieces)
        return pl.pallas_call(
            functools.partial(join_kernel, len(pieces)),
            out_shape=jax.ShapeDtypeStruct((blocks, block, half), BF16),
            in_specs=[vmem()] * len(pieces) + [anywhere()],
            out_specs=vmem(),
            compiler_params=params(2),
            name="join",
        )(*map(held, pieces), gate)

    left, right = columns
    got_left = swap(left, "tensor", 1, tensor_size)
    third = fetch(lm_weight, 2 * quarter, quarter, left)
    right = [right] + [swap(right, "group", d, group_size) for d in above]
    left = join([left, got_left], third)
    got_left = [swap(left, "group", d, group_size) for d in above]
    across = swap(jnp.concatenate(right), "tensor", 1, tensor_size)
    across = jnp.split(across, len(right))
    right = [x for pair in zip(right, across) for x in pair]
    halves = []
    for tokens in (jnp.concatenate([left] + got_left), jnp.concatenate(right)):
        tokens = tokens.reshape(-1, half)
        halves.append((tokens, swap(tokens, "group", 1, group_size)))
    spots = [(g + c, t + x) for c in (0, 1) for g, x in here for t in order]
    total_rows = 2 * tokens.shape[0]
    narrow = 1536 if vocab % 1536 == 0 else vocab
    limit = 10 if total_rows <= 256 else 24
    work = 2 * total_rows * (half) * vocab
    first, last = pl.pallas_call(
        functools.partial(first_kernel, narrow),
        out_shape=[pltpu.VMEM((total_rows, vocab), F32), pltpu.VMEM((quarter, vocab), BF16)],
        in_specs=[vmem()] * 4 + [anywhere()],
        out_specs=[vmem()] * 2,
        scratch_shapes=[
            pltpu.VMEM((total_rows, half), BF16),
            pltpu.SemaphoreType.DMA((4,)),
        ],
        compiler_params=params(limit),
        cost_estimate=cost(flops=work),
        name="logits_first",
    )(*map(held, (*halves[0], first_quarter, second_quarter)), stored(lm_weight))
    stats = pl.pallas_call(
        functools.partial(logits_kernel, vocab, spots, tensor_size),
        out_shape=jax.ShapeDtypeStruct((group_size * tensor_size, 1, 128), F32),
        in_specs=[vmem()] * 6,
        out_specs=vmem(),
        scratch_shapes=[pltpu.VMEM((total_rows, half), BF16)]
        + [pltpu.VMEM((total_rows, 128), F32)] * 3
        + [pltpu.VMEM((total_rows, 1), i32)],
        compiler_params=params(limit),
        cost_estimate=cost(flops=work),
        name="logits",
    )(*map(held, (first, *halves[1])), wanted, held(third), held(last))

    stats = lax.all_to_all(stats, ("group", "tensor"), 0, 0, tiled=True)
    return pl.pallas_call(
        functools.partial(final_kernel, share),
        out_shape=jax.ShapeDtypeStruct((share,), F32),
        in_specs=[vmem()] * 2,
        out_specs=vmem(),
        compiler_params=params(4),
        name="final",
    )(held(live), held(stats))


def solution(mesh):
    return jax.shard_map(
        functools.partial(local, mesh.shape["group"], mesh.shape["tensor"]),
        mesh=mesh,
        in_specs=(
            P("group", "tensor"),
            P("group", "tensor"),
            P("group", "tensor"),
            P("group", "tensor"),
            P("group", "tensor"),
            P("group"),
            P("group"),
            P("group", None),
            P("tensor", None),
            P(),
            P(None, ("group", "tensor")),
            P(),
        ),
        out_specs=P(("group", "tensor")),
        check_vma=False,
    )
```

```python
import functools

import jax
import jax.numpy as jnp
from jax import lax
from jax.experimental import pallas as pl
from jax.experimental.pallas import tpu as pltpu
from jax.sharding import PartitionSpec as P

HEAD_DIM = 128
PLEN = 512
NEG = -1e30
BF16 = jnp.bfloat16
F32 = jnp.float32
MIB = 1024 * 1024


def params(mib):
    return pltpu.CompilerParams(vmem_limit_bytes=mib * MIB)


def held(x):
    return pltpu.with_memory_space_constraint(x, pltpu.VMEM)


def stored(x):
    return pltpu.with_memory_space_constraint(x, pltpu.HBM)


def anywhere():
    return pl.BlockSpec(memory_space=pl.ANY)


def cost(flops=0, moved=0):
    return pl.CostEstimate(flops=flops, bytes_accessed=moved, transcendentals=0)


def vmem():
    return pl.BlockSpec(memory_space=pltpu.VMEM)


def smem():
    return pl.BlockSpec(memory_space=pltpu.SMEM)


def swap(x, axis, distance, size):
    return lax.ppermute(x, axis, [(i, i ^ distance) for i in range(size)])


def attend(jobs):
    factor = HEAD_DIM**-0.5
    scores = [
        lax.dot_general(q, k, (((1,), (1,)), ((), ())), preferred_element_type=F32)
        for q, k, _, _ in jobs
    ]
    scores = [
        s if job[3] is None else jnp.where(job[3], s, NEG) for s, job in zip(scores, jobs)
    ]
    peaks = [jnp.max(s, axis=1, keepdims=True) for s in scores]
    weights = [jnp.exp((s - peak) * factor) for s, peak in zip(scores, peaks)]
    weights = [
        w if job[3] is None else jnp.where(job[3], w, 0.0) for w, job in zip(weights, jobs)
    ]
    weights = [w.astype(BF16) for w in weights]
    totals = [jnp.sum(w.astype(F32), axis=1, keepdims=True) for w in weights]
    mixed = [
        jnp.dot(w, job[2], preferred_element_type=F32) for w, job in zip(weights, jobs)
    ]
    return [
        (m / total, peak * factor + jnp.log(total))
        for m, total, peak in zip(mixed, totals, peaks)
    ]


def pack_logs(logs, rows):
    lane = lax.broadcasted_iota(jnp.int32, (rows, 128), 1)
    packed = jnp.zeros((rows, 128), F32)
    for head, log in enumerate(logs):
        first = log.astype(BF16).astype(F32)
        second = (log - first).astype(BF16).astype(F32)
        third = log - first - second
        for part, value in enumerate((first, second, third)):
            packed = jnp.where(lane == 3 * head + part, value, packed)
    return packed.astype(BF16)


def pass_kernel(count, *refs):
    for ref, out_ref in zip(refs, refs[-count:]):
        out_ref[...] = ref[...]


def load_kernel(count, gate_ref, *refs):
    sems = refs[2 * count]
    copies = [
        pltpu.make_async_copy(refs[i], refs[count + i], sems.at[i]) for i in range(count)
    ]
    for copy in copies:
        copy.start()
    for copy in copies:
        copy.wait()


def carried(source_ref, start, out_ref, sems):
    count = sems.shape[0]
    rows = out_ref.shape[0] // count
    return [
        pltpu.make_async_copy(
            source_ref.at[pl.ds(start + i * rows, rows)], out_ref.at[pl.ds(i * rows, rows)], sems.at[i]
        )
        for i in range(count)
    ]


def own_kernel(
    heads,
    seq,
    share,
    lengths_ref,
    prompt_ref,
    q_ref,
    rk_ref,
    rv_ref,
    k_ref,
    v_ref,
    source_ref,
    gate_ref,
    own_ref,
    live_ref,
    weight_ref,
    sems,
):
    copies = carried(source_ref, 0, weight_ref, sems)
    for copy in copies:
        copy.start()
    rows = q_ref.shape[0]
    row = lax.broadcasted_iota(jnp.int32, (rows, rows), 0)
    col = lax.broadcasted_iota(jnp.int32, (rows, rows), 1)
    live = jnp.zeros((rows, rows), jnp.int32)
    for r in range(rows // seq):
        live = jnp.where(col // seq == r, lengths_ref[r], live)
    allowed = (row // seq == col // seq) & (col <= row) & (col % seq < live)
    parts = [slice(h * HEAD_DIM, (h + 1) * HEAD_DIM) for h in range(heads)]
    found = attend(
        [(q_ref[:, p], rk_ref[:, p], rv_ref[:, p], allowed) for p in parts]
        + [(q_ref[:, p], k_ref[:, p], v_ref[:, p], None) for p in parts]
    )
    here = wanted_prompts(seq, rows, prompt_ref) == lax.axis_index("group") * k_ref.shape[0] // PLEN
    lane = lax.broadcasted_iota(jnp.int32, (rows, 128), 1)
    packed = jnp.zeros((rows, 128), F32)
    for h, p in enumerate(parts):
        (first, log), (second, other) = found[h], found[heads + h]
        other = jnp.where(here, other, NEG)
        peak = jnp.maximum(log, other)
        left, right = jnp.exp(log - peak), jnp.exp(other - peak)
        own_ref[:, p] = (first * left + second * right) / (left + right)
        packed = jnp.where(lane == h, peak + jnp.log(left + right), packed)
    own_ref[:, heads * HEAD_DIM :] = packed
    token = lax.broadcasted_iota(jnp.int32, live_ref.shape, 1) + lax.axis_index("tensor") * share
    length = jnp.zeros(live_ref.shape, jnp.int32)
    for r in range(rows // seq):
        length = jnp.where(token // seq == r, lengths_ref[r], length)
    live_ref[...] = jnp.where(token % seq < length, 1.0, 0.0)
    for copy in copies:
        copy.wait()


def wanted_prompts(seq, rows, prompt_ref):
    row = lax.broadcasted_iota(jnp.int32, (rows, 1), 0)
    wanted = jnp.zeros((rows, 1), jnp.int32)
    for r in range(rows // seq):
        wanted = jnp.where(row // seq == r, prompt_ref[r], wanted)
    return wanted


def prefix_kernel(heads, count, *refs):
    q_refs, (k_ref, v_ref), out_refs = refs[:count], refs[count : count + 2], refs[count + 2 :]
    rows = q_refs[0].shape[0]
    parts = [slice(h * HEAD_DIM, (h + 1) * HEAD_DIM) for h in range(heads)]
    found = attend(
        [
            (jnp.concatenate([ref[:, p] for ref in q_refs], axis=0), k_ref[:, p], v_ref[:, p], None)
            for p in parts
        ]
    )
    for i in range(count):
        rung = slice(i * rows, (i + 1) * rows)
        for h, p in enumerate(parts):
            out_refs[i][:, p] = found[h][0][rung].astype(BF16)
        out_refs[i][:, heads * HEAD_DIM :] = pack_logs([log[rung] for _, log in found], rows)


def project_kernel(heads, seq, wide, group_size, key_rows, prompt_ref, own_ref, *refs):
    got_refs, refs = refs[: group_size - 1], refs[group_size - 1 :]
    weight_ref, send_left_ref, keep_left_ref, send_right_ref, keep_right_ref = refs[:5]
    attended_ref, partial_ref = refs[5:]
    rows = own_ref.shape[0]
    wanted = wanted_prompts(seq, rows, prompt_ref)
    group = lax.axis_index("group")
    holders = [(group ^ d) * key_rows // PLEN for d in range(group_size - 1, 0, -1)]
    for h in range(heads):
        part = slice(h * HEAD_DIM, (h + 1) * HEAD_DIM)
        at = heads * HEAD_DIM
        logs = [own_ref[:, at + h : at + h + 1]]
        values = [own_ref[:, part]]
        for holder, ref in zip(holders, got_refs):
            three = ref[:, at : at + 128].astype(F32)
            log = (
                three[:, 3 * h : 3 * h + 1]
                + three[:, 3 * h + 1 : 3 * h + 2]
                + three[:, 3 * h + 2 : 3 * h + 3]
            )
            logs.append(jnp.where(wanted == holder, log, NEG))
            values.append(ref[:, part].astype(F32))
        peak = functools.reduce(jnp.maximum, logs)
        loads = [jnp.exp(log - peak) for log in logs]
        total = functools.reduce(jnp.add, loads)
        mixed = functools.reduce(jnp.add, [w * v for w, v in zip(loads, values)])
        attended_ref[:, part] = (mixed / total).astype(BF16)

    me = lax.axis_index("tensor") % 4
    block = rows // 4
    half = send_left_ref.shape[2]

    def multiply(columns):
        partial = jnp.dot(attended_ref[...], weight_ref[:, columns], preferred_element_type=F32)
        for b in range(4):
            partial_ref[b] = partial[b * block : (b + 1) * block]

    @pl.loop(0, half // wide)
    def _(n):
        columns = pl.ds(pl.multiple_of(n * wide, 128), wide)
        multiply(columns)
        for i in range(2):
            keep_left_ref[i, :, columns] = partial_ref[me ^ (2 * i)]
            send_left_ref[i, :, columns] = partial_ref[me ^ (2 * i + 1)].astype(BF16)

    @pl.loop(0, half // wide)
    def _(n):
        columns = pl.ds(pl.multiple_of(n * wide, 128), wide)
        multiply(pl.ds(pl.multiple_of(half + n * wide, 128), wide))
        for i in range(2):
            keep_right_ref[i, :, columns] = partial_ref[me ^ i]
            send_right_ref[i, :, columns] = partial_ref[me ^ (i + 2)].astype(BF16)


def fold_kernel(keep_ref, got_ref, *refs):
    own_ref, send_ref = refs[-2:]
    own_ref[...] = keep_ref[0] + got_ref[0].astype(F32)
    send_ref[...] = (keep_ref[1] + got_ref[1].astype(F32)).astype(BF16)


def side_kernel(left_ref, got_left_ref, right_ref, got_right_ref, own_ref, send_ref):
    half = left_ref.shape[1]
    for i, (ref, got_ref) in enumerate(((left_ref, got_left_ref), (right_ref, got_right_ref))):
        total = ref[...] + got_ref[...].astype(F32)
        own_ref[:, i * half : (i + 1) * half] = total
        send_ref[:, i * half : (i + 1) * half] = total.astype(BF16)


def add_kernel(own_ref, got_ref, out_ref, send_ref):
    total = own_ref[...] + got_ref[...].astype(F32)
    out_ref[...] = total
    send_ref[...] = total.astype(BF16)


def fetch_kernel(start, source_ref, gate_ref, out_ref, sems):
    copies = carried(source_ref, start, out_ref, sems)
    for copy in copies:
        copy.start()
    for copy in copies:
        copy.wait()


def norm_kernel(residual_ref, gain_ref, gate_ref, own_ref, got_ref, *out_refs):
    hidden = residual_ref[lax.axis_index("tensor") % 4].astype(F32)
    hidden = hidden + (own_ref[...] + got_ref[...].astype(F32))
    squares = jnp.mean(hidden * hidden, axis=-1, keepdims=True)
    normed = (hidden * lax.rsqrt(squares + 1e-06) * gain_ref[...].astype(F32)).astype(BF16)
    start = 0
    for ref in out_refs:
        width = ref.shape[2]
        ref[0] = normed[:, start : start + width]
        start += width


def place_tokens(x_ref, start, places, left_ref, right_ref):
    block, width = left_ref.shape[1:]
    for side, ref in enumerate((left_ref, right_ref)):
        for i, place in enumerate(places):
            row = (side * len(places) + i) * block
            x_ref[row : row + block, start : start + width] = ref[place]


def tokens_dot(x_ref, start, weight):
    x = x_ref[:, start : start + weight.shape[0]]
    return jnp.dot(x, weight, preferred_element_type=F32)


def first_kernel(
    narrow, places, left_ref, right_ref, weight_ref, source_ref, out_ref, last_ref, x_ref, sems
):
    copies = carried(source_ref, source_ref.shape[0] - last_ref.shape[0], last_ref, sems)
    for copy in copies:
        copy.start()
    place_tokens(x_ref, 0, places, left_ref, right_ref)

    @pl.loop(0, weight_ref.shape[1] // narrow)
    def _(n):
        columns = pl.ds(n * narrow if narrow % 128 else pl.multiple_of(n * narrow, 128), narrow)
        out_ref[:, columns] = tokens_dot(x_ref, 0, weight_ref[:, columns])

    for copy in copies:
        copy.wait()


def logits_kernel(
    spots,
    tensor_size,
    orders,
    sum_in_ref,
    left_ref,
    right_ref,
    next_left_ref,
    next_right_ref,
    target_ref,
    *refs,
):
    weight_ref, last_ref, source_ref, out_ref, x_ref, near_ref, sems, wanted_ref = refs
    rows = x_ref.shape[0]
    width = left_ref.shape[2]
    copies = carried(source_ref, source_ref.shape[0] - last_ref.shape[0] - near_ref.shape[0], near_ref, sems)
    for copy in copies:
        copy.start()
    place_tokens(x_ref, 0, orders[0], left_ref, right_ref)
    place_tokens(x_ref, width, orders[1], next_left_ref, next_right_ref)
    share = target_ref.shape[1]
    group, tensor = lax.axis_index("group"), lax.axis_index("tensor")
    vocab = sum_in_ref.shape[1]
    shares = tensor_size // 4
    places = [
        (group ^ g) * tensor_size + shares * ((tensor % 4) ^ d) + i for g, d in spots for i in range(shares)
    ]
    for i, place in enumerate(places):
        wanted_ref[i * share : (i + 1) * share] = target_ref[place]
    wanted = wanted_ref[...] - (group * tensor_size + tensor) * vocab
    wanted_ref[...] = jnp.where((wanted >= 0) & (wanted < vocab), wanted, -1)
    logits = sum_in_ref[...] + tokens_dot(x_ref, 0, weight_ref[...])
    logits = logits + tokens_dot(x_ref, width, last_ref[...])
    for copy in copies:
        copy.wait()
    logits = logits + tokens_dot(x_ref, width - near_ref.shape[0], near_ref[...])
    parts = [logits[:, c : c + 128] for c in range(0, vocab, 128)]
    if vocab % 128:
        spare = jnp.full((rows, 128 - vocab % 128), NEG, F32)
        parts[-1] = jnp.concatenate([parts[-1], spare], axis=1)
    lane = lax.broadcasted_iota(jnp.int32, (rows, 128), 1)
    target = wanted_ref[...]
    higher = functools.reduce(jnp.maximum, parts)
    total = jnp.zeros((rows, 128), F32)
    picked = jnp.zeros((rows, 128), F32)
    for c, part in enumerate(parts):
        total = total + jnp.exp(part - higher)
        picked = picked + jnp.where(lane + c * 128 == target, part, 0.0)
    peak = jnp.max(higher, axis=1, keepdims=True)
    sums = jnp.sum(total * jnp.exp(higher - peak), axis=1, keepdims=True)
    pick = jnp.sum(picked, axis=1, keepdims=True)
    row = lax.broadcasted_iota(jnp.int32, (rows, 128), 0)
    lane = lax.broadcasted_iota(jnp.int32, (rows, 128), 1)
    three = jnp.where(lane // share == 0, peak, jnp.where(lane // share == 1, sums, pick))
    three = jnp.where((row - lane) % share == 0, three, 0.0)
    for i, place in enumerate(places):
        out_ref[place] = jnp.sum(three[i * share : (i + 1) * share], axis=0, keepdims=True)


def final_kernel(share, live_ref, stats_ref, out_ref):
    stats = stats_ref[...].reshape(stats_ref.shape[0], 128)
    peak = jnp.max(stats, axis=0, keepdims=True)
    sums = pltpu.roll(stats, 128 - share, 1)
    picks = pltpu.roll(stats, 128 - 2 * share, 1)
    total = jnp.sum(sums * jnp.exp(stats - peak), axis=0, keepdims=True)
    values = jnp.sum(picks, axis=0, keepdims=True) - peak - jnp.log(total)
    out_ref[...] = jnp.where(live_ref[:1] > 0.0, values, 0.0)[0, :share]


def local(
    group_size,
    tensor_size,
    resp_query,
    resp_key,
    resp_value,
    prompt_keys,
    prompt_values,
    prompt_of,
    lengths,
    residual,
    out_weight,
    norm_gain,
    lm_weight,
    targets,
):
    rows, span = resp_query.shape
    heads = span // HEAD_DIM
    seq = rows // prompt_of.shape[0]
    key_rows = prompt_keys.shape[0]
    assert PLEN % key_rows == 0
    share = rows // tensor_size
    depth = out_weight.shape[1]
    vocab = lm_weight.shape[1]
    i32 = jnp.int32

    wanted = targets.reshape(-1, share, 1)
    above = list(range(2, group_size, 2))
    distances = list(range(group_size - 1, 0, -1))
    far_queries = [swap(resp_query, "group", a, group_size) for a in above]
    queries = {1: swap(resp_query, "group", 1, group_size)}
    far_queries = pl.pallas_call(
        functools.partial(pass_kernel, len(above)),
        out_shape=[jax.ShapeDtypeStruct(x.shape, x.dtype) for x in far_queries],
        in_specs=[vmem()] * len(above) + [anywhere()],
        out_specs=[vmem()] * len(above),
        compiler_params=params(1),
        name="pass",
    )(*map(held, far_queries), wanted)
    for a, x in zip(above, far_queries):
        queries[a] = x
        queries[a + 1] = swap(x, "group", 1, group_size)
    queries = [queries[d] for d in distances]
    inputs = (resp_query, resp_key, resp_value, prompt_keys, prompt_values)
    loaded = pl.pallas_call(
        functools.partial(load_kernel, len(inputs)),
        out_shape=[pltpu.VMEM(x.shape, x.dtype) for x in inputs],
        in_specs=[anywhere()] * (1 + len(inputs)),
        out_specs=[vmem()] * len(inputs),
        scratch_shapes=[pltpu.SemaphoreType.DMA((len(inputs),))],
        compiler_params=params(1),
        cost_estimate=cost(moved=2 * MIB),
        name="load",
    )(far_queries[0], *map(stored, inputs))
    query, own_keys, own_values, keys, values = map(held, loaded)
    answers = pl.pallas_call(
        functools.partial(prefix_kernel, heads, len(distances)),
        out_shape=[jax.ShapeDtypeStruct((rows, span + 128), BF16)] * len(distances),
        in_specs=[vmem()] * (len(distances) + 2),
        out_specs=[vmem()] * len(distances),
        compiler_params=params(8),
        name="prefix_attention",
    )(*map(held, queries), keys, values)
    got = [swap(x, "group", d, group_size) for x, d in zip(answers, distances)]
    own, live, weight = pl.pallas_call(
        functools.partial(own_kernel, heads, seq, share),
        out_shape=[
            jax.ShapeDtypeStruct((rows, span + 128), F32),
            jax.ShapeDtypeStruct((8, 128), F32),
            pltpu.VMEM(out_weight.shape, BF16),
        ],
        in_specs=[smem()] * 2 + [vmem()] * 5 + [anywhere()] * 2,
        out_specs=[vmem()] * 3,
        scratch_shapes=[pltpu.SemaphoreType.DMA((4,))],
        compiler_params=params(6),
        cost_estimate=cost(moved=8 * MIB),
        name="own_attention",
    )(
        stored(lengths),
        stored(prompt_of),
        query,
        own_keys,
        own_values,
        keys,
        values,
        stored(out_weight),
        answers[0],
    )

    def fetch(source, start, count, gate):
        return held(
            pl.pallas_call(
                functools.partial(fetch_kernel, start),
                out_shape=pltpu.VMEM((count, source.shape[1]), BF16),
                in_specs=[anywhere()] * 2,
                out_specs=vmem(),
                scratch_shapes=[pltpu.SemaphoreType.DMA((4,))],
                compiler_params=params(1),
                cost_estimate=cost(moved=count * source.shape[1] * 2),
                name="fetch",
            )(stored(source), gate)
        )

    half = depth // 2
    wide = 1280 if half % 1280 == 0 else half
    block = rows // 4
    send_left, keep_left, send_right, keep_right = pl.pallas_call(
        functools.partial(project_kernel, heads, seq, wide, group_size, key_rows),
        out_shape=[
            jax.ShapeDtypeStruct((2, block, half), BF16),
            jax.ShapeDtypeStruct((2, block, half), F32),
        ]
        * 2,
        in_specs=[smem()] + [vmem()] * (2 + len(distances)),
        out_specs=[vmem()] * 4,
        scratch_shapes=[
            pltpu.VMEM((rows, span), BF16),
            pltpu.VMEM((4, block, wide), F32),
        ],
        compiler_params=params(6),
        name="project",
    )(stored(prompt_of), *map(held, (own, *got)), held(weight))

    def add(kernel, name, size, *operands, gates=()):
        return pl.pallas_call(
            kernel,
            out_shape=[jax.ShapeDtypeStruct(size, F32), jax.ShapeDtypeStruct(size, BF16)],
            in_specs=[vmem()] * len(operands) + [anywhere()] * len(gates),
            out_specs=[vmem()] * 2,
            compiler_params=params(2),
            name=name,
        )(*map(held, operands), *gates)

    unit = depth // 20
    widths = [7 * unit, 7 * unit, 6 * unit]
    second_rows = 4 * unit
    second_weight = fetch(lm_weight, widths[0], second_rows, send_left)

    got_left = swap(send_left, "tensor", 1, tensor_size)
    got_right = swap(send_right, "tensor", 2, tensor_size)
    left, send_left = add(fold_kernel, "fold_left", (block, half), keep_left, got_left, gates=(second_weight,))
    right, send_right = add(fold_kernel, "fold_right", (block, half), keep_right, got_right)
    got_left = swap(send_left, "tensor", 2, tensor_size)
    got_right = swap(send_right, "tensor", 1, tensor_size)
    total, send = add(side_kernel, "side", (block, depth), left, got_left, right, got_right)
    first_weight = fetch(lm_weight, 0, widths[0], send)
    far = 4
    while 2 * far < tensor_size:
        total, send = add(
            add_kernel, "add", (block, depth), total, swap(send, "tensor", far, tensor_size)
        )
        far = 2 * far
    normed = pl.pallas_call(
        norm_kernel,
        out_shape=[jax.ShapeDtypeStruct((1, block, width), BF16) for width in widths],
        in_specs=[vmem()] * 2 + [anywhere()] + [vmem()] * 2,
        out_specs=[vmem()] * len(widths),
        compiler_params=params(4),
        name="norm",
    )(
        *map(held, (residual.reshape(4, block, depth), norm_gain[None])),
        first_weight,
        *map(held, (total, swap(send, "tensor", far, tensor_size))),
    )

    axes = {
        "x": [("tensor", 1)],
        "z": [("tensor", 2)],
        "y": [("group", d) for d in above],
    }
    arrays, labels = list(normed), [[(0, 0)] for _ in normed]
    for stage in range(3):
        for n, route in enumerate(("zxy", "xyz", "yzx")):
            x, steps = arrays[n], axes[route[stage]]
            got = [
                swap(x, axis, d, group_size if axis == "group" else tensor_size) for axis, d in steps
            ]
            labels[n] = labels[n] + [
                (g + d, t) if axis == "group" else (g, t + d) for axis, d in steps for g, t in labels[n]
            ]
            arrays[n] = (x, got) if stage == 2 else jnp.concatenate([x] + got)
    arrays = [jnp.concatenate([x] + got) for x, got in arrays]
    others = [swap(x, "group", 1, group_size) for x in arrays]
    spots = [(g + c, t) for c in (0, 1) for g, t in labels[0]]
    orders = [tuple(order.index(label) for label in labels[0]) for order in labels]
    total_rows = len(spots) * block
    narrow = 1536 if vocab % 1536 == 0 else vocab
    limit = 10 if total_rows <= 256 else 24
    first, last = pl.pallas_call(
        functools.partial(first_kernel, narrow, orders[0]),
        out_shape=[pltpu.VMEM((total_rows, vocab), F32), pltpu.VMEM((widths[2], vocab), BF16)],
        in_specs=[vmem()] * 3 + [anywhere()],
        out_specs=[vmem()] * 2,
        scratch_shapes=[
            pltpu.VMEM((total_rows, widths[0]), BF16),
            pltpu.SemaphoreType.DMA((4,)),
        ],
        compiler_params=params(limit),
        cost_estimate=cost(flops=2 * total_rows * widths[0] * vocab),
        name="logits_first",
    )(*map(held, (arrays[0], others[0], first_weight)), stored(lm_weight))
    stats = pl.pallas_call(
        functools.partial(logits_kernel, spots, tensor_size, orders[1:]),
        out_shape=jax.ShapeDtypeStruct((group_size * tensor_size, 1, 128), F32),
        in_specs=[vmem()] * 8 + [anywhere()],
        out_specs=vmem(),
        scratch_shapes=[
            pltpu.VMEM((total_rows, widths[1] + widths[2]), BF16),
            pltpu.VMEM((widths[1] - second_rows, vocab), BF16),
            pltpu.SemaphoreType.DMA((4,)),
            pltpu.VMEM((total_rows, 1), i32),
        ],
        compiler_params=params(limit + 6),
        cost_estimate=cost(flops=2 * total_rows * (widths[1] + widths[2]) * vocab),
        name="logits",
    )(
        *map(held, (first, arrays[1], others[1], arrays[2], others[2])),
        wanted,
        *map(held, (second_weight, last)),
        stored(lm_weight),
    )

    stats = lax.all_to_all(stats, ("group", "tensor"), 0, 0, tiled=True)
    return pl.pallas_call(
        functools.partial(final_kernel, share),
        out_shape=jax.ShapeDtypeStruct((share,), F32),
        in_specs=[vmem()] * 2,
        out_specs=vmem(),
        compiler_params=params(4),
        name="final",
    )(held(live), held(stats))


def solution(mesh):
    return jax.shard_map(
        functools.partial(local, mesh.shape["group"], mesh.shape["tensor"]),
        mesh=mesh,
        in_specs=(
            P("group", "tensor"),
            P("group", "tensor"),
            P("group", "tensor"),
            P("group", "tensor"),
            P("group", "tensor"),
            P("group"),
            P("group"),
            P("group", None),
            P("tensor", None),
            P(),
            P(None, ("group", "tensor")),
            P(),
        ),
        out_specs=P(("group", "tensor")),
        check_vma=False,
    )
```

```python
import functools

import jax
import jax.numpy as jnp
from jax import lax
from jax.experimental import pallas as pl
from jax.experimental.pallas import tpu as pltpu
from jax.sharding import PartitionSpec as P

HEAD_DIM = 128
PLEN = 512
NEG = -1e30
BF16 = jnp.bfloat16
F32 = jnp.float32
MIB = 1024 * 1024


def params(mib):
    return pltpu.CompilerParams(vmem_limit_bytes=mib * MIB)


def held(x):
    return pltpu.with_memory_space_constraint(x, pltpu.VMEM)


def stored(x):
    return pltpu.with_memory_space_constraint(x, pltpu.HBM)


def anywhere():
    return pl.BlockSpec(memory_space=pl.ANY)


def cost(flops=0, moved=0):
    return pl.CostEstimate(flops=flops, bytes_accessed=moved, transcendentals=0)


def vmem():
    return pl.BlockSpec(memory_space=pltpu.VMEM)


def smem():
    return pl.BlockSpec(memory_space=pltpu.SMEM)


def swap(x, axis, distance, size):
    return lax.ppermute(x, axis, [(i, i ^ distance) for i in range(size)])


def attend(jobs):
    factor = HEAD_DIM**-0.5
    scores = [
        lax.dot_general(q, k, (((1,), (1,)), ((), ())), preferred_element_type=F32)
        for q, k, _, _ in jobs
    ]
    scores = [
        s if job[3] is None else jnp.where(job[3], s, NEG) for s, job in zip(scores, jobs)
    ]
    peaks = [jnp.max(s, axis=1, keepdims=True) for s in scores]
    weights = [jnp.exp((s - peak) * factor) for s, peak in zip(scores, peaks)]
    weights = [
        w if job[3] is None else jnp.where(job[3], w, 0.0) for w, job in zip(weights, jobs)
    ]
    weights = [w.astype(BF16) for w in weights]
    totals = [jnp.sum(w.astype(F32), axis=1, keepdims=True) for w in weights]
    mixed = [
        jnp.dot(w, job[2], preferred_element_type=F32) for w, job in zip(weights, jobs)
    ]
    return [
        (m / total, peak * factor + jnp.log(total))
        for m, total, peak in zip(mixed, totals, peaks)
    ]


def pack_logs(logs, rows):
    lane = lax.broadcasted_iota(jnp.int32, (rows, 128), 1)
    packed = jnp.zeros((rows, 128), F32)
    for head, log in enumerate(logs):
        first = log.astype(BF16).astype(F32)
        second = (log - first).astype(BF16).astype(F32)
        third = log - first - second
        for part, value in enumerate((first, second, third)):
            packed = jnp.where(lane == 3 * head + part, value, packed)
    return packed.astype(BF16)


def pass_kernel(count, *refs):
    for ref, out_ref in zip(refs, refs[-count:]):
        out_ref[...] = ref[...]


def load_kernel(count, gate_ref, *refs):
    sems = refs[2 * count]
    copies = [
        pltpu.make_async_copy(refs[i], refs[count + i], sems.at[i]) for i in range(count)
    ]
    for copy in copies:
        copy.start()
    for copy in copies:
        copy.wait()


def carried(source_ref, start, out_ref, sems):
    count = sems.shape[0]
    rows = out_ref.shape[0] // count
    return [
        pltpu.make_async_copy(
            source_ref.at[pl.ds(start + i * rows, rows)], out_ref.at[pl.ds(i * rows, rows)], sems.at[i]
        )
        for i in range(count)
    ]


def column_copies(source_ref, start, out_ref, sems):
    count = sems.shape[0]
    width = out_ref.shape[1] // count
    return [
        pltpu.make_async_copy(
            source_ref.at[:, pl.ds(start + i * width, width)],
            out_ref.at[:, pl.ds(i * width, width)],
            sems.at[i],
        )
        for i in range(count)
    ]


def own_kernel(
    heads,
    seq,
    share,
    lengths_ref,
    prompt_ref,
    q_ref,
    rk_ref,
    rv_ref,
    k_ref,
    v_ref,
    source_ref,
    gate_ref,
    own_ref,
    live_ref,
    weight_ref,
    sems,
):
    copies = column_copies(source_ref, 0, weight_ref, sems)
    for copy in copies:
        copy.start()
    rows = q_ref.shape[0]
    row = lax.broadcasted_iota(jnp.int32, (rows, rows), 0)
    col = lax.broadcasted_iota(jnp.int32, (rows, rows), 1)
    live = jnp.zeros((rows, rows), jnp.int32)
    for r in range(rows // seq):
        live = jnp.where(col // seq == r, lengths_ref[r], live)
    allowed = (row // seq == col // seq) & (col <= row) & (col % seq < live)
    parts = [slice(h * HEAD_DIM, (h + 1) * HEAD_DIM) for h in range(heads)]
    found = attend(
        [(q_ref[:, p], rk_ref[:, p], rv_ref[:, p], allowed) for p in parts]
        + [(q_ref[:, p], k_ref[:, p], v_ref[:, p], None) for p in parts]
    )
    here = wanted_prompts(seq, rows, prompt_ref) == lax.axis_index("group") * k_ref.shape[0] // PLEN
    lane = lax.broadcasted_iota(jnp.int32, (rows, 128), 1)
    packed = jnp.zeros((rows, 128), F32)
    for h, p in enumerate(parts):
        (first, log), (second, other) = found[h], found[heads + h]
        other = jnp.where(here, other, NEG)
        peak = jnp.maximum(log, other)
        left, right = jnp.exp(log - peak), jnp.exp(other - peak)
        own_ref[:, p] = (first * left + second * right) / (left + right)
        packed = jnp.where(lane == h, peak + jnp.log(left + right), packed)
    own_ref[:, heads * HEAD_DIM :] = packed
    token = lax.broadcasted_iota(jnp.int32, live_ref.shape, 1) + lax.axis_index("tensor") * share
    length = jnp.zeros(live_ref.shape, jnp.int32)
    for r in range(rows // seq):
        length = jnp.where(token // seq == r, lengths_ref[r], length)
    live_ref[...] = jnp.where(token % seq < length, 1.0, 0.0)
    for copy in copies:
        copy.wait()


def wanted_prompts(seq, rows, prompt_ref):
    row = lax.broadcasted_iota(jnp.int32, (rows, 1), 0)
    wanted = jnp.zeros((rows, 1), jnp.int32)
    for r in range(rows // seq):
        wanted = jnp.where(row // seq == r, prompt_ref[r], wanted)
    return wanted


def prefix_kernel(heads, count, *refs):
    q_refs, (k_ref, v_ref), out_refs = refs[:count], refs[count : count + 2], refs[count + 2 :]
    rows = q_refs[0].shape[0]
    parts = [slice(h * HEAD_DIM, (h + 1) * HEAD_DIM) for h in range(heads)]
    found = attend(
        [
            (jnp.concatenate([ref[:, p] for ref in q_refs], axis=0), k_ref[:, p], v_ref[:, p], None)
            for p in parts
        ]
    )
    for i in range(count):
        rung = slice(i * rows, (i + 1) * rows)
        for h, p in enumerate(parts):
            out_refs[i][:, p] = found[h][0][rung].astype(BF16)
        out_refs[i][:, heads * HEAD_DIM :] = pack_logs([log[rung] for _, log in found], rows)


def project_kernel(heads, seq, wide, group_size, key_rows, prompt_ref, own_ref, *refs):
    got_refs, refs = refs[: group_size - 1], refs[group_size - 1 :]
    weight_ref, source_ref, send_left_ref, keep_left_ref, send_right_ref, keep_right_ref = refs[:6]
    attended_ref, partial_ref, near_ref, sems = refs[6:]
    copies = column_copies(source_ref, near_ref.shape[1], near_ref, sems)
    for copy in copies:
        copy.start()
    rows = own_ref.shape[0]
    wanted = wanted_prompts(seq, rows, prompt_ref)
    group = lax.axis_index("group")
    holders = [(group ^ d) * key_rows // PLEN for d in range(group_size - 1, 0, -1)]
    for h in range(heads):
        part = slice(h * HEAD_DIM, (h + 1) * HEAD_DIM)
        at = heads * HEAD_DIM
        logs = [own_ref[:, at + h : at + h + 1]]
        values = [own_ref[:, part]]
        for holder, ref in zip(holders, got_refs):
            three = ref[:, at : at + 128].astype(F32)
            log = (
                three[:, 3 * h : 3 * h + 1]
                + three[:, 3 * h + 1 : 3 * h + 2]
                + three[:, 3 * h + 2 : 3 * h + 3]
            )
            logs.append(jnp.where(wanted == holder, log, NEG))
            values.append(ref[:, part].astype(F32))
        peak = functools.reduce(jnp.maximum, logs)
        loads = [jnp.exp(log - peak) for log in logs]
        total = functools.reduce(jnp.add, loads)
        mixed = functools.reduce(jnp.add, [w * v for w, v in zip(loads, values)])
        attended_ref[:, part] = (mixed / total).astype(BF16)

    me = lax.axis_index("tensor") % 4
    block = rows // 4
    half = send_left_ref.shape[2]

    def multiply(ref, columns):
        partial = jnp.dot(attended_ref[...], ref[:, columns], preferred_element_type=F32)
        for b in range(4):
            partial_ref[b] = partial[b * block : (b + 1) * block]

    @pl.loop(0, half // wide)
    def _(n):
        columns = pl.ds(pl.multiple_of(n * wide, 128), wide)
        multiply(weight_ref, columns)
        for i in range(2):
            keep_left_ref[i, :, columns] = partial_ref[me ^ (2 * i)]
            send_left_ref[i, :, columns] = partial_ref[me ^ (2 * i + 1)].astype(BF16)

    for copy in copies:
        copy.wait()

    @pl.loop(0, half // wide)
    def _(n):
        columns = pl.ds(pl.multiple_of(n * wide, 128), wide)
        multiply(near_ref, columns)
        for i in range(2):
            keep_right_ref[i, :, columns] = partial_ref[me ^ i]
            send_right_ref[i, :, columns] = partial_ref[me ^ (i + 2)].astype(BF16)


def fold_kernel(keep_ref, got_ref, *refs):
    own_ref, send_ref = refs[-2:]
    own_ref[...] = keep_ref[0] + got_ref[0].astype(F32)
    send_ref[...] = (keep_ref[1] + got_ref[1].astype(F32)).astype(BF16)


def side_kernel(left_ref, got_left_ref, right_ref, got_right_ref, own_ref, send_ref):
    half = left_ref.shape[1]
    for i, (ref, got_ref) in enumerate(((left_ref, got_left_ref), (right_ref, got_right_ref))):
        total = ref[...] + got_ref[...].astype(F32)
        own_ref[:, i * half : (i + 1) * half] = total
        send_ref[:, i * half : (i + 1) * half] = total.astype(BF16)


def add_kernel(own_ref, got_ref, out_ref, send_ref):
    total = own_ref[...] + got_ref[...].astype(F32)
    out_ref[...] = total
    send_ref[...] = total.astype(BF16)


def fetch_kernel(start, source_ref, gate_ref, out_ref, sems):
    copies = carried(source_ref, start, out_ref, sems)
    for copy in copies:
        copy.start()
    for copy in copies:
        copy.wait()


def column_kernel(count, *refs):
    terms, out_refs = refs[:count], refs[-2:]
    width = out_refs[0].shape[2]
    for i, ref in enumerate(terms):
        for half, out_ref in enumerate(out_refs):
            out_ref[i] = ref[:, half * width : (half + 1) * width]


def norm_kernel(residual_ref, gain_ref, gate_ref, own_ref, got_ref, out_ref):
    hidden = residual_ref[lax.axis_index("tensor") % 4].astype(F32)
    hidden = hidden + (own_ref[...] + got_ref[...].astype(F32))
    squares = jnp.mean(hidden * hidden, axis=-1, keepdims=True)
    out_ref[...] = (hidden * lax.rsqrt(squares + 1e-06) * gain_ref[...].astype(F32)).astype(BF16)


def join_kernel(count, *refs):
    out_ref = refs[-1]
    start = 0
    for ref in refs[:count]:
        out_ref[start : start + ref.shape[0]] = ref[...]
        start += ref.shape[0]


def quarter_dots(x_ref, weight_refs, columns):
    start, total = 0, None
    for ref in weight_refs:
        stop = start + ref.shape[0]
        part = jnp.dot(x_ref[:, start:stop], ref[:, columns], preferred_element_type=F32)
        total = part if total is None else total + part
        start = stop
    return total


def first_kernel(
    narrow, left_ref, right_ref, weight_ref, next_ref, source_ref, out_ref, last_ref, x_ref, sems
):
    copies = carried(source_ref, source_ref.shape[0] - last_ref.shape[0], last_ref, sems)
    for copy in copies:
        copy.start()
    half = left_ref.shape[0]
    x_ref[:half] = left_ref[...]
    x_ref[half:] = right_ref[...]

    @pl.loop(0, weight_ref.shape[1] // narrow)
    def _(n):
        columns = pl.ds(n * narrow if narrow % 128 else pl.multiple_of(n * narrow, 128), narrow)
        out_ref[:, columns] = quarter_dots(x_ref, (weight_ref, next_ref), columns)

    for copy in copies:
        copy.wait()


def logits_kernel(
    narrow,
    spots,
    tensor_size,
    sum_in_ref,
    left_ref,
    right_ref,
    target_ref,
    weight_ref,
    next_ref,
    out_ref,
    x_ref,
    peak_ref,
    sum_ref,
    pick_ref,
    wanted_ref,
):
    half = left_ref.shape[0]
    rows = 2 * half
    share = target_ref.shape[1]
    group, tensor = lax.axis_index("group"), lax.axis_index("tensor")
    vocab = weight_ref.shape[1]
    shares = tensor_size // 4
    places = [
        (group ^ g) * tensor_size + shares * ((tensor % 4) ^ d) + i for g, d in spots for i in range(shares)
    ]
    for i, place in enumerate(places):
        wanted_ref[i * share : (i + 1) * share] = target_ref[place]
    wanted = wanted_ref[...] - (group * tensor_size + tensor) * vocab
    wanted_ref[...] = jnp.where((wanted >= 0) & (wanted < vocab), wanted, -1)
    x_ref[:half] = left_ref[...]
    x_ref[half:] = right_ref[...]
    peak_ref[...] = jnp.full_like(peak_ref, NEG)
    sum_ref[...] = jnp.zeros_like(sum_ref)
    pick_ref[...] = jnp.zeros_like(pick_ref)

    @pl.loop(0, weight_ref.shape[1] // narrow)
    def _(n):
        columns = pl.ds(n * narrow if narrow % 128 else pl.multiple_of(n * narrow, 128), narrow)
        logits = sum_in_ref[:, columns] + quarter_dots(x_ref, (weight_ref, next_ref), columns)
        parts = [logits[:, c : c + 128] for c in range(0, narrow, 128)]
        if narrow % 128:
            spare = jnp.full((rows, 128 - narrow % 128), NEG, F32)
            parts[-1] = jnp.concatenate([parts[-1], spare], axis=1)
        lane = lax.broadcasted_iota(jnp.int32, (rows, 128), 1) + n * narrow
        peak = peak_ref[...]
        higher = functools.reduce(jnp.maximum, parts, peak)
        total = sum_ref[...] * jnp.exp(peak - higher)
        picked = pick_ref[...]
        target = wanted_ref[...]
        for c, part in enumerate(parts):
            total = total + jnp.exp(part - higher)
            picked = picked + jnp.where(lane + c * 128 == target, part, 0.0)
        peak_ref[...] = higher
        sum_ref[...] = total
        pick_ref[...] = picked

    higher = peak_ref[...]
    peak = jnp.max(higher, axis=1, keepdims=True)
    sums = jnp.sum(sum_ref[...] * jnp.exp(higher - peak), axis=1, keepdims=True)
    pick = jnp.sum(pick_ref[...], axis=1, keepdims=True)
    row = lax.broadcasted_iota(jnp.int32, (rows, 128), 0)
    lane = lax.broadcasted_iota(jnp.int32, (rows, 128), 1)
    three = jnp.where(lane // share == 0, peak, jnp.where(lane // share == 1, sums, pick))
    three = jnp.where((row - lane) % share == 0, three, 0.0)
    for i, place in enumerate(places):
        out_ref[place] = jnp.sum(three[i * share : (i + 1) * share], axis=0, keepdims=True)


def final_kernel(share, live_ref, stats_ref, out_ref):
    stats = stats_ref[...].reshape(stats_ref.shape[0], 128)
    peak = jnp.max(stats, axis=0, keepdims=True)
    sums = pltpu.roll(stats, 128 - share, 1)
    picks = pltpu.roll(stats, 128 - 2 * share, 1)
    total = jnp.sum(sums * jnp.exp(stats - peak), axis=0, keepdims=True)
    values = jnp.sum(picks, axis=0, keepdims=True) - peak - jnp.log(total)
    out_ref[...] = jnp.where(live_ref[:1] > 0.0, values, 0.0)[0, :share]


def local(
    group_size,
    tensor_size,
    resp_query,
    resp_key,
    resp_value,
    prompt_keys,
    prompt_values,
    prompt_of,
    lengths,
    residual,
    out_weight,
    norm_gain,
    lm_weight,
    targets,
):
    rows, span = resp_query.shape
    heads = span // HEAD_DIM
    seq = rows // prompt_of.shape[0]
    key_rows = prompt_keys.shape[0]
    assert PLEN % key_rows == 0
    share = rows // tensor_size
    depth = out_weight.shape[1]
    vocab = lm_weight.shape[1]
    i32 = jnp.int32

    wanted = targets.reshape(-1, share, 1)
    above = list(range(2, group_size, 2))
    distances = list(range(group_size - 1, 0, -1))
    far_queries = [swap(resp_query, "group", a, group_size) for a in above]
    queries = {1: swap(resp_query, "group", 1, group_size)}
    inputs = (resp_query, resp_key, resp_value, prompt_keys, prompt_values)
    loaded = pl.pallas_call(
        functools.partial(load_kernel, len(inputs)),
        out_shape=[pltpu.VMEM(x.shape, x.dtype) for x in inputs],
        in_specs=[anywhere()] * (1 + len(inputs)),
        out_specs=[vmem()] * len(inputs),
        scratch_shapes=[pltpu.SemaphoreType.DMA((len(inputs),))],
        compiler_params=params(1),
        cost_estimate=cost(moved=2 * MIB),
        name="load",
    )(wanted, *map(stored, inputs))
    query, own_keys, own_values, keys, values = map(held, loaded)
    far_queries = pl.pallas_call(
        functools.partial(pass_kernel, len(above)),
        out_shape=[jax.ShapeDtypeStruct(x.shape, x.dtype) for x in far_queries],
        in_specs=[vmem()] * len(above) + [anywhere()],
        out_specs=[vmem()] * len(above),
        compiler_params=params(1),
        name="pass",
    )(*map(held, far_queries), loaded[0])
    for a, x in zip(above, far_queries):
        queries[a] = x
        queries[a + 1] = swap(x, "group", 1, group_size)
    queries = [queries[d] for d in distances]
    answers = pl.pallas_call(
        functools.partial(prefix_kernel, heads, len(distances)),
        out_shape=[jax.ShapeDtypeStruct((rows, span + 128), BF16)] * len(distances),
        in_specs=[vmem()] * (len(distances) + 2),
        out_specs=[vmem()] * len(distances),
        compiler_params=params(8),
        name="prefix_attention",
    )(*map(held, queries), keys, values)
    got = [swap(x, "group", d, group_size) for x, d in zip(answers, distances)]
    own, live, weight = pl.pallas_call(
        functools.partial(own_kernel, heads, seq, share),
        out_shape=[
            jax.ShapeDtypeStruct((rows, span + 128), F32),
            jax.ShapeDtypeStruct((8, 128), F32),
            pltpu.VMEM((span, depth // 2), BF16),
        ],
        in_specs=[smem()] * 2 + [vmem()] * 5 + [anywhere()] * 2,
        out_specs=[vmem()] * 3,
        scratch_shapes=[pltpu.SemaphoreType.DMA((2,))],
        compiler_params=params(6),
        cost_estimate=cost(moved=8 * MIB),
        name="own_attention",
    )(
        stored(lengths),
        stored(prompt_of),
        query,
        own_keys,
        own_values,
        keys,
        values,
        stored(out_weight),
        answers[0],
    )

    def fetch(source, start, count, gate):
        return held(
            pl.pallas_call(
                functools.partial(fetch_kernel, start),
                out_shape=pltpu.VMEM((count, source.shape[1]), BF16),
                in_specs=[anywhere()] * 2,
                out_specs=vmem(),
                scratch_shapes=[pltpu.SemaphoreType.DMA((4,))],
                compiler_params=params(1),
                cost_estimate=cost(moved=count * source.shape[1] * 2),
                name="fetch",
            )(stored(source), gate)
        )

    half = depth // 2
    quarter = depth // 4
    wide = 1280 if half % 1280 == 0 else half
    block = rows // 4
    send_left, keep_left, send_right, keep_right = pl.pallas_call(
        functools.partial(project_kernel, heads, seq, wide, group_size, key_rows),
        out_shape=[
            jax.ShapeDtypeStruct((2, block, half), BF16),
            jax.ShapeDtypeStruct((2, block, half), F32),
        ]
        * 2,
        in_specs=[smem()] + [vmem()] * (2 + len(distances)) + [anywhere()],
        out_specs=[vmem()] * 4,
        scratch_shapes=[
            pltpu.VMEM((rows, span), BF16),
            pltpu.VMEM((4, block, wide), F32),
            pltpu.VMEM((span, half), BF16),
            pltpu.SemaphoreType.DMA((2,)),
        ],
        compiler_params=params(8),
        name="project",
    )(stored(prompt_of), *map(held, (own, *got)), held(weight), stored(out_weight))

    def add(kernel, name, size, *operands, gates=()):
        return pl.pallas_call(
            kernel,
            out_shape=[jax.ShapeDtypeStruct(size, F32), jax.ShapeDtypeStruct(size, BF16)],
            in_specs=[vmem()] * len(operands) + [anywhere()] * len(gates),
            out_specs=[vmem()] * 2,
            compiler_params=params(2),
            name=name,
        )(*map(held, operands), *gates)

    early_rows = 1024 if half > 1024 else half // 2
    first_quarter = fetch(lm_weight, 0, early_rows, send_left)

    got_left = swap(send_left, "tensor", 1, tensor_size)
    got_right = swap(send_right, "tensor", 2, tensor_size)
    left, send_left = add(fold_kernel, "fold_left", (block, half), keep_left, got_left, gates=(first_quarter,))
    right, send_right = add(fold_kernel, "fold_right", (block, half), keep_right, got_right)
    got_left = swap(send_left, "tensor", 2, tensor_size)
    got_right = swap(send_right, "tensor", 1, tensor_size)
    total, send = add(side_kernel, "side", (block, depth), left, got_left, right, got_right)
    second_quarter = fetch(lm_weight, early_rows, half - early_rows, send)
    far = 4
    while 2 * far < tensor_size:
        total, send = add(
            add_kernel, "add", (block, depth), total, swap(send, "tensor", far, tensor_size)
        )
        far = 2 * far
    normed = pl.pallas_call(
        norm_kernel,
        out_shape=jax.ShapeDtypeStruct((block, depth), BF16),
        in_specs=[vmem()] * 2 + [anywhere()] + [vmem()] * 2,
        out_specs=vmem(),
        compiler_params=params(4),
        name="norm",
    )(
        *map(held, (residual.reshape(4, block, depth), norm_gain[None])),
        second_quarter,
        *map(held, (total, swap(send, "tensor", far, tensor_size))),
    )

    order = [0, 2]
    here = [(g, x) for g in [0] + above for x in (0, 1)]
    column = [normed, swap(normed, "tensor", 2, tensor_size)]
    columns = pl.pallas_call(
        functools.partial(column_kernel, len(column)),
        out_shape=[jax.ShapeDtypeStruct((len(column), block, half), BF16)] * 2,
        in_specs=[vmem()] * len(column),
        out_specs=[vmem()] * 2,
        compiler_params=params(2),
        name="column",
    )(*map(held, column))

    def join(pieces, gate):
        blocks = sum(x.shape[0] for x in pieces)
        return pl.pallas_call(
            functools.partial(join_kernel, len(pieces)),
            out_shape=jax.ShapeDtypeStruct((blocks, block, half), BF16),
            in_specs=[vmem()] * len(pieces) + [anywhere()],
            out_specs=vmem(),
            compiler_params=params(2),
            name="join",
        )(*map(held, pieces), gate)

    left, right = columns
    got_left = swap(left, "tensor", 1, tensor_size)
    right = [right] + [swap(right, "group", d, group_size) for d in above]
    left = jnp.concatenate([left, got_left])
    got_left = [swap(left, "group", d, group_size) for d in above]
    third = fetch(lm_weight, 2 * quarter, quarter, left)
    across = swap(jnp.concatenate(right), "tensor", 1, tensor_size)
    across = jnp.split(across, len(right))
    right = [x for pair in zip(right, across) for x in pair]
    halves = []
    for tokens in (join([left] + got_left, third), jnp.concatenate(right)):
        tokens = tokens.reshape(-1, half)
        halves.append((tokens, swap(tokens, "group", 1, group_size)))
    spots = [(g + c, t + x) for c in (0, 1) for g, x in here for t in order]
    total_rows = 2 * tokens.shape[0]
    narrow = 1536 if vocab % 1536 == 0 else vocab
    limit = 10 if total_rows <= 256 else 24
    work = 2 * total_rows * (half) * vocab
    first, last = pl.pallas_call(
        functools.partial(first_kernel, narrow),
        out_shape=[pltpu.VMEM((total_rows, vocab), F32), pltpu.VMEM((quarter, vocab), BF16)],
        in_specs=[vmem()] * 4 + [anywhere()],
        out_specs=[vmem()] * 2,
        scratch_shapes=[
            pltpu.VMEM((total_rows, half), BF16),
            pltpu.SemaphoreType.DMA((4,)),
        ],
        compiler_params=params(limit),
        cost_estimate=cost(flops=work),
        name="logits_first",
    )(*map(held, (*halves[0], first_quarter, second_quarter)), stored(lm_weight))
    stats = pl.pallas_call(
        functools.partial(logits_kernel, vocab, spots, tensor_size),
        out_shape=jax.ShapeDtypeStruct((group_size * tensor_size, 1, 128), F32),
        in_specs=[vmem()] * 6,
        out_specs=vmem(),
        scratch_shapes=[pltpu.VMEM((total_rows, half), BF16)]
        + [pltpu.VMEM((total_rows, 128), F32)] * 3
        + [pltpu.VMEM((total_rows, 1), i32)],
        compiler_params=params(limit),
        cost_estimate=cost(flops=work),
        name="logits",
    )(*map(held, (first, *halves[1])), wanted, held(third), held(last))

    stats = lax.all_to_all(stats, ("group", "tensor"), 0, 0, tiled=True)
    return pl.pallas_call(
        functools.partial(final_kernel, share),
        out_shape=jax.ShapeDtypeStruct((share,), F32),
        in_specs=[vmem()] * 2,
        out_specs=vmem(),
        compiler_params=params(4),
        name="final",
    )(held(live), held(stats))


def solution(mesh):
    return jax.shard_map(
        functools.partial(local, mesh.shape["group"], mesh.shape["tensor"]),
        mesh=mesh,
        in_specs=(
            P("group", "tensor"),
            P("group", "tensor"),
            P("group", "tensor"),
            P("group", "tensor"),
            P("group", "tensor"),
            P("group"),
            P("group"),
            P("group", None),
            P("tensor", None),
            P(),
            P(None, ("group", "tensor")),
            P(),
        ),
        out_specs=P(("group", "tensor")),
        check_vma=False,
    )
```

```python
import functools

import jax
import jax.numpy as jnp
from jax import lax
from jax.experimental import pallas as pl
from jax.experimental.pallas import tpu as pltpu
from jax.sharding import PartitionSpec as P

HEAD_DIM = 128
PLEN = 512
NEG = -1e30
BF16 = jnp.bfloat16
F32 = jnp.float32
MIB = 1024 * 1024


def params(mib):
    return pltpu.CompilerParams(vmem_limit_bytes=mib * MIB)


def held(x):
    return pltpu.with_memory_space_constraint(x, pltpu.VMEM)


def stored(x):
    return pltpu.with_memory_space_constraint(x, pltpu.HBM)


def anywhere():
    return pl.BlockSpec(memory_space=pl.ANY)


def cost(flops=0, moved=0):
    return pl.CostEstimate(flops=flops, bytes_accessed=moved, transcendentals=0)


def vmem():
    return pl.BlockSpec(memory_space=pltpu.VMEM)


def smem():
    return pl.BlockSpec(memory_space=pltpu.SMEM)


def swap(x, axis, distance, size):
    return lax.ppermute(x, axis, [(i, i ^ distance) for i in range(size)])


def attend(jobs):
    factor = HEAD_DIM**-0.5
    scores = [
        lax.dot_general(q, k, (((1,), (1,)), ((), ())), preferred_element_type=F32)
        for q, k, _, _ in jobs
    ]
    scores = [
        s if job[3] is None else jnp.where(job[3], s, NEG) for s, job in zip(scores, jobs)
    ]
    peaks = [jnp.max(s, axis=1, keepdims=True) for s in scores]
    weights = [jnp.exp((s - peak) * factor) for s, peak in zip(scores, peaks)]
    weights = [
        w if job[3] is None else jnp.where(job[3], w, 0.0) for w, job in zip(weights, jobs)
    ]
    weights = [w.astype(BF16) for w in weights]
    totals = [jnp.sum(w.astype(F32), axis=1, keepdims=True) for w in weights]
    mixed = [
        jnp.dot(w, job[2], preferred_element_type=F32) for w, job in zip(weights, jobs)
    ]
    return [
        (m / total, peak * factor + jnp.log(total))
        for m, total, peak in zip(mixed, totals, peaks)
    ]


def pack_logs(logs, rows):
    lane = lax.broadcasted_iota(jnp.int32, (rows, 128), 1)
    packed = jnp.zeros((rows, 128), F32)
    for head, log in enumerate(logs):
        first = log.astype(BF16).astype(F32)
        second = (log - first).astype(BF16).astype(F32)
        third = log - first - second
        for part, value in enumerate((first, second, third)):
            packed = jnp.where(lane == 3 * head + part, value, packed)
    return packed.astype(BF16)


def pass_kernel(count, *refs):
    for ref, out_ref in zip(refs, refs[-count:]):
        out_ref[...] = ref[...]


def load_kernel(count, gate_ref, *refs):
    sems = refs[2 * count]
    copies = [
        pltpu.make_async_copy(refs[i], refs[count + i], sems.at[i]) for i in range(count)
    ]
    for copy in copies:
        copy.start()
    for copy in copies:
        copy.wait()


def carried(source_ref, start, out_ref, sems):
    count = sems.shape[0]
    rows = out_ref.shape[0] // count
    return [
        pltpu.make_async_copy(
            source_ref.at[pl.ds(start + i * rows, rows)], out_ref.at[pl.ds(i * rows, rows)], sems.at[i]
        )
        for i in range(count)
    ]


def own_kernel(
    heads,
    seq,
    share,
    lengths_ref,
    prompt_ref,
    q_ref,
    rk_ref,
    rv_ref,
    k_ref,
    v_ref,
    source_ref,
    gate_ref,
    own_ref,
    live_ref,
    weight_ref,
    sems,
):
    copies = carried(source_ref, 0, weight_ref, sems)
    for copy in copies:
        copy.start()
    rows = q_ref.shape[0]
    row = lax.broadcasted_iota(jnp.int32, (rows, rows), 0)
    col = lax.broadcasted_iota(jnp.int32, (rows, rows), 1)
    live = jnp.zeros((rows, rows), jnp.int32)
    for r in range(rows // seq):
        live = jnp.where(col // seq == r, lengths_ref[r], live)
    allowed = (row // seq == col // seq) & (col <= row) & (col % seq < live)
    parts = [slice(h * HEAD_DIM, (h + 1) * HEAD_DIM) for h in range(heads)]
    found = attend(
        [(q_ref[:, p], rk_ref[:, p], rv_ref[:, p], allowed) for p in parts]
        + [(q_ref[:, p], k_ref[:, p], v_ref[:, p], None) for p in parts]
    )
    here = wanted_prompts(seq, rows, prompt_ref) == lax.axis_index("group") * k_ref.shape[0] // PLEN
    lane = lax.broadcasted_iota(jnp.int32, (rows, 128), 1)
    packed = jnp.zeros((rows, 128), F32)
    for h, p in enumerate(parts):
        (first, log), (second, other) = found[h], found[heads + h]
        other = jnp.where(here, other, NEG)
        peak = jnp.maximum(log, other)
        left, right = jnp.exp(log - peak), jnp.exp(other - peak)
        own_ref[:, p] = (first * left + second * right) / (left + right)
        packed = jnp.where(lane == h, peak + jnp.log(left + right), packed)
    own_ref[:, heads * HEAD_DIM :] = packed
    token = lax.broadcasted_iota(jnp.int32, live_ref.shape, 1) + lax.axis_index("tensor") * share
    length = jnp.zeros(live_ref.shape, jnp.int32)
    for r in range(rows // seq):
        length = jnp.where(token // seq == r, lengths_ref[r], length)
    live_ref[...] = jnp.where(token % seq < length, 1.0, 0.0)
    for copy in copies:
        copy.wait()


def wanted_prompts(seq, rows, prompt_ref):
    row = lax.broadcasted_iota(jnp.int32, (rows, 1), 0)
    wanted = jnp.zeros((rows, 1), jnp.int32)
    for r in range(rows // seq):
        wanted = jnp.where(row // seq == r, prompt_ref[r], wanted)
    return wanted


def prefix_kernel(heads, count, *refs):
    q_refs, (k_ref, v_ref), out_refs = refs[:count], refs[count : count + 2], refs[count + 2 :]
    rows = q_refs[0].shape[0]
    parts = [slice(h * HEAD_DIM, (h + 1) * HEAD_DIM) for h in range(heads)]
    found = attend(
        [
            (jnp.concatenate([ref[:, p] for ref in q_refs], axis=0), k_ref[:, p], v_ref[:, p], None)
            for p in parts
        ]
    )
    for i in range(count):
        rung = slice(i * rows, (i + 1) * rows)
        for h, p in enumerate(parts):
            out_refs[i][:, p] = found[h][0][rung].astype(BF16)
        out_refs[i][:, heads * HEAD_DIM :] = pack_logs([log[rung] for _, log in found], rows)


def project_kernel(heads, seq, wide, group_size, key_rows, prompt_ref, own_ref, *refs):
    got_refs, refs = refs[: group_size - 1], refs[group_size - 1 :]
    weight_ref, send_left_ref, keep_left_ref, send_right_ref, keep_right_ref = refs[:5]
    attended_ref, partial_ref = refs[5:]
    rows = own_ref.shape[0]
    wanted = wanted_prompts(seq, rows, prompt_ref)
    group = lax.axis_index("group")
    holders = [(group ^ d) * key_rows // PLEN for d in range(group_size - 1, 0, -1)]
    for h in range(heads):
        part = slice(h * HEAD_DIM, (h + 1) * HEAD_DIM)
        at = heads * HEAD_DIM
        logs = [own_ref[:, at + h : at + h + 1]]
        values = [own_ref[:, part]]
        for holder, ref in zip(holders, got_refs):
            three = ref[:, at : at + 128].astype(F32)
            log = (
                three[:, 3 * h : 3 * h + 1]
                + three[:, 3 * h + 1 : 3 * h + 2]
                + three[:, 3 * h + 2 : 3 * h + 3]
            )
            logs.append(jnp.where(wanted == holder, log, NEG))
            values.append(ref[:, part].astype(F32))
        peak = functools.reduce(jnp.maximum, logs)
        loads = [jnp.exp(log - peak) for log in logs]
        total = functools.reduce(jnp.add, loads)
        mixed = functools.reduce(jnp.add, [w * v for w, v in zip(loads, values)])
        attended_ref[:, part] = (mixed / total).astype(BF16)

    me = lax.axis_index("tensor") % 4
    block = rows // 4
    half = send_left_ref.shape[2]

    def multiply(columns):
        partial = jnp.dot(attended_ref[...], weight_ref[:, columns], preferred_element_type=F32)
        for b in range(4):
            partial_ref[b] = partial[b * block : (b + 1) * block]

    @pl.loop(0, half // wide)
    def _(n):
        columns = pl.ds(pl.multiple_of(n * wide, 128), wide)
        multiply(columns)
        for i in range(2):
            keep_left_ref[i, :, columns] = partial_ref[me ^ (2 * i)]
            send_left_ref[i, :, columns] = partial_ref[me ^ (2 * i + 1)].astype(BF16)

    @pl.loop(0, half // wide)
    def _(n):
        columns = pl.ds(pl.multiple_of(n * wide, 128), wide)
        multiply(pl.ds(pl.multiple_of(half + n * wide, 128), wide))
        for i in range(2):
            keep_right_ref[i, :, columns] = partial_ref[me ^ i]
            send_right_ref[i, :, columns] = partial_ref[me ^ (i + 2)].astype(BF16)


def fold_kernel(keep_ref, got_ref, own_ref, send_ref):
    own_ref[...] = keep_ref[0] + got_ref[0].astype(F32)
    send_ref[...] = (keep_ref[1] + got_ref[1].astype(F32)).astype(BF16)


def side_kernel(left_ref, got_left_ref, right_ref, got_right_ref, own_ref, send_ref):
    half = left_ref.shape[1]
    for i, (ref, got_ref) in enumerate(((left_ref, got_left_ref), (right_ref, got_right_ref))):
        total = ref[...] + got_ref[...].astype(F32)
        own_ref[:, i * half : (i + 1) * half] = total
        send_ref[:, i * half : (i + 1) * half] = total.astype(BF16)


def add_kernel(own_ref, got_ref, out_ref, send_ref):
    total = own_ref[...] + got_ref[...].astype(F32)
    out_ref[...] = total
    send_ref[...] = total.astype(BF16)


def fetch_kernel(start, source_ref, gate_ref, out_ref, sems):
    copies = carried(source_ref, start, out_ref, sems)
    for copy in copies:
        copy.start()
    for copy in copies:
        copy.wait()


def column_kernel(count, *refs):
    terms, out_refs = refs[:count], refs[-2:]
    width = out_refs[0].shape[2]
    for i, ref in enumerate(terms):
        for half, out_ref in enumerate(out_refs):
            out_ref[i] = ref[:, half * width : (half + 1) * width]


def norm_kernel(residual_ref, gain_ref, first_gate_ref, second_gate_ref, own_ref, got_ref, out_ref):
    hidden = residual_ref[lax.axis_index("tensor") % 4].astype(F32)
    hidden = hidden + (own_ref[...] + got_ref[...].astype(F32))
    squares = jnp.mean(hidden * hidden, axis=-1, keepdims=True)
    out_ref[...] = (hidden * lax.rsqrt(squares + 1e-06) * gain_ref[...].astype(F32)).astype(BF16)


def join_kernel(count, *refs):
    out_ref = refs[-1]
    start = 0
    for ref in refs[:count]:
        out_ref[start : start + ref.shape[0]] = ref[...]
        start += ref.shape[0]


def quarter_dots(x_ref, weight_refs, columns):
    depth = weight_refs[0].shape[0]
    return functools.reduce(
        jnp.add,
        [
            jnp.dot(x_ref[:, i * depth : (i + 1) * depth], ref[:, columns], preferred_element_type=F32)
            for i, ref in enumerate(weight_refs)
        ],
    )


def first_kernel(
    narrow, left_ref, right_ref, weight_ref, next_ref, source_ref, out_ref, last_ref, x_ref, sems
):
    copies = carried(source_ref, source_ref.shape[0] - last_ref.shape[0], last_ref, sems)
    for copy in copies:
        copy.start()
    half = left_ref.shape[0]
    x_ref[:half] = left_ref[...]
    x_ref[half:] = right_ref[...]

    @pl.loop(0, weight_ref.shape[1] // narrow)
    def _(n):
        columns = pl.ds(n * narrow if narrow % 128 else pl.multiple_of(n * narrow, 128), narrow)
        out_ref[:, columns] = quarter_dots(x_ref, (weight_ref, next_ref), columns)

    for copy in copies:
        copy.wait()


def logits_kernel(
    narrow,
    spots,
    tensor_size,
    sum_in_ref,
    left_ref,
    right_ref,
    target_ref,
    weight_ref,
    next_ref,
    out_ref,
    other_ref,
    x_ref,
    peak_ref,
    sum_ref,
    pick_ref,
    wanted_ref,
):
    half = left_ref.shape[0]
    rows = 2 * half
    share = target_ref.shape[1]
    group, tensor = lax.axis_index("group"), lax.axis_index("tensor")
    vocab = weight_ref.shape[1]
    shares = tensor_size // 4
    places = [
        (group ^ g) * tensor_size + shares * ((tensor % 4) ^ d) + i for g, d in spots for i in range(shares)
    ]
    for i, place in enumerate(places):
        wanted_ref[i * share : (i + 1) * share] = target_ref[place]
    wanted = wanted_ref[...] - (group * tensor_size + tensor) * vocab
    wanted_ref[...] = jnp.where((wanted >= 0) & (wanted < vocab), wanted, -1)
    x_ref[:half] = left_ref[...]
    x_ref[half:] = right_ref[...]
    peak_ref[...] = jnp.full_like(peak_ref, NEG)
    sum_ref[...] = jnp.zeros_like(sum_ref)
    pick_ref[...] = jnp.zeros_like(pick_ref)

    @pl.loop(0, weight_ref.shape[1] // narrow)
    def _(n):
        columns = pl.ds(n * narrow if narrow % 128 else pl.multiple_of(n * narrow, 128), narrow)
        logits = sum_in_ref[:, columns] + quarter_dots(x_ref, (weight_ref, next_ref), columns)
        parts = [logits[:, c : c + 128] for c in range(0, narrow, 128)]
        if narrow % 128:
            spare = jnp.full((rows, 128 - narrow % 128), NEG, F32)
            parts[-1] = jnp.concatenate([parts[-1], spare], axis=1)
        lane = lax.broadcasted_iota(jnp.int32, (rows, 128), 1) + n * narrow
        peak = peak_ref[...]
        higher = functools.reduce(jnp.maximum, parts, peak)
        total = sum_ref[...] * jnp.exp(peak - higher)
        picked = pick_ref[...]
        target = wanted_ref[...]
        for c, part in enumerate(parts):
            total = total + jnp.exp(part - higher)
            picked = picked + jnp.where(lane + c * 128 == target, part, 0.0)
        peak_ref[...] = higher
        sum_ref[...] = total
        pick_ref[...] = picked

    higher = peak_ref[...]
    peak = jnp.max(higher, axis=1, keepdims=True)
    sums = jnp.sum(sum_ref[...] * jnp.exp(higher - peak), axis=1, keepdims=True)
    pick = jnp.sum(pick_ref[...], axis=1, keepdims=True)
    row = lax.broadcasted_iota(jnp.int32, (rows, 128), 0)
    lane = lax.broadcasted_iota(jnp.int32, (rows, 128), 1)
    three = jnp.where(lane // share == 0, peak, jnp.where(lane // share == 1, sums, pick))
    three = jnp.where((row - lane) % share == 0, three, 0.0)
    mine = len(places) // 2
    for i, place in enumerate(places):
        near = place // (2 * tensor_size) * tensor_size + place % tensor_size
        ref = out_ref if i < mine else other_ref
        ref[near] = jnp.sum(three[i * share : (i + 1) * share], axis=0, keepdims=True)


def pair_kernel(share, left_ref, right_ref, out_ref):
    left = left_ref[...].reshape(left_ref.shape[0], 128)
    right = right_ref[...].reshape(left_ref.shape[0], 128)
    lane = lax.broadcasted_iota(jnp.int32, left.shape, 1) // share
    peak = jnp.maximum(left, right)
    shifted = pltpu.roll(peak, share, 1)
    sums = left * jnp.exp(jnp.where(lane == 1, pltpu.roll(left, share, 1) - shifted, 0.0))
    sums = sums + right * jnp.exp(jnp.where(lane == 1, pltpu.roll(right, share, 1) - shifted, 0.0))
    out_ref[...] = jnp.where(lane == 0, peak, jnp.where(lane < 3, sums, 0.0)).reshape(out_ref.shape)


def final_kernel(share, live_ref, stats_ref, out_ref):
    stats = stats_ref[...].reshape(stats_ref.shape[0], 128)
    peak = jnp.max(stats, axis=0, keepdims=True)
    sums = pltpu.roll(stats, 128 - share, 1)
    picks = pltpu.roll(stats, 128 - 2 * share, 1)
    total = jnp.sum(sums * jnp.exp(stats - peak), axis=0, keepdims=True)
    values = jnp.sum(picks, axis=0, keepdims=True) - peak - jnp.log(total)
    out_ref[...] = jnp.where(live_ref[:1] > 0.0, values, 0.0)[0, :share]


def local(
    group_size,
    tensor_size,
    resp_query,
    resp_key,
    resp_value,
    prompt_keys,
    prompt_values,
    prompt_of,
    lengths,
    residual,
    out_weight,
    norm_gain,
    lm_weight,
    targets,
):
    rows, span = resp_query.shape
    heads = span // HEAD_DIM
    seq = rows // prompt_of.shape[0]
    key_rows = prompt_keys.shape[0]
    assert PLEN % key_rows == 0
    share = rows // tensor_size
    depth = out_weight.shape[1]
    vocab = lm_weight.shape[1]
    i32 = jnp.int32

    wanted = targets.reshape(-1, share, 1)
    above = list(range(2, group_size, 2))
    distances = list(range(group_size - 1, 0, -1))
    far_queries = [swap(resp_query, "group", a, group_size) for a in above]
    queries = {1: swap(resp_query, "group", 1, group_size)}
    far_queries = pl.pallas_call(
        functools.partial(pass_kernel, len(above)),
        out_shape=[jax.ShapeDtypeStruct(x.shape, x.dtype) for x in far_queries],
        in_specs=[vmem()] * len(above) + [anywhere()],
        out_specs=[vmem()] * len(above),
        compiler_params=params(1),
        name="pass",
    )(*map(held, far_queries), wanted)
    for a, x in zip(above, far_queries):
        queries[a] = x
        queries[a + 1] = swap(x, "group", 1, group_size)
    queries = [queries[d] for d in distances]
    inputs = (resp_query, resp_key, resp_value, prompt_keys, prompt_values)
    loaded = pl.pallas_call(
        functools.partial(load_kernel, len(inputs)),
        out_shape=[pltpu.VMEM(x.shape, x.dtype) for x in inputs],
        in_specs=[anywhere()] * (1 + len(inputs)),
        out_specs=[vmem()] * len(inputs),
        scratch_shapes=[pltpu.SemaphoreType.DMA((len(inputs),))],
        compiler_params=params(1),
        cost_estimate=cost(moved=2 * MIB),
        name="load",
    )(far_queries[0], *map(stored, inputs))
    query, own_keys, own_values, keys, values = map(held, loaded)
    answers = pl.pallas_call(
        functools.partial(prefix_kernel, heads, len(distances)),
        out_shape=[jax.ShapeDtypeStruct((rows, span + 128), BF16)] * len(distances),
        in_specs=[vmem()] * (len(distances) + 2),
        out_specs=[vmem()] * len(distances),
        compiler_params=params(8),
        name="prefix_attention",
    )(*map(held, queries), keys, values)
    got = [swap(x, "group", d, group_size) for x, d in zip(answers, distances)]
    own, live, weight = pl.pallas_call(
        functools.partial(own_kernel, heads, seq, share),
        out_shape=[
            jax.ShapeDtypeStruct((rows, span + 128), F32),
            jax.ShapeDtypeStruct((8, 128), F32),
            pltpu.VMEM(out_weight.shape, BF16),
        ],
        in_specs=[smem()] * 2 + [vmem()] * 5 + [anywhere()] * 2,
        out_specs=[vmem()] * 3,
        scratch_shapes=[pltpu.SemaphoreType.DMA((4,))],
        compiler_params=params(6),
        cost_estimate=cost(moved=8 * MIB),
        name="own_attention",
    )(
        stored(lengths),
        stored(prompt_of),
        query,
        own_keys,
        own_values,
        keys,
        values,
        stored(out_weight),
        answers[0],
    )

    def fetch(source, start, count, gate):
        return held(
            pl.pallas_call(
                functools.partial(fetch_kernel, start),
                out_shape=pltpu.VMEM((count, source.shape[1]), BF16),
                in_specs=[anywhere()] * 2,
                out_specs=vmem(),
                scratch_shapes=[pltpu.SemaphoreType.DMA((4,))],
                compiler_params=params(1),
                cost_estimate=cost(moved=count * source.shape[1] * 2),
                name="fetch",
            )(stored(source), gate)
        )

    half = depth // 2
    quarter = depth // 4
    wide = 1280 if half % 1280 == 0 else half
    block = rows // 4
    send_left, keep_left, send_right, keep_right = pl.pallas_call(
        functools.partial(project_kernel, heads, seq, wide, group_size, key_rows),
        out_shape=[
            jax.ShapeDtypeStruct((2, block, half), BF16),
            jax.ShapeDtypeStruct((2, block, half), F32),
        ]
        * 2,
        in_specs=[smem()] + [vmem()] * (2 + len(distances)),
        out_specs=[vmem()] * 4,
        scratch_shapes=[
            pltpu.VMEM((rows, span), BF16),
            pltpu.VMEM((4, block, wide), F32),
        ],
        compiler_params=params(6),
        name="project",
    )(stored(prompt_of), *map(held, (own, *got)), held(weight))

    def add(kernel, name, size, *operands):
        return pl.pallas_call(
            kernel,
            out_shape=[jax.ShapeDtypeStruct(size, F32), jax.ShapeDtypeStruct(size, BF16)],
            in_specs=[vmem()] * len(operands),
            out_specs=[vmem()] * 2,
            compiler_params=params(2),
            name=name,
        )(*map(held, operands))

    got_left = swap(send_left, "tensor", 1, tensor_size)
    got_right = swap(send_right, "tensor", 2, tensor_size)
    left, send_left = add(fold_kernel, "fold_left", (block, half), keep_left, got_left)
    right, send_right = add(fold_kernel, "fold_right", (block, half), keep_right, got_right)
    got_left = swap(send_left, "tensor", 2, tensor_size)
    got_right = swap(send_right, "tensor", 1, tensor_size)
    total, send = add(side_kernel, "side", (block, depth), left, got_left, right, got_right)
    first_quarter = fetch(lm_weight, 0, quarter, send)
    second_quarter = fetch(lm_weight, quarter, quarter, send)
    far = 4
    while 2 * far < tensor_size:
        total, send = add(
            add_kernel, "add", (block, depth), total, swap(send, "tensor", far, tensor_size)
        )
        far = 2 * far
    normed = pl.pallas_call(
        norm_kernel,
        out_shape=jax.ShapeDtypeStruct((block, depth), BF16),
        in_specs=[vmem()] * 2 + [anywhere()] * 2 + [vmem()] * 2,
        out_specs=vmem(),
        compiler_params=params(4),
        name="norm",
    )(
        *map(held, (residual.reshape(4, block, depth), norm_gain[None])),
        first_quarter,
        second_quarter,
        *map(held, (total, swap(send, "tensor", far, tensor_size))),
    )

    order = [0, 2]
    here = [(g, x) for g in [0] + above for x in (0, 1)]
    column = [normed, swap(normed, "tensor", 2, tensor_size)]
    columns = pl.pallas_call(
        functools.partial(column_kernel, len(column)),
        out_shape=[jax.ShapeDtypeStruct((len(column), block, half), BF16)] * 2,
        in_specs=[vmem()] * len(column),
        out_specs=[vmem()] * 2,
        compiler_params=params(2),
        name="column",
    )(*map(held, column))

    def join(pieces, gate):
        blocks = sum(x.shape[0] for x in pieces)
        return pl.pallas_call(
            functools.partial(join_kernel, len(pieces)),
            out_shape=jax.ShapeDtypeStruct((blocks, block, half), BF16),
            in_specs=[vmem()] * len(pieces) + [anywhere()],
            out_specs=vmem(),
            compiler_params=params(2),
            name="join",
        )(*map(held, pieces), gate)

    left, right = columns
    got_left = swap(left, "tensor", 1, tensor_size)
    third = fetch(lm_weight, 2 * quarter, quarter, left)
    right = [right] + [swap(right, "group", d, group_size) for d in above]
    left = join([left, got_left], third)
    got_left = [swap(left, "group", d, group_size) for d in above]
    across = swap(jnp.concatenate(right), "tensor", 1, tensor_size)
    across = jnp.split(across, len(right))
    right = [x for pair in zip(right, across) for x in pair]
    halves = []
    for tokens in (jnp.concatenate([left] + got_left), jnp.concatenate(right)):
        tokens = tokens.reshape(-1, half)
        halves.append((tokens, swap(tokens, "group", 1, group_size)))
    spots = [(g + c, t + x) for c in (0, 1) for g, x in here for t in order]
    total_rows = 2 * tokens.shape[0]
    narrow = 1536 if vocab % 1536 == 0 else vocab
    limit = 10 if total_rows <= 256 else 24
    work = 2 * total_rows * (half) * vocab
    first, last = pl.pallas_call(
        functools.partial(first_kernel, narrow),
        out_shape=[pltpu.VMEM((total_rows, vocab), F32), pltpu.VMEM((quarter, vocab), BF16)],
        in_specs=[vmem()] * 4 + [anywhere()],
        out_specs=[vmem()] * 2,
        scratch_shapes=[
            pltpu.VMEM((total_rows, half), BF16),
            pltpu.SemaphoreType.DMA((4,)),
        ],
        compiler_params=params(limit),
        cost_estimate=cost(flops=work),
        name="logits_first",
    )(*map(held, (*halves[0], first_quarter, second_quarter)), stored(lm_weight))
    stats, other = pl.pallas_call(
        functools.partial(logits_kernel, vocab, spots, tensor_size),
        out_shape=[jax.ShapeDtypeStruct((group_size * tensor_size // 2, 1, 128), F32)] * 2,
        in_specs=[vmem()] * 6,
        out_specs=[vmem()] * 2,
        scratch_shapes=[pltpu.VMEM((total_rows, half), BF16)]
        + [pltpu.VMEM((total_rows, 128), F32)] * 3
        + [pltpu.VMEM((total_rows, 1), i32)],
        compiler_params=params(limit),
        cost_estimate=cost(flops=work),
        name="logits",
    )(*map(held, (first, *halves[1])), wanted, held(third), held(last))

    stats = pl.pallas_call(
        functools.partial(pair_kernel, share),
        out_shape=jax.ShapeDtypeStruct(stats.shape, F32),
        in_specs=[vmem()] * 2,
        out_specs=vmem(),
        compiler_params=params(2),
        name="pair",
    )(held(stats), held(swap(other, "group", 1, group_size)))
    alike = [
        [g * tensor_size + t for g in range(core, group_size, 2) for t in range(tensor_size)]
        for core in (0, 1)
    ]
    stats = lax.all_to_all(
        stats, ("group", "tensor"), 0, 0, axis_index_groups=alike, tiled=True
    )
    return pl.pallas_call(
        functools.partial(final_kernel, share),
        out_shape=jax.ShapeDtypeStruct((share,), F32),
        in_specs=[vmem()] * 2,
        out_specs=vmem(),
        compiler_params=params(4),
        name="final",
    )(held(live), held(stats))


def solution(mesh):
    return jax.shard_map(
        functools.partial(local, mesh.shape["group"], mesh.shape["tensor"]),
        mesh=mesh,
        in_specs=(
            P("group", "tensor"),
            P("group", "tensor"),
            P("group", "tensor"),
            P("group", "tensor"),
            P("group", "tensor"),
            P("group"),
            P("group"),
            P("group", None),
            P("tensor", None),
            P(),
            P(None, ("group", "tensor")),
            P(),
        ),
        out_specs=P(("group", "tensor")),
        check_vma=False,
    )
```

```python
import functools

import jax
import jax.numpy as jnp
from jax import lax
from jax.experimental import pallas as pl
from jax.experimental.pallas import tpu as pltpu
from jax.sharding import PartitionSpec as P

HEAD_DIM = 128
PLEN = 512
NEG = -1e30
BF16 = jnp.bfloat16
F32 = jnp.float32
MIB = 1024 * 1024


def params(mib):
    return pltpu.CompilerParams(vmem_limit_bytes=mib * MIB)


def held(x):
    return pltpu.with_memory_space_constraint(x, pltpu.VMEM)


def stored(x):
    return pltpu.with_memory_space_constraint(x, pltpu.HBM)


def anywhere():
    return pl.BlockSpec(memory_space=pl.ANY)


def cost(flops=0, moved=0):
    return pl.CostEstimate(flops=flops, bytes_accessed=moved, transcendentals=0)


def vmem():
    return pl.BlockSpec(memory_space=pltpu.VMEM)


def smem():
    return pl.BlockSpec(memory_space=pltpu.SMEM)


def swap(x, axis, distance, size):
    return lax.ppermute(x, axis, [(i, i ^ distance) for i in range(size)])


def attend(jobs):
    factor = HEAD_DIM**-0.5
    scores = [
        lax.dot_general(q, k, (((1,), (1,)), ((), ())), preferred_element_type=F32)
        for q, k, _, _ in jobs
    ]
    scores = [
        s if job[3] is None else jnp.where(job[3], s, NEG) for s, job in zip(scores, jobs)
    ]
    peaks = [jnp.max(s, axis=1, keepdims=True) for s in scores]
    weights = [jnp.exp((s - peak) * factor) for s, peak in zip(scores, peaks)]
    weights = [
        w if job[3] is None else jnp.where(job[3], w, 0.0) for w, job in zip(weights, jobs)
    ]
    weights = [w.astype(BF16) for w in weights]
    totals = [jnp.sum(w.astype(F32), axis=1, keepdims=True) for w in weights]
    mixed = [
        jnp.dot(w, job[2], preferred_element_type=F32) for w, job in zip(weights, jobs)
    ]
    return [
        (m / total, peak * factor + jnp.log(total))
        for m, total, peak in zip(mixed, totals, peaks)
    ]


def pack_logs(logs, rows):
    lane = lax.broadcasted_iota(jnp.int32, (rows, 128), 1)
    packed = jnp.zeros((rows, 128), F32)
    for head, log in enumerate(logs):
        first = log.astype(BF16).astype(F32)
        second = (log - first).astype(BF16).astype(F32)
        third = log - first - second
        for part, value in enumerate((first, second, third)):
            packed = jnp.where(lane == 3 * head + part, value, packed)
    return packed.astype(BF16)


def pass_kernel(count, *refs):
    for ref, out_ref in zip(refs, refs[-count:]):
        out_ref[...] = ref[...]


def load_kernel(count, gate_ref, *refs):
    sems = refs[2 * count]
    copies = [
        pltpu.make_async_copy(refs[i], refs[count + i], sems.at[i]) for i in range(count)
    ]
    for copy in copies:
        copy.start()
    for copy in copies:
        copy.wait()


def carried(source_ref, start, out_ref, sems):
    count = sems.shape[0]
    rows = out_ref.shape[0] // count
    return [
        pltpu.make_async_copy(
            source_ref.at[pl.ds(start + i * rows, rows)], out_ref.at[pl.ds(i * rows, rows)], sems.at[i]
        )
        for i in range(count)
    ]


def own_kernel(
    heads,
    seq,
    share,
    lengths_ref,
    prompt_ref,
    q_ref,
    rk_ref,
    rv_ref,
    k_ref,
    v_ref,
    source_ref,
    gate_ref,
    own_ref,
    live_ref,
    weight_ref,
    sems,
):
    copies = carried(source_ref, 0, weight_ref, sems)
    for copy in copies:
        copy.start()
    rows = q_ref.shape[0]
    row = lax.broadcasted_iota(jnp.int32, (rows, rows), 0)
    col = lax.broadcasted_iota(jnp.int32, (rows, rows), 1)
    live = jnp.zeros((rows, rows), jnp.int32)
    for r in range(rows // seq):
        live = jnp.where(col // seq == r, lengths_ref[r], live)
    allowed = (row // seq == col // seq) & (col <= row) & (col % seq < live)
    parts = [slice(h * HEAD_DIM, (h + 1) * HEAD_DIM) for h in range(heads)]
    found = attend(
        [(q_ref[:, p], rk_ref[:, p], rv_ref[:, p], allowed) for p in parts]
        + [(q_ref[:, p], k_ref[:, p], v_ref[:, p], None) for p in parts]
    )
    here = wanted_prompts(seq, rows, prompt_ref) == lax.axis_index("group") * k_ref.shape[0] // PLEN
    lane = lax.broadcasted_iota(jnp.int32, (rows, 128), 1)
    packed = jnp.zeros((rows, 128), F32)
    for h, p in enumerate(parts):
        (first, log), (second, other) = found[h], found[heads + h]
        other = jnp.where(here, other, NEG)
        peak = jnp.maximum(log, other)
        left, right = jnp.exp(log - peak), jnp.exp(other - peak)
        own_ref[:, p] = (first * left + second * right) / (left + right)
        packed = jnp.where(lane == h, peak + jnp.log(left + right), packed)
    own_ref[:, heads * HEAD_DIM :] = packed
    token = lax.broadcasted_iota(jnp.int32, live_ref.shape, 1) + lax.axis_index("tensor") * share
    length = jnp.zeros(live_ref.shape, jnp.int32)
    for r in range(rows // seq):
        length = jnp.where(token // seq == r, lengths_ref[r], length)
    live_ref[...] = jnp.where(token % seq < length, 1.0, 0.0)
    for copy in copies:
        copy.wait()


def wanted_prompts(seq, rows, prompt_ref):
    row = lax.broadcasted_iota(jnp.int32, (rows, 1), 0)
    wanted = jnp.zeros((rows, 1), jnp.int32)
    for r in range(rows // seq):
        wanted = jnp.where(row // seq == r, prompt_ref[r], wanted)
    return wanted


def prefix_kernel(heads, count, *refs):
    q_refs, (k_ref, v_ref), out_refs = refs[:count], refs[count : count + 2], refs[count + 2 :]
    rows = q_refs[0].shape[0]
    parts = [slice(h * HEAD_DIM, (h + 1) * HEAD_DIM) for h in range(heads)]
    found = attend(
        [
            (jnp.concatenate([ref[:, p] for ref in q_refs], axis=0), k_ref[:, p], v_ref[:, p], None)
            for p in parts
        ]
    )
    for i in range(count):
        rung = slice(i * rows, (i + 1) * rows)
        for h, p in enumerate(parts):
            out_refs[i][:, p] = found[h][0][rung].astype(BF16)
        out_refs[i][:, heads * HEAD_DIM :] = pack_logs([log[rung] for _, log in found], rows)


def project_kernel(heads, seq, wide, group_size, key_rows, prompt_ref, own_ref, *refs):
    got_refs, refs = refs[: group_size - 1], refs[group_size - 1 :]
    weight_ref, send_left_ref, keep_left_ref, send_right_ref, keep_right_ref = refs[:5]
    attended_ref, partial_ref = refs[5:]
    rows = own_ref.shape[0]
    wanted = wanted_prompts(seq, rows, prompt_ref)
    group = lax.axis_index("group")
    holders = [(group ^ d) * key_rows // PLEN for d in range(group_size - 1, 0, -1)]
    for h in range(heads):
        part = slice(h * HEAD_DIM, (h + 1) * HEAD_DIM)
        at = heads * HEAD_DIM
        logs = [own_ref[:, at + h : at + h + 1]]
        values = [own_ref[:, part]]
        for holder, ref in zip(holders, got_refs):
            three = ref[:, at : at + 128].astype(F32)
            log = (
                three[:, 3 * h : 3 * h + 1]
                + three[:, 3 * h + 1 : 3 * h + 2]
                + three[:, 3 * h + 2 : 3 * h + 3]
            )
            logs.append(jnp.where(wanted == holder, log, NEG))
            values.append(ref[:, part].astype(F32))
        peak = functools.reduce(jnp.maximum, logs)
        loads = [jnp.exp(log - peak) for log in logs]
        total = functools.reduce(jnp.add, loads)
        mixed = functools.reduce(jnp.add, [w * v for w, v in zip(loads, values)])
        attended_ref[:, part] = (mixed / total).astype(BF16)

    me = lax.axis_index("tensor") % 4
    block = rows // 4
    half = send_left_ref.shape[2]

    def multiply(columns):
        partial = jnp.dot(attended_ref[...], weight_ref[:, columns], preferred_element_type=F32)
        for b in range(4):
            partial_ref[b] = partial[b * block : (b + 1) * block]

    @pl.loop(0, half // wide)
    def _(n):
        columns = pl.ds(pl.multiple_of(n * wide, 128), wide)
        multiply(columns)
        for i in range(2):
            keep_left_ref[i, :, columns] = partial_ref[me ^ (2 * i)]
            send_left_ref[i, :, columns] = partial_ref[me ^ (2 * i + 1)].astype(BF16)

    @pl.loop(0, half // wide)
    def _(n):
        columns = pl.ds(pl.multiple_of(n * wide, 128), wide)
        multiply(pl.ds(pl.multiple_of(half + n * wide, 128), wide))
        for i in range(2):
            keep_right_ref[i, :, columns] = partial_ref[me ^ i]
            send_right_ref[i, :, columns] = partial_ref[me ^ (i + 2)].astype(BF16)


def fold_kernel(keep_ref, got_ref, *refs):
    own_ref, send_ref = refs[-2:]
    own_ref[...] = keep_ref[0] + got_ref[0].astype(F32)
    send_ref[...] = (keep_ref[1] + got_ref[1].astype(F32)).astype(BF16)


def side_kernel(left_ref, got_left_ref, right_ref, got_right_ref, own_ref, send_ref):
    half = left_ref.shape[1]
    for i, (ref, got_ref) in enumerate(((left_ref, got_left_ref), (right_ref, got_right_ref))):
        total = ref[...] + got_ref[...].astype(F32)
        own_ref[:, i * half : (i + 1) * half] = total
        send_ref[:, i * half : (i + 1) * half] = total.astype(BF16)


def add_kernel(own_ref, got_ref, out_ref, send_ref):
    total = own_ref[...] + got_ref[...].astype(F32)
    out_ref[...] = total
    send_ref[...] = total.astype(BF16)


def fetch_kernel(start, source_ref, gate_ref, out_ref, sems):
    copies = carried(source_ref, start, out_ref, sems)
    for copy in copies:
        copy.start()
    for copy in copies:
        copy.wait()


def cut_kernel(*refs):
    left_ref, right_ref = refs[-2:]
    count, width = left_ref.shape[0], left_ref.shape[2]
    for i in range(count):
        left_ref[i] = refs[i][:, :width]
    for i in range(right_ref.shape[0]):
        right_ref[i] = refs[count + i][:, width:]


def tokens_kernel(count, split, *refs):
    blocks, out_refs = refs[:count], refs[-2:]
    rows = blocks[0].shape[0]
    width = out_refs[0].shape[1]
    for half, (stacks, out_ref) in enumerate(zip((refs[count:split], refs[split:-2]), out_refs)):
        for i, ref in enumerate(blocks):
            out_ref[i * rows : (i + 1) * rows] = ref[:, half * width : (half + 1) * width]
        place = count * rows
        for ref in stacks:
            for i in range(ref.shape[0]):
                out_ref[place : place + rows] = ref[i]
                place += rows


def norm_kernel(residual_ref, gain_ref, gate_ref, own_ref, got_ref, out_ref):
    hidden = residual_ref[lax.axis_index("tensor") % 4].astype(F32)
    hidden = hidden + (own_ref[...] + got_ref[...].astype(F32))
    squares = jnp.mean(hidden * hidden, axis=-1, keepdims=True)
    out_ref[...] = (hidden * lax.rsqrt(squares + 1e-06) * gain_ref[...].astype(F32)).astype(BF16)


def quarter_dots(x_ref, weight_refs, columns):
    start, total = 0, None
    for ref in weight_refs:
        stop = start + ref.shape[0]
        part = jnp.dot(x_ref[:, start:stop], ref[:, columns], preferred_element_type=F32)
        total = part if total is None else total + part
        start = stop
    return total


def first_kernel(
    narrow, left_ref, right_ref, weight_ref, next_ref, source_ref, out_ref, last_ref, x_ref, sems
):
    copies = carried(source_ref, source_ref.shape[0] - last_ref.shape[0], last_ref, sems)
    for copy in copies:
        copy.start()
    half = left_ref.shape[0]
    x_ref[:half] = left_ref[...]
    x_ref[half:] = right_ref[...]

    @pl.loop(0, weight_ref.shape[1] // narrow)
    def _(n):
        columns = pl.ds(n * narrow if narrow % 128 else pl.multiple_of(n * narrow, 128), narrow)
        out_ref[:, columns] = quarter_dots(x_ref, (weight_ref, next_ref), columns)

    for copy in copies:
        copy.wait()


def logits_kernel(
    narrow,
    spots,
    tensor_size,
    sum_in_ref,
    left_ref,
    right_ref,
    target_ref,
    weight_ref,
    next_ref,
    out_ref,
    x_ref,
    peak_ref,
    sum_ref,
    pick_ref,
    wanted_ref,
):
    half = left_ref.shape[0]
    rows = 2 * half
    share = target_ref.shape[1]
    group, tensor = lax.axis_index("group"), lax.axis_index("tensor")
    vocab = weight_ref.shape[1]
    shares = tensor_size // 4
    places = [
        (group ^ g) * tensor_size + shares * ((tensor % 4) ^ d) + i for g, d in spots for i in range(shares)
    ]
    for i, place in enumerate(places):
        wanted_ref[i * share : (i + 1) * share] = target_ref[place]
    wanted = wanted_ref[...] - (group * tensor_size + tensor) * vocab
    wanted_ref[...] = jnp.where((wanted >= 0) & (wanted < vocab), wanted, -1)
    x_ref[:half] = left_ref[...]
    x_ref[half:] = right_ref[...]
    peak_ref[...] = jnp.full_like(peak_ref, NEG)
    sum_ref[...] = jnp.zeros_like(sum_ref)
    pick_ref[...] = jnp.zeros_like(pick_ref)

    @pl.loop(0, weight_ref.shape[1] // narrow)
    def _(n):
        columns = pl.ds(n * narrow if narrow % 128 else pl.multiple_of(n * narrow, 128), narrow)
        logits = sum_in_ref[:, columns] + quarter_dots(x_ref, (weight_ref, next_ref), columns)
        parts = [logits[:, c : c + 128] for c in range(0, narrow, 128)]
        if narrow % 128:
            spare = jnp.full((rows, 128 - narrow % 128), NEG, F32)
            parts[-1] = jnp.concatenate([parts[-1], spare], axis=1)
        lane = lax.broadcasted_iota(jnp.int32, (rows, 128), 1) + n * narrow
        peak = peak_ref[...]
        higher = functools.reduce(jnp.maximum, parts, peak)
        total = sum_ref[...] * jnp.exp(peak - higher)
        picked = pick_ref[...]
        target = wanted_ref[...]
        for c, part in enumerate(parts):
            total = total + jnp.exp(part - higher)
            picked = picked + jnp.where(lane + c * 128 == target, part, 0.0)
        peak_ref[...] = higher
        sum_ref[...] = total
        pick_ref[...] = picked

    higher = peak_ref[...]
    peak = jnp.max(higher, axis=1, keepdims=True)
    sums = jnp.sum(sum_ref[...] * jnp.exp(higher - peak), axis=1, keepdims=True)
    pick = jnp.sum(pick_ref[...], axis=1, keepdims=True)
    row = lax.broadcasted_iota(jnp.int32, (rows, 128), 0)
    lane = lax.broadcasted_iota(jnp.int32, (rows, 128), 1)
    three = jnp.where(lane // share == 0, peak, jnp.where(lane // share == 1, sums, pick))
    three = jnp.where((row - lane) % share == 0, three, 0.0)
    for i, place in enumerate(places):
        out_ref[place] = jnp.sum(three[i * share : (i + 1) * share], axis=0, keepdims=True)


def final_kernel(share, live_ref, stats_ref, out_ref):
    stats = stats_ref[...].reshape(stats_ref.shape[0], 128)
    peak = jnp.max(stats, axis=0, keepdims=True)
    sums = pltpu.roll(stats, 128 - share, 1)
    picks = pltpu.roll(stats, 128 - 2 * share, 1)
    total = jnp.sum(sums * jnp.exp(stats - peak), axis=0, keepdims=True)
    values = jnp.sum(picks, axis=0, keepdims=True) - peak - jnp.log(total)
    out_ref[...] = jnp.where(live_ref[:1] > 0.0, values, 0.0)[0, :share]


def local(
    group_size,
    tensor_size,
    resp_query,
    resp_key,
    resp_value,
    prompt_keys,
    prompt_values,
    prompt_of,
    lengths,
    residual,
    out_weight,
    norm_gain,
    lm_weight,
    targets,
):
    rows, span = resp_query.shape
    heads = span // HEAD_DIM
    seq = rows // prompt_of.shape[0]
    key_rows = prompt_keys.shape[0]
    assert PLEN % key_rows == 0
    share = rows // tensor_size
    depth = out_weight.shape[1]
    vocab = lm_weight.shape[1]
    i32 = jnp.int32

    wanted = targets.reshape(-1, share, 1)
    above = list(range(2, group_size, 2))
    distances = list(range(group_size - 1, 0, -1))
    far_queries = [swap(resp_query, "group", a, group_size) for a in above]
    queries = {1: swap(resp_query, "group", 1, group_size)}
    far_queries = pl.pallas_call(
        functools.partial(pass_kernel, len(above)),
        out_shape=[jax.ShapeDtypeStruct(x.shape, x.dtype) for x in far_queries],
        in_specs=[vmem()] * len(above) + [anywhere()],
        out_specs=[vmem()] * len(above),
        compiler_params=params(1),
        name="pass",
    )(*map(held, far_queries), wanted)
    for a, x in zip(above, far_queries):
        queries[a] = x
        queries[a + 1] = swap(x, "group", 1, group_size)
    queries = [queries[d] for d in distances]
    inputs = (resp_query, resp_key, resp_value, prompt_keys, prompt_values)
    loaded = pl.pallas_call(
        functools.partial(load_kernel, len(inputs)),
        out_shape=[pltpu.VMEM(x.shape, x.dtype) for x in inputs],
        in_specs=[anywhere()] * (1 + len(inputs)),
        out_specs=[vmem()] * len(inputs),
        scratch_shapes=[pltpu.SemaphoreType.DMA((len(inputs),))],
        compiler_params=params(1),
        cost_estimate=cost(moved=2 * MIB),
        name="load",
    )(far_queries[0], *map(stored, inputs))
    query, own_keys, own_values, keys, values = map(held, loaded)
    answers = pl.pallas_call(
        functools.partial(prefix_kernel, heads, len(distances)),
        out_shape=[jax.ShapeDtypeStruct((rows, span + 128), BF16)] * len(distances),
        in_specs=[vmem()] * (len(distances) + 2),
        out_specs=[vmem()] * len(distances),
        compiler_params=params(8),
        name="prefix_attention",
    )(*map(held, queries), keys, values)
    got = [swap(x, "group", d, group_size) for x, d in zip(answers, distances)]
    own, live, weight = pl.pallas_call(
        functools.partial(own_kernel, heads, seq, share),
        out_shape=[
            jax.ShapeDtypeStruct((rows, span + 128), F32),
            jax.ShapeDtypeStruct((8, 128), F32),
            pltpu.VMEM(out_weight.shape, BF16),
        ],
        in_specs=[smem()] * 2 + [vmem()] * 5 + [anywhere()] * 2,
        out_specs=[vmem()] * 3,
        scratch_shapes=[pltpu.SemaphoreType.DMA((4,))],
        compiler_params=params(6),
        cost_estimate=cost(moved=8 * MIB),
        name="own_attention",
    )(
        stored(lengths),
        stored(prompt_of),
        query,
        own_keys,
        own_values,
        keys,
        values,
        stored(out_weight),
        answers[0],
    )

    def fetch(source, start, count, gate):
        return held(
            pl.pallas_call(
                functools.partial(fetch_kernel, start),
                out_shape=pltpu.VMEM((count, source.shape[1]), BF16),
                in_specs=[anywhere()] * 2,
                out_specs=vmem(),
                scratch_shapes=[pltpu.SemaphoreType.DMA((4,))],
                compiler_params=params(1),
                cost_estimate=cost(moved=count * source.shape[1] * 2),
                name="fetch",
            )(stored(source), gate)
        )

    half = depth // 2
    quarter = depth // 4
    wide = 1280 if half % 1280 == 0 else half
    block = rows // 4
    send_left, keep_left, send_right, keep_right = pl.pallas_call(
        functools.partial(project_kernel, heads, seq, wide, group_size, key_rows),
        out_shape=[
            jax.ShapeDtypeStruct((2, block, half), BF16),
            jax.ShapeDtypeStruct((2, block, half), F32),
        ]
        * 2,
        in_specs=[smem()] + [vmem()] * (2 + len(distances)),
        out_specs=[vmem()] * 4,
        scratch_shapes=[
            pltpu.VMEM((rows, span), BF16),
            pltpu.VMEM((4, block, wide), F32),
        ],
        compiler_params=params(6),
        name="project",
    )(stored(prompt_of), *map(held, (own, *got)), held(weight))

    def add(kernel, name, size, *operands, gates=()):
        return pl.pallas_call(
            kernel,
            out_shape=[jax.ShapeDtypeStruct(size, F32), jax.ShapeDtypeStruct(size, BF16)],
            in_specs=[vmem()] * len(operands) + [anywhere()] * len(gates),
            out_specs=[vmem()] * 2,
            compiler_params=params(2),
            name=name,
        )(*map(held, operands), *gates)

    early_rows = 1024 if half > 1024 else half // 2
    first_quarter = fetch(lm_weight, 0, early_rows, send_left)

    got_left = swap(send_left, "tensor", 1, tensor_size)
    got_right = swap(send_right, "tensor", 2, tensor_size)
    left, send_left = add(fold_kernel, "fold_left", (block, half), keep_left, got_left, gates=(first_quarter,))
    right, send_right = add(fold_kernel, "fold_right", (block, half), keep_right, got_right)
    got_left = swap(send_left, "tensor", 2, tensor_size)
    got_right = swap(send_right, "tensor", 1, tensor_size)
    total, send = add(side_kernel, "side", (block, depth), left, got_left, right, got_right)
    second_quarter = fetch(lm_weight, early_rows, half - early_rows, send)
    far = 4
    while 2 * far < tensor_size:
        total, send = add(
            add_kernel, "add", (block, depth), total, swap(send, "tensor", far, tensor_size)
        )
        far = 2 * far
    normed = pl.pallas_call(
        norm_kernel,
        out_shape=jax.ShapeDtypeStruct((block, depth), BF16),
        in_specs=[vmem()] * 2 + [anywhere()] + [vmem()] * 2,
        out_specs=vmem(),
        compiler_params=params(4),
        name="norm",
    )(
        *map(held, (residual.reshape(4, block, depth), norm_gain[None])),
        second_quarter,
        *map(held, (total, swap(send, "tensor", far, tensor_size))),
    )

    def around(x):
        along = [swap(x, "group", d, group_size) for d in above]
        return swap(x, "tensor", 1, tensor_size), along

    sides = [around(normed)]
    near = [normed, swap(normed, "tensor", 2, tensor_size)]
    sides.append(around(near[1]))
    third = fetch(lm_weight, 2 * quarter, quarter, near[1])

    across = [x for x, _ in sides]
    along = [ys[i] for i in range(len(above)) for _, ys in sides]
    left, right = pl.pallas_call(
        cut_kernel,
        out_shape=[
            jax.ShapeDtypeStruct((len(pieces), block, half), BF16) for pieces in (across, along)
        ],
        in_specs=[vmem()] * (len(across) + len(along)) + [anywhere()],
        out_specs=[vmem()] * 2,
        compiler_params=params(2),
        name="cut",
    )(*map(held, (*across, *along)), third)
    left = [swap(left, "group", d, group_size) for d in above]
    right = [swap(right, "tensor", 1, tensor_size)]
    whole = near + across + along
    count = (len(whole) + len(across) * len(above)) * block
    halves = pl.pallas_call(
        functools.partial(tokens_kernel, len(whole), len(whole) + len(left)),
        out_shape=[jax.ShapeDtypeStruct((count, half), BF16)] * 2,
        in_specs=[vmem()] * (len(whole) + len(left) + len(right)),
        out_specs=[vmem()] * 2,
        compiler_params=params(2),
        name="tokens",
    )(*map(held, (*whole, *left, *right)))
    halves = [(tokens, swap(tokens, "group", 1, group_size)) for tokens in halves]
    here = [(0, 0), (0, 1)] + [(g, 0) for g in above] + [(g, 1) for g in above]
    order = [0, 2]
    spots = [(g + c, t + x) for c in (0, 1) for g, x in here for t in order]
    total_rows = 2 * count
    narrow = 1536 if vocab % 1536 == 0 else vocab
    limit = 10 if total_rows <= 256 else 24
    work = 2 * total_rows * (half) * vocab
    first, last = pl.pallas_call(
        functools.partial(first_kernel, narrow),
        out_shape=[pltpu.VMEM((total_rows, vocab), F32), pltpu.VMEM((quarter, vocab), BF16)],
        in_specs=[vmem()] * 4 + [anywhere()],
        out_specs=[vmem()] * 2,
        scratch_shapes=[
            pltpu.VMEM((total_rows, half), BF16),
            pltpu.SemaphoreType.DMA((4,)),
        ],
        compiler_params=params(limit),
        cost_estimate=cost(flops=work),
        name="logits_first",
    )(*map(held, (*halves[0], first_quarter, second_quarter)), stored(lm_weight))
    stats = pl.pallas_call(
        functools.partial(logits_kernel, vocab, spots, tensor_size),
        out_shape=jax.ShapeDtypeStruct((group_size * tensor_size, 1, 128), F32),
        in_specs=[vmem()] * 6,
        out_specs=vmem(),
        scratch_shapes=[pltpu.VMEM((total_rows, half), BF16)]
        + [pltpu.VMEM((total_rows, 128), F32)] * 3
        + [pltpu.VMEM((total_rows, 1), i32)],
        compiler_params=params(limit),
        cost_estimate=cost(flops=work),
        name="logits",
    )(*map(held, (first, *halves[1])), wanted, held(third), held(last))

    stats = lax.all_to_all(stats, ("group", "tensor"), 0, 0, tiled=True)
    return pl.pallas_call(
        functools.partial(final_kernel, share),
        out_shape=jax.ShapeDtypeStruct((share,), F32),
        in_specs=[vmem()] * 2,
        out_specs=vmem(),
        compiler_params=params(4),
        name="final",
    )(held(live), held(stats))


def solution(mesh):
    return jax.shard_map(
        functools.partial(local, mesh.shape["group"], mesh.shape["tensor"]),
        mesh=mesh,
        in_specs=(
            P("group", "tensor"),
            P("group", "tensor"),
            P("group", "tensor"),
            P("group", "tensor"),
            P("group", "tensor"),
            P("group"),
            P("group"),
            P("group", None),
            P("tensor", None),
            P(),
            P(None, ("group", "tensor")),
            P(),
        ),
        out_specs=P(("group", "tensor")),
        check_vma=False,
    )
```

```python
import functools

import jax
import jax.numpy as jnp
from jax import lax
from jax.experimental import pallas as pl
from jax.experimental.pallas import tpu as pltpu
from jax.sharding import PartitionSpec as P

HEAD_DIM = 128
PLEN = 512
NEG = -1e30
BF16 = jnp.bfloat16
F32 = jnp.float32
MIB = 1024 * 1024


def params(mib):
    return pltpu.CompilerParams(vmem_limit_bytes=mib * MIB)


def held(x):
    return pltpu.with_memory_space_constraint(x, pltpu.VMEM)


def stored(x):
    return pltpu.with_memory_space_constraint(x, pltpu.HBM)


def anywhere():
    return pl.BlockSpec(memory_space=pl.ANY)


def cost(flops=0, moved=0):
    return pl.CostEstimate(flops=flops, bytes_accessed=moved, transcendentals=0)


def vmem():
    return pl.BlockSpec(memory_space=pltpu.VMEM)


def smem():
    return pl.BlockSpec(memory_space=pltpu.SMEM)


def swap(x, axis, distance, size):
    return lax.ppermute(x, axis, [(i, i ^ distance) for i in range(size)])


def attend(jobs):
    factor = HEAD_DIM**-0.5
    scores = [
        lax.dot_general(q, k, (((1,), (1,)), ((), ())), preferred_element_type=F32)
        for q, k, _, _ in jobs
    ]
    scores = [
        s if job[3] is None else jnp.where(job[3], s, NEG) for s, job in zip(scores, jobs)
    ]
    peaks = [jnp.max(s, axis=1, keepdims=True) for s in scores]
    weights = [jnp.exp((s - peak) * factor) for s, peak in zip(scores, peaks)]
    weights = [
        w if job[3] is None else jnp.where(job[3], w, 0.0) for w, job in zip(weights, jobs)
    ]
    weights = [w.astype(BF16) for w in weights]
    totals = [jnp.sum(w.astype(F32), axis=1, keepdims=True) for w in weights]
    mixed = [
        jnp.dot(w, job[2], preferred_element_type=F32) for w, job in zip(weights, jobs)
    ]
    return [
        (m / total, peak * factor + jnp.log(total))
        for m, total, peak in zip(mixed, totals, peaks)
    ]


def pack_logs(logs, rows):
    lane = lax.broadcasted_iota(jnp.int32, (rows, 128), 1)
    packed = jnp.zeros((rows, 128), F32)
    for head, log in enumerate(logs):
        first = log.astype(BF16).astype(F32)
        second = (log - first).astype(BF16).astype(F32)
        third = log - first - second
        for part, value in enumerate((first, second, third)):
            packed = jnp.where(lane == 3 * head + part, value, packed)
    return packed.astype(BF16)


def pass_kernel(count, *refs):
    for ref, out_ref in zip(refs, refs[-count:]):
        out_ref[...] = ref[...]


def load_kernel(count, gate_ref, *refs):
    sems = refs[2 * count]
    copies = [
        pltpu.make_async_copy(refs[i], refs[count + i], sems.at[i]) for i in range(count)
    ]
    for copy in copies:
        copy.start()
    for copy in copies:
        copy.wait()


def carried(source_ref, start, out_ref, sems):
    count = sems.shape[0]
    rows = out_ref.shape[0] // count
    return [
        pltpu.make_async_copy(
            source_ref.at[pl.ds(start + i * rows, rows)], out_ref.at[pl.ds(i * rows, rows)], sems.at[i]
        )
        for i in range(count)
    ]


def own_kernel(
    heads,
    seq,
    share,
    lengths_ref,
    prompt_ref,
    q_ref,
    rk_ref,
    rv_ref,
    k_ref,
    v_ref,
    source_ref,
    gate_ref,
    own_ref,
    live_ref,
    weight_ref,
    sems,
):
    copies = carried(source_ref, 0, weight_ref, sems)
    for copy in copies:
        copy.start()
    rows = q_ref.shape[0]
    row = lax.broadcasted_iota(jnp.int32, (rows, rows), 0)
    col = lax.broadcasted_iota(jnp.int32, (rows, rows), 1)
    live = jnp.zeros((rows, rows), jnp.int32)
    for r in range(rows // seq):
        live = jnp.where(col // seq == r, lengths_ref[r], live)
    allowed = (row // seq == col // seq) & (col <= row) & (col % seq < live)
    parts = [slice(h * HEAD_DIM, (h + 1) * HEAD_DIM) for h in range(heads)]
    found = attend(
        [(q_ref[:, p], rk_ref[:, p], rv_ref[:, p], allowed) for p in parts]
        + [(q_ref[:, p], k_ref[:, p], v_ref[:, p], None) for p in parts]
    )
    here = wanted_prompts(seq, rows, prompt_ref) == lax.axis_index("group") * k_ref.shape[0] // PLEN
    lane = lax.broadcasted_iota(jnp.int32, (rows, 128), 1)
    packed = jnp.zeros((rows, 128), F32)
    for h, p in enumerate(parts):
        (first, log), (second, other) = found[h], found[heads + h]
        other = jnp.where(here, other, NEG)
        peak = jnp.maximum(log, other)
        left, right = jnp.exp(log - peak), jnp.exp(other - peak)
        own_ref[:, p] = (first * left + second * right) / (left + right)
        packed = jnp.where(lane == h, peak + jnp.log(left + right), packed)
    own_ref[:, heads * HEAD_DIM :] = packed
    token = lax.broadcasted_iota(jnp.int32, live_ref.shape, 1) + lax.axis_index("tensor") * share
    length = jnp.zeros(live_ref.shape, jnp.int32)
    for r in range(rows // seq):
        length = jnp.where(token // seq == r, lengths_ref[r], length)
    live_ref[...] = jnp.where(token % seq < length, 1.0, 0.0)
    for copy in copies:
        copy.wait()


def wanted_prompts(seq, rows, prompt_ref):
    row = lax.broadcasted_iota(jnp.int32, (rows, 1), 0)
    wanted = jnp.zeros((rows, 1), jnp.int32)
    for r in range(rows // seq):
        wanted = jnp.where(row // seq == r, prompt_ref[r], wanted)
    return wanted


def prefix_kernel(heads, count, *refs):
    q_refs, (k_ref, v_ref), out_refs = refs[:count], refs[count : count + 2], refs[count + 2 :]
    rows = q_refs[0].shape[0]
    parts = [slice(h * HEAD_DIM, (h + 1) * HEAD_DIM) for h in range(heads)]
    found = attend(
        [
            (jnp.concatenate([ref[:, p] for ref in q_refs], axis=0), k_ref[:, p], v_ref[:, p], None)
            for p in parts
        ]
    )
    for i in range(count):
        rung = slice(i * rows, (i + 1) * rows)
        for h, p in enumerate(parts):
            out_refs[i][:, p] = found[h][0][rung].astype(BF16)
        out_refs[i][:, heads * HEAD_DIM :] = pack_logs([log[rung] for _, log in found], rows)


def project_kernel(heads, seq, wide, group_size, key_rows, prompt_ref, own_ref, *refs):
    got_refs, refs = refs[: group_size - 1], refs[group_size - 1 :]
    weight_ref, send_left_ref, keep_left_ref, send_right_ref, keep_right_ref = refs[:5]
    attended_ref, partial_ref = refs[5:]
    rows = own_ref.shape[0]
    wanted = wanted_prompts(seq, rows, prompt_ref)
    group = lax.axis_index("group")
    holders = [(group ^ d) * key_rows // PLEN for d in range(group_size - 1, 0, -1)]
    for h in range(heads):
        part = slice(h * HEAD_DIM, (h + 1) * HEAD_DIM)
        at = heads * HEAD_DIM
        logs = [own_ref[:, at + h : at + h + 1]]
        values = [own_ref[:, part]]
        for holder, ref in zip(holders, got_refs):
            three = ref[:, at : at + 128].astype(F32)
            log = (
                three[:, 3 * h : 3 * h + 1]
                + three[:, 3 * h + 1 : 3 * h + 2]
                + three[:, 3 * h + 2 : 3 * h + 3]
            )
            logs.append(jnp.where(wanted == holder, log, NEG))
            values.append(ref[:, part].astype(F32))
        peak = functools.reduce(jnp.maximum, logs)
        loads = [jnp.exp(log - peak) for log in logs]
        total = functools.reduce(jnp.add, loads)
        mixed = functools.reduce(jnp.add, [w * v for w, v in zip(loads, values)])
        attended_ref[:, part] = (mixed / total).astype(BF16)

    me = lax.axis_index("tensor") % 4
    block = rows // 4
    half = send_left_ref.shape[2]

    def multiply(columns):
        partial = jnp.dot(attended_ref[...], weight_ref[:, columns], preferred_element_type=F32)
        for b in range(4):
            partial_ref[b] = partial[b * block : (b + 1) * block]

    @pl.loop(0, half // wide)
    def _(n):
        columns = pl.ds(pl.multiple_of(n * wide, 128), wide)
        multiply(columns)
        for i in range(2):
            keep_left_ref[i, :, columns] = partial_ref[me ^ (2 * i)]
            send_left_ref[i, :, columns] = partial_ref[me ^ (2 * i + 1)].astype(BF16)

    @pl.loop(0, half // wide)
    def _(n):
        columns = pl.ds(pl.multiple_of(n * wide, 128), wide)
        multiply(pl.ds(pl.multiple_of(half + n * wide, 128), wide))
        for i in range(2):
            keep_right_ref[i, :, columns] = partial_ref[me ^ i]
            send_right_ref[i, :, columns] = partial_ref[me ^ (i + 2)].astype(BF16)


def fold_kernel(keep_ref, got_ref, *refs):
    own_ref, send_ref = refs[-2:]
    own_ref[...] = keep_ref[0] + got_ref[0].astype(F32)
    send_ref[...] = (keep_ref[1] + got_ref[1].astype(F32)).astype(BF16)


def side_kernel(left_ref, got_left_ref, right_ref, got_right_ref, own_ref, send_ref):
    half = left_ref.shape[1]
    for i, (ref, got_ref) in enumerate(((left_ref, got_left_ref), (right_ref, got_right_ref))):
        total = ref[...] + got_ref[...].astype(F32)
        own_ref[:, i * half : (i + 1) * half] = total
        send_ref[:, i * half : (i + 1) * half] = total.astype(BF16)


def add_kernel(own_ref, got_ref, out_ref, send_ref):
    total = own_ref[...] + got_ref[...].astype(F32)
    out_ref[...] = total
    send_ref[...] = total.astype(BF16)


def fetch_kernel(start, source_ref, gate_ref, out_ref, sems):
    copies = carried(source_ref, start, out_ref, sems)
    for copy in copies:
        copy.start()
    for copy in copies:
        copy.wait()


def tokens_kernel(count, *refs):
    out_refs = refs[-2:]
    rows, width = refs[0].shape[0], out_refs[0].shape[1]
    for half, out_ref in enumerate(out_refs):
        for i, ref in enumerate(refs[:count]):
            out_ref[i * rows : (i + 1) * rows] = ref[:, half * width : (half + 1) * width]


def norm_kernel(residual_ref, gain_ref, gate_ref, own_ref, got_ref, out_ref):
    hidden = residual_ref[lax.axis_index("tensor") % 4].astype(F32)
    hidden = hidden + (own_ref[...] + got_ref[...].astype(F32))
    squares = jnp.mean(hidden * hidden, axis=-1, keepdims=True)
    out_ref[...] = (hidden * lax.rsqrt(squares + 1e-06) * gain_ref[...].astype(F32)).astype(BF16)


def quarter_dots(x_ref, weight_refs, columns):
    start, total = 0, None
    for ref in weight_refs:
        stop = start + ref.shape[0]
        part = jnp.dot(x_ref[:, start:stop], ref[:, columns], preferred_element_type=F32)
        total = part if total is None else total + part
        start = stop
    return total


def first_kernel(
    narrow, left_ref, right_ref, weight_ref, next_ref, source_ref, out_ref, last_ref, x_ref, sems
):
    copies = carried(source_ref, source_ref.shape[0] - last_ref.shape[0], last_ref, sems)
    for copy in copies:
        copy.start()
    half = left_ref.shape[0]
    x_ref[:half] = left_ref[...]
    x_ref[half:] = right_ref[...]

    @pl.loop(0, weight_ref.shape[1] // narrow)
    def _(n):
        columns = pl.ds(n * narrow if narrow % 128 else pl.multiple_of(n * narrow, 128), narrow)
        out_ref[:, columns] = quarter_dots(x_ref, (weight_ref, next_ref), columns)

    for copy in copies:
        copy.wait()


def logits_kernel(
    narrow,
    spots,
    tensor_size,
    sum_in_ref,
    left_ref,
    right_ref,
    target_ref,
    weight_ref,
    next_ref,
    out_ref,
    x_ref,
    peak_ref,
    sum_ref,
    pick_ref,
    wanted_ref,
):
    half = left_ref.shape[0]
    rows = 2 * half
    share = target_ref.shape[1]
    group, tensor = lax.axis_index("group"), lax.axis_index("tensor")
    vocab = weight_ref.shape[1]
    shares = tensor_size // 4
    places = [
        (group ^ g) * tensor_size + shares * ((tensor % 4) ^ d) + i for g, d in spots for i in range(shares)
    ]
    for i, place in enumerate(places):
        wanted_ref[i * share : (i + 1) * share] = target_ref[place]
    wanted = wanted_ref[...] - (group * tensor_size + tensor) * vocab
    wanted_ref[...] = jnp.where((wanted >= 0) & (wanted < vocab), wanted, -1)
    x_ref[:half] = left_ref[...]
    x_ref[half:] = right_ref[...]
    peak_ref[...] = jnp.full_like(peak_ref, NEG)
    sum_ref[...] = jnp.zeros_like(sum_ref)
    pick_ref[...] = jnp.zeros_like(pick_ref)

    @pl.loop(0, weight_ref.shape[1] // narrow)
    def _(n):
        columns = pl.ds(n * narrow if narrow % 128 else pl.multiple_of(n * narrow, 128), narrow)
        logits = sum_in_ref[:, columns] + quarter_dots(x_ref, (weight_ref, next_ref), columns)
        parts = [logits[:, c : c + 128] for c in range(0, narrow, 128)]
        if narrow % 128:
            spare = jnp.full((rows, 128 - narrow % 128), NEG, F32)
            parts[-1] = jnp.concatenate([parts[-1], spare], axis=1)
        lane = lax.broadcasted_iota(jnp.int32, (rows, 128), 1) + n * narrow
        peak = peak_ref[...]
        higher = functools.reduce(jnp.maximum, parts, peak)
        total = sum_ref[...] * jnp.exp(peak - higher)
        picked = pick_ref[...]
        target = wanted_ref[...]
        for c, part in enumerate(parts):
            total = total + jnp.exp(part - higher)
            picked = picked + jnp.where(lane + c * 128 == target, part, 0.0)
        peak_ref[...] = higher
        sum_ref[...] = total
        pick_ref[...] = picked

    higher = peak_ref[...]
    peak = jnp.max(higher, axis=1, keepdims=True)
    sums = jnp.sum(sum_ref[...] * jnp.exp(higher - peak), axis=1, keepdims=True)
    pick = jnp.sum(pick_ref[...], axis=1, keepdims=True)
    row = lax.broadcasted_iota(jnp.int32, (rows, 128), 0)
    lane = lax.broadcasted_iota(jnp.int32, (rows, 128), 1)
    three = jnp.where(lane // share == 0, peak, jnp.where(lane // share == 1, sums, pick))
    three = jnp.where((row - lane) % share == 0, three, 0.0)
    for i, place in enumerate(places):
        out_ref[place] = jnp.sum(three[i * share : (i + 1) * share], axis=0, keepdims=True)


def final_kernel(share, live_ref, stats_ref, out_ref):
    stats = stats_ref[...].reshape(stats_ref.shape[0], 128)
    peak = jnp.max(stats, axis=0, keepdims=True)
    sums = pltpu.roll(stats, 128 - share, 1)
    picks = pltpu.roll(stats, 128 - 2 * share, 1)
    total = jnp.sum(sums * jnp.exp(stats - peak), axis=0, keepdims=True)
    values = jnp.sum(picks, axis=0, keepdims=True) - peak - jnp.log(total)
    out_ref[...] = jnp.where(live_ref[:1] > 0.0, values, 0.0)[0, :share]


def local(
    group_size,
    tensor_size,
    resp_query,
    resp_key,
    resp_value,
    prompt_keys,
    prompt_values,
    prompt_of,
    lengths,
    residual,
    out_weight,
    norm_gain,
    lm_weight,
    targets,
):
    rows, span = resp_query.shape
    heads = span // HEAD_DIM
    seq = rows // prompt_of.shape[0]
    key_rows = prompt_keys.shape[0]
    assert PLEN % key_rows == 0
    share = rows // tensor_size
    depth = out_weight.shape[1]
    vocab = lm_weight.shape[1]
    i32 = jnp.int32

    wanted = targets.reshape(-1, share, 1)
    above = list(range(2, group_size, 2))
    distances = list(range(group_size - 1, 0, -1))
    far_queries = [swap(resp_query, "group", a, group_size) for a in above]
    queries = {1: swap(resp_query, "group", 1, group_size)}
    far_queries = pl.pallas_call(
        functools.partial(pass_kernel, len(above)),
        out_shape=[jax.ShapeDtypeStruct(x.shape, x.dtype) for x in far_queries],
        in_specs=[vmem()] * len(above) + [anywhere()],
        out_specs=[vmem()] * len(above),
        compiler_params=params(1),
        name="pass",
    )(*map(held, far_queries), wanted)
    for a, x in zip(above, far_queries):
        queries[a] = x
        queries[a + 1] = swap(x, "group", 1, group_size)
    queries = [queries[d] for d in distances]
    inputs = (resp_query, resp_key, resp_value, prompt_keys, prompt_values)
    loaded = pl.pallas_call(
        functools.partial(load_kernel, len(inputs)),
        out_shape=[pltpu.VMEM(x.shape, x.dtype) for x in inputs],
        in_specs=[anywhere()] * (1 + len(inputs)),
        out_specs=[vmem()] * len(inputs),
        scratch_shapes=[pltpu.SemaphoreType.DMA((len(inputs),))],
        compiler_params=params(1),
        cost_estimate=cost(moved=2 * MIB),
        name="load",
    )(far_queries[0], *map(stored, inputs))
    query, own_keys, own_values, keys, values = map(held, loaded)
    answers = pl.pallas_call(
        functools.partial(prefix_kernel, heads, len(distances)),
        out_shape=[jax.ShapeDtypeStruct((rows, span + 128), BF16)] * len(distances),
        in_specs=[vmem()] * (len(distances) + 2),
        out_specs=[vmem()] * len(distances),
        compiler_params=params(8),
        name="prefix_attention",
    )(*map(held, queries), keys, values)
    got = [swap(x, "group", d, group_size) for x, d in zip(answers, distances)]
    own, live, weight = pl.pallas_call(
        functools.partial(own_kernel, heads, seq, share),
        out_shape=[
            jax.ShapeDtypeStruct((rows, span + 128), F32),
            jax.ShapeDtypeStruct((8, 128), F32),
            pltpu.VMEM(out_weight.shape, BF16),
        ],
        in_specs=[smem()] * 2 + [vmem()] * 5 + [anywhere()] * 2,
        out_specs=[vmem()] * 3,
        scratch_shapes=[pltpu.SemaphoreType.DMA((4,))],
        compiler_params=params(6),
        cost_estimate=cost(moved=8 * MIB),
        name="own_attention",
    )(
        stored(lengths),
        stored(prompt_of),
        query,
        own_keys,
        own_values,
        keys,
        values,
        stored(out_weight),
        answers[0],
    )

    def fetch(source, start, count, gate):
        return held(
            pl.pallas_call(
                functools.partial(fetch_kernel, start),
                out_shape=pltpu.VMEM((count, source.shape[1]), BF16),
                in_specs=[anywhere()] * 2,
                out_specs=vmem(),
                scratch_shapes=[pltpu.SemaphoreType.DMA((4,))],
                compiler_params=params(1),
                cost_estimate=cost(moved=count * source.shape[1] * 2),
                name="fetch",
            )(stored(source), gate)
        )

    half = depth // 2
    quarter = depth // 4
    wide = 1280 if half % 1280 == 0 else half
    block = rows // 4
    send_left, keep_left, send_right, keep_right = pl.pallas_call(
        functools.partial(project_kernel, heads, seq, wide, group_size, key_rows),
        out_shape=[
            jax.ShapeDtypeStruct((2, block, half), BF16),
            jax.ShapeDtypeStruct((2, block, half), F32),
        ]
        * 2,
        in_specs=[smem()] + [vmem()] * (2 + len(distances)),
        out_specs=[vmem()] * 4,
        scratch_shapes=[
            pltpu.VMEM((rows, span), BF16),
            pltpu.VMEM((4, block, wide), F32),
        ],
        compiler_params=params(6),
        name="project",
    )(stored(prompt_of), *map(held, (own, *got)), held(weight))

    def add(kernel, name, size, *operands, gates=()):
        return pl.pallas_call(
            kernel,
            out_shape=[jax.ShapeDtypeStruct(size, F32), jax.ShapeDtypeStruct(size, BF16)],
            in_specs=[vmem()] * len(operands) + [anywhere()] * len(gates),
            out_specs=[vmem()] * 2,
            compiler_params=params(2),
            name=name,
        )(*map(held, operands), *gates)

    early_rows = 1024 if half > 1024 else half // 2
    first_quarter = fetch(lm_weight, 0, early_rows, send_left)

    got_left = swap(send_left, "tensor", 1, tensor_size)
    got_right = swap(send_right, "tensor", 2, tensor_size)
    left, send_left = add(fold_kernel, "fold_left", (block, half), keep_left, got_left, gates=(first_quarter,))
    right, send_right = add(fold_kernel, "fold_right", (block, half), keep_right, got_right)
    got_left = swap(send_left, "tensor", 2, tensor_size)
    got_right = swap(send_right, "tensor", 1, tensor_size)
    total, send = add(side_kernel, "side", (block, depth), left, got_left, right, got_right)
    second_quarter = fetch(lm_weight, early_rows, half - early_rows, send)
    far = 4
    while 2 * far < tensor_size:
        total, send = add(
            add_kernel, "add", (block, depth), total, swap(send, "tensor", far, tensor_size)
        )
        far = 2 * far
    normed = pl.pallas_call(
        norm_kernel,
        out_shape=jax.ShapeDtypeStruct((block, depth), BF16),
        in_specs=[vmem()] * 2 + [anywhere()] + [vmem()] * 2,
        out_specs=vmem(),
        compiler_params=params(4),
        name="norm",
    )(
        *map(held, (residual.reshape(4, block, depth), norm_gain[None])),
        second_quarter,
        *map(held, (total, swap(send, "tensor", far, tensor_size))),
    )

    mesh_ids = [(g, t) for g in range(group_size) for t in range(tensor_size)]
    here = [(g, x) for g in [0] + above for x in (0, 1)]
    routes = {
        (g, x): [(a * tensor_size + b, (a ^ g) * tensor_size + (b ^ x)) for a, b in mesh_ids]
        for g, x in here
    }

    def around(x):
        sent = [lax.ppermute(x, ("group", "tensor"), routes[place]) for place in here[:0:-1]]
        return [x] + sent[::-1]

    sides = [around(normed)]
    near = swap(normed, "tensor", 2, tensor_size)
    sides.append(around(near))
    third = fetch(lm_weight, 2 * quarter, quarter, near)
    blocks = [x for pair in zip(*sides) for x in pair]
    count = len(blocks) * block
    halves = pl.pallas_call(
        functools.partial(tokens_kernel, len(blocks)),
        out_shape=[jax.ShapeDtypeStruct((count, half), BF16)] * 2,
        in_specs=[vmem()] * len(blocks) + [anywhere()],
        out_specs=[vmem()] * 2,
        compiler_params=params(2),
        name="tokens",
    )(*map(held, blocks), third)
    halves = [(tokens, swap(tokens, "group", 1, group_size)) for tokens in halves]
    order = [0, 2]
    spots = [(g + c, t + x) for c in (0, 1) for g, x in here for t in order]
    total_rows = 2 * count
    narrow = 1536 if vocab % 1536 == 0 else vocab
    limit = 10 if total_rows <= 256 else 24
    work = 2 * total_rows * (half) * vocab
    first, last = pl.pallas_call(
        functools.partial(first_kernel, narrow),
        out_shape=[pltpu.VMEM((total_rows, vocab), F32), pltpu.VMEM((quarter, vocab), BF16)],
        in_specs=[vmem()] * 4 + [anywhere()],
        out_specs=[vmem()] * 2,
        scratch_shapes=[
            pltpu.VMEM((total_rows, half), BF16),
            pltpu.SemaphoreType.DMA((4,)),
        ],
        compiler_params=params(limit),
        cost_estimate=cost(flops=work),
        name="logits_first",
    )(*map(held, (*halves[0], first_quarter, second_quarter)), stored(lm_weight))
    stats = pl.pallas_call(
        functools.partial(logits_kernel, vocab, spots, tensor_size),
        out_shape=jax.ShapeDtypeStruct((group_size * tensor_size, 1, 128), F32),
        in_specs=[vmem()] * 6,
        out_specs=vmem(),
        scratch_shapes=[pltpu.VMEM((total_rows, half), BF16)]
        + [pltpu.VMEM((total_rows, 128), F32)] * 3
        + [pltpu.VMEM((total_rows, 1), i32)],
        compiler_params=params(limit),
        cost_estimate=cost(flops=work),
        name="logits",
    )(*map(held, (first, *halves[1])), wanted, held(third), held(last))

    stats = lax.all_to_all(stats, ("group", "tensor"), 0, 0, tiled=True)
    return pl.pallas_call(
        functools.partial(final_kernel, share),
        out_shape=jax.ShapeDtypeStruct((share,), F32),
        in_specs=[vmem()] * 2,
        out_specs=vmem(),
        compiler_params=params(4),
        name="final",
    )(held(live), held(stats))


def solution(mesh):
    return jax.shard_map(
        functools.partial(local, mesh.shape["group"], mesh.shape["tensor"]),
        mesh=mesh,
        in_specs=(
            P("group", "tensor"),
            P("group", "tensor"),
            P("group", "tensor"),
            P("group", "tensor"),
            P("group", "tensor"),
            P("group"),
            P("group"),
            P("group", None),
            P("tensor", None),
            P(),
            P(None, ("group", "tensor")),
            P(),
        ),
        out_specs=P(("group", "tensor")),
        check_vma=False,
    )
```

```python
import functools

import jax
import jax.numpy as jnp
from jax import lax
from jax.experimental import pallas as pl
from jax.experimental.pallas import tpu as pltpu
from jax.sharding import PartitionSpec as P

HEAD_DIM = 128
PLEN = 512
NEG = -1e30
BF16 = jnp.bfloat16
F32 = jnp.float32
MIB = 1024 * 1024


def params(mib):
    return pltpu.CompilerParams(vmem_limit_bytes=mib * MIB)


def held(x):
    return pltpu.with_memory_space_constraint(x, pltpu.VMEM)


def stored(x):
    return pltpu.with_memory_space_constraint(x, pltpu.HBM)


def anywhere():
    return pl.BlockSpec(memory_space=pl.ANY)


def cost(flops=0, moved=0):
    return pl.CostEstimate(flops=flops, bytes_accessed=moved, transcendentals=0)


def vmem():
    return pl.BlockSpec(memory_space=pltpu.VMEM)


def smem():
    return pl.BlockSpec(memory_space=pltpu.SMEM)


def swap(x, axis, distance, size):
    return lax.ppermute(x, axis, [(i, i ^ distance) for i in range(size)])


def attend(jobs):
    factor = HEAD_DIM**-0.5
    scores = [
        lax.dot_general(q, k, (((1,), (1,)), ((), ())), preferred_element_type=F32)
        for q, k, _, _ in jobs
    ]
    scores = [
        s if job[3] is None else jnp.where(job[3], s, NEG) for s, job in zip(scores, jobs)
    ]
    peaks = [jnp.max(s, axis=1, keepdims=True) for s in scores]
    weights = [jnp.exp((s - peak) * factor) for s, peak in zip(scores, peaks)]
    weights = [
        w if job[3] is None else jnp.where(job[3], w, 0.0) for w, job in zip(weights, jobs)
    ]
    weights = [w.astype(BF16) for w in weights]
    totals = [jnp.sum(w.astype(F32), axis=1, keepdims=True) for w in weights]
    mixed = [
        jnp.dot(w, job[2], preferred_element_type=F32) for w, job in zip(weights, jobs)
    ]
    return [
        (m / total, peak * factor + jnp.log(total))
        for m, total, peak in zip(mixed, totals, peaks)
    ]


def pack_logs(logs, rows):
    lane = lax.broadcasted_iota(jnp.int32, (rows, 128), 1)
    packed = jnp.zeros((rows, 128), F32)
    for head, log in enumerate(logs):
        first = log.astype(BF16).astype(F32)
        second = (log - first).astype(BF16).astype(F32)
        third = log - first - second
        for part, value in enumerate((first, second, third)):
            packed = jnp.where(lane == 3 * head + part, value, packed)
    return packed.astype(BF16)


def pass_kernel(count, *refs):
    for ref, out_ref in zip(refs, refs[-count:]):
        out_ref[...] = ref[...]


def load_kernel(count, gate_ref, *refs):
    sems = refs[2 * count]
    copies = [
        pltpu.make_async_copy(refs[i], refs[count + i], sems.at[i]) for i in range(count)
    ]
    for copy in copies:
        copy.start()
    for copy in copies:
        copy.wait()


def carried(source_ref, start, out_ref, sems):
    count = sems.shape[0]
    rows = out_ref.shape[0] // count
    return [
        pltpu.make_async_copy(
            source_ref.at[pl.ds(start + i * rows, rows)], out_ref.at[pl.ds(i * rows, rows)], sems.at[i]
        )
        for i in range(count)
    ]


def own_kernel(
    heads,
    seq,
    share,
    lengths_ref,
    prompt_ref,
    q_ref,
    rk_ref,
    rv_ref,
    k_ref,
    v_ref,
    source_ref,
    gate_ref,
    own_ref,
    live_ref,
    weight_ref,
    sems,
):
    copies = carried(source_ref, 0, weight_ref, sems)
    for copy in copies:
        copy.start()
    rows = q_ref.shape[0]
    row = lax.broadcasted_iota(jnp.int32, (rows, rows), 0)
    col = lax.broadcasted_iota(jnp.int32, (rows, rows), 1)
    live = jnp.zeros((rows, rows), jnp.int32)
    for r in range(rows // seq):
        live = jnp.where(col // seq == r, lengths_ref[r], live)
    allowed = (row // seq == col // seq) & (col <= row) & (col % seq < live)
    parts = [slice(h * HEAD_DIM, (h + 1) * HEAD_DIM) for h in range(heads)]
    found = attend(
        [(q_ref[:, p], rk_ref[:, p], rv_ref[:, p], allowed) for p in parts]
        + [(q_ref[:, p], k_ref[:, p], v_ref[:, p], None) for p in parts]
    )
    here = wanted_prompts(seq, rows, prompt_ref) == lax.axis_index("group") * k_ref.shape[0] // PLEN
    lane = lax.broadcasted_iota(jnp.int32, (rows, 128), 1)
    packed = jnp.zeros((rows, 128), F32)
    for h, p in enumerate(parts):
        (first, log), (second, other) = found[h], found[heads + h]
        other = jnp.where(here, other, NEG)
        peak = jnp.maximum(log, other)
        left, right = jnp.exp(log - peak), jnp.exp(other - peak)
        own_ref[:, p] = (first * left + second * right) / (left + right)
        packed = jnp.where(lane == h, peak + jnp.log(left + right), packed)
    own_ref[:, heads * HEAD_DIM :] = packed
    token = lax.broadcasted_iota(jnp.int32, live_ref.shape, 1) + lax.axis_index("tensor") * share
    length = jnp.zeros(live_ref.shape, jnp.int32)
    for r in range(rows // seq):
        length = jnp.where(token // seq == r, lengths_ref[r], length)
    live_ref[...] = jnp.where(token % seq < length, 1.0, 0.0)
    for copy in copies:
        copy.wait()


def wanted_prompts(seq, rows, prompt_ref):
    row = lax.broadcasted_iota(jnp.int32, (rows, 1), 0)
    wanted = jnp.zeros((rows, 1), jnp.int32)
    for r in range(rows // seq):
        wanted = jnp.where(row // seq == r, prompt_ref[r], wanted)
    return wanted


def prefix_kernel(heads, count, *refs):
    q_refs, (k_ref, v_ref), out_refs = refs[:count], refs[count : count + 2], refs[count + 2 :]
    rows = q_refs[0].shape[0]
    parts = [slice(h * HEAD_DIM, (h + 1) * HEAD_DIM) for h in range(heads)]
    found = attend(
        [
            (jnp.concatenate([ref[:, p] for ref in q_refs], axis=0), k_ref[:, p], v_ref[:, p], None)
            for p in parts
        ]
    )
    for i in range(count):
        rung = slice(i * rows, (i + 1) * rows)
        for h, p in enumerate(parts):
            out_refs[i][:, p] = found[h][0][rung].astype(BF16)
        out_refs[i][:, heads * HEAD_DIM :] = pack_logs([log[rung] for _, log in found], rows)


def project_kernel(heads, seq, wide, group_size, key_rows, prompt_ref, own_ref, *refs):
    got_refs, refs = refs[: group_size - 1], refs[group_size - 1 :]
    weight_ref, send_left_ref, keep_left_ref, send_right_ref, keep_right_ref = refs[:5]
    attended_ref, partial_ref = refs[5:]
    rows = own_ref.shape[0]
    wanted = wanted_prompts(seq, rows, prompt_ref)
    group = lax.axis_index("group")
    holders = [(group ^ d) * key_rows // PLEN for d in range(group_size - 1, 0, -1)]
    for h in range(heads):
        part = slice(h * HEAD_DIM, (h + 1) * HEAD_DIM)
        at = heads * HEAD_DIM
        logs = [own_ref[:, at + h : at + h + 1]]
        values = [own_ref[:, part]]
        for holder, ref in zip(holders, got_refs):
            three = ref[:, at : at + 128].astype(F32)
            log = (
                three[:, 3 * h : 3 * h + 1]
                + three[:, 3 * h + 1 : 3 * h + 2]
                + three[:, 3 * h + 2 : 3 * h + 3]
            )
            logs.append(jnp.where(wanted == holder, log, NEG))
            values.append(ref[:, part].astype(F32))
        peak = functools.reduce(jnp.maximum, logs)
        loads = [jnp.exp(log - peak) for log in logs]
        total = functools.reduce(jnp.add, loads)
        mixed = functools.reduce(jnp.add, [w * v for w, v in zip(loads, values)])
        attended_ref[:, part] = (mixed / total).astype(BF16)

    me = lax.axis_index("tensor") % 4
    block = rows // 4
    half = send_left_ref.shape[2]

    def multiply(columns):
        partial = jnp.dot(attended_ref[...], weight_ref[:, columns], preferred_element_type=F32)
        for b in range(4):
            partial_ref[b] = partial[b * block : (b + 1) * block]

    @pl.loop(0, half // wide)
    def _(n):
        columns = pl.ds(pl.multiple_of(n * wide, 128), wide)
        multiply(columns)
        for i in range(2):
            keep_left_ref[i, :, columns] = partial_ref[me ^ (2 * i)]
            send_left_ref[i, :, columns] = partial_ref[me ^ (2 * i + 1)].astype(BF16)

    @pl.loop(0, half // wide)
    def _(n):
        columns = pl.ds(pl.multiple_of(n * wide, 128), wide)
        multiply(pl.ds(pl.multiple_of(half + n * wide, 128), wide))
        for i in range(2):
            keep_right_ref[i, :, columns] = partial_ref[me ^ i]
            send_right_ref[i, :, columns] = partial_ref[me ^ (i + 2)].astype(BF16)


def fold_kernel(keep_ref, got_ref, own_ref, send_ref):
    own_ref[...] = keep_ref[0] + got_ref[0].astype(F32)
    send_ref[...] = (keep_ref[1] + got_ref[1].astype(F32)).astype(BF16)


def side_kernel(left_ref, got_left_ref, right_ref, got_right_ref, own_ref, send_ref):
    half = left_ref.shape[1]
    for i, (ref, got_ref) in enumerate(((left_ref, got_left_ref), (right_ref, got_right_ref))):
        total = ref[...] + got_ref[...].astype(F32)
        own_ref[:, i * half : (i + 1) * half] = total
        send_ref[:, i * half : (i + 1) * half] = total.astype(BF16)


def add_kernel(own_ref, got_ref, out_ref, send_ref):
    total = own_ref[...] + got_ref[...].astype(F32)
    out_ref[...] = total
    send_ref[...] = total.astype(BF16)


def fetch_kernel(start, source_ref, gate_ref, out_ref, sems):
    copies = carried(source_ref, start, out_ref, sems)
    for copy in copies:
        copy.start()
    for copy in copies:
        copy.wait()


def tokens_kernel(count, *refs):
    out_refs = refs[-2:]
    rows, width = refs[0].shape[0], out_refs[0].shape[1]
    for half, out_ref in enumerate(out_refs):
        for i, ref in enumerate(refs[:count]):
            out_ref[i * rows : (i + 1) * rows] = ref[:, half * width : (half + 1) * width]


def norm_kernel(residual_ref, gain_ref, first_gate_ref, second_gate_ref, own_ref, got_ref, out_ref):
    hidden = residual_ref[lax.axis_index("tensor") % 4].astype(F32)
    hidden = hidden + (own_ref[...] + got_ref[...].astype(F32))
    squares = jnp.mean(hidden * hidden, axis=-1, keepdims=True)
    out_ref[...] = (hidden * lax.rsqrt(squares + 1e-06) * gain_ref[...].astype(F32)).astype(BF16)


def quarter_dots(x_ref, weight_refs, columns):
    start, total = 0, None
    for ref in weight_refs:
        stop = start + ref.shape[0]
        part = jnp.dot(x_ref[:, start:stop], ref[:, columns], preferred_element_type=F32)
        total = part if total is None else total + part
        start = stop
    return total


def first_kernel(
    narrow, left_ref, right_ref, weight_ref, next_ref, source_ref, out_ref, last_ref, x_ref, sems
):
    copies = carried(source_ref, source_ref.shape[0] - last_ref.shape[0], last_ref, sems)
    for copy in copies:
        copy.start()
    half = left_ref.shape[0]
    x_ref[:half] = left_ref[...]
    x_ref[half:] = right_ref[...]

    @pl.loop(0, weight_ref.shape[1] // narrow)
    def _(n):
        columns = pl.ds(n * narrow if narrow % 128 else pl.multiple_of(n * narrow, 128), narrow)
        out_ref[:, columns] = quarter_dots(x_ref, (weight_ref, next_ref), columns)

    for copy in copies:
        copy.wait()


def logits_kernel(
    narrow,
    spots,
    tensor_size,
    sum_in_ref,
    left_ref,
    right_ref,
    target_ref,
    weight_ref,
    next_ref,
    out_ref,
    x_ref,
    peak_ref,
    sum_ref,
    pick_ref,
    wanted_ref,
):
    half = left_ref.shape[0]
    rows = 2 * half
    share = target_ref.shape[1]
    group, tensor = lax.axis_index("group"), lax.axis_index("tensor")
    vocab = weight_ref.shape[1]
    shares = tensor_size // 4
    places = [
        (group ^ g) * tensor_size + shares * ((tensor % 4) ^ d) + i for g, d in spots for i in range(shares)
    ]
    for i, place in enumerate(places):
        wanted_ref[i * share : (i + 1) * share] = target_ref[place]
    wanted = wanted_ref[...] - (group * tensor_size + tensor) * vocab
    wanted_ref[...] = jnp.where((wanted >= 0) & (wanted < vocab), wanted, -1)
    x_ref[:half] = left_ref[...]
    x_ref[half:] = right_ref[...]
    peak_ref[...] = jnp.full_like(peak_ref, NEG)
    sum_ref[...] = jnp.zeros_like(sum_ref)
    pick_ref[...] = jnp.zeros_like(pick_ref)

    @pl.loop(0, weight_ref.shape[1] // narrow)
    def _(n):
        columns = pl.ds(n * narrow if narrow % 128 else pl.multiple_of(n * narrow, 128), narrow)
        logits = sum_in_ref[:, columns] + quarter_dots(x_ref, (weight_ref, next_ref), columns)
        parts = [logits[:, c : c + 128] for c in range(0, narrow, 128)]
        if narrow % 128:
            spare = jnp.full((rows, 128 - narrow % 128), NEG, F32)
            parts[-1] = jnp.concatenate([parts[-1], spare], axis=1)
        lane = lax.broadcasted_iota(jnp.int32, (rows, 128), 1) + n * narrow
        peak = peak_ref[...]
        higher = functools.reduce(jnp.maximum, parts, peak)
        total = sum_ref[...] * jnp.exp(peak - higher)
        picked = pick_ref[...]
        target = wanted_ref[...]
        for c, part in enumerate(parts):
            total = total + jnp.exp(part - higher)
            picked = picked + jnp.where(lane + c * 128 == target, part, 0.0)
        peak_ref[...] = higher
        sum_ref[...] = total
        pick_ref[...] = picked

    higher = peak_ref[...]
    peak = jnp.max(higher, axis=1, keepdims=True)
    sums = jnp.sum(sum_ref[...] * jnp.exp(higher - peak), axis=1, keepdims=True)
    pick = jnp.sum(pick_ref[...], axis=1, keepdims=True)
    row = lax.broadcasted_iota(jnp.int32, (rows, 128), 0)
    lane = lax.broadcasted_iota(jnp.int32, (rows, 128), 1)
    three = jnp.where(lane // share == 0, peak, jnp.where(lane // share == 1, sums, pick))
    three = jnp.where((row - lane) % share == 0, three, 0.0)
    for i, place in enumerate(places):
        out_ref[place] = jnp.sum(three[i * share : (i + 1) * share], axis=0, keepdims=True)


def final_kernel(share, live_ref, stats_ref, out_ref):
    stats = stats_ref[...].reshape(stats_ref.shape[0], 128)
    peak = jnp.max(stats, axis=0, keepdims=True)
    sums = pltpu.roll(stats, 128 - share, 1)
    picks = pltpu.roll(stats, 128 - 2 * share, 1)
    total = jnp.sum(sums * jnp.exp(stats - peak), axis=0, keepdims=True)
    values = jnp.sum(picks, axis=0, keepdims=True) - peak - jnp.log(total)
    out_ref[...] = jnp.where(live_ref[:1] > 0.0, values, 0.0)[0, :share]


def local(
    group_size,
    tensor_size,
    resp_query,
    resp_key,
    resp_value,
    prompt_keys,
    prompt_values,
    prompt_of,
    lengths,
    residual,
    out_weight,
    norm_gain,
    lm_weight,
    targets,
):
    rows, span = resp_query.shape
    heads = span // HEAD_DIM
    seq = rows // prompt_of.shape[0]
    key_rows = prompt_keys.shape[0]
    assert PLEN % key_rows == 0
    share = rows // tensor_size
    depth = out_weight.shape[1]
    vocab = lm_weight.shape[1]
    i32 = jnp.int32

    wanted = targets.reshape(-1, share, 1)
    above = list(range(2, group_size, 2))
    distances = list(range(group_size - 1, 0, -1))
    far_queries = [swap(resp_query, "group", a, group_size) for a in above]
    queries = {1: swap(resp_query, "group", 1, group_size)}
    far_queries = pl.pallas_call(
        functools.partial(pass_kernel, len(above)),
        out_shape=[jax.ShapeDtypeStruct(x.shape, x.dtype) for x in far_queries],
        in_specs=[vmem()] * len(above) + [anywhere()],
        out_specs=[vmem()] * len(above),
        compiler_params=params(1),
        name="pass",
    )(*map(held, far_queries), wanted)
    for a, x in zip(above, far_queries):
        queries[a] = x
        queries[a + 1] = swap(x, "group", 1, group_size)
    queries = [queries[d] for d in distances]
    inputs = (resp_query, resp_key, resp_value, prompt_keys, prompt_values)
    loaded = pl.pallas_call(
        functools.partial(load_kernel, len(inputs)),
        out_shape=[pltpu.VMEM(x.shape, x.dtype) for x in inputs],
        in_specs=[anywhere()] * (1 + len(inputs)),
        out_specs=[vmem()] * len(inputs),
        scratch_shapes=[pltpu.SemaphoreType.DMA((len(inputs),))],
        compiler_params=params(1),
        cost_estimate=cost(moved=2 * MIB),
        name="load",
    )(far_queries[0], *map(stored, inputs))
    query, own_keys, own_values, keys, values = map(held, loaded)
    answers = pl.pallas_call(
        functools.partial(prefix_kernel, heads, len(distances)),
        out_shape=[jax.ShapeDtypeStruct((rows, span + 128), BF16)] * len(distances),
        in_specs=[vmem()] * (len(distances) + 2),
        out_specs=[vmem()] * len(distances),
        compiler_params=params(8),
        name="prefix_attention",
    )(*map(held, queries), keys, values)
    got = [swap(x, "group", d, group_size) for x, d in zip(answers, distances)]
    own, live, weight = pl.pallas_call(
        functools.partial(own_kernel, heads, seq, share),
        out_shape=[
            jax.ShapeDtypeStruct((rows, span + 128), F32),
            jax.ShapeDtypeStruct((8, 128), F32),
            pltpu.VMEM(out_weight.shape, BF16),
        ],
        in_specs=[smem()] * 2 + [vmem()] * 5 + [anywhere()] * 2,
        out_specs=[vmem()] * 3,
        scratch_shapes=[pltpu.SemaphoreType.DMA((4,))],
        compiler_params=params(6),
        cost_estimate=cost(moved=8 * MIB),
        name="own_attention",
    )(
        stored(lengths),
        stored(prompt_of),
        query,
        own_keys,
        own_values,
        keys,
        values,
        stored(out_weight),
        answers[0],
    )

    def fetch(source, start, count, gate):
        return held(
            pl.pallas_call(
                functools.partial(fetch_kernel, start),
                out_shape=pltpu.VMEM((count, source.shape[1]), BF16),
                in_specs=[anywhere()] * 2,
                out_specs=vmem(),
                scratch_shapes=[pltpu.SemaphoreType.DMA((4,))],
                compiler_params=params(1),
                cost_estimate=cost(moved=count * source.shape[1] * 2),
                name="fetch",
            )(stored(source), gate)
        )

    half = depth // 2
    quarter = depth // 4
    wide = 1280 if half % 1280 == 0 else half
    block = rows // 4
    send_left, keep_left, send_right, keep_right = pl.pallas_call(
        functools.partial(project_kernel, heads, seq, wide, group_size, key_rows),
        out_shape=[
            jax.ShapeDtypeStruct((2, block, half), BF16),
            jax.ShapeDtypeStruct((2, block, half), F32),
        ]
        * 2,
        in_specs=[smem()] + [vmem()] * (2 + len(distances)),
        out_specs=[vmem()] * 4,
        scratch_shapes=[
            pltpu.VMEM((rows, span), BF16),
            pltpu.VMEM((4, block, wide), F32),
        ],
        compiler_params=params(6),
        name="project",
    )(stored(prompt_of), *map(held, (own, *got)), held(weight))

    def add(kernel, name, size, *operands):
        return pl.pallas_call(
            kernel,
            out_shape=[jax.ShapeDtypeStruct(size, F32), jax.ShapeDtypeStruct(size, BF16)],
            in_specs=[vmem()] * len(operands),
            out_specs=[vmem()] * 2,
            compiler_params=params(2),
            name=name,
        )(*map(held, operands))


    got_left = swap(send_left, "tensor", 1, tensor_size)
    got_right = swap(send_right, "tensor", 2, tensor_size)
    left, send_left = add(fold_kernel, "fold_left", (block, half), keep_left, got_left)
    right, send_right = add(fold_kernel, "fold_right", (block, half), keep_right, got_right)
    got_left = swap(send_left, "tensor", 2, tensor_size)
    got_right = swap(send_right, "tensor", 1, tensor_size)
    total, send = add(side_kernel, "side", (block, depth), left, got_left, right, got_right)
    first_quarter = fetch(lm_weight, 0, quarter, send)
    second_quarter = fetch(lm_weight, quarter, quarter, send)
    far = 4
    while 2 * far < tensor_size:
        total, send = add(
            add_kernel, "add", (block, depth), total, swap(send, "tensor", far, tensor_size)
        )
        far = 2 * far
    normed = pl.pallas_call(
        norm_kernel,
        out_shape=jax.ShapeDtypeStruct((block, depth), BF16),
        in_specs=[vmem()] * 2 + [anywhere()] * 2 + [vmem()] * 2,
        out_specs=vmem(),
        compiler_params=params(4),
        name="norm",
    )(
        *map(held, (residual.reshape(4, block, depth), norm_gain[None])),
        first_quarter,
        second_quarter,
        *map(held, (total, swap(send, "tensor", far, tensor_size))),
    )

    mesh_ids = [(g, t) for g in range(group_size) for t in range(tensor_size)]
    here = [(g, x) for g in [0] + above for x in (0, 1)]
    routes = {
        (g, x): [(a * tensor_size + b, (a ^ g) * tensor_size + (b ^ x)) for a, b in mesh_ids]
        for g, x in here
    }

    def around(x):
        sent = [lax.ppermute(x, ("group", "tensor"), routes[place]) for place in here[:0:-1]]
        return [x] + sent[::-1]

    sides = [around(normed)]
    near = swap(normed, "tensor", 2, tensor_size)
    sides.append(around(near))
    third = fetch(lm_weight, 2 * quarter, quarter, near)
    blocks = [x for pair in zip(*sides) for x in pair]
    count = len(blocks) * block
    halves = pl.pallas_call(
        functools.partial(tokens_kernel, len(blocks)),
        out_shape=[jax.ShapeDtypeStruct((count, half), BF16)] * 2,
        in_specs=[vmem()] * len(blocks) + [anywhere()],
        out_specs=[vmem()] * 2,
        compiler_params=params(2),
        name="tokens",
    )(*map(held, blocks), third)
    halves = [(tokens, swap(tokens, "group", 1, group_size)) for tokens in halves]
    order = [0, 2]
    spots = [(g + c, t + x) for c in (0, 1) for g, x in here for t in order]
    total_rows = 2 * count
    narrow = 1536 if vocab % 1536 == 0 else vocab
    limit = 10 if total_rows <= 256 else 24
    work = 2 * total_rows * (half) * vocab
    first, last = pl.pallas_call(
        functools.partial(first_kernel, narrow),
        out_shape=[pltpu.VMEM((total_rows, vocab), F32), pltpu.VMEM((quarter, vocab), BF16)],
        in_specs=[vmem()] * 4 + [anywhere()],
        out_specs=[vmem()] * 2,
        scratch_shapes=[
            pltpu.VMEM((total_rows, half), BF16),
            pltpu.SemaphoreType.DMA((4,)),
        ],
        compiler_params=params(limit),
        cost_estimate=cost(flops=work),
        name="logits_first",
    )(*map(held, (*halves[0], first_quarter, second_quarter)), stored(lm_weight))
    stats = pl.pallas_call(
        functools.partial(logits_kernel, vocab, spots, tensor_size),
        out_shape=jax.ShapeDtypeStruct((group_size * tensor_size, 1, 128), F32),
        in_specs=[vmem()] * 6,
        out_specs=vmem(),
        scratch_shapes=[pltpu.VMEM((total_rows, half), BF16)]
        + [pltpu.VMEM((total_rows, 128), F32)] * 3
        + [pltpu.VMEM((total_rows, 1), i32)],
        compiler_params=params(limit),
        cost_estimate=cost(flops=work),
        name="logits",
    )(*map(held, (first, *halves[1])), wanted, held(third), held(last))

    stats = lax.all_to_all(stats, ("group", "tensor"), 0, 0, tiled=True)
    return pl.pallas_call(
        functools.partial(final_kernel, share),
        out_shape=jax.ShapeDtypeStruct((share,), F32),
        in_specs=[vmem()] * 2,
        out_specs=vmem(),
        compiler_params=params(4),
        name="final",
    )(held(live), held(stats))


def solution(mesh):
    return jax.shard_map(
        functools.partial(local, mesh.shape["group"], mesh.shape["tensor"]),
        mesh=mesh,
        in_specs=(
            P("group", "tensor"),
            P("group", "tensor"),
            P("group", "tensor"),
            P("group", "tensor"),
            P("group", "tensor"),
            P("group"),
            P("group"),
            P("group", None),
            P("tensor", None),
            P(),
            P(None, ("group", "tensor")),
            P(),
        ),
        out_specs=P(("group", "tensor")),
        check_vma=False,
    )
```

```python
import functools

import jax
import jax.numpy as jnp
from jax import lax
from jax.experimental import pallas as pl
from jax.experimental.pallas import tpu as pltpu
from jax.sharding import PartitionSpec as P

HEAD_DIM = 128
PLEN = 512
NEG = -1e30
BF16 = jnp.bfloat16
F32 = jnp.float32
MIB = 1024 * 1024


def params(mib):
    return pltpu.CompilerParams(vmem_limit_bytes=mib * MIB)


def held(x):
    return pltpu.with_memory_space_constraint(x, pltpu.VMEM)


def stored(x):
    return pltpu.with_memory_space_constraint(x, pltpu.HBM)


def anywhere():
    return pl.BlockSpec(memory_space=pl.ANY)


def cost(flops=0, moved=0):
    return pl.CostEstimate(flops=flops, bytes_accessed=moved, transcendentals=0)


def vmem():
    return pl.BlockSpec(memory_space=pltpu.VMEM)


def smem():
    return pl.BlockSpec(memory_space=pltpu.SMEM)


def swap(x, axis, distance, size):
    return lax.ppermute(x, axis, [(i, i ^ distance) for i in range(size)])


def attend(jobs):
    factor = HEAD_DIM**-0.5
    scores = [
        lax.dot_general(q, k, (((1,), (1,)), ((), ())), preferred_element_type=F32)
        for q, k, _, _ in jobs
    ]
    scores = [
        s if job[3] is None else jnp.where(job[3], s, NEG) for s, job in zip(scores, jobs)
    ]
    peaks = [jnp.max(s, axis=1, keepdims=True) for s in scores]
    weights = [jnp.exp((s - peak) * factor) for s, peak in zip(scores, peaks)]
    weights = [
        w if job[3] is None else jnp.where(job[3], w, 0.0) for w, job in zip(weights, jobs)
    ]
    weights = [w.astype(BF16) for w in weights]
    totals = [jnp.sum(w.astype(F32), axis=1, keepdims=True) for w in weights]
    mixed = [
        jnp.dot(w, job[2], preferred_element_type=F32) for w, job in zip(weights, jobs)
    ]
    return [
        (m / total, peak * factor + jnp.log(total))
        for m, total, peak in zip(mixed, totals, peaks)
    ]


def pack_logs(logs, rows):
    lane = lax.broadcasted_iota(jnp.int32, (rows, 128), 1)
    packed = jnp.zeros((rows, 128), F32)
    for head, log in enumerate(logs):
        first = log.astype(BF16).astype(F32)
        second = (log - first).astype(BF16).astype(F32)
        third = log - first - second
        for part, value in enumerate((first, second, third)):
            packed = jnp.where(lane == 3 * head + part, value, packed)
    return packed.astype(BF16)


def pass_kernel(count, *refs):
    for ref, out_ref in zip(refs, refs[-count:]):
        out_ref[...] = ref[...]


def load_kernel(count, gate_ref, *refs):
    sems = refs[2 * count]
    copies = [
        pltpu.make_async_copy(refs[i], refs[count + i], sems.at[i]) for i in range(count)
    ]
    for copy in copies:
        copy.start()
    for copy in copies:
        copy.wait()


def carried(source_ref, start, out_ref, sems):
    count = sems.shape[0]
    rows = out_ref.shape[0] // count
    return [
        pltpu.make_async_copy(
            source_ref.at[pl.ds(start + i * rows, rows)], out_ref.at[pl.ds(i * rows, rows)], sems.at[i]
        )
        for i in range(count)
    ]


def own_kernel(
    heads,
    seq,
    share,
    lengths_ref,
    prompt_ref,
    q_ref,
    rk_ref,
    rv_ref,
    k_ref,
    v_ref,
    source_ref,
    gate_ref,
    own_ref,
    live_ref,
    weight_ref,
    sems,
):
    copies = carried(source_ref, 0, weight_ref, sems)
    for copy in copies:
        copy.start()
    rows = q_ref.shape[0]
    row = lax.broadcasted_iota(jnp.int32, (rows, rows), 0)
    col = lax.broadcasted_iota(jnp.int32, (rows, rows), 1)
    live = jnp.zeros((rows, rows), jnp.int32)
    for r in range(rows // seq):
        live = jnp.where(col // seq == r, lengths_ref[r], live)
    allowed = (row // seq == col // seq) & (col <= row) & (col % seq < live)
    parts = [slice(h * HEAD_DIM, (h + 1) * HEAD_DIM) for h in range(heads)]
    found = attend(
        [(q_ref[:, p], rk_ref[:, p], rv_ref[:, p], allowed) for p in parts]
        + [(q_ref[:, p], k_ref[:, p], v_ref[:, p], None) for p in parts]
    )
    here = wanted_prompts(seq, rows, prompt_ref) == lax.axis_index("group") * k_ref.shape[0] // PLEN
    lane = lax.broadcasted_iota(jnp.int32, (rows, 128), 1)
    packed = jnp.zeros((rows, 128), F32)
    for h, p in enumerate(parts):
        (first, log), (second, other) = found[h], found[heads + h]
        other = jnp.where(here, other, NEG)
        peak = jnp.maximum(log, other)
        left, right = jnp.exp(log - peak), jnp.exp(other - peak)
        own_ref[:, p] = (first * left + second * right) / (left + right)
        packed = jnp.where(lane == h, peak + jnp.log(left + right), packed)
    own_ref[:, heads * HEAD_DIM :] = packed
    token = lax.broadcasted_iota(jnp.int32, live_ref.shape, 1) + lax.axis_index("tensor") * share
    length = jnp.zeros(live_ref.shape, jnp.int32)
    for r in range(rows // seq):
        length = jnp.where(token // seq == r, lengths_ref[r], length)
    live_ref[...] = jnp.where(token % seq < length, 1.0, 0.0)
    for copy in copies:
        copy.wait()


def wanted_prompts(seq, rows, prompt_ref):
    row = lax.broadcasted_iota(jnp.int32, (rows, 1), 0)
    wanted = jnp.zeros((rows, 1), jnp.int32)
    for r in range(rows // seq):
        wanted = jnp.where(row // seq == r, prompt_ref[r], wanted)
    return wanted


def prefix_kernel(heads, count, *refs):
    q_refs, (k_ref, v_ref), out_refs = refs[:count], refs[count : count + 2], refs[count + 2 :]
    rows = q_refs[0].shape[0]
    parts = [slice(h * HEAD_DIM, (h + 1) * HEAD_DIM) for h in range(heads)]
    found = attend(
        [
            (jnp.concatenate([ref[:, p] for ref in q_refs], axis=0), k_ref[:, p], v_ref[:, p], None)
            for p in parts
        ]
    )
    for i in range(count):
        rung = slice(i * rows, (i + 1) * rows)
        for h, p in enumerate(parts):
            out_refs[i][:, p] = found[h][0][rung].astype(BF16)
        out_refs[i][:, heads * HEAD_DIM :] = pack_logs([log[rung] for _, log in found], rows)


def project_kernel(heads, seq, wide, group_size, key_rows, prompt_ref, own_ref, *refs):
    got_refs, refs = refs[: group_size - 1], refs[group_size - 1 :]
    weight_ref, send_left_ref, keep_left_ref, send_right_ref, keep_right_ref = refs[:5]
    attended_ref, partial_ref = refs[5:]
    rows = own_ref.shape[0]
    wanted = wanted_prompts(seq, rows, prompt_ref)
    group = lax.axis_index("group")
    holders = [(group ^ d) * key_rows // PLEN for d in range(group_size - 1, 0, -1)]
    for h in range(heads):
        part = slice(h * HEAD_DIM, (h + 1) * HEAD_DIM)
        at = heads * HEAD_DIM
        logs = [own_ref[:, at + h : at + h + 1]]
        values = [own_ref[:, part]]
        for holder, ref in zip(holders, got_refs):
            three = ref[:, at : at + 128].astype(F32)
            log = (
                three[:, 3 * h : 3 * h + 1]
                + three[:, 3 * h + 1 : 3 * h + 2]
                + three[:, 3 * h + 2 : 3 * h + 3]
            )
            logs.append(jnp.where(wanted == holder, log, NEG))
            values.append(ref[:, part].astype(F32))
        peak = functools.reduce(jnp.maximum, logs)
        loads = [jnp.exp(log - peak) for log in logs]
        total = functools.reduce(jnp.add, loads)
        mixed = functools.reduce(jnp.add, [w * v for w, v in zip(loads, values)])
        attended_ref[:, part] = (mixed / total).astype(BF16)

    me = lax.axis_index("tensor") % 4
    block = rows // 4
    half = send_left_ref.shape[2]

    def multiply(columns):
        partial = jnp.dot(attended_ref[...], weight_ref[:, columns], preferred_element_type=F32)
        for b in range(4):
            partial_ref[b] = partial[b * block : (b + 1) * block]

    @pl.loop(0, half // wide)
    def _(n):
        columns = pl.ds(pl.multiple_of(n * wide, 128), wide)
        multiply(columns)
        for i in range(2):
            keep_left_ref[i, :, columns] = partial_ref[me ^ (2 * i)]
            send_left_ref[i, :, columns] = partial_ref[me ^ (2 * i + 1)].astype(BF16)

    @pl.loop(0, half // wide)
    def _(n):
        columns = pl.ds(pl.multiple_of(n * wide, 128), wide)
        multiply(pl.ds(pl.multiple_of(half + n * wide, 128), wide))
        for i in range(2):
            keep_right_ref[i, :, columns] = partial_ref[me ^ i]
            send_right_ref[i, :, columns] = partial_ref[me ^ (i + 2)].astype(BF16)


def fold_kernel(keep_ref, got_ref, own_ref, send_ref):
    own_ref[...] = keep_ref[0] + got_ref[0].astype(F32)
    send_ref[...] = (keep_ref[1] + got_ref[1].astype(F32)).astype(BF16)


def side_kernel(left_ref, got_left_ref, right_ref, got_right_ref, own_ref, send_ref):
    half = left_ref.shape[1]
    for i, (ref, got_ref) in enumerate(((left_ref, got_left_ref), (right_ref, got_right_ref))):
        total = ref[...] + got_ref[...].astype(F32)
        own_ref[:, i * half : (i + 1) * half] = total
        send_ref[:, i * half : (i + 1) * half] = total.astype(BF16)


def add_kernel(own_ref, got_ref, out_ref, send_ref):
    total = own_ref[...] + got_ref[...].astype(F32)
    out_ref[...] = total
    send_ref[...] = total.astype(BF16)


def fetch_kernel(start, source_ref, gate_ref, out_ref, sems):
    copies = carried(source_ref, start, out_ref, sems)
    for copy in copies:
        copy.start()
    for copy in copies:
        copy.wait()


def tokens_kernel(count, *refs):
    out_refs = refs[-2:]
    rows, width = refs[0].shape[0], out_refs[0].shape[1]
    for half, out_ref in enumerate(out_refs):
        for i, ref in enumerate(refs[:count]):
            out_ref[i * rows : (i + 1) * rows] = ref[:, half * width : (half + 1) * width]


def norm_kernel(residual_ref, gain_ref, first_gate_ref, second_gate_ref, own_ref, got_ref, out_ref):
    hidden = residual_ref[lax.axis_index("tensor") % 4].astype(F32)
    hidden = hidden + (own_ref[...] + got_ref[...].astype(F32))
    squares = jnp.mean(hidden * hidden, axis=-1, keepdims=True)
    out_ref[...] = (hidden * lax.rsqrt(squares + 1e-06) * gain_ref[...].astype(F32)).astype(BF16)


def quarter_dots(x_ref, weight_refs, columns):
    start, total = 0, None
    for ref in weight_refs:
        stop = start + ref.shape[0]
        part = jnp.dot(x_ref[:, start:stop], ref[:, columns], preferred_element_type=F32)
        total = part if total is None else total + part
        start = stop
    return total


def first_kernel(
    narrow, left_ref, right_ref, weight_ref, next_ref, source_ref, out_ref, last_ref, x_ref, sems
):
    copies = carried(source_ref, source_ref.shape[0] - last_ref.shape[0], last_ref, sems)
    for copy in copies:
        copy.start()
    half = left_ref.shape[0]
    x_ref[:half] = left_ref[...]
    x_ref[half:] = right_ref[...]

    @pl.loop(0, weight_ref.shape[1] // narrow)
    def _(n):
        columns = pl.ds(n * narrow if narrow % 128 else pl.multiple_of(n * narrow, 128), narrow)
        out_ref[:, columns] = quarter_dots(x_ref, (weight_ref, next_ref), columns)

    for copy in copies:
        copy.wait()


def logits_kernel(
    narrow,
    spots,
    tensor_size,
    sum_in_ref,
    left_ref,
    right_ref,
    target_ref,
    weight_ref,
    next_ref,
    out_ref,
    x_ref,
    peak_ref,
    sum_ref,
    pick_ref,
    wanted_ref,
):
    half = left_ref.shape[0]
    rows = 2 * half
    share = target_ref.shape[1]
    group, tensor = lax.axis_index("group"), lax.axis_index("tensor")
    vocab = weight_ref.shape[1]
    shares = tensor_size // 4
    places = [
        (group ^ g) * tensor_size + shares * ((tensor % 4) ^ d) + i for g, d in spots for i in range(shares)
    ]
    for i, place in enumerate(places):
        wanted_ref[i * share : (i + 1) * share] = target_ref[place]
    wanted = wanted_ref[...] - (group * tensor_size + tensor) * vocab
    wanted_ref[...] = jnp.where((wanted >= 0) & (wanted < vocab), wanted, -1)
    x_ref[:half] = left_ref[...]
    x_ref[half:] = right_ref[...]
    peak_ref[...] = jnp.full_like(peak_ref, NEG)
    sum_ref[...] = jnp.zeros_like(sum_ref)
    pick_ref[...] = jnp.zeros_like(pick_ref)

    @pl.loop(0, weight_ref.shape[1] // narrow)
    def _(n):
        columns = pl.ds(n * narrow if narrow % 128 else pl.multiple_of(n * narrow, 128), narrow)
        logits = sum_in_ref[:, columns] + quarter_dots(x_ref, (weight_ref, next_ref), columns)
        parts = [logits[:, c : c + 128] for c in range(0, narrow, 128)]
        if narrow % 128:
            spare = jnp.full((rows, 128 - narrow % 128), NEG, F32)
            parts[-1] = jnp.concatenate([parts[-1], spare], axis=1)
        lane = lax.broadcasted_iota(jnp.int32, (rows, 128), 1) + n * narrow
        peak = peak_ref[...]
        higher = functools.reduce(jnp.maximum, parts, peak)
        total = sum_ref[...] * jnp.exp(peak - higher)
        picked = pick_ref[...]
        target = wanted_ref[...]
        for c, part in enumerate(parts):
            total = total + jnp.exp(part - higher)
            picked = picked + jnp.where(lane + c * 128 == target, part, 0.0)
        peak_ref[...] = higher
        sum_ref[...] = total
        pick_ref[...] = picked

    higher = peak_ref[...]
    peak = jnp.max(higher, axis=1, keepdims=True)
    sums = jnp.sum(sum_ref[...] * jnp.exp(higher - peak), axis=1, keepdims=True)
    pick = jnp.sum(pick_ref[...], axis=1, keepdims=True)
    row = lax.broadcasted_iota(jnp.int32, (rows, 128), 0)
    lane = lax.broadcasted_iota(jnp.int32, (rows, 128), 1)
    three = jnp.where(lane // share == 0, peak, jnp.where(lane // share == 1, sums, pick))
    three = jnp.where((row - lane) % share == 0, three, 0.0)
    for i, place in enumerate(places):
        out_ref[place] = jnp.sum(three[i * share : (i + 1) * share], axis=0, keepdims=True)


def final_kernel(share, live_ref, stats_ref, out_ref):
    stats = stats_ref[...].reshape(stats_ref.shape[0], 128)
    peak = jnp.max(stats, axis=0, keepdims=True)
    sums = pltpu.roll(stats, 128 - share, 1)
    picks = pltpu.roll(stats, 128 - 2 * share, 1)
    total = jnp.sum(sums * jnp.exp(stats - peak), axis=0, keepdims=True)
    values = jnp.sum(picks, axis=0, keepdims=True) - peak - jnp.log(total)
    out_ref[...] = jnp.where(live_ref[:1] > 0.0, values, 0.0)[0, :share]


def local(
    group_size,
    tensor_size,
    resp_query,
    resp_key,
    resp_value,
    prompt_keys,
    prompt_values,
    prompt_of,
    lengths,
    residual,
    out_weight,
    norm_gain,
    lm_weight,
    targets,
):
    rows, span = resp_query.shape
    heads = span // HEAD_DIM
    seq = rows // prompt_of.shape[0]
    key_rows = prompt_keys.shape[0]
    assert PLEN % key_rows == 0
    share = rows // tensor_size
    depth = out_weight.shape[1]
    vocab = lm_weight.shape[1]
    i32 = jnp.int32

    wanted = targets.reshape(-1, share, 1)
    gain = norm_gain[None]
    above = list(range(2, group_size, 2))
    distances = list(range(group_size - 1, 0, -1))
    far_queries = [swap(resp_query, "group", a, group_size) for a in above]
    queries = {1: swap(resp_query, "group", 1, group_size)}
    far_queries = pl.pallas_call(
        functools.partial(pass_kernel, len(above)),
        out_shape=[jax.ShapeDtypeStruct(x.shape, x.dtype) for x in far_queries],
        in_specs=[vmem()] * len(above) + [anywhere()] * 2,
        out_specs=[vmem()] * len(above),
        compiler_params=params(1),
        name="pass",
    )(*map(held, far_queries), wanted, gain)
    for a, x in zip(above, far_queries):
        queries[a] = x
        queries[a + 1] = swap(x, "group", 1, group_size)
    queries = [queries[d] for d in distances]
    inputs = (resp_query, resp_key, resp_value, prompt_keys, prompt_values)
    loaded = pl.pallas_call(
        functools.partial(load_kernel, len(inputs)),
        out_shape=[pltpu.VMEM(x.shape, x.dtype) for x in inputs],
        in_specs=[anywhere()] * (1 + len(inputs)),
        out_specs=[vmem()] * len(inputs),
        scratch_shapes=[pltpu.SemaphoreType.DMA((len(inputs),))],
        compiler_params=params(1),
        cost_estimate=cost(moved=2 * MIB),
        name="load",
    )(far_queries[0], *map(stored, inputs))
    query, own_keys, own_values, keys, values = map(held, loaded)
    answers = pl.pallas_call(
        functools.partial(prefix_kernel, heads, len(distances)),
        out_shape=[jax.ShapeDtypeStruct((rows, span + 128), BF16)] * len(distances),
        in_specs=[vmem()] * (len(distances) + 2),
        out_specs=[vmem()] * len(distances),
        compiler_params=params(8),
        name="prefix_attention",
    )(*map(held, queries), keys, values)
    got = [swap(x, "group", d, group_size) for x, d in zip(answers, distances)]
    own, live, weight = pl.pallas_call(
        functools.partial(own_kernel, heads, seq, share),
        out_shape=[
            jax.ShapeDtypeStruct((rows, span + 128), F32),
            jax.ShapeDtypeStruct((8, 128), F32),
            pltpu.VMEM(out_weight.shape, BF16),
        ],
        in_specs=[smem()] * 2 + [vmem()] * 5 + [anywhere()] * 2,
        out_specs=[vmem()] * 3,
        scratch_shapes=[pltpu.SemaphoreType.DMA((4,))],
        compiler_params=params(6),
        cost_estimate=cost(moved=8 * MIB),
        name="own_attention",
    )(
        stored(lengths),
        stored(prompt_of),
        query,
        own_keys,
        own_values,
        keys,
        values,
        stored(out_weight),
        answers[0],
    )

    def fetch(source, start, count, gate):
        return held(
            pl.pallas_call(
                functools.partial(fetch_kernel, start),
                out_shape=pltpu.VMEM((count, source.shape[1]), BF16),
                in_specs=[anywhere()] * 2,
                out_specs=vmem(),
                scratch_shapes=[pltpu.SemaphoreType.DMA((4,))],
                compiler_params=params(1),
                cost_estimate=cost(moved=count * source.shape[1] * 2),
                name="fetch",
            )(stored(source), gate)
        )

    half = depth // 2
    quarter = depth // 4
    wide = 1280 if half % 1280 == 0 else half
    block = rows // 4
    send_left, keep_left, send_right, keep_right = pl.pallas_call(
        functools.partial(project_kernel, heads, seq, wide, group_size, key_rows),
        out_shape=[
            jax.ShapeDtypeStruct((2, block, half), BF16),
            jax.ShapeDtypeStruct((2, block, half), F32),
        ]
        * 2,
        in_specs=[smem()] + [vmem()] * (2 + len(distances)),
        out_specs=[vmem()] * 4,
        scratch_shapes=[
            pltpu.VMEM((rows, span), BF16),
            pltpu.VMEM((4, block, wide), F32),
        ],
        compiler_params=params(6),
        name="project",
    )(stored(prompt_of), *map(held, (own, *got)), held(weight))

    def add(kernel, name, size, *operands):
        return pl.pallas_call(
            kernel,
            out_shape=[jax.ShapeDtypeStruct(size, F32), jax.ShapeDtypeStruct(size, BF16)],
            in_specs=[vmem()] * len(operands),
            out_specs=[vmem()] * 2,
            compiler_params=params(2),
            name=name,
        )(*map(held, operands))


    got_left = swap(send_left, "tensor", 1, tensor_size)
    got_right = swap(send_right, "tensor", 2, tensor_size)
    left, send_left = add(fold_kernel, "fold_left", (block, half), keep_left, got_left)
    right, send_right = add(fold_kernel, "fold_right", (block, half), keep_right, got_right)
    got_left = swap(send_left, "tensor", 2, tensor_size)
    got_right = swap(send_right, "tensor", 1, tensor_size)
    total, send = add(side_kernel, "side", (block, depth), left, got_left, right, got_right)
    first_quarter = fetch(lm_weight, 0, quarter, send)
    second_quarter = fetch(lm_weight, quarter, quarter, send)
    far = 4
    while 2 * far < tensor_size:
        total, send = add(
            add_kernel, "add", (block, depth), total, swap(send, "tensor", far, tensor_size)
        )
        far = 2 * far
    normed = pl.pallas_call(
        norm_kernel,
        out_shape=jax.ShapeDtypeStruct((block, depth), BF16),
        in_specs=[vmem()] * 2 + [anywhere()] * 2 + [vmem()] * 2,
        out_specs=vmem(),
        compiler_params=params(4),
        name="norm",
    )(
        *map(held, (residual.reshape(4, block, depth), gain)),
        first_quarter,
        second_quarter,
        *map(held, (total, swap(send, "tensor", far, tensor_size))),
    )

    mesh_ids = [(g, t) for g in range(group_size) for t in range(tensor_size)]
    here = [(g, x) for g in [0] + above for x in (0, 1)]
    routes = {
        (g, x): [(a * tensor_size + b, (a ^ g) * tensor_size + (b ^ x)) for a, b in mesh_ids]
        for g, x in here
    }

    def around(x):
        sent = [lax.ppermute(x, ("group", "tensor"), routes[place]) for place in here[:0:-1]]
        return [x] + sent[::-1]

    sides = [around(normed)]
    near = swap(normed, "tensor", 2, tensor_size)
    sides.append(around(near))
    third = fetch(lm_weight, 2 * quarter, quarter, near)
    blocks = [x for pair in zip(*sides) for x in pair]
    count = len(blocks) * block
    halves = pl.pallas_call(
        functools.partial(tokens_kernel, len(blocks)),
        out_shape=[jax.ShapeDtypeStruct((count, half), BF16)] * 2,
        in_specs=[vmem()] * len(blocks) + [anywhere()],
        out_specs=[vmem()] * 2,
        compiler_params=params(2),
        name="tokens",
    )(*map(held, blocks), third)
    halves = [(tokens, swap(tokens, "group", 1, group_size)) for tokens in halves]
    order = [0, 2]
    spots = [(g + c, t + x) for c in (0, 1) for g, x in here for t in order]
    total_rows = 2 * count
    narrow = 1536 if vocab % 1536 == 0 else vocab
    limit = 10 if total_rows <= 256 else 24
    work = 2 * total_rows * (half) * vocab
    first, last = pl.pallas_call(
        functools.partial(first_kernel, narrow),
        out_shape=[pltpu.VMEM((total_rows, vocab), F32), pltpu.VMEM((quarter, vocab), BF16)],
        in_specs=[vmem()] * 4 + [anywhere()],
        out_specs=[vmem()] * 2,
        scratch_shapes=[
            pltpu.VMEM((total_rows, half), BF16),
            pltpu.SemaphoreType.DMA((4,)),
        ],
        compiler_params=params(limit),
        cost_estimate=cost(flops=work),
        name="logits_first",
    )(*map(held, (*halves[0], first_quarter, second_quarter)), stored(lm_weight))
    stats = pl.pallas_call(
        functools.partial(logits_kernel, vocab, spots, tensor_size),
        out_shape=jax.ShapeDtypeStruct((group_size * tensor_size, 1, 128), F32),
        in_specs=[vmem()] * 6,
        out_specs=vmem(),
        scratch_shapes=[pltpu.VMEM((total_rows, half), BF16)]
        + [pltpu.VMEM((total_rows, 128), F32)] * 3
        + [pltpu.VMEM((total_rows, 1), i32)],
        compiler_params=params(limit),
        cost_estimate=cost(flops=work),
        name="logits",
    )(*map(held, (first, *halves[1])), wanted, held(third), held(last))

    stats = lax.all_to_all(stats, ("group", "tensor"), 0, 0, tiled=True)
    return pl.pallas_call(
        functools.partial(final_kernel, share),
        out_shape=jax.ShapeDtypeStruct((share,), F32),
        in_specs=[vmem()] * 2,
        out_specs=vmem(),
        compiler_params=params(4),
        name="final",
    )(held(live), held(stats))


def solution(mesh):
    return jax.shard_map(
        functools.partial(local, mesh.shape["group"], mesh.shape["tensor"]),
        mesh=mesh,
        in_specs=(
            P("group", "tensor"),
            P("group", "tensor"),
            P("group", "tensor"),
            P("group", "tensor"),
            P("group", "tensor"),
            P("group"),
            P("group"),
            P("group", None),
            P("tensor", None),
            P(),
            P(None, ("group", "tensor")),
            P(),
        ),
        out_specs=P(("group", "tensor")),
        check_vma=False,
    )
```
